128 devices in a mesh: dp: 8 (over z, core), head: 16 (over x, y).
Axes of the slice: x: 4, y: 4, z: 4, core: 2. Of those that a mesh axis runs over, the one named last changes fastest.
Arguments:
- tokens: bfloat16 [16, 1024, 2048], P('dp', 'head'), may hold values from -6 to 6
- cotangent: bfloat16 [16, 1024, 2048], P('dp', 'head'), may hold values from -6 to 6
- seq_lengths: int32 [16], P('dp'), may hold values from 256 to 1024, as said below
- exit_layers: int32 [16, 1024], P('dp'), may hold values from 1 to 24, as said below
- layer_index: int32 [1], replicated, may hold values from 6 to 17
- ln1_gain: float32 [2048], replicated, may hold values from 0.5 to 1.5
- ln1_shift: float32 [2048], replicated, may hold values from -4 to 4
- q_weight: float32 [2048, 2048], P('dp', 'head'), may hold values from -0.1875 to 0.1875
- q_bias: float32 [2048], replicated, may hold values from -4 to 4
- k_weight: float32 [2048, 2048], P('dp', 'head'), may hold values from -0.1875 to 0.1875
- v_weight: float32 [2048, 2048], P('dp', 'head'), may hold values from -0.125 to 0.125
- v_bias: float32 [2048], replicated, may hold values from -4 to 4
- out_weight: float32 [2048, 2048], P('dp', 'head'), may hold values from -0.5 to 0.5
- out_bias: float32 [2048], replicated, may hold values from -4 to 4
- ln2_gain: float32 [2048], replicated, may hold values from 0.5 to 1.5
- ln2_shift: float32 [2048], replicated, may hold values from -4 to 4
- up_weight: float32 [2048, 8192], P('dp', 'head'), may hold values from -0.125 to 0.125
- up_bias: float32 [8192], replicated, may hold values from -6 to 6
- down_weight: float32 [2048, 8192], P('dp', 'head'), may hold values from -0.0625 to 0.0625
- down_bias: float32 [2048], replicated, may hold values from -4 to 4
Outputs:
- result: bfloat16 [16, 1024, 2048], P('dp', 'head')
- grad_tokens: float32 [16, 1024, 2048], P('dp', 'head')
- grad_ln1_gain: float32 [2048], replicated
- grad_ln1_shift: float32 [2048], replicated
- grad_q_weight: float32 [2048, 2048], P('dp', 'head')
- grad_q_bias: float32 [2048], replicated
- grad_k_weight: float32 [2048, 2048], P('dp', 'head')
- grad_v_weight: float32 [2048, 2048], P('dp', 'head')
- grad_v_bias: float32 [2048], replicated
- grad_out_weight: float32 [2048, 2048], P('dp', 'head')
- grad_out_bias: float32 [2048], replicated
- grad_ln2_gain: float32 [2048], replicated
- grad_ln2_shift: float32 [2048], replicated
- grad_up_weight: float32 [2048, 8192], P('dp', 'head')
- grad_up_bias: float32 [8192], replicated
- grad_down_weight: float32 [2048, 8192], P('dp', 'head')
- grad_down_bias: float32 [2048], replicated
The draws below stay inside these ranges and needn't reach their ends.
Inputs may be any that keep to these rules, and one draw needn't show every extreme that they name: `seq_lengths`: in the 2 sequences of each dp index one has 1024 tokens and exit layer 24 at every position. `exit_layers`: every other sequence's exit layers fall linearly over its own length: max(1, 24 - floor(p * r / length)) at position p, with a whole r of 12 to 23 of its own.
All inputs are finite; a program needn't handle non-finite values.
Results may differ from the reference program's by a relative error of at most 0.022.
Values may be sent and summed in bfloat16 or wider, within the bound.
No kernel may reach another device: no remote copies, remote signals or barrier semaphores. Data moves between devices by JAX's collectives and lax.ppermute only.
A program may use at most 384 MiB of HBM per device.

```python
from functools import partial
import jax
import jax.numpy as jnp
from jax import lax

D = 2048
HEADS = 32
HEAD_DIM = 64
FF = 8192
LAYERS = 24
LEN = 1024
SEQS = 2
BATCH = 16
MIN_LEN = 256


def chosen_rows(key):
    groups = BATCH // SEQS
    picked = jax.random.randint(jax.random.fold_in(key, 11), (groups,), 0, SEQS)
    return (jnp.arange(SEQS)[None, :] == picked[:, None]).reshape(BATCH)


def length_rows(key):
    marked = chosen_rows(key)
    key_first, key_second = jax.random.split(jax.random.fold_in(key, 13))
    halvings = jax.random.randint(key_first, (BATCH,), 0, 4)
    spread_len = jnp.right_shift(jnp.full((BATCH,), LEN - MIN_LEN, jnp.int32), halvings)
    extra_len = jax.random.randint(key_second, (BATCH,), 0, spread_len + 1)
    return (marked, jnp.where(marked, LEN, MIN_LEN + extra_len).astype(jnp.int32))


def draw_seq_lengths(key, part):
    marked, lengths = length_rows(key)
    return lengths


def draw_exit_layers(key, part):
    marked, lengths = length_rows(key)
    key = jax.random.fold_in(key, 2)
    drop_rate = jax.random.randint(key, (BATCH,), LAYERS // 2, LAYERS)
    drop_rate = jnp.where(marked, 0, drop_rate)
    positions = jnp.arange(LEN, dtype=jnp.int32)
    fallen = LAYERS - positions[None, :] * drop_rate[:, None] // lengths[:, None]
    return jnp.maximum(fallen, 1).astype(jnp.int32)


def shard_levels(stream_key, dims, shards, smallest, top_value):
    def one(position, parts):
        heights = jax.random.uniform(jax.random.fold_in(jax.random.fold_in(stream_key, 6), position), (parts,), jnp.float32, smallest / len(shards), top_value / len(shards))
        return jnp.repeat(jnp.exp(heights), dims[position] // parts).reshape((-1,) + (1,) * (len(dims) - position - 1))

    gain = one(*shards[0])
    for cut in shards[1:]:
        gain = gain * one(*cut)
    return gain


def gaussian(rng, shape, scale, limit, shards=(), held_as=jnp.bfloat16):
    drawn = scale * jax.random.normal(rng, shape, jnp.float32)
    if shards:
        drawn = drawn * shard_levels(rng, shape, shards, -0.22, 0.18)
    return jnp.clip(drawn, -limit, limit).astype(held_as)


def setup_inputs(seed: int = 0) -> dict:
    arg_keys = jax.random.split(jax.random.key(seed), 21)
    return {
        "tokens": gaussian(arg_keys[0], (BATCH, LEN, D), 1.0, 6.0, ((0, 8), (1, 16))),
        "cotangent": gaussian(arg_keys[1], (BATCH, LEN, D), 1.0, 6.0, ((0, 8), (1, 16))),
        "seq_lengths": draw_seq_lengths(jax.random.fold_in(arg_keys[20], 71), 0),
        "exit_layers": draw_exit_layers(jax.random.fold_in(arg_keys[20], 71), 0),
        "layer_index": jax.random.randint(arg_keys[4], (1,), LAYERS // 4, 3 * LAYERS // 4).astype(jnp.int32),
        "ln1_gain": jnp.clip(1.0 + 0.1 * jax.random.normal(arg_keys[5], (D,), jnp.float32), 0.5, 1.5),
        "ln1_shift": gaussian(arg_keys[6], (D,), 0.3, 4.0, (), jnp.float32),
        "q_weight": gaussian(arg_keys[7], (D, D), (D // 2) ** -0.5, 0.1875, ((0, 8), (1, 16)), jnp.float32),
        "q_bias": gaussian(arg_keys[8], (D,), 0.3, 4.0, (), jnp.float32),
        "k_weight": gaussian(arg_keys[9], (D, D), (D // 2) ** -0.5, 0.1875, ((0, 8), (1, 16)), jnp.float32),
        "v_weight": gaussian(arg_keys[10], (D, D), D ** -0.5, 0.125, ((0, 8), (1, 16)), jnp.float32),
        "v_bias": gaussian(arg_keys[11], (D,), 0.3, 4.0, (), jnp.float32),
        "out_weight": gaussian(arg_keys[12], (D, D), (D // 16) ** -0.5, 0.5, ((0, 8), (1, 16)), jnp.float32),
        "out_bias": gaussian(arg_keys[13], (D,), 0.3, 4.0, (), jnp.float32),
        "ln2_gain": jnp.clip(1.0 + 0.1 * jax.random.normal(arg_keys[14], (D,), jnp.float32), 0.5, 1.5),
        "ln2_shift": gaussian(arg_keys[15], (D,), 0.3, 4.0, (), jnp.float32),
        "up_weight": gaussian(arg_keys[16], (D, FF), D ** -0.5, 0.125, ((0, 8), (1, 16)), jnp.float32),
        "up_bias": gaussian(arg_keys[17], (FF,), 0.5, 6.0, (), jnp.float32),
        "down_weight": gaussian(arg_keys[18], (D, FF), FF ** -0.5, 0.0625, ((0, 8), (1, 16)), jnp.float32),
        "down_bias": gaussian(arg_keys[19], (D,), 0.3, 4.0, (), jnp.float32),
    }


@jax.custom_vjp
def low(v):
    return lax.optimization_barrier(v.astype(jnp.bfloat16)).astype(jnp.float32)

@jax.custom_vjp
def low_back(v):
    return v

def low_keep(v):
    return (low(v), None)

def low_pass(kept, grad):
    return (grad,)

def back_keep(v):
    return (v, None)

def back_low(kept, grad):
    return (low(grad),)
low.defvjp(low_keep, low_pass)
low_back.defvjp(back_keep, back_low)

def round_both(value_in):
    return low_back(low(value_in))

def highest(left_side, right_side):
    return jnp.dot(left_side, right_side, precision=lax.Precision.HIGHEST)

def layer_norm(values, gain_vec, shift_vec):
    average = lax.optimization_barrier(jnp.mean(values, -1, keepdims=True))
    centered = values - average
    spread = lax.optimization_barrier(jnp.mean(centered * centered, -1, keepdims=True))
    return centered * lax.rsqrt(spread + 1e-05) * gain_vec + shift_vec

def attend_one(packed):
    query_rows, key_rows, value_rows, live_keys = packed
    seq_len = query_rows.shape[0]
    q_heads = query_rows.reshape(seq_len, HEADS, HEAD_DIM)
    k_heads = key_rows.reshape(seq_len, HEADS, HEAD_DIM)
    v_heads = value_rows.reshape(seq_len, HEADS, HEAD_DIM)
    scores = jnp.einsum('qhd,khd->hqk', q_heads, k_heads, precision=lax.Precision.HIGHEST) * HEAD_DIM ** (-0.5)
    scores = low_back(scores)
    places = jnp.arange(seq_len)
    allowed = (places[None, :] <= places[:, None]) & live_keys[None, :]
    scores = jnp.where(allowed[None], scores, -1000000000.0)
    maximum = lax.optimization_barrier(jnp.max(scores, -1, keepdims=True))
    exp_terms = jnp.exp(scores - maximum)
    prob_rows = exp_terms / lax.optimization_barrier(jnp.sum(exp_terms, -1, keepdims=True))
    mixed_heads = jnp.einsum('hqk,khd->qhd', low(prob_rows), v_heads, precision=lax.Precision.HIGHEST)
    return mixed_heads.reshape(seq_len, HEADS * HEAD_DIM)

def forward(live_rows, inputs, ln1_gain, ln1_shift, q_weight, q_bias, k_weight, v_weight, v_bias, out_weight, out_bias, ln2_gain, ln2_shift, up_weight, up_bias, down_weight, down_bias):
    keep_rows = live_rows.reshape(-1, 1).astype(inputs.dtype)
    flat_rows = inputs.reshape(-1, D)
    norm1 = low(layer_norm(flat_rows, ln1_gain, ln1_shift))
    query_proj = round_both(highest(norm1, low(q_weight)) + q_bias)
    key_proj = round_both(highest(norm1, low(k_weight)))
    value_proj = round_both(highest(norm1, low(v_weight)) + v_bias)
    mixed_heads = lax.map(jax.checkpoint(attend_one), (query_proj.reshape(BATCH, LEN, D), key_proj.reshape(BATCH, LEN, D), value_proj.reshape(BATCH, LEN, D), live_rows))
    heads_out = round_both(mixed_heads.reshape(-1, D))
    branch_one = low_back(highest(heads_out, low(out_weight).T) + out_bias)
    middle = flat_rows + keep_rows * branch_one
    norm2 = low(layer_norm(middle, ln2_gain, ln2_shift))
    up_proj = low_back(highest(norm2, low(up_weight)) + up_bias)
    hidden = low(jax.nn.gelu(up_proj, approximate=False))
    branch_two = low_back(highest(hidden, low(down_weight).T) + down_bias)
    return (middle + keep_rows * branch_two).reshape(inputs.shape)

def reference(tokens, cotangent, seq_lengths, exit_layers, layer_index, ln1_gain, ln1_shift, q_weight, q_bias, k_weight, v_weight, v_bias, out_weight, out_bias, ln2_gain, ln2_shift, up_weight, up_bias, down_weight, down_bias):
    places = jnp.arange(LEN)
    live_rows = (places[None, :] < seq_lengths[:, None]) & (exit_layers > layer_index[0])
    inputs = tokens.astype(jnp.float32)
    params = (ln1_gain, ln1_shift, q_weight, q_bias, k_weight, v_weight, v_bias, out_weight, out_bias, ln2_gain, ln2_shift, up_weight, up_bias, down_weight, down_bias)
    result, pullback = jax.vjp(partial(forward, live_rows), inputs, *params)
    gradients = pullback(cotangent.astype(jnp.float32))
    return (result.astype(jnp.bfloat16), gradients[0], gradients[1], gradients[2], gradients[3], gradients[4], gradients[5], gradients[6], gradients[7], gradients[8], gradients[9], gradients[10], gradients[11], gradients[12], gradients[13], gradients[14], gradients[15])
```

```python
from functools import partial

import jax
import jax.numpy as jnp
from jax import lax
from jax.experimental import pallas as pl
from jax.experimental.pallas import tpu as pltpu
from jax.sharding import Mesh
from jax.sharding import PartitionSpec as P

HEAD_DIM = 64
SPAN = 256
LOW = jnp.bfloat16
WIDE = jnp.float32
RING = 4
ROWS = ("z", "c")
COLS = ("x", "y")


def dot(left, right):
    return jnp.dot(left, right, preferred_element_type=WIDE)


def dot_t(left, right):
    return lax.dot_general(left, right, (((1,), (1,)), ((), ())), preferred_element_type=WIDE)


def dot_0(left, right):
    return lax.dot_general(left, right, (((0,), (0,)), ((), ())), preferred_element_type=WIDE)


def call(body, out_shape, grid, in_specs, out_specs, flops, traffic, scratch=(), prefetch=0, vmem=40):
    return pl.pallas_call(
        body,
        out_shape=out_shape,
        grid_spec=pltpu.PrefetchScalarGridSpec(
            num_scalar_prefetch=prefetch,
            grid=grid,
            in_specs=in_specs,
            out_specs=out_specs,
            scratch_shapes=list(scratch),
        ),
        compiler_params=pltpu.CompilerParams(vmem_limit_bytes=vmem * 2**20),
        cost_estimate=pl.CostEstimate(flops=flops, bytes_accessed=traffic, transcendentals=0),
    )


def whole(shape):
    return pl.BlockSpec(shape, lambda *_: (0,) * len(shape))


def struct(shape, dtype):
    return jax.ShapeDtypeStruct(shape, dtype)


def spread(array, axes, size):
    return lax.all_to_all(jnp.broadcast_to(array[None], (size,) + array.shape), axes, 0, 0)


def collect(parts, axes):
    return jnp.sum(lax.all_to_all(parts, axes, 0, 0).astype(WIDE), 0)


def swap(parts, axes):
    return lax.all_to_all(parts, axes, 0, 0)


def gather_weight(shard):
    full = lax.all_gather(shard, ("z", "c", "x"), axis=0)
    return full.reshape((8, 4) + shard.shape)


def settle(gradient):
    total = lax.psum_scatter(
        gradient.reshape((32,) + gradient.shape[2:]), ("z", "c", "x"), scatter_dimension=0
    )
    return total.astype(WIDE)


def qkv_body(rows_ref, weight_ref, bias_ref, out_ref):
    weight = weight_ref[...].reshape(rows_ref.shape[1], -1)
    out_ref[...] = (dot(rows_ref[...], weight) + bias_ref[...]).astype(LOW)


def qkv_project(rows, weight, bias):
    count, width = rows.shape
    zc, xs, piece, cols = weight.shape
    return call(
        qkv_body,
        struct((xs, count, cols), LOW),
        (xs,),
        [
            whole((count, width)),
            pl.BlockSpec((zc, None, piece, cols), lambda i: (0, i, 0, 0)),
            pl.BlockSpec((None, 1, cols), lambda i: (i, 0, 0)),
        ],
        pl.BlockSpec((None, count, cols), lambda i: (i, 0, 0)),
        2 * count * width * xs * cols,
        10 * 2**20,
    )(rows, weight, bias)


def out_body(heads_ref, weight_ref, out_ref, joined):
    @pl.when(pl.program_id(0) == 0)
    def _():
        joined[...] = jnp.concatenate([heads_ref[i] for i in range(RING)], 1)

    weight = jnp.concatenate([weight_ref[i] for i in range(RING)], 1)
    out_ref[...] = dot_t(joined[...], weight).astype(LOW)


def out_project(heads, weight):
    xs, count, cols = heads.shape
    zc, _, piece, _ = weight.shape
    return call(
        out_body,
        struct((count, zc * piece), LOW),
        (zc,),
        [
            whole(heads.shape),
            pl.BlockSpec((None, xs, piece, cols), lambda i: (i, 0, 0, 0)),
        ],
        pl.BlockSpec((count, piece), lambda i: (0, i)),
        2 * count * zc * piece * xs * cols,
        5 * 2**20,
        scratch=[pltpu.VMEM((count, xs * cols), LOW)],
    )(heads, weight)


def heads_grad_body(rows_ref, weight_ref, out_ref):
    weight = weight_ref[...].reshape(rows_ref.shape[1], -1)
    out_ref[...] = dot(rows_ref[...], weight).astype(LOW)


def heads_grad(rows, weight):
    count, width = rows.shape
    zc, xs, piece, cols = weight.shape
    return call(
        heads_grad_body,
        struct((xs, count, cols), LOW),
        (xs,),
        [
            whole((count, width)),
            pl.BlockSpec((zc, None, piece, cols), lambda i: (0, i, 0, 0)),
        ],
        pl.BlockSpec((None, count, cols), lambda i: (i, 0, 0)),
        2 * count * width * xs * cols,
        5 * 2**20,
    )(rows, weight)


def out_weight_body(rows_ref, heads_ref, out_ref):
    out_ref[...] = dot_0(rows_ref[...], heads_ref[...]).astype(LOW).reshape(out_ref.shape)


def out_weight_grad(rows, heads):
    count, width = rows.shape
    xs, _, cols = heads.shape
    piece = width // 8
    return call(
        out_weight_body,
        struct((8, xs, piece, cols), LOW),
        (xs,),
        [whole((count, width)), pl.BlockSpec((None, count, cols), lambda i: (i, 0, 0))],
        pl.BlockSpec((8, None, piece, cols), lambda i: (0, i, 0, 0)),
        2 * count * width * xs * cols,
        5 * 2**20,
    )(rows, heads)


def qkv_grad_body(norm_ref, grad_ref, weight_ref, weight_grad_ref, norm_grad_ref, total):
    step = pl.program_id(0)
    grad = grad_ref[...]
    weight_grad_ref[...] = dot_0(norm_ref[...], grad).astype(LOW).reshape(weight_grad_ref.shape)
    term = dot_t(grad, weight_ref[...].reshape(norm_ref.shape[1], -1))

    @pl.when(step == 0)
    def _():
        total[...] = term

    @pl.when(step > 0)
    def _():
        total[...] += term

    @pl.when(step == RING - 1)
    def _():
        norm_grad_ref[...] = total[...].astype(LOW)


def qkv_grad(norm_rows, grads, weight):
    count, width = norm_rows.shape
    zc, xs, piece, cols = weight.shape
    block = pl.BlockSpec((zc, None, piece, cols), lambda i: (0, i, 0, 0))
    return call(
        qkv_grad_body,
        (struct(weight.shape, LOW), struct((count, width), LOW)),
        (xs,),
        [whole((count, width)), pl.BlockSpec((None, count, cols), lambda i: (i, 0, 0)), block],
        (block, whole((count, width))),
        4 * count * width * xs * cols,
        20 * 2**20,
        scratch=[pltpu.VMEM((count, width), WIDE)],
    )(norm_rows, grads, weight)


def ffn_body(
    norm_ref, cot_ref, up_ref, down_ref, bias_ref,
    branch_ref, norm_grad_ref, weight_grad_ref, bias_grad_ref,
    branch_total, norm_total,
):
    step = pl.program_id(0)
    width = norm_ref.shape[1]
    cols = up_ref.shape[-1]
    up_w = up_ref[...].reshape(width, cols)
    down_w = down_ref[...].reshape(width, cols)
    up = dot(norm_ref[...], up_w) + bias_ref[...]
    normal = 0.5 * (1.0 + lax.erf(up * 0.7071067811865476))
    hidden = (up * normal).astype(LOW)
    slope = normal + up * (jnp.exp(-0.5 * up * up) * 0.3989422804014327)
    grad_up = (dot(cot_ref[...], down_w) * slope).astype(LOW)
    branch = dot_t(hidden, down_w)
    norm_grad = dot_t(grad_up, up_w)

    @pl.when(step == 0)
    def _():
        branch_total[...] = branch
        norm_total[...] = norm_grad

    @pl.when(step > 0)
    def _():
        branch_total[...] += branch
        norm_total[...] += norm_grad

    half = step % 2
    size = weight_grad_ref.shape[-1] // 4
    zc, piece, _ = weight_grad_ref.shape
    weight_grad_ref[:, :, pl.ds(pl.multiple_of(half * size, size), size)] = (
        dot_0(norm_ref[...], grad_up).astype(LOW).reshape(zc, piece, cols)
    )
    weight_grad_ref[:, :, pl.ds(pl.multiple_of((half + 2) * size, size), size)] = (
        dot_0(cot_ref[...], hidden).astype(LOW).reshape(zc, piece, cols)
    )
    bias_grad_ref[...] = jnp.sum(grad_up.astype(WIDE), 0, keepdims=True)

    @pl.when(step == pl.num_programs(0) - 1)
    def _():
        branch_ref[...] = branch_total[...].astype(LOW)
        norm_grad_ref[...] = norm_total[...].astype(LOW)


def feed_forward(norm_rows, cot_rows, weight, bias):
    count, width = norm_rows.shape
    zc, xs, piece, cols = weight.shape
    size = cols // 4
    steps = 2 * xs
    return call(
        ffn_body,
        (
            struct((count, width), LOW),
            struct((count, width), LOW),
            struct(weight.shape, LOW),
            struct((steps, 1, size), WIDE),
        ),
        (steps,),
        [
            whole((count, width)),
            whole((count, width)),
            pl.BlockSpec((zc, None, piece, size), lambda i: (0, i // 2, 0, i % 2)),
            pl.BlockSpec((zc, None, piece, size), lambda i: (0, i // 2, 0, 2 + i % 2)),
            pl.BlockSpec((None, 1, size), lambda i: (i, 0, 0)),
        ],
        (
            whole((count, width)),
            whole((count, width)),
            pl.BlockSpec((zc, None, piece, cols), lambda i: (0, i // 2, 0, 0)),
            pl.BlockSpec((None, 1, size), lambda i: (i, 0, 0)),
        ),
        12 * count * width * steps * size,
        40 * 2**20,
        scratch=[pltpu.VMEM((count, width), WIDE), pltpu.VMEM((count, width), WIDE)],
        vmem=56,
    )(norm_rows, cot_rows, weight, weight, bias)


def only_head(array, head):
    lane = lax.broadcasted_iota(jnp.int32, array.shape, 1)
    return jnp.where(lane // HEAD_DIM == head, array, jnp.zeros_like(array))


def allowed_keys(start, extent, live_count):
    q_place = start + lax.broadcasted_iota(jnp.int32, (SPAN, extent), 0)
    k_place = lax.broadcasted_iota(jnp.int32, (SPAN, extent), 1)
    return k_place <= jnp.minimum(q_place, live_count - 1)


def attend_body(live_ref, qkv_ref, heads_ref, exact_ref, log_ref):
    live_count = live_ref[pl.program_id(0)]
    length = exact_ref.shape[0]
    width = exact_ref.shape[1]
    qkv = qkv_ref[...].reshape(length, 3 * width)
    key = qkv[:, width : 2 * width]
    value = qkv[:, 2 * width :]
    per_x = SPAN // heads_ref.shape[2]
    for span in range(length // SPAN):
        start, extent = span * SPAN, (span + 1) * SPAN
        here = slice(start, extent)

        @pl.when(start < live_count)
        def _():
            query = qkv[here, :width]
            allowed = allowed_keys(start, extent, live_count)
            mixed, logs = [], []
            for head in range(width // HEAD_DIM):
                scores = dot_t(only_head(query, head), key[:extent]) * HEAD_DIM**-0.5
                scores = jnp.where(allowed, scores, -1e9)
                top = jnp.max(scores, 1, keepdims=True)
                terms = jnp.exp(scores - top)
                denom = jnp.sum(terms, 1, keepdims=True)
                mixed.append(dot(terms.astype(LOW), value[:extent]) / denom)
                logs.append(top + jnp.log(denom))
            lane = lax.broadcasted_iota(jnp.int32, (SPAN, width), 1)
            out = jnp.where(lane < HEAD_DIM, mixed[0], mixed[1])
            exact_ref[here] = out
            log_ref[here] = jnp.where(lane < HEAD_DIM, logs[0], logs[1])
            heads_ref[span] = out.astype(LOW).reshape(heads_ref.shape[1:])

        @pl.when(start >= live_count)
        def _():
            exact_ref[here] = jnp.zeros((SPAN, width), WIDE)
            log_ref[here] = jnp.zeros((SPAN, width), WIDE)
            heads_ref[span] = jnp.zeros(heads_ref.shape[1:], LOW)


def row_block(rows, cols):
    return pl.BlockSpec((4, 4, None, rows, cols), lambda s, *_: (0, 0, s, 0, 0))


def attend(live_counts, qkv, width):
    xs, ys, seqs, rows, _ = qkv.shape
    length = xs * ys * rows
    flat = pl.BlockSpec((None, length, width), lambda s, *_: (s, 0, 0))
    return call(
        attend_body,
        (
            struct((xs, ys, seqs, rows, width), LOW),
            struct((seqs, length, width), WIDE),
            struct((seqs, length, width), WIDE),
        ),
        (seqs,),
        [row_block(rows, 3 * width)],
        (row_block(rows, width), flat, flat),
        4 * 10**9,
        4 * 2**20,
        prefetch=1,
    )(live_counts, qkv)


def attend_back_body(
    live_ref, qkv_ref, grad_ref, exact_ref, log_ref, out_ref, sum_ref, key_total, value_total
):
    live_count = live_ref[pl.program_id(0)]
    length, width = exact_ref.shape
    factor = HEAD_DIM**-0.5
    qkv = qkv_ref[...].reshape(length, 3 * width)
    grads = grad_ref[...].reshape(length, width)
    key = qkv[:, width : 2 * width]
    value = qkv[:, 2 * width :]
    key_total[...] = jnp.zeros_like(key_total)
    value_total[...] = jnp.zeros_like(value_total)
    sum_ref[...] = jnp.zeros_like(sum_ref)
    piece = out_ref.shape[1:3]
    for span in range(length // SPAN):
        start, extent = span * SPAN, (span + 1) * SPAN
        here = slice(start, extent)

        @pl.when(start < live_count)
        def _():
            query = qkv[here, :width]
            grad = grads[here]
            inner = grad.astype(WIDE) * exact_ref[here]
            logs = log_ref[here]
            allowed = allowed_keys(start, extent, live_count)
            query_total = jnp.zeros((SPAN, width), WIDE)
            for head in range(width // HEAD_DIM):
                query_h = only_head(query, head)
                grad_h = only_head(grad, head)
                log_h = logs[:, head * HEAD_DIM : head * HEAD_DIM + 1]
                row_inner = jnp.sum(only_head(inner, head), 1, keepdims=True)
                scores = dot_t(query_h, key[:extent]) * factor
                probs = jnp.exp(jnp.where(allowed, scores, -1e9) - log_h)
                d_probs = dot_t(grad_h, value[:extent])
                value_total[:extent] += dot_0(probs.astype(LOW), grad_h)
                d_scores = (probs * (d_probs - row_inner)).astype(LOW)
                query_total += dot(d_scores, only_head(key[:extent], head))
                key_total[:extent] += dot_0(d_scores, query_h)
            out = (query_total * factor).astype(LOW)
            out_ref[span, :, :, :width] = out.reshape(piece + (width,))
            sum_ref[:, :width] += jnp.sum(out.astype(WIDE), 0, keepdims=True)

        @pl.when(start >= live_count)
        def _():
            out_ref[span, :, :, :width] = jnp.zeros(piece + (width,), LOW)

    whole_shape = out_ref.shape[:3] + (width,)
    out_ref[:, :, :, width : 2 * width] = (
        (key_total[...] * factor).astype(LOW).reshape(whole_shape)
    )
    out = value_total[...].astype(LOW)
    out_ref[:, :, :, 2 * width :] = out.reshape(whole_shape)
    sum_ref[:, 2 * width :] = jnp.sum(out.astype(WIDE), 0, keepdims=True)


def attend_back(live_counts, qkv, grads, exact, logs):
    xs, ys, seqs, rows, _ = qkv.shape
    _, length, width = exact.shape
    flat = pl.BlockSpec((None, length, width), lambda s, *_: (s, 0, 0))
    return call(
        attend_back_body,
        (struct(qkv.shape, LOW), struct((seqs, 1, 3 * width), WIDE)),
        (seqs,),
        [row_block(rows, 3 * width), row_block(rows, width), flat, flat],
        (
            row_block(rows, 3 * width),
            pl.BlockSpec((None, 1, 3 * width), lambda s, *_: (s, 0, 0)),
        ),
        8 * 10**9,
        8 * 2**20,
        scratch=[pltpu.VMEM((length, width), WIDE), pltpu.VMEM((length, width), WIDE)],
        prefetch=1,
        vmem=48,
    )(live_counts, qkv, grads, exact, logs)


def norm_parts(values, gain_vec, shift_vec):
    average = jnp.mean(values, -1, keepdims=True)
    centered = values - average
    inverse = lax.rsqrt(jnp.mean(centered * centered, -1, keepdims=True) + 1e-05)
    unit_rows = centered * inverse
    return (unit_rows * gain_vec + shift_vec, unit_rows, inverse)


def norm_back(gradient, unit_rows, inverse, gain_vec):
    scaled = gradient * gain_vec
    return inverse * (
        scaled
        - jnp.mean(scaled, -1, keepdims=True)
        - unit_rows * jnp.mean(scaled * unit_rows, -1, keepdims=True)
    )


def vector_totals(vectors):
    flat = jnp.concatenate([v.reshape(-1) for v in vectors])
    part = collect(flat.reshape(16, -1, 128), COLS)
    part = jnp.sum(spread(part, ROWS, 8), 0)
    flat = spread(part, COLS, 16).reshape(-1)
    totals, start = [], 0
    for v in vectors:
        totals.append(flat[start : start + v.size])
        start += v.size
    return totals


def shards(
    tokens, cotangent, seq_lengths, exit_layers, layer_index,
    ln1_gain, ln1_shift, q_weight, q_bias, k_weight, v_weight, v_bias, out_weight, out_bias,
    ln2_gain, ln2_shift, up_weight, up_bias, down_weight, down_bias,
):
    seqs, own_rows, width = tokens.shape
    own = seqs * own_rows
    full_len = exit_layers.shape[1]
    x_at, y_at = lax.axis_index("x"), lax.axis_index("y")
    head_at = x_at * RING + y_at
    head_cols = q_weight.shape[1]
    ff_cols = up_weight.shape[1]

    positions = jnp.arange(full_len)
    live_all = (positions[None, :] < seq_lengths[:, None]) & (exit_layers > layer_index[0])
    live_counts = jnp.sum(live_all.astype(jnp.int32), 1)
    live_mine = lax.dynamic_slice_in_dim(live_all, head_at * own_rows, own_rows, 1)
    keep = live_mine.reshape(-1, 1).astype(WIDE)

    w_qkv = gather_weight(jnp.concatenate([q_weight, k_weight, v_weight], 1).astype(LOW))
    w_out = gather_weight(out_weight.astype(LOW))
    w_ff = gather_weight(jnp.concatenate([up_weight, down_weight], 1).astype(LOW))

    inputs = tokens.astype(WIDE).reshape(own, width)
    normed1, unit1, inverse1 = norm_parts(inputs, ln1_gain, ln1_shift)
    norm1 = spread(normed1.astype(LOW), "y", RING).reshape(RING * own, width)
    grad_y = cotangent.astype(WIDE).reshape(own, width)
    g_ffn = (keep * grad_y).astype(LOW)
    cot_rows = spread(g_ffn, "y", RING).reshape(RING * own, width)

    def mine(vector, cols):
        return lax.dynamic_index_in_dim(vector.reshape(RING, RING, cols), y_at, 1, False)

    bias = jnp.concatenate(
        [mine(q_bias, head_cols), jnp.zeros((RING, head_cols), WIDE), mine(v_bias, head_cols)], 1
    ).reshape(RING, 1, 3 * head_cols)
    qkv = qkv_project(norm1, w_qkv, bias)
    rows5 = (RING, RING, seqs, own_rows)
    qkv = swap(qkv, "x").reshape(rows5 + (3 * head_cols,))
    heads, exact, logs = attend(live_counts, qkv, head_cols)
    heads = swap(heads.reshape(RING, RING * own, head_cols), "x")
    branch1 = collect(out_project(heads, w_out).reshape(RING, own, width), "y") + out_bias
    middle = inputs + keep * branch1
    normed2, unit2, inverse2 = norm_parts(middle, ln2_gain, ln2_shift)
    norm2 = spread(normed2.astype(LOW), "y", RING).reshape(RING * own, width)

    ff_bias = mine(up_bias, ff_cols).reshape(2 * RING, 1, ff_cols // 2)
    branch2, g_norm2, ff_grad, up_bias_part = feed_forward(norm2, cot_rows, w_ff, ff_bias)
    g_norm2 = collect(g_norm2.reshape(RING, own, width), "y")
    ff_grad = settle(ff_grad)
    grad_mid = grad_y + norm_back(g_norm2, unit2, inverse2, ln2_gain)
    g_attn = (keep * grad_mid).astype(LOW)
    attn_rows = spread(g_attn, "y", RING).reshape(RING * own, width)
    g_heads = swap(heads_grad(attn_rows, w_out), "x").reshape(rows5 + (head_cols,))
    out_grad = settle(out_weight_grad(attn_rows, heads))
    d_qkv, d_sums = attend_back(live_counts, qkv, g_heads, exact, logs)
    d_qkv = swap(d_qkv.reshape(RING, RING * own, 3 * head_cols), "x")
    qkv_weight_grad, g_norm1 = qkv_grad(norm1, d_qkv, w_qkv)
    qkv_weight_grad = settle(qkv_weight_grad)
    g_norm1 = collect(g_norm1.reshape(RING, own, width), "y")
    grad_tokens = (grad_mid + norm_back(g_norm1, unit1, inverse1, ln1_gain)).reshape(tokens.shape)

    branch2 = collect(branch2.reshape(RING, own, width), "y") + down_bias
    result = (middle + keep * branch2).astype(LOW).reshape(tokens.shape)

    d_sums = jnp.sum(d_sums, 0).reshape(3, head_cols)

    def placed(row):
        blank = jnp.zeros((RING * RING, head_cols), WIDE)
        return lax.dynamic_update_slice_in_dim(blank, row[None], head_at, 0)

    up_bias_full = lax.dynamic_update_slice_in_dim(
        jnp.zeros((RING, RING, ff_cols), WIDE), up_bias_part.reshape(RING, 1, ff_cols), y_at, 1
    )
    totals = vector_totals(
        (
            jnp.sum(g_norm1 * unit1, 0),
            jnp.sum(g_norm1, 0),
            placed(d_sums[0]),
            placed(d_sums[2]),
            jnp.sum(g_attn.astype(WIDE), 0),
            jnp.sum(g_norm2 * unit2, 0),
            jnp.sum(g_norm2, 0),
            up_bias_full,
            jnp.sum(g_ffn.astype(WIDE), 0),
        )
    )
    return (
        result,
        grad_tokens,
        totals[0],
        totals[1],
        qkv_weight_grad[:, :head_cols],
        totals[2],
        qkv_weight_grad[:, head_cols : 2 * head_cols],
        qkv_weight_grad[:, 2 * head_cols :],
        totals[3],
        out_grad,
        totals[4],
        totals[5],
        totals[6],
        ff_grad[:, :ff_cols],
        totals[7],
        ff_grad[:, ff_cols:],
        totals[8],
    )


def solution(mesh):
    wide = Mesh(mesh.devices.reshape(4, 2, 4, 4), ("z", "c", "x", "y"))
    act = P(ROWS, COLS, None)
    weight = P(ROWS, COLS)
    vector = P()
    in_specs = (
        act, act, P(ROWS), P(ROWS, None), vector, vector, vector,
        weight, vector, weight, weight, vector, weight, vector, vector, vector,
        weight, vector, weight, vector,
    )
    out_specs = (
        act, act, vector, vector, weight, vector, weight, weight, vector, weight,
        vector, vector, vector, weight, vector, weight, vector,
    )
    return jax.shard_map(
        shards, mesh=wide, in_specs=in_specs, out_specs=out_specs, check_vma=False
    )
```

```python
from functools import partial

import jax
import jax.numpy as jnp
from jax import lax
from jax.experimental import pallas as pl
from jax.experimental.pallas import tpu as pltpu
from jax.sharding import Mesh
from jax.sharding import PartitionSpec as P

HEAD_DIM = 64
SPAN = 256
LOW = jnp.bfloat16
WIDE = jnp.float32
RING = 4
ROWS = ("z", "c")
COLS = ("x", "y")


def dot(left, right):
    return jnp.dot(left, right, preferred_element_type=WIDE)


def dot_t(left, right):
    return lax.dot_general(left, right, (((1,), (1,)), ((), ())), preferred_element_type=WIDE)


def dot_0(left, right):
    return lax.dot_general(left, right, (((0,), (0,)), ((), ())), preferred_element_type=WIDE)


def call(body, out_shape, grid, in_specs, out_specs, flops, traffic, scratch=(), prefetch=0, vmem=40):
    return pl.pallas_call(
        body,
        out_shape=out_shape,
        grid_spec=pltpu.PrefetchScalarGridSpec(
            num_scalar_prefetch=prefetch,
            grid=grid,
            in_specs=in_specs,
            out_specs=out_specs,
            scratch_shapes=list(scratch),
        ),
        compiler_params=pltpu.CompilerParams(vmem_limit_bytes=vmem * 2**20),
        cost_estimate=pl.CostEstimate(flops=flops, bytes_accessed=traffic, transcendentals=0),
    )


def whole(shape):
    return pl.BlockSpec(shape, lambda *_: (0,) * len(shape))


def struct(shape, dtype):
    return jax.ShapeDtypeStruct(shape, dtype)


def spread(array, axes, size):
    return lax.all_to_all(jnp.broadcast_to(array[None], (size,) + array.shape), axes, 0, 0)


def collect(parts, axes):
    return jnp.sum(lax.all_to_all(parts, axes, 0, 0).astype(WIDE), 0)


def swap(parts, axes):
    return lax.all_to_all(parts, axes, 0, 0)


def ring(array, step):
    return lax.ppermute(array, "y", [(i, (i + step) % RING) for i in range(RING)])


def ring_gather(rows):
    half = rows.shape[0] // 2
    first, second = rows[:half], rows[half:]
    before_first, after_second = ring(first, 1), ring(second, -1)
    before_second, after_first = ring(second, 1), ring(first, -1)
    across_first, across_second = ring(before_first, 1), ring(after_second, -1)
    return jnp.concatenate(
        [
            first, second, before_first, before_second,
            after_first, after_second, across_first, across_second,
        ],
        0,
    )


def ring_sum(rows):
    own = rows.shape[0] // RING
    half = own // 2
    start, before, after, across = (rows[i * own : (i + 1) * own] for i in range(RING))
    from_before, from_after = ring(across[:half], 1), ring(across[half:], -1)
    second_after, first_before = ring(after[half:], 1), ring(before[:half], -1)
    first_after = ring((after[:half].astype(WIDE) + from_before.astype(WIDE)).astype(LOW), 1)
    second_before = ring((before[half:].astype(WIDE) + from_after.astype(WIDE)).astype(LOW), -1)
    first = start[:half].astype(WIDE) + first_after.astype(WIDE) + first_before.astype(WIDE)
    second = start[half:].astype(WIDE) + second_after.astype(WIDE) + second_before.astype(WIDE)
    return jnp.concatenate([first, second], 0)


def after(value, *others):
    return lax.optimization_barrier((value,) + others)[0]


def gather_weight(shard):
    full = lax.all_gather(shard, ("z", "c", "x"), axis=0)
    return full.reshape((8, 4) + shard.shape)


def settle(gradient):
    total = lax.psum_scatter(
        gradient.reshape((32,) + gradient.shape[2:]), ("z", "c", "x"), scatter_dimension=0
    )
    return total.astype(WIDE)


def qkv_body(rows_ref, weight_ref, bias_ref, out_ref):
    weight = weight_ref[...].reshape(rows_ref.shape[1], -1)
    out_ref[...] = (dot(rows_ref[...], weight) + bias_ref[...]).astype(LOW)


def qkv_project(rows, weight, bias):
    count, width = rows.shape
    zc, xs, piece, cols = weight.shape
    return call(
        qkv_body,
        struct((xs, count, cols), LOW),
        (xs,),
        [
            whole((count, width)),
            pl.BlockSpec((zc, None, piece, cols), lambda i: (0, i, 0, 0)),
            pl.BlockSpec((None, 1, cols), lambda i: (i, 0, 0)),
        ],
        pl.BlockSpec((None, count, cols), lambda i: (i, 0, 0)),
        2 * count * width * xs * cols,
        10 * 2**20,
    )(rows, weight, bias)


def out_body(heads_ref, weight_ref, out_ref, joined):
    @pl.when(pl.program_id(0) == 0)
    def _():
        joined[...] = jnp.concatenate([heads_ref[i] for i in range(RING)], 1)

    weight = jnp.concatenate([weight_ref[i] for i in range(RING)], 1)
    out_ref[...] = dot_t(joined[...], weight).astype(LOW)


def out_project(heads, weight):
    xs, count, cols = heads.shape
    zc, _, piece, _ = weight.shape
    return call(
        out_body,
        struct((count, zc * piece), LOW),
        (zc,),
        [
            whole(heads.shape),
            pl.BlockSpec((None, xs, piece, cols), lambda i: (i, 0, 0, 0)),
        ],
        pl.BlockSpec((count, piece), lambda i: (0, i)),
        2 * count * zc * piece * xs * cols,
        5 * 2**20,
        scratch=[pltpu.VMEM((count, xs * cols), LOW)],
    )(heads, weight)


def heads_grad_body(rows_ref, weight_ref, out_ref):
    weight = weight_ref[...].reshape(rows_ref.shape[1], -1)
    out_ref[...] = dot(rows_ref[...], weight).astype(LOW)


def heads_grad(rows, weight):
    count, width = rows.shape
    zc, xs, piece, cols = weight.shape
    return call(
        heads_grad_body,
        struct((xs, count, cols), LOW),
        (xs,),
        [
            whole((count, width)),
            pl.BlockSpec((zc, None, piece, cols), lambda i: (0, i, 0, 0)),
        ],
        pl.BlockSpec((None, count, cols), lambda i: (i, 0, 0)),
        2 * count * width * xs * cols,
        5 * 2**20,
    )(rows, weight)


def weight_grad_body(place_ref, norm_ref, qkv_ref, attn_ref, heads_ref, keep_ref, send_ref):
    cols = qkv_ref.shape[-1]
    parts = (
        (dot_0(norm_ref[...], qkv_ref[...]), slice(0, cols)),
        (dot_0(attn_ref[...], heads_ref[...]), slice(cols, None)),
    )
    first = place_ref[0] == 0
    for value, where in parts:
        value = value.astype(LOW).reshape(4, 2, -1, value.shape[-1])
        keep_ref[:, :, where] = jnp.where(first, value[:, 0], value[:, 1])
        send_ref[:, :, where] = jnp.where(first, value[:, 1], value[:, 0])


def weight_grads(core_at, norm_rows, d_qkv, attn_rows, heads):
    count, width = norm_rows.shape
    xs, _, qkv_cols = d_qkv.shape
    cols = heads.shape[-1]
    piece = width // 8
    half = struct((4, xs, piece, qkv_cols + cols), LOW)
    block = pl.BlockSpec((4, None, piece, qkv_cols + cols), lambda i, *_: (0, i, 0, 0))
    return call(
        weight_grad_body,
        (half, half),
        (xs,),
        [
            whole((count, width)),
            pl.BlockSpec((None, count, qkv_cols), lambda i, *_: (i, 0, 0)),
            whole((count, width)),
            pl.BlockSpec((None, count, cols), lambda i, *_: (i, 0, 0)),
        ],
        (block, block),
        2 * count * width * xs * (cols + qkv_cols),
        20 * 2**20,
        prefetch=1,
        vmem=48,
    )(core_at, norm_rows, d_qkv, attn_rows, heads)


def add_up(total, term):
    @pl.when(pl.program_id(0) == 0)
    def _():
        total[...] = term

    @pl.when(pl.program_id(0) > 0)
    def _():
        total[...] += term


def ffn_first_body(
    norm_ref, cot_ref, up_ref, down_ref, bias_ref,
    hidden_ref, grad_up_ref, norm_grad_ref, bias_grad_ref, total,
):
    width, cols = norm_ref.shape[1], up_ref.shape[-1]
    up_w = up_ref[...].reshape(width, cols)
    up = dot(norm_ref[...], up_w) + bias_ref[...]
    normal = 0.5 * (1.0 + lax.erf(up * 0.7071067811865476))
    hidden_ref[...] = (up * normal).astype(LOW)
    slope = normal + up * (jnp.exp(-0.5 * up * up) * 0.3989422804014327)
    grad_up = (dot(cot_ref[...], down_ref[...].reshape(width, cols)) * slope).astype(LOW)
    grad_up_ref[...] = grad_up
    bias_grad_ref[...] = jnp.sum(grad_up.astype(WIDE), 0, keepdims=True)
    add_up(total, dot_t(grad_up, up_w))

    @pl.when(pl.program_id(0) == pl.num_programs(0) - 1)
    def _():
        norm_grad_ref[...] = total[...].astype(LOW)


def ffn_first(norm_rows, cot_rows, weight, bias):
    count, width = norm_rows.shape
    zc, xs, piece, cols = weight.shape
    size = cols // 2
    rows = whole((count, width))
    vector = pl.BlockSpec((None, 1, size), lambda i: (i, 0, 0))
    wide = pl.BlockSpec((count, size), lambda i: (0, i))
    return call(
        ffn_first_body,
        (
            struct((count, xs * size), LOW),
            struct((count, xs * size), LOW),
            struct((count, width), LOW),
            struct((xs, 1, size), WIDE),
        ),
        (xs,),
        [
            rows,
            rows,
            pl.BlockSpec((zc, None, piece, size), lambda i: (0, i, 0, 0)),
            pl.BlockSpec((zc, None, piece, size), lambda i: (0, i, 0, 1)),
            vector,
        ],
        (wide, wide, rows, vector),
        6 * count * width * xs * size,
        25 * 2**20,
        scratch=[pltpu.VMEM((count, width), WIDE)],
        vmem=56,
    )(norm_rows, cot_rows, weight, weight, bias)


def ffn_second_body(
    norm_ref, cot_ref, hidden_ref, grad_up_ref, down_ref, branch_ref, weight_grad_ref, total
):
    width, cols = norm_ref.shape[1], down_ref.shape[-1]
    zc, piece, _ = weight_grad_ref.shape
    hidden = hidden_ref[...]
    weight_grad_ref[:, :, :cols] = (
        dot_0(norm_ref[...], grad_up_ref[...]).astype(LOW).reshape(zc, piece, cols)
    )
    weight_grad_ref[:, :, cols:] = dot_0(cot_ref[...], hidden).astype(LOW).reshape(zc, piece, cols)
    add_up(total, dot_t(hidden, down_ref[...].reshape(width, cols)))

    @pl.when(pl.program_id(0) == pl.num_programs(0) - 1)
    def _():
        branch_ref[...] = total[...].astype(LOW)


def ffn_second(norm_rows, cot_rows, hidden, grad_up, weight):
    count, width = norm_rows.shape
    zc, xs, piece, cols = weight.shape
    size = cols // 2
    rows = whole((count, width))
    wide = pl.BlockSpec((count, size), lambda i: (0, i))
    return call(
        ffn_second_body,
        (struct((count, width), LOW), struct(weight.shape, LOW)),
        (xs,),
        [rows, rows, wide, wide, pl.BlockSpec((zc, None, piece, size), lambda i: (0, i, 0, 1))],
        (rows, pl.BlockSpec((zc, None, piece, cols), lambda i: (0, i, 0, 0))),
        6 * count * width * xs * size,
        40 * 2**20,
        scratch=[pltpu.VMEM((count, width), WIDE)],
        vmem=56,
    )(norm_rows, cot_rows, hidden, grad_up, weight)


def only_head(array, head):
    lane = lax.broadcasted_iota(jnp.int32, array.shape, 1)
    return jnp.where(lane // HEAD_DIM == head, array, jnp.zeros_like(array))


def allowed_keys(start, extent, live_count):
    q_place = start + lax.broadcasted_iota(jnp.int32, (SPAN, extent), 0)
    k_place = lax.broadcasted_iota(jnp.int32, (SPAN, extent), 1)
    return k_place <= jnp.minimum(q_place, live_count - 1)


def slot_of(place, own):
    apart = (place - own + RING) % RING
    return jnp.where(apart == 0, 0, jnp.where(apart == RING - 1, 1, apart + 1))


def load_ordered(blocks_ref, own, into):
    rows = blocks_ref.shape[2]
    for x in range(RING):
        for y in range(RING):
            at = (x * RING + y) * rows
            into[at : at + rows] = blocks_ref[x, slot_of(y, own)]


def store_ordered(blocks_ref, x, own, cols, value):
    rows = blocks_ref.shape[2]
    for y in range(RING):
        blocks_ref[x, slot_of(y, own), :, cols] = value[y * rows : (y + 1) * rows]


def attend_body(live_ref, qkv_ref, heads_ref, exact_ref, log_ref, qkv):
    live_count = live_ref[pl.program_id(0)]
    own = live_ref[pl.num_programs(0)]
    length = exact_ref.shape[0]
    width = exact_ref.shape[1]
    load_ordered(qkv_ref, own, qkv)
    key = qkv[:, width : 2 * width]
    value = qkv[:, 2 * width :]
    for span in range(length // SPAN):
        start, extent = span * SPAN, (span + 1) * SPAN
        here = slice(start, extent)

        @pl.when(start < live_count)
        def _():
            query = qkv[here, :width]
            allowed = allowed_keys(start, extent, live_count)
            mixed, logs = [], []
            for head in range(width // HEAD_DIM):
                scores = dot_t(only_head(query, head), key[:extent]) * HEAD_DIM**-0.5
                scores = jnp.where(allowed, scores, -1e9)
                top = jnp.max(scores, 1, keepdims=True)
                terms = jnp.exp(scores - top)
                denom = jnp.sum(terms, 1, keepdims=True)
                mixed.append(dot(terms.astype(LOW), value[:extent]) / denom)
                logs.append(top + jnp.log(denom))
            lane = lax.broadcasted_iota(jnp.int32, (SPAN, width), 1)
            out = jnp.where(lane < HEAD_DIM, mixed[0], mixed[1])
            exact_ref[here] = out
            log_ref[here] = jnp.where(lane < HEAD_DIM, logs[0], logs[1])
            store_ordered(heads_ref, span, own, slice(None), out.astype(LOW))

        @pl.when(start >= live_count)
        def _():
            exact_ref[here] = jnp.zeros((SPAN, width), WIDE)
            log_ref[here] = jnp.zeros((SPAN, width), WIDE)
            heads_ref[span] = jnp.zeros(heads_ref.shape[1:], LOW)


def row_block(rows, cols):
    return pl.BlockSpec((4, 4, None, rows, cols), lambda s, *_: (0, 0, s, 0, 0))


def attend(live_counts, qkv, width):
    xs, ys, seqs, rows, _ = qkv.shape
    length = xs * ys * rows
    flat = pl.BlockSpec((None, length, width), lambda s, *_: (s, 0, 0))
    return call(
        attend_body,
        (
            struct((xs, ys, seqs, rows, width), LOW),
            struct((seqs, length, width), WIDE),
            struct((seqs, length, width), WIDE),
        ),
        (seqs,),
        [row_block(rows, 3 * width)],
        (row_block(rows, width), flat, flat),
        4 * 10**9,
        4 * 2**20,
        scratch=[pltpu.VMEM((length, 3 * width), LOW)],
        prefetch=1,
    )(live_counts, qkv)


def attend_back_body(
    live_ref, qkv_ref, grad_ref, exact_ref, log_ref, out_ref, sum_ref,
    key_total, value_total, qkv, grads,
):
    live_count = live_ref[pl.program_id(0)]
    own = live_ref[pl.num_programs(0)]
    length, width = exact_ref.shape
    factor = HEAD_DIM**-0.5
    load_ordered(qkv_ref, own, qkv)
    load_ordered(grad_ref, own, grads)
    key = qkv[:, width : 2 * width]
    value = qkv[:, 2 * width :]
    key_total[...] = jnp.zeros_like(key_total)
    value_total[...] = jnp.zeros_like(value_total)
    sum_ref[...] = jnp.zeros_like(sum_ref)
    for span in range(length // SPAN):
        start, extent = span * SPAN, (span + 1) * SPAN
        here = slice(start, extent)

        @pl.when(start < live_count)
        def _():
            query = qkv[here, :width]
            grad = grads[here]
            inner = grad.astype(WIDE) * exact_ref[here]
            logs = log_ref[here]
            allowed = allowed_keys(start, extent, live_count)
            query_total = jnp.zeros((SPAN, width), WIDE)
            for head in range(width // HEAD_DIM):
                query_h = only_head(query, head)
                grad_h = only_head(grad, head)
                log_h = logs[:, head * HEAD_DIM : head * HEAD_DIM + 1]
                row_inner = jnp.sum(only_head(inner, head), 1, keepdims=True)
                scores = dot_t(query_h, key[:extent]) * factor
                probs = jnp.exp(jnp.where(allowed, scores, -1e9) - log_h)
                d_probs = dot_t(grad_h, value[:extent])
                value_total[:extent] += dot_0(probs.astype(LOW), grad_h)
                d_scores = (probs * (d_probs - row_inner)).astype(LOW)
                query_total += dot(d_scores, only_head(key[:extent], head))
                key_total[:extent] += dot_0(d_scores, query_h)
            out = (query_total * factor).astype(LOW)
            store_ordered(out_ref, span, own, slice(0, width), out)
            sum_ref[:, :width] += jnp.sum(out.astype(WIDE), 0, keepdims=True)

        @pl.when(start >= live_count)
        def _():
            out_ref[span, :, :, :width] = jnp.zeros(out_ref.shape[1:3] + (width,), LOW)

    key_grad = (key_total[...] * factor).astype(LOW)
    value_grad = value_total[...].astype(LOW)
    for span in range(RING):
        here = slice(span * SPAN, (span + 1) * SPAN)
        store_ordered(out_ref, span, own, slice(width, 2 * width), key_grad[here])
        store_ordered(out_ref, span, own, slice(2 * width, None), value_grad[here])
    sum_ref[:, 2 * width :] = jnp.sum(value_grad.astype(WIDE), 0, keepdims=True)


def attend_back(live_counts, qkv, grads, exact, logs):
    xs, ys, seqs, rows, _ = qkv.shape
    _, length, width = exact.shape
    flat = pl.BlockSpec((None, length, width), lambda s, *_: (s, 0, 0))
    return call(
        attend_back_body,
        (struct(qkv.shape, LOW), struct((seqs, 1, 3 * width), WIDE)),
        (seqs,),
        [row_block(rows, 3 * width), row_block(rows, width), flat, flat],
        (
            row_block(rows, 3 * width),
            pl.BlockSpec((None, 1, 3 * width), lambda s, *_: (s, 0, 0)),
        ),
        8 * 10**9,
        8 * 2**20,
        scratch=[
            pltpu.VMEM((length, width), WIDE),
            pltpu.VMEM((length, width), WIDE),
            pltpu.VMEM((length, 3 * width), LOW),
            pltpu.VMEM((length, width), LOW),
        ],
        prefetch=1,
        vmem=48,
    )(live_counts, qkv, grads, exact, logs)


def norm_parts(values, gain_vec, shift_vec):
    average = jnp.mean(values, -1, keepdims=True)
    centered = values - average
    inverse = lax.rsqrt(jnp.mean(centered * centered, -1, keepdims=True) + 1e-05)
    unit_rows = centered * inverse
    return (unit_rows * gain_vec + shift_vec, unit_rows, inverse)


def norm_back(gradient, unit_rows, inverse, gain_vec):
    scaled = gradient * gain_vec
    return inverse * (
        scaled
        - jnp.mean(scaled, -1, keepdims=True)
        - unit_rows * jnp.mean(scaled * unit_rows, -1, keepdims=True)
    )


def split_back(flat, vectors):
    pieces, start = [], 0
    for v in vectors:
        pieces.append(flat[start : start + v.size])
        start += v.size
    return pieces


def vector_totals(vectors):
    flat = jnp.concatenate([v.reshape(-1) for v in vectors])
    part = collect(flat.reshape(16, -1, 128), COLS)
    part = jnp.sum(spread(part, ROWS, 8), 0)
    return split_back(spread(part, COLS, 16).reshape(-1), vectors)


def short_totals(vectors, columns):
    shared = jnp.concatenate([v.reshape(-1, 128) for v in vectors], 0)
    rows = shared.shape[0]
    parts = spread(jnp.concatenate([shared, columns], 0), COLS, 16)
    part = jnp.concatenate([jnp.sum(parts[:, :rows], 0), parts[:, rows:].reshape(-1, 128)], 0)
    part = jnp.sum(spread(part, ROWS, 8), 0)
    placed = part[rows:].reshape(16, -1, 128)
    return split_back(part[:rows].reshape(-1), vectors) + [
        placed[:, i].reshape(-1) for i in range(columns.shape[0])
    ]


def shards(
    tokens, cotangent, seq_lengths, exit_layers, layer_index,
    ln1_gain, ln1_shift, q_weight, q_bias, k_weight, v_weight, v_bias, out_weight, out_bias,
    ln2_gain, ln2_shift, up_weight, up_bias, down_weight, down_bias,
):
    seqs, own_rows, width = tokens.shape
    own = seqs * own_rows
    full_len = exit_layers.shape[1]
    x_at, y_at = lax.axis_index("x"), lax.axis_index("y")
    core_at = lax.axis_index("c").astype(jnp.int32).reshape(1)
    head_at = x_at * RING + y_at
    head_cols = q_weight.shape[1]
    ff_cols = up_weight.shape[1]

    positions = jnp.arange(full_len)
    live_all = (positions[None, :] < seq_lengths[:, None]) & (exit_layers > layer_index[0])
    live_counts = jnp.concatenate(
        [jnp.sum(live_all.astype(jnp.int32), 1), y_at.astype(jnp.int32).reshape(1)]
    )
    live_mine = lax.dynamic_slice_in_dim(live_all, head_at * own_rows, own_rows, 1)
    keep = live_mine.reshape(-1, 1).astype(WIDE)

    w_qkv = gather_weight(jnp.concatenate([q_weight, k_weight, v_weight], 1).astype(LOW))
    w_out = gather_weight(out_weight.astype(LOW))
    w_ff = gather_weight(jnp.concatenate([up_weight, down_weight], 1).astype(LOW))

    inputs = tokens.astype(WIDE).reshape(own, width)
    normed1, unit1, inverse1 = norm_parts(inputs, ln1_gain, ln1_shift)
    norm1 = ring_gather(normed1.astype(LOW))
    grad_y = cotangent.astype(WIDE).reshape(own, width)
    g_ffn = (keep * grad_y).astype(LOW)
    cot_rows = ring_gather(after(g_ffn, norm1))

    def mine(vector, cols):
        return lax.dynamic_index_in_dim(vector.reshape(RING, RING, cols), y_at, 1, False)

    bias = jnp.concatenate(
        [mine(q_bias, head_cols), jnp.zeros((RING, head_cols), WIDE), mine(v_bias, head_cols)], 1
    ).reshape(RING, 1, 3 * head_cols)
    qkv = qkv_project(after(norm1, cot_rows), w_qkv, bias)
    rows5 = (RING, RING, seqs, own_rows)
    qkv = swap(qkv, "x").reshape(rows5 + (3 * head_cols,))
    heads, exact, logs = attend(live_counts, qkv, head_cols)
    heads = swap(heads.reshape(RING, RING * own, head_cols), "x")
    branch1 = ring_sum(out_project(heads, w_out)) + out_bias
    middle = inputs + keep * branch1
    normed2, unit2, inverse2 = norm_parts(middle, ln2_gain, ln2_shift)
    norm2 = ring_gather(normed2.astype(LOW))

    ff_bias = mine(up_bias, ff_cols).reshape(RING, 1, ff_cols)
    hidden, grad_up, g_norm2, up_bias_part = ffn_first(norm2, cot_rows, w_ff, ff_bias)
    g_norm2 = ring_sum(g_norm2)
    branch2, ff_grad = ffn_second(norm2, cot_rows, hidden, grad_up, w_ff)
    ff_grad = settle(ff_grad)
    grad_mid = grad_y + norm_back(g_norm2, unit2, inverse2, ln2_gain)
    g_attn = (keep * grad_mid).astype(LOW)
    attn_rows = ring_gather(g_attn)
    branch2 = ring_sum(after(branch2, attn_rows)) + down_bias
    result = (middle + keep * branch2).astype(LOW).reshape(tokens.shape)
    g_heads = swap(heads_grad(attn_rows, w_out), "x").reshape(rows5 + (head_cols,))
    d_qkv, d_sums = attend_back(live_counts, qkv, g_heads, exact, logs)
    d_qkv = swap(d_qkv.reshape(RING, RING * own, 3 * head_cols), "x")

    kept, sent = weight_grads(core_at, norm1, d_qkv, attn_rows, heads)
    other = lax.ppermute(sent, "c", [(0, 1), (1, 0)])
    g_norm1 = ring_sum(out_project(after(d_qkv, sent), w_qkv))
    both = (kept.astype(WIDE) + other.astype(WIDE)).astype(LOW)
    small_grad = collect(both.reshape((16,) + both.shape[2:]), ("z", "x"))
    grad_tokens = (grad_mid + norm_back(g_norm1, unit1, inverse1, ln1_gain)).reshape(tokens.shape)

    up_bias_full = lax.dynamic_update_slice_in_dim(
        jnp.zeros((RING, RING, ff_cols), WIDE), up_bias_part.reshape(RING, 1, ff_cols), y_at, 1
    )
    out_bias_sum, ln2_gain_sum, ln2_shift_sum, up_bias_sum, down_bias_sum = vector_totals(
        (
            jnp.sum(g_attn.astype(WIDE), 0),
            jnp.sum(g_norm2 * unit2, 0),
            jnp.sum(g_norm2, 0),
            up_bias_full,
            jnp.sum(g_ffn.astype(WIDE), 0),
        )
    )
    d_sums = jnp.sum(d_sums, 0).reshape(3, head_cols)
    ln1_gain_sum, ln1_shift_sum, q_bias_sum, v_bias_sum = short_totals(
        (jnp.sum(g_norm1 * unit1, 0), jnp.sum(g_norm1, 0)), d_sums[::2]
    )
    return (
        result,
        grad_tokens,
        ln1_gain_sum,
        ln1_shift_sum,
        small_grad[:, :head_cols],
        q_bias_sum,
        small_grad[:, head_cols : 2 * head_cols],
        small_grad[:, 2 * head_cols : 3 * head_cols],
        v_bias_sum,
        small_grad[:, 3 * head_cols :],
        out_bias_sum,
        ln2_gain_sum,
        ln2_shift_sum,
        ff_grad[:, :ff_cols],
        up_bias_sum,
        ff_grad[:, ff_cols:],
        down_bias_sum,
    )


def solution(mesh):
    wide = Mesh(mesh.devices.reshape(4, 2, 4, 4), ("z", "c", "x", "y"))
    act = P(ROWS, COLS, None)
    weight = P(ROWS, COLS)
    vector = P()
    in_specs = (
        act, act, P(ROWS), P(ROWS, None), vector, vector, vector,
        weight, vector, weight, weight, vector, weight, vector, vector, vector,
        weight, vector, weight, vector,
    )
    out_specs = (
        act, act, vector, vector, weight, vector, weight, weight, vector, weight,
        vector, vector, vector, weight, vector, weight, vector,
    )
    return jax.shard_map(
        shards, mesh=wide, in_specs=in_specs, out_specs=out_specs, check_vma=False
    )
```

```python
from functools import partial

import jax
import jax.numpy as jnp
from jax import lax
from jax.experimental import pallas as pl
from jax.experimental.pallas import tpu as pltpu
from jax.sharding import Mesh
from jax.sharding import PartitionSpec as P

HEAD_DIM = 64
SPAN = 256
LOW = jnp.bfloat16
WIDE = jnp.float32
RING = 4
ROWS = ("z", "c")
COLS = ("x", "y")


def dot(left, right):
    return jnp.dot(left, right, preferred_element_type=WIDE)


def dot_t(left, right):
    return lax.dot_general(left, right, (((1,), (1,)), ((), ())), preferred_element_type=WIDE)


def dot_0(left, right):
    return lax.dot_general(left, right, (((0,), (0,)), ((), ())), preferred_element_type=WIDE)


def call(body, out_shape, grid, in_specs, out_specs, flops, traffic, scratch=(), prefetch=0, vmem=40):
    return pl.pallas_call(
        body,
        out_shape=out_shape,
        grid_spec=pltpu.PrefetchScalarGridSpec(
            num_scalar_prefetch=prefetch,
            grid=grid,
            in_specs=in_specs,
            out_specs=out_specs,
            scratch_shapes=list(scratch),
        ),
        compiler_params=pltpu.CompilerParams(vmem_limit_bytes=vmem * 2**20),
        cost_estimate=pl.CostEstimate(flops=flops, bytes_accessed=traffic, transcendentals=0),
    )


def whole(shape):
    return pl.BlockSpec(shape, lambda *_: (0,) * len(shape))


def struct(shape, dtype):
    return jax.ShapeDtypeStruct(shape, dtype)


def spread(array, axes, size):
    return lax.all_to_all(jnp.broadcast_to(array[None], (size,) + array.shape), axes, 0, 0)


def collect(parts, axes):
    return jnp.sum(lax.all_to_all(parts, axes, 0, 0).astype(WIDE), 0)


def swap(parts, axes):
    return lax.all_to_all(parts, axes, 0, 0)


def ring(array, step, axis="y"):
    return lax.ppermute(array, axis, [(i, (i + step) % RING) for i in range(RING)])


def ring_collect(parts, axis, dim):
    here = lax.axis_index(axis)

    def part(step):
        return lax.dynamic_index_in_dim(parts, (here + step) % RING, dim, False)

    terms = [part(0)] + [ring(part(step), step, axis) for step in (1, 2, 3)]
    return sum(term.astype(WIDE) for term in terms)


def cube_collect(parts, beside):
    half = parts.shape[2] // 2
    first = ring_collect(parts[:, :, :half], "z", 0).astype(LOW)
    second = ring_collect(parts[:, :, half:], "x", 1).astype(LOW)
    first, second, beside = tie(first, second, beside)
    return jnp.concatenate([ring_collect(first, "x", 0), ring_collect(second, "z", 0)], 0), beside


def ring_gather(rows):
    half = rows.shape[0] // 2
    first, second = rows[:half], rows[half:]
    before_first, after_second = ring(first, 1), ring(second, -1)
    before_second, after_first = ring(second, 1), ring(first, -1)
    across_first, across_second = ring(before_first, 1), ring(after_second, -1)
    return jnp.concatenate(
        [
            first, second, before_first, before_second,
            after_first, after_second, across_first, across_second,
        ],
        0,
    )


def ring_sum(rows, beside=None):
    own = rows.shape[0] // RING
    half = own // 2
    start, before, after, across = (rows[i * own : (i + 1) * own] for i in range(RING))
    from_before, from_after = ring(across[:half], 1), ring(across[half:], -1)
    second_after, first_before = ring(after[half:], 1), ring(before[:half], -1)
    first_after = ring((after[:half].astype(WIDE) + from_before.astype(WIDE)).astype(LOW), 1)
    second_before = ring((before[half:].astype(WIDE) + from_after.astype(WIDE)).astype(LOW), -1)
    came = (first_after, first_before, second_after, second_before)
    if beside is not None:
        came, beside = tie(came, beside)
    first = start[:half].astype(WIDE) + came[0].astype(WIDE) + came[1].astype(WIDE)
    second = start[half:].astype(WIDE) + came[2].astype(WIDE) + came[3].astype(WIDE)
    total = jnp.concatenate([first, second], 0)
    return total if beside is None else (total, beside)


def tie(*arrays):
    return lax.optimization_barrier(arrays)


def gather_weight(shard):
    full = lax.all_gather(shard, ("z", "c", "x"), axis=0)
    return full.reshape((8, 4) + shard.shape)


def settle(gradient):
    total = lax.psum_scatter(
        gradient.reshape((32,) + gradient.shape[2:]), ("z", "c", "x"), scatter_dimension=0
    )
    return total.astype(WIDE)


def qkv_body(rows_ref, weight_ref, bias_ref, out_ref):
    weight = weight_ref[...].reshape(rows_ref.shape[1], -1)
    out_ref[...] = (dot(rows_ref[...], weight) + bias_ref[...]).astype(LOW)


def qkv_project(rows, weight, bias):
    count, width = rows.shape
    zc, xs, piece, cols = weight.shape
    return call(
        qkv_body,
        struct((xs, count, cols), LOW),
        (xs,),
        [
            whole((count, width)),
            pl.BlockSpec((zc, None, piece, cols), lambda i: (0, i, 0, 0)),
            pl.BlockSpec((None, 1, cols), lambda i: (i, 0, 0)),
        ],
        pl.BlockSpec((None, count, cols), lambda i: (i, 0, 0)),
        2 * count * width * xs * cols,
        10 * 2**20,
    )(rows, weight, bias)


def out_body(heads_ref, weight_ref, out_ref, joined):
    @pl.when(pl.program_id(0) == 0)
    def _():
        joined[...] = jnp.concatenate([heads_ref[i] for i in range(RING)], 1)

    weight = jnp.concatenate([weight_ref[i] for i in range(RING)], 1)
    out_ref[...] = dot_t(joined[...], weight).astype(LOW)


def out_project(heads, weight):
    xs, count, cols = heads.shape
    zc, _, piece, _ = weight.shape
    return call(
        out_body,
        struct((count, zc * piece), LOW),
        (zc,),
        [
            whole(heads.shape),
            pl.BlockSpec((None, xs, piece, cols), lambda i: (i, 0, 0, 0)),
        ],
        pl.BlockSpec((count, piece), lambda i: (0, i)),
        2 * count * zc * piece * xs * cols,
        5 * 2**20,
        scratch=[pltpu.VMEM((count, xs * cols), LOW)],
    )(heads, weight)


def heads_grad_body(rows_ref, weight_ref, out_ref):
    weight = weight_ref[...].reshape(rows_ref.shape[1], -1)
    out_ref[...] = dot(rows_ref[...], weight).astype(LOW)


def heads_grad(rows, weight):
    count, width = rows.shape
    zc, xs, piece, cols = weight.shape
    return call(
        heads_grad_body,
        struct((xs, count, cols), LOW),
        (xs,),
        [
            whole((count, width)),
            pl.BlockSpec((zc, None, piece, cols), lambda i: (0, i, 0, 0)),
        ],
        pl.BlockSpec((None, count, cols), lambda i: (i, 0, 0)),
        2 * count * width * xs * cols,
        5 * 2**20,
    )(rows, weight)


def weight_grad_body(place_ref, rows_ref, grad_ref, keep_ref, send_ref):
    value = dot_0(rows_ref[...], grad_ref[...]).astype(LOW)
    value = value.reshape(4, 2, -1, value.shape[-1])
    first = place_ref[0] == 0
    keep_ref[...] = jnp.where(first, value[:, 0], value[:, 1])
    send_ref[...] = jnp.where(first, value[:, 1], value[:, 0])


def weight_grads(core_at, rows, columns):
    count, width = rows.shape
    xs, _, cols = columns.shape
    piece = width // 8
    half = struct((4, xs, piece, cols), LOW)
    block = pl.BlockSpec((4, None, piece, cols), lambda i, *_: (0, i, 0, 0))
    return call(
        weight_grad_body,
        (half, half),
        (xs,),
        [whole((count, width)), pl.BlockSpec((None, count, cols), lambda i, *_: (i, 0, 0))],
        (block, block),
        2 * count * width * xs * cols,
        15 * 2**20,
        prefetch=1,
    )(core_at, rows, columns)


def core_sum(kept, sent):
    other = lax.ppermute(sent, "c", [(0, 1), (1, 0)])
    return (kept.astype(WIDE) + other.astype(WIDE)).astype(LOW)


def add_up(total, term):
    @pl.when(pl.program_id(0) == 0)
    def _():
        total[...] = term

    @pl.when(pl.program_id(0) > 0)
    def _():
        total[...] += term


def ffn_first_body(
    norm_ref, cot_ref, up_ref, down_ref, bias_ref,
    hidden_ref, grad_up_ref, norm_grad_ref, bias_grad_ref, total,
):
    width, cols = norm_ref.shape[1], up_ref.shape[-1]
    up_w = up_ref[...].reshape(width, cols)
    up = dot(norm_ref[...], up_w) + bias_ref[...]
    normal = 0.5 * (1.0 + lax.erf(up * 0.7071067811865476))
    hidden_ref[...] = (up * normal).astype(LOW)
    slope = normal + up * (jnp.exp(-0.5 * up * up) * 0.3989422804014327)
    grad_up = (dot(cot_ref[...], down_ref[...].reshape(width, cols)) * slope).astype(LOW)
    grad_up_ref[...] = grad_up
    bias_grad_ref[...] = jnp.sum(grad_up.astype(WIDE), 0, keepdims=True)
    add_up(total, dot_t(grad_up, up_w))

    @pl.when(pl.program_id(0) == pl.num_programs(0) - 1)
    def _():
        norm_grad_ref[...] = total[...].astype(LOW)


def ffn_first(norm_rows, cot_rows, weight, bias):
    count, width = norm_rows.shape
    zc, xs, piece, cols = weight.shape
    size = cols // 2
    rows = whole((count, width))
    vector = pl.BlockSpec((None, 1, size), lambda i: (i, 0, 0))
    wide = pl.BlockSpec((count, size), lambda i: (0, i))
    return call(
        ffn_first_body,
        (
            struct((count, xs * size), LOW),
            struct((count, xs * size), LOW),
            struct((count, width), LOW),
            struct((xs, 1, size), WIDE),
        ),
        (xs,),
        [
            rows,
            rows,
            pl.BlockSpec((zc, None, piece, size), lambda i: (0, i, 0, 0)),
            pl.BlockSpec((zc, None, piece, size), lambda i: (0, i, 0, 1)),
            vector,
        ],
        (wide, wide, rows, vector),
        6 * count * width * xs * size,
        25 * 2**20,
        scratch=[pltpu.VMEM((count, width), WIDE)],
        vmem=56,
    )(norm_rows, cot_rows, weight, weight, bias)


def ffn_second_body(
    norm_ref, cot_ref, hidden_ref, grad_up_ref, down_ref, branch_ref, weight_grad_ref, total
):
    width, cols = norm_ref.shape[1], down_ref.shape[-1]
    zc, piece, _ = weight_grad_ref.shape
    hidden = hidden_ref[...]
    weight_grad_ref[:, :, :cols] = (
        dot_0(norm_ref[...], grad_up_ref[...]).astype(LOW).reshape(zc, piece, cols)
    )
    weight_grad_ref[:, :, cols:] = dot_0(cot_ref[...], hidden).astype(LOW).reshape(zc, piece, cols)
    add_up(total, dot_t(hidden, down_ref[...].reshape(width, cols)))

    @pl.when(pl.program_id(0) == pl.num_programs(0) - 1)
    def _():
        branch_ref[...] = total[...].astype(LOW)


def ffn_second(norm_rows, cot_rows, hidden, grad_up, weight):
    count, width = norm_rows.shape
    zc, xs, piece, cols = weight.shape
    size = cols // 2
    rows = whole((count, width))
    wide = pl.BlockSpec((count, size), lambda i: (0, i))
    return call(
        ffn_second_body,
        (struct((count, width), LOW), struct(weight.shape, LOW)),
        (xs,),
        [rows, rows, wide, wide, pl.BlockSpec((zc, None, piece, size), lambda i: (0, i, 0, 1))],
        (rows, pl.BlockSpec((zc, None, piece, cols), lambda i: (0, i, 0, 0))),
        6 * count * width * xs * size,
        40 * 2**20,
        scratch=[pltpu.VMEM((count, width), WIDE)],
        vmem=56,
    )(norm_rows, cot_rows, hidden, grad_up, weight)


def only_head(array, head):
    lane = lax.broadcasted_iota(jnp.int32, array.shape, 1)
    return jnp.where(lane // HEAD_DIM == head, array, jnp.zeros_like(array))


def allowed_keys(start, extent, live_count):
    q_place = start + lax.broadcasted_iota(jnp.int32, (SPAN, extent), 0)
    k_place = lax.broadcasted_iota(jnp.int32, (SPAN, extent), 1)
    return k_place <= jnp.minimum(q_place, live_count - 1)


def slot_of(place, own):
    apart = (place - own + RING) % RING
    return jnp.where(apart == 0, 0, jnp.where(apart == RING - 1, 1, apart + 1))


def load_ordered(blocks_ref, own, into):
    rows = blocks_ref.shape[2]
    for x in range(RING):
        for y in range(RING):
            at = (x * RING + y) * rows
            into[at : at + rows] = blocks_ref[x, slot_of(y, own)]


def store_ordered(blocks_ref, x, own, cols, value):
    rows = blocks_ref.shape[2]
    for y in range(RING):
        blocks_ref[x, slot_of(y, own), :, cols] = value[y * rows : (y + 1) * rows]


def attend_body(live_ref, qkv_ref, heads_ref, exact_ref, log_ref, qkv):
    live_count = live_ref[pl.program_id(0)]
    own = live_ref[pl.num_programs(0)]
    length = exact_ref.shape[0]
    width = exact_ref.shape[1]
    load_ordered(qkv_ref, own, qkv)
    key = qkv[:, width : 2 * width]
    value = qkv[:, 2 * width :]
    for span in range(length // SPAN):
        start, extent = span * SPAN, (span + 1) * SPAN
        here = slice(start, extent)

        @pl.when(start < live_count)
        def _():
            query = qkv[here, :width]
            allowed = allowed_keys(start, extent, live_count)
            mixed, logs = [], []
            for head in range(width // HEAD_DIM):
                scores = dot_t(only_head(query, head), key[:extent]) * HEAD_DIM**-0.5
                scores = jnp.where(allowed, scores, -1e9)
                top = jnp.max(scores, 1, keepdims=True)
                terms = jnp.exp(scores - top)
                denom = jnp.sum(terms, 1, keepdims=True)
                mixed.append(dot(terms.astype(LOW), value[:extent]) / denom)
                logs.append(top + jnp.log(denom))
            lane = lax.broadcasted_iota(jnp.int32, (SPAN, width), 1)
            out = jnp.where(lane < HEAD_DIM, mixed[0], mixed[1])
            exact_ref[here] = out
            log_ref[here] = jnp.where(lane < HEAD_DIM, logs[0], logs[1])
            store_ordered(heads_ref, span, own, slice(None), out.astype(LOW))

        @pl.when(start >= live_count)
        def _():
            exact_ref[here] = jnp.zeros((SPAN, width), WIDE)
            log_ref[here] = jnp.zeros((SPAN, width), WIDE)
            heads_ref[span] = jnp.zeros(heads_ref.shape[1:], LOW)


def row_block(rows, cols):
    return pl.BlockSpec((4, 4, None, rows, cols), lambda s, *_: (0, 0, s, 0, 0))


def attend(live_counts, qkv, width):
    xs, ys, seqs, rows, _ = qkv.shape
    length = xs * ys * rows
    flat = pl.BlockSpec((None, length, width), lambda s, *_: (s, 0, 0))
    return call(
        attend_body,
        (
            struct((xs, ys, seqs, rows, width), LOW),
            struct((seqs, length, width), WIDE),
            struct((seqs, length, width), WIDE),
        ),
        (seqs,),
        [row_block(rows, 3 * width)],
        (row_block(rows, width), flat, flat),
        4 * 10**9,
        4 * 2**20,
        scratch=[pltpu.VMEM((length, 3 * width), LOW)],
        prefetch=1,
    )(live_counts, qkv)


def attend_back_body(
    live_ref, qkv_ref, grad_ref, exact_ref, log_ref, out_ref, sum_ref,
    key_total, value_total, qkv, grads,
):
    live_count = live_ref[pl.program_id(0)]
    own = live_ref[pl.num_programs(0)]
    length, width = exact_ref.shape
    factor = HEAD_DIM**-0.5
    load_ordered(qkv_ref, own, qkv)
    load_ordered(grad_ref, own, grads)
    key = qkv[:, width : 2 * width]
    value = qkv[:, 2 * width :]
    key_total[...] = jnp.zeros_like(key_total)
    value_total[...] = jnp.zeros_like(value_total)
    sum_ref[...] = jnp.zeros_like(sum_ref)
    for span in range(length // SPAN):
        start, extent = span * SPAN, (span + 1) * SPAN
        here = slice(start, extent)

        @pl.when(start < live_count)
        def _():
            query = qkv[here, :width]
            grad = grads[here]
            inner = grad.astype(WIDE) * exact_ref[here]
            logs = log_ref[here]
            allowed = allowed_keys(start, extent, live_count)
            query_total = jnp.zeros((SPAN, width), WIDE)
            for head in range(width // HEAD_DIM):
                query_h = only_head(query, head)
                grad_h = only_head(grad, head)
                log_h = logs[:, head * HEAD_DIM : head * HEAD_DIM + 1]
                row_inner = jnp.sum(only_head(inner, head), 1, keepdims=True)
                scores = dot_t(query_h, key[:extent]) * factor
                probs = jnp.exp(jnp.where(allowed, scores, -1e9) - log_h)
                d_probs = dot_t(grad_h, value[:extent])
                value_total[:extent] += dot_0(probs.astype(LOW), grad_h)
                d_scores = (probs * (d_probs - row_inner)).astype(LOW)
                query_total += dot(d_scores, only_head(key[:extent], head))
                key_total[:extent] += dot_0(d_scores, query_h)
            out = (query_total * factor).astype(LOW)
            store_ordered(out_ref, span, own, slice(0, width), out)
            sum_ref[:, :width] += jnp.sum(out.astype(WIDE), 0, keepdims=True)

        @pl.when(start >= live_count)
        def _():
            out_ref[span, :, :, :width] = jnp.zeros(out_ref.shape[1:3] + (width,), LOW)

    key_grad = (key_total[...] * factor).astype(LOW)
    value_grad = value_total[...].astype(LOW)
    for span in range(RING):
        here = slice(span * SPAN, (span + 1) * SPAN)
        store_ordered(out_ref, span, own, slice(width, 2 * width), key_grad[here])
        store_ordered(out_ref, span, own, slice(2 * width, None), value_grad[here])
    sum_ref[:, 2 * width :] = jnp.sum(value_grad.astype(WIDE), 0, keepdims=True)


def attend_back(live_counts, qkv, grads, exact, logs):
    xs, ys, seqs, rows, _ = qkv.shape
    _, length, width = exact.shape
    flat = pl.BlockSpec((None, length, width), lambda s, *_: (s, 0, 0))
    return call(
        attend_back_body,
        (struct(qkv.shape, LOW), struct((seqs, 1, 3 * width), WIDE)),
        (seqs,),
        [row_block(rows, 3 * width), row_block(rows, width), flat, flat],
        (
            row_block(rows, 3 * width),
            pl.BlockSpec((None, 1, 3 * width), lambda s, *_: (s, 0, 0)),
        ),
        8 * 10**9,
        8 * 2**20,
        scratch=[
            pltpu.VMEM((length, width), WIDE),
            pltpu.VMEM((length, width), WIDE),
            pltpu.VMEM((length, 3 * width), LOW),
            pltpu.VMEM((length, width), LOW),
        ],
        prefetch=1,
        vmem=48,
    )(live_counts, qkv, grads, exact, logs)


def norm_parts(values, gain_vec, shift_vec):
    average = jnp.mean(values, -1, keepdims=True)
    centered = values - average
    inverse = lax.rsqrt(jnp.mean(centered * centered, -1, keepdims=True) + 1e-05)
    unit_rows = centered * inverse
    return (unit_rows * gain_vec + shift_vec, unit_rows, inverse)


def norm_back(gradient, unit_rows, inverse, gain_vec):
    scaled = gradient * gain_vec
    return inverse * (
        scaled
        - jnp.mean(scaled, -1, keepdims=True)
        - unit_rows * jnp.mean(scaled * unit_rows, -1, keepdims=True)
    )


def split_back(flat, vectors):
    pieces, start = [], 0
    for v in vectors:
        pieces.append(flat[start : start + v.size])
        start += v.size
    return pieces


def short_totals(vectors, columns):
    shared = jnp.concatenate([v.reshape(-1, 128) for v in vectors], 0)
    rows = shared.shape[0]
    parts = spread(jnp.concatenate([shared, columns], 0), COLS, 16)
    part = jnp.concatenate([jnp.sum(parts[:, :rows], 0), parts[:, rows:].reshape(-1, 128)], 0)
    part = jnp.sum(spread(part, ROWS, 8), 0)
    placed = part[rows:].reshape(16, -1, 128)
    return split_back(part[:rows].reshape(-1), vectors) + [
        placed[:, i].reshape(-1) for i in range(columns.shape[0])
    ]


def shards(
    tokens, cotangent, seq_lengths, exit_layers, layer_index,
    ln1_gain, ln1_shift, q_weight, q_bias, k_weight, v_weight, v_bias, out_weight, out_bias,
    ln2_gain, ln2_shift, up_weight, up_bias, down_weight, down_bias,
):
    seqs, own_rows, width = tokens.shape
    own = seqs * own_rows
    full_len = exit_layers.shape[1]
    x_at, y_at = lax.axis_index("x"), lax.axis_index("y")
    core_at = lax.axis_index("c").astype(jnp.int32).reshape(1)
    head_at = x_at * RING + y_at
    head_cols = q_weight.shape[1]
    ff_cols = up_weight.shape[1]

    positions = jnp.arange(full_len)
    live_all = (positions[None, :] < seq_lengths[:, None]) & (exit_layers > layer_index[0])
    live_counts = jnp.concatenate(
        [jnp.sum(live_all.astype(jnp.int32), 1), y_at.astype(jnp.int32).reshape(1)]
    )
    live_mine = lax.dynamic_slice_in_dim(live_all, head_at * own_rows, own_rows, 1)
    keep = live_mine.reshape(-1, 1).astype(WIDE)

    w_qkv = gather_weight(jnp.concatenate([q_weight, k_weight, v_weight], 1).astype(LOW))
    w_out = gather_weight(out_weight.astype(LOW))
    w_ff = gather_weight(jnp.concatenate([up_weight, down_weight], 1).astype(LOW))

    inputs = tokens.astype(WIDE).reshape(own, width)
    normed1, unit1, inverse1 = norm_parts(inputs, ln1_gain, ln1_shift)
    norm1 = ring_gather(normed1.astype(LOW))
    grad_y = cotangent.astype(WIDE).reshape(own, width)
    g_ffn = (keep * grad_y).astype(LOW)
    norm1, g_ffn = tie(norm1, g_ffn)
    norm1, cot_rows = tie(norm1, ring_gather(g_ffn))

    def mine(vector, cols):
        return lax.dynamic_index_in_dim(vector.reshape(RING, RING, cols), y_at, 1, False)

    bias = jnp.concatenate(
        [mine(q_bias, head_cols), jnp.zeros((RING, head_cols), WIDE), mine(v_bias, head_cols)], 1
    ).reshape(RING, 1, 3 * head_cols)
    qkv = qkv_project(norm1, w_qkv, bias)
    rows5 = (RING, RING, seqs, own_rows)
    qkv = swap(qkv, "x").reshape(rows5 + (3 * head_cols,))
    heads, exact, logs = attend(live_counts, qkv, head_cols)
    heads = swap(heads.reshape(RING, RING * own, head_cols), "x")
    branch1 = ring_sum(out_project(heads, w_out)) + out_bias
    middle = inputs + keep * branch1
    normed2, unit2, inverse2 = norm_parts(middle, ln2_gain, ln2_shift)
    norm2 = ring_gather(normed2.astype(LOW))

    ff_bias = mine(up_bias, ff_cols).reshape(RING, 1, ff_cols)
    hidden, grad_up, g_norm2, up_bias_part = ffn_first(norm2, cot_rows, w_ff, ff_bias)
    branch2, ff_grad = ffn_second(norm2, cot_rows, hidden, grad_up, w_ff)
    g_norm2, (branch2, ff_grad) = ring_sum(g_norm2, (branch2, ff_grad))
    ff_grad = settle(ff_grad)
    grad_mid = grad_y + norm_back(g_norm2, unit2, inverse2, ln2_gain)
    g_attn = (keep * grad_mid).astype(LOW)
    up_bias_full = lax.dynamic_update_slice_in_dim(
        jnp.zeros((RING, RING, ff_cols), WIDE), up_bias_part.reshape(RING, 1, ff_cols), y_at, 1
    )
    early = (
        jnp.sum(g_attn.astype(WIDE), 0),
        jnp.sum(g_norm2 * unit2, 0),
        jnp.sum(g_norm2, 0),
        up_bias_full,
        jnp.sum(g_ffn.astype(WIDE), 0),
    )
    part = collect(jnp.concatenate([v.reshape(-1) for v in early]).reshape(16, -1, 128), COLS)
    attn_rows = ring_gather(g_attn)
    attn_rows, part = tie(attn_rows, part)
    g_heads = swap(heads_grad(attn_rows, w_out), "x").reshape(rows5 + (head_cols,))
    part = jnp.sum(spread(part, ROWS, 8), 0)
    g_heads, part = tie(g_heads, part)
    early_totals = spread(part, COLS, 16).reshape(-1)
    d_qkv, d_sums = attend_back(live_counts, qkv, g_heads, exact, logs)
    d_qkv, early_totals, attn_rows, branch2 = tie(d_qkv, early_totals, attn_rows, branch2)
    out_bias_sum, ln2_gain_sum, ln2_shift_sum, up_bias_sum, down_bias_sum = split_back(
        early_totals, early
    )
    out_both = core_sum(*weight_grads(core_at, attn_rows, heads))
    branch2 = ring_sum(branch2) + down_bias
    result = (middle + keep * branch2).astype(LOW).reshape(tokens.shape)
    d_qkv = swap(d_qkv.reshape(RING, RING * own, 3 * head_cols), "x")
    d_qkv, out_both, result = tie(d_qkv, out_both, result)

    kept, sent = weight_grads(core_at, norm1, d_qkv)
    d_qkv, kept, sent = tie(d_qkv, kept, sent)
    g_norm1 = out_project(d_qkv, w_qkv)
    both = jnp.concatenate([core_sum(kept, sent), out_both], 3)
    g_norm1, both = tie(g_norm1, both)
    small_grad, g_norm1 = cube_collect(both, ring_sum(g_norm1))
    grad_tokens = (grad_mid + norm_back(g_norm1, unit1, inverse1, ln1_gain)).reshape(tokens.shape)
    d_sums = jnp.sum(d_sums, 0).reshape(3, head_cols)
    ln1_gain_sum, ln1_shift_sum, q_bias_sum, v_bias_sum = short_totals(
        (jnp.sum(g_norm1 * unit1, 0), jnp.sum(g_norm1, 0)), d_sums[::2]
    )
    return (
        result,
        grad_tokens,
        ln1_gain_sum,
        ln1_shift_sum,
        small_grad[:, :head_cols],
        q_bias_sum,
        small_grad[:, head_cols : 2 * head_cols],
        small_grad[:, 2 * head_cols : 3 * head_cols],
        v_bias_sum,
        small_grad[:, 3 * head_cols :],
        out_bias_sum,
        ln2_gain_sum,
        ln2_shift_sum,
        ff_grad[:, :ff_cols],
        up_bias_sum,
        ff_grad[:, ff_cols:],
        down_bias_sum,
    )


def solution(mesh):
    wide = Mesh(mesh.devices.reshape(4, 2, 4, 4), ("z", "c", "x", "y"))
    act = P(ROWS, COLS, None)
    weight = P(ROWS, COLS)
    vector = P()
    in_specs = (
        act, act, P(ROWS), P(ROWS, None), vector, vector, vector,
        weight, vector, weight, weight, vector, weight, vector, vector, vector,
        weight, vector, weight, vector,
    )
    out_specs = (
        act, act, vector, vector, weight, vector, weight, weight, vector, weight,
        vector, vector, vector, weight, vector, weight, vector,
    )
    return jax.shard_map(
        shards, mesh=wide, in_specs=in_specs, out_specs=out_specs, check_vma=False
    )
```

```python
from functools import partial

import jax
import jax.numpy as jnp
from jax import lax
from jax.experimental import pallas as pl
from jax.experimental.pallas import tpu as pltpu
from jax.sharding import Mesh
from jax.sharding import PartitionSpec as P

HEAD_DIM = 64
SPAN = 256
LOW = jnp.bfloat16
WIDE = jnp.float32
RING = 4
ROWS = ("z", "c")
COLS = ("x", "y")


def dot(left, right):
    return jnp.dot(left, right, preferred_element_type=WIDE)


def dot_t(left, right):
    return lax.dot_general(left, right, (((1,), (1,)), ((), ())), preferred_element_type=WIDE)


def dot_0(left, right):
    return lax.dot_general(left, right, (((0,), (0,)), ((), ())), preferred_element_type=WIDE)


def call(body, out_shape, grid, in_specs, out_specs, flops, traffic, scratch=(), prefetch=0, vmem=60):
    return pl.pallas_call(
        body,
        out_shape=out_shape,
        grid_spec=pltpu.PrefetchScalarGridSpec(
            num_scalar_prefetch=prefetch,
            grid=grid,
            in_specs=in_specs,
            out_specs=out_specs,
            scratch_shapes=list(scratch),
        ),
        compiler_params=pltpu.CompilerParams(vmem_limit_bytes=vmem * 2**20),
        cost_estimate=pl.CostEstimate(flops=flops, bytes_accessed=traffic, transcendentals=0),
    )


def whole(shape):
    return pl.BlockSpec(shape, lambda *_: (0,) * len(shape))


def struct(shape, dtype):
    return jax.ShapeDtypeStruct(shape, dtype)


def spread(array, axes, size):
    return lax.all_to_all(jnp.broadcast_to(array[None], (size,) + array.shape), axes, 0, 0)


def collect(parts, axes):
    return jnp.sum(lax.all_to_all(parts, axes, 0, 0).astype(WIDE), 0)


def swap(parts, axes):
    return lax.all_to_all(parts, axes, 0, 0)


def ring(array, step, axis="y"):
    return lax.ppermute(array, axis, [(i, (i + step) % RING) for i in range(RING)])


def ring_collect(parts, axis, dim):
    here = lax.axis_index(axis)

    def part(step):
        return lax.dynamic_index_in_dim(parts, (here + step) % RING, dim, False)

    terms = [part(0)] + [ring(part(step), step, axis) for step in (1, 2, 3)]
    return sum(term.astype(WIDE) for term in terms)


def cube_collect(parts, beside):
    half = parts.shape[2] // 2
    first = ring_collect(parts[:, :, :half], "z", 0).astype(LOW)
    second = ring_collect(parts[:, :, half:], "x", 1).astype(LOW)
    first, second, beside = tie(first, second, beside)
    return jnp.concatenate([ring_collect(first, "x", 0), ring_collect(second, "z", 0)], 0), beside


def ring_gather(rows):
    half = rows.shape[0] // 2
    first, second = rows[:half], rows[half:]
    before_first, after_second = ring(first, 1), ring(second, -1)
    before_second, after_first = ring(second, 1), ring(first, -1)
    across_first, across_second = ring(before_first, 1), ring(after_second, -1)
    return jnp.concatenate(
        [
            first, second, before_first, before_second,
            after_first, after_second, across_first, across_second,
        ],
        0,
    )


def ring_sum(rows):
    own = rows.shape[0] // RING
    half = own // 2
    start, before, after, across = (rows[i * own : (i + 1) * own] for i in range(RING))
    from_before, from_after = ring(across[:half], 1), ring(across[half:], -1)
    second_after, first_before = ring(after[half:], 1), ring(before[:half], -1)
    first_after = ring((after[:half].astype(WIDE) + from_before.astype(WIDE)).astype(LOW), 1)
    second_before = ring((before[half:].astype(WIDE) + from_after.astype(WIDE)).astype(LOW), -1)
    first = start[:half].astype(WIDE) + first_after.astype(WIDE) + first_before.astype(WIDE)
    second = start[half:].astype(WIDE) + second_after.astype(WIDE) + second_before.astype(WIDE)
    return jnp.concatenate([first, second], 0)


def tie(*arrays):
    return lax.optimization_barrier(arrays)


def gather_weight(shard):
    full = lax.all_gather(shard, ("z", "c", "x"), axis=0)
    return full.reshape((8, 4) + shard.shape)


def settle(gradient):
    total = lax.psum_scatter(
        gradient.reshape((32,) + gradient.shape[2:]), ("z", "c", "x"), scatter_dimension=0
    )
    return total.astype(WIDE)


def qkv_body(rows_ref, weight_ref, bias_ref, out_ref):
    weight = weight_ref[...].reshape(rows_ref.shape[1], -1)
    out_ref[...] = (dot(rows_ref[...], weight) + bias_ref[...]).astype(LOW)


def qkv_project(rows, weight, bias):
    count, width = rows.shape
    zc, xs, piece, _ = weight.shape
    cols = bias.shape[-1]
    return call(
        qkv_body,
        struct((xs, count, cols), LOW),
        (xs,),
        [
            whole((count, width)),
            pl.BlockSpec((zc, None, piece, cols), lambda i: (0, i, 0, 0)),
            pl.BlockSpec((None, 1, cols), lambda i: (i, 0, 0)),
        ],
        pl.BlockSpec((None, count, cols), lambda i: (i, 0, 0)),
        2 * count * width * xs * cols,
        10 * 2**20,
    )(rows, weight, bias)


def out_body(place_ref, heads_ref, weight_ref, out_ref, joined):
    @pl.when(pl.program_id(0) == 0)
    def _():
        joined[...] = jnp.concatenate([heads_ref[i] for i in range(RING)], 1)

    weight = jnp.concatenate([weight_ref[i] for i in range(RING)], 1)
    store_rows(out_ref, place_ref, dot_t(joined[...], weight).astype(LOW))


def store_rows(out_ref, place_ref, value):
    rows = value.shape[0] // RING
    for slot in range(RING):
        at = pl.multiple_of(place_ref[slot] * rows, rows)
        out_ref[pl.ds(at, rows)] = value[slot * rows : (slot + 1) * rows]


def out_project(places, heads, weight, at):
    xs, count, cols = heads.shape
    zc, _, piece, _ = weight.shape
    return call(
        out_body,
        struct((count, zc * piece), LOW),
        (zc,),
        [
            whole(heads.shape),
            pl.BlockSpec((None, xs, piece, cols), lambda i, *_: (i, 0, 0, at)),
        ],
        pl.BlockSpec((count, piece), lambda i, *_: (0, i)),
        2 * count * zc * piece * xs * cols,
        5 * 2**20,
        scratch=[pltpu.VMEM((count, xs * cols), LOW)],
        prefetch=1,
    )(places, heads, weight)


def heads_grad_body(rows_ref, weight_ref, out_ref):
    weight = weight_ref[...].reshape(rows_ref.shape[1], -1)
    out_ref[...] = dot(rows_ref[...], weight).astype(LOW)


def heads_grad(rows, weight, cols, at):
    count, width = rows.shape
    zc, xs, piece, _ = weight.shape
    return call(
        heads_grad_body,
        struct((xs, count, cols), LOW),
        (xs,),
        [
            whole((count, width)),
            pl.BlockSpec((zc, None, piece, cols), lambda i: (0, i, 0, at)),
        ],
        pl.BlockSpec((None, count, cols), lambda i: (i, 0, 0)),
        2 * count * width * xs * cols,
        5 * 2**20,
    )(rows, weight)


def weight_grad_body(place_ref, rows_ref, grad_ref, keep_ref, send_ref):
    value = dot_0(rows_ref[...], grad_ref[...]).astype(LOW)
    value = value.reshape(4, 2, -1, value.shape[-1])
    first = place_ref[0] == 0
    keep_ref[...] = jnp.where(first, value[:, 0], value[:, 1])
    send_ref[...] = jnp.where(first, value[:, 1], value[:, 0])


def weight_grads(core_at, rows, columns):
    count, width = rows.shape
    xs, _, cols = columns.shape
    piece = width // 8
    half = struct((4, xs, piece, cols), LOW)
    block = pl.BlockSpec((4, None, piece, cols), lambda i, *_: (0, i, 0, 0))
    return call(
        weight_grad_body,
        (half, half),
        (xs,),
        [whole((count, width)), pl.BlockSpec((None, count, cols), lambda i, *_: (i, 0, 0))],
        (block, block),
        2 * count * width * xs * cols,
        15 * 2**20,
        prefetch=1,
    )(core_at, rows, columns)


def core_sum(kept, sent):
    other = lax.ppermute(sent, "c", [(0, 1), (1, 0)])
    return (kept.astype(WIDE) + other.astype(WIDE)).astype(LOW)


def add_up(total, term):
    @pl.when(pl.program_id(0) == 0)
    def _():
        total[...] = term

    @pl.when(pl.program_id(0) > 0)
    def _():
        total[...] += term


def ffn_first_body(
    place_ref, norm_ref, cot_ref, up_ref, down_ref, bias_ref,
    hidden_ref, grad_up_ref, norm_grad_ref, bias_grad_ref, total,
):
    width, cols = norm_ref.shape[1], up_ref.shape[-1]
    up_w = up_ref[...].reshape(width, cols)
    up = dot(norm_ref[...], up_w) + bias_ref[...]
    normal = 0.5 * (1.0 + lax.erf(up * 0.7071067811865476))
    hidden_ref[...] = (up * normal).astype(LOW)
    slope = normal + up * (jnp.exp(-0.5 * up * up) * 0.3989422804014327)
    grad_up = (dot(cot_ref[...], down_ref[...].reshape(width, cols)) * slope).astype(LOW)
    grad_up_ref[...] = grad_up
    bias_grad_ref[...] = jnp.sum(grad_up.astype(WIDE), 0, keepdims=True)
    add_up(total, dot_t(grad_up, up_w))

    @pl.when(pl.program_id(0) == pl.num_programs(0) - 1)
    def _():
        store_rows(norm_grad_ref, place_ref, total[...].astype(LOW))


def ffn_first(places, norm_rows, cot_rows, weight, bias):
    count, width = norm_rows.shape
    zc, xs, piece, cols = weight.shape
    size = cols // 2
    rows = whole((count, width))
    vector = pl.BlockSpec((None, 1, size), lambda i, *_: (i, 0, 0))
    wide = pl.BlockSpec((count, size), lambda i, *_: (0, i))
    return call(
        ffn_first_body,
        (
            struct((count, xs * size), LOW),
            struct((count, xs * size), LOW),
            struct((count, width), LOW),
            struct((xs, 1, size), WIDE),
        ),
        (xs,),
        [
            rows,
            rows,
            pl.BlockSpec((zc, None, piece, size), lambda i, *_: (0, i, 0, 0)),
            pl.BlockSpec((zc, None, piece, size), lambda i, *_: (0, i, 0, 1)),
            vector,
        ],
        (wide, wide, rows, vector),
        6 * count * width * xs * size,
        25 * 2**20,
        scratch=[pltpu.VMEM((count, width), WIDE)],
        prefetch=1,
    )(places, norm_rows, cot_rows, weight, weight, bias)


def ffn_second_body(
    norm_ref, cot_ref, hidden_ref, grad_up_ref, down_ref, branch_ref, weight_grad_ref, total
):
    width, cols = norm_ref.shape[1], down_ref.shape[-1]
    zc, piece, _ = weight_grad_ref.shape
    hidden = hidden_ref[...]
    weight_grad_ref[:, :, :cols] = (
        dot_0(norm_ref[...], grad_up_ref[...]).astype(LOW).reshape(zc, piece, cols)
    )
    weight_grad_ref[:, :, cols:] = dot_0(cot_ref[...], hidden).astype(LOW).reshape(zc, piece, cols)
    add_up(total, dot_t(hidden, down_ref[...].reshape(width, cols)))

    @pl.when(pl.program_id(0) == pl.num_programs(0) - 1)
    def _():
        branch_ref[...] = total[...].astype(LOW)


def ffn_second(norm_rows, cot_rows, hidden, grad_up, weight):
    count, width = norm_rows.shape
    zc, xs, piece, cols = weight.shape
    size = cols // 2
    rows = whole((count, width))
    wide = pl.BlockSpec((count, size), lambda i: (0, i))
    return call(
        ffn_second_body,
        (struct((count, width), LOW), struct(weight.shape, LOW)),
        (xs,),
        [rows, rows, wide, wide, pl.BlockSpec((zc, None, piece, size), lambda i: (0, i, 0, 1))],
        (rows, pl.BlockSpec((zc, None, piece, cols), lambda i: (0, i, 0, 0))),
        6 * count * width * xs * size,
        40 * 2**20,
        scratch=[pltpu.VMEM((count, width), WIDE)],
    )(norm_rows, cot_rows, hidden, grad_up, weight)


def only_head(array, head):
    lane = lax.broadcasted_iota(jnp.int32, array.shape, 1)
    return jnp.where(lane // HEAD_DIM == head, array, jnp.zeros_like(array))


def allowed_keys(start, extent, live_count):
    q_place = start + lax.broadcasted_iota(jnp.int32, (SPAN, extent), 0)
    k_place = lax.broadcasted_iota(jnp.int32, (SPAN, extent), 1)
    return k_place <= jnp.minimum(q_place, live_count - 1)


def slot_of(place, own):
    apart = (place - own + RING) % RING
    return jnp.where(apart == 0, 0, jnp.where(apart == RING - 1, 1, apart + 1))


def load_ordered(blocks_ref, own, into):
    rows = blocks_ref.shape[2]
    for x in range(RING):
        for y in range(RING):
            at = (x * RING + y) * rows
            into[at : at + rows] = blocks_ref[x, slot_of(y, own)]


def store_ordered(blocks_ref, x, own, cols, value):
    rows = blocks_ref.shape[2]
    for y in range(RING):
        blocks_ref[x, slot_of(y, own), :, cols] = value[y * rows : (y + 1) * rows]


def attend_body(live_ref, qkv_ref, heads_ref, exact_ref, log_ref, qkv):
    live_count = live_ref[pl.program_id(0)]
    own = live_ref[pl.num_programs(0)]
    length = exact_ref.shape[0]
    width = exact_ref.shape[1]
    load_ordered(qkv_ref, own, qkv)
    key = qkv[:, width : 2 * width]
    value = qkv[:, 2 * width :]
    for span in range(length // SPAN):
        start, extent = span * SPAN, (span + 1) * SPAN
        here = slice(start, extent)

        @pl.when(start < live_count)
        def _():
            query = qkv[here, :width]
            allowed = allowed_keys(start, extent, live_count)
            mixed, logs = [], []
            for head in range(width // HEAD_DIM):
                scores = dot_t(only_head(query, head), key[:extent]) * HEAD_DIM**-0.5
                scores = jnp.where(allowed, scores, -1e9)
                top = jnp.max(scores, 1, keepdims=True)
                terms = jnp.exp(scores - top)
                denom = jnp.sum(terms, 1, keepdims=True)
                mixed.append(dot(terms.astype(LOW), value[:extent]) / denom)
                logs.append(top + jnp.log(denom))
            lane = lax.broadcasted_iota(jnp.int32, (SPAN, width), 1)
            out = jnp.where(lane < HEAD_DIM, mixed[0], mixed[1])
            exact_ref[here] = out
            log_ref[here] = jnp.where(lane < HEAD_DIM, logs[0], logs[1])
            store_ordered(heads_ref, span, own, slice(None), out.astype(LOW))

        @pl.when(start >= live_count)
        def _():
            exact_ref[here] = jnp.zeros((SPAN, width), WIDE)
            log_ref[here] = jnp.zeros((SPAN, width), WIDE)
            heads_ref[span] = jnp.zeros(heads_ref.shape[1:], LOW)


def row_block(rows, cols):
    return pl.BlockSpec((4, 4, None, rows, cols), lambda s, *_: (0, 0, s, 0, 0))


def attend(live_counts, qkv, width):
    xs, ys, seqs, rows, _ = qkv.shape
    length = xs * ys * rows
    flat = pl.BlockSpec((None, length, width), lambda s, *_: (s, 0, 0))
    return call(
        attend_body,
        (
            struct((xs, ys, seqs, rows, width), LOW),
            struct((seqs, length, width), WIDE),
            struct((seqs, length, width), WIDE),
        ),
        (seqs,),
        [row_block(rows, 3 * width)],
        (row_block(rows, width), flat, flat),
        4 * 10**9,
        4 * 2**20,
        scratch=[pltpu.VMEM((length, 3 * width), LOW)],
        prefetch=1,
    )(live_counts, qkv)


def attend_back_body(
    live_ref, qkv_ref, grad_ref, exact_ref, log_ref, out_ref, sum_ref,
    key_total, value_total, qkv, grads,
):
    live_count = live_ref[pl.program_id(0)]
    own = live_ref[pl.num_programs(0)]
    length, width = exact_ref.shape
    factor = HEAD_DIM**-0.5
    load_ordered(qkv_ref, own, qkv)
    load_ordered(grad_ref, own, grads)
    key = qkv[:, width : 2 * width]
    value = qkv[:, 2 * width :]
    key_total[...] = jnp.zeros_like(key_total)
    value_total[...] = jnp.zeros_like(value_total)
    sum_ref[...] = jnp.zeros_like(sum_ref)
    for span in range(length // SPAN):
        start, extent = span * SPAN, (span + 1) * SPAN
        here = slice(start, extent)

        @pl.when(start < live_count)
        def _():
            query = qkv[here, :width]
            grad = grads[here]
            inner = grad.astype(WIDE) * exact_ref[here]
            logs = log_ref[here]
            allowed = allowed_keys(start, extent, live_count)
            query_total = jnp.zeros((SPAN, width), WIDE)
            for head in range(width // HEAD_DIM):
                query_h = only_head(query, head)
                grad_h = only_head(grad, head)
                log_h = logs[:, head * HEAD_DIM : head * HEAD_DIM + 1]
                row_inner = jnp.sum(only_head(inner, head), 1, keepdims=True)
                scores = dot_t(query_h, key[:extent]) * factor
                probs = jnp.exp(jnp.where(allowed, scores, -1e9) - log_h)
                d_probs = dot_t(grad_h, value[:extent])
                value_total[:extent] += dot_0(probs.astype(LOW), grad_h)
                d_scores = (probs * (d_probs - row_inner)).astype(LOW)
                query_total += dot(d_scores, only_head(key[:extent], head))
                key_total[:extent] += dot_0(d_scores, query_h)
            out = (query_total * factor).astype(LOW)
            store_ordered(out_ref, span, own, slice(0, width), out)
            sum_ref[:, :width] += jnp.sum(out.astype(WIDE), 0, keepdims=True)

        @pl.when(start >= live_count)
        def _():
            out_ref[span, :, :, :width] = jnp.zeros(out_ref.shape[1:3] + (width,), LOW)

    key_grad = (key_total[...] * factor).astype(LOW)
    value_grad = value_total[...].astype(LOW)
    for span in range(RING):
        here = slice(span * SPAN, (span + 1) * SPAN)
        store_ordered(out_ref, span, own, slice(width, 2 * width), key_grad[here])
        store_ordered(out_ref, span, own, slice(2 * width, None), value_grad[here])
    sum_ref[:, 2 * width :] = jnp.sum(value_grad.astype(WIDE), 0, keepdims=True)


def attend_back(live_counts, qkv, grads, exact, logs):
    xs, ys, seqs, rows, _ = qkv.shape
    _, length, width = exact.shape
    flat = pl.BlockSpec((None, length, width), lambda s, *_: (s, 0, 0))
    return call(
        attend_back_body,
        (struct(qkv.shape, LOW), struct((seqs, 1, 3 * width), WIDE)),
        (seqs,),
        [row_block(rows, 3 * width), row_block(rows, width), flat, flat],
        (
            row_block(rows, 3 * width),
            pl.BlockSpec((None, 1, 3 * width), lambda s, *_: (s, 0, 0)),
        ),
        8 * 10**9,
        8 * 2**20,
        scratch=[
            pltpu.VMEM((length, width), WIDE),
            pltpu.VMEM((length, width), WIDE),
            pltpu.VMEM((length, 3 * width), LOW),
            pltpu.VMEM((length, width), LOW),
        ],
        prefetch=1,
    )(live_counts, qkv, grads, exact, logs)


def norm_parts(values, gain_vec, shift_vec):
    average = jnp.mean(values, -1, keepdims=True)
    centered = values - average
    inverse = lax.rsqrt(jnp.mean(centered * centered, -1, keepdims=True) + 1e-05)
    unit_rows = centered * inverse
    return (unit_rows * gain_vec + shift_vec, unit_rows, inverse)


def norm_back(gradient, unit_rows, inverse, gain_vec):
    scaled = gradient * gain_vec
    return inverse * (
        scaled
        - jnp.mean(scaled, -1, keepdims=True)
        - unit_rows * jnp.mean(scaled * unit_rows, -1, keepdims=True)
    )


def split_back(flat, vectors):
    pieces, start = [], 0
    for v in vectors:
        pieces.append(flat[start : start + v.size])
        start += v.size
    return pieces


def last_totals(vectors, columns, ready):
    shared = jnp.concatenate([v.reshape(-1, 128) for v in vectors], 0)
    rows, more = shared.shape[0], columns.shape[0]
    parts = spread(jnp.concatenate([shared, columns, ready], 0), COLS, 16)
    part = jnp.sum(parts[:, :rows], 0)
    part = jnp.concatenate([part, parts[:, rows : rows + more].reshape(-1, 128)], 0)
    part = jnp.sum(spread(part, ROWS, 8), 0)
    placed = part[rows:].reshape(16, more, 128)
    totals = split_back(part[:rows].reshape(-1), vectors)
    return totals + [placed[:, i].reshape(-1) for i in range(more)], parts[:, rows + more :]


def shards(
    tokens, cotangent, seq_lengths, exit_layers, layer_index,
    ln1_gain, ln1_shift, q_weight, q_bias, k_weight, v_weight, v_bias, out_weight, out_bias,
    ln2_gain, ln2_shift, up_weight, up_bias, down_weight, down_bias,
):
    seqs, own_rows, width = tokens.shape
    own = seqs * own_rows
    full_len = exit_layers.shape[1]
    x_at, y_at = lax.axis_index("x"), lax.axis_index("y")
    core_at = lax.axis_index("c").astype(jnp.int32).reshape(1)
    head_at = x_at * RING + y_at
    head_cols = q_weight.shape[1]
    ff_cols = up_weight.shape[1]

    positions = jnp.arange(full_len)
    live_all = (positions[None, :] < seq_lengths[:, None]) & (exit_layers > layer_index[0])
    live_counts = jnp.concatenate(
        [jnp.sum(live_all.astype(jnp.int32), 1), y_at.astype(jnp.int32).reshape(1)]
    )
    slots = jnp.arange(RING, dtype=jnp.int32)
    places = (y_at.astype(jnp.int32) + jnp.array([0, RING - 1, 1, 2], jnp.int32)) % RING
    live_mine = lax.dynamic_slice_in_dim(live_all, head_at * own_rows, own_rows, 1)
    keep = live_mine.reshape(-1, 1).astype(WIDE)

    w_attn = gather_weight(
        jnp.concatenate([q_weight, k_weight, v_weight, out_weight], 1).astype(LOW)
    )
    w_ff = gather_weight(jnp.concatenate([up_weight, down_weight], 1).astype(LOW))

    inputs = tokens.astype(WIDE).reshape(own, width)
    normed1, unit1, inverse1 = norm_parts(inputs, ln1_gain, ln1_shift)
    norm1 = ring_gather(normed1.astype(LOW))
    grad_y = cotangent.astype(WIDE).reshape(own, width)
    g_ffn = (keep * grad_y).astype(LOW)
    norm1, g_ffn = tie(norm1, g_ffn)
    norm1, cot_rows = tie(norm1, ring_gather(g_ffn))

    def mine(vector, cols):
        return lax.dynamic_index_in_dim(vector.reshape(RING, RING, cols), y_at, 1, False)

    bias = jnp.concatenate(
        [mine(q_bias, head_cols), jnp.zeros((RING, head_cols), WIDE), mine(v_bias, head_cols)], 1
    ).reshape(RING, 1, 3 * head_cols)
    qkv = qkv_project(norm1, w_attn, bias)
    rows5 = (RING, RING, seqs, own_rows)
    qkv = swap(qkv, "x").reshape(rows5 + (3 * head_cols,))
    heads, exact, logs = attend(live_counts, qkv, head_cols)
    heads = swap(heads.reshape(RING, RING * own, head_cols), "x")
    branch1 = ring_sum(out_project(slots, heads, w_attn, 3)) + out_bias
    middle = inputs + keep * branch1
    normed2, unit2, inverse2 = norm_parts(middle, ln2_gain, ln2_shift)
    norm2 = ring_gather(normed2.astype(LOW))

    ff_bias = mine(up_bias, ff_cols).reshape(RING, 1, ff_cols)
    hidden, grad_up, g_norm2, up_bias_part = ffn_first(places, norm2, cot_rows, w_ff, ff_bias)
    g_norm2 = swap(g_norm2.reshape(RING, own, width), "y")
    g_norm2, branch2, ff_grad = tie(
        g_norm2, *ffn_second(norm2, cot_rows, hidden, grad_up, w_ff)
    )
    g_norm2 = jnp.sum(g_norm2.astype(WIDE), 0)
    ff_grad = settle(ff_grad)
    grad_mid = grad_y + norm_back(g_norm2, unit2, inverse2, ln2_gain)
    g_attn = (keep * grad_mid).astype(LOW)
    attn_rows = ring_gather(g_attn)
    g_heads, branch2 = tie(heads_grad(attn_rows, w_attn, head_cols, 3), branch2)
    g_heads = swap(g_heads, "x").reshape(rows5 + (head_cols,))
    branch2 = ring_sum(branch2) + down_bias
    result = (middle + keep * branch2).astype(LOW).reshape(tokens.shape)
    d_qkv, d_sums = attend_back(live_counts, qkv, g_heads, exact, logs)
    d_qkv, attn_rows = tie(d_qkv, attn_rows)
    out_both = core_sum(*weight_grads(core_at, attn_rows, heads))
    d_qkv = swap(d_qkv.reshape(RING, RING * own, 3 * head_cols), "x")

    up_bias_full = lax.dynamic_update_slice_in_dim(
        jnp.zeros((RING, RING, ff_cols), WIDE), up_bias_part.reshape(RING, 1, ff_cols), y_at, 1
    )
    early = (
        jnp.sum(g_attn.astype(WIDE), 0),
        jnp.sum(g_norm2 * unit2, 0),
        jnp.sum(g_norm2, 0),
        up_bias_full,
        jnp.sum(g_ffn.astype(WIDE), 0),
    )
    early_flat = jnp.concatenate([v.reshape(-1) for v in early]).reshape(16, -1, 128)
    d_qkv, out_both, result, early_flat = tie(d_qkv, out_both, result, early_flat)
    part = collect(early_flat, COLS)
    kept, sent = weight_grads(core_at, norm1, d_qkv)
    d_qkv, kept, sent, part = tie(d_qkv, kept, sent, part)
    part = jnp.sum(spread(part, ROWS, 8), 0)
    g_norm1 = out_project(places, d_qkv, w_attn, 0)
    both = jnp.concatenate([core_sum(kept, sent), out_both], 3)
    g_norm1, both, part = tie(g_norm1, both, part)
    g_norm1 = jnp.sum(swap(g_norm1.reshape(RING, own, width), "y").astype(WIDE), 0)
    small_grad, g_norm1 = cube_collect(both, g_norm1)
    grad_tokens = (grad_mid + norm_back(g_norm1, unit1, inverse1, ln1_gain)).reshape(tokens.shape)
    d_sums = jnp.sum(d_sums, 0).reshape(3, head_cols)
    (ln1_gain_sum, ln1_shift_sum, q_bias_sum, v_bias_sum), early_totals = last_totals(
        (jnp.sum(g_norm1 * unit1, 0), jnp.sum(g_norm1, 0)), d_sums[::2], part
    )
    out_bias_sum, ln2_gain_sum, ln2_shift_sum, up_bias_sum, down_bias_sum = split_back(
        early_totals.reshape(-1), early
    )
    return (
        result,
        grad_tokens,
        ln1_gain_sum,
        ln1_shift_sum,
        small_grad[:, :head_cols],
        q_bias_sum,
        small_grad[:, head_cols : 2 * head_cols],
        small_grad[:, 2 * head_cols : 3 * head_cols],
        v_bias_sum,
        small_grad[:, 3 * head_cols :],
        out_bias_sum,
        ln2_gain_sum,
        ln2_shift_sum,
        ff_grad[:, :ff_cols],
        up_bias_sum,
        ff_grad[:, ff_cols:],
        down_bias_sum,
    )


def solution(mesh):
    wide = Mesh(mesh.devices.reshape(4, 2, 4, 4), ("z", "c", "x", "y"))
    act = P(ROWS, COLS, None)
    weight = P(ROWS, COLS)
    vector = P()
    in_specs = (
        act, act, P(ROWS), P(ROWS, None), vector, vector, vector,
        weight, vector, weight, weight, vector, weight, vector, vector, vector,
        weight, vector, weight, vector,
    )
    out_specs = (
        act, act, vector, vector, weight, vector, weight, weight, vector, weight,
        vector, vector, vector, weight, vector, weight, vector,
    )
    return jax.shard_map(
        shards, mesh=wide, in_specs=in_specs, out_specs=out_specs, check_vma=False
    )
```

```python
from functools import partial

import jax
import jax.numpy as jnp
from jax import lax
from jax.experimental import pallas as pl
from jax.experimental.pallas import tpu as pltpu
from jax.sharding import Mesh
from jax.sharding import PartitionSpec as P

HEAD_DIM = 64
SPAN = 256
LOW = jnp.bfloat16
WIDE = jnp.float32
RING = 4
ROWS = ("z", "c")
COLS = ("x", "y")


def dot(left, right):
    return jnp.dot(left, right, preferred_element_type=WIDE)


def dot_t(left, right):
    return lax.dot_general(left, right, (((1,), (1,)), ((), ())), preferred_element_type=WIDE)


def dot_0(left, right):
    return lax.dot_general(left, right, (((0,), (0,)), ((), ())), preferred_element_type=WIDE)


def call(body, out_shape, grid, in_specs, out_specs, flops, traffic, scratch=(), prefetch=0, vmem=40, aliases=None):
    return pl.pallas_call(
        body,
        out_shape=out_shape,
        grid_spec=pltpu.PrefetchScalarGridSpec(
            num_scalar_prefetch=prefetch,
            grid=grid,
            in_specs=in_specs,
            out_specs=out_specs,
            scratch_shapes=list(scratch),
        ),
        compiler_params=pltpu.CompilerParams(vmem_limit_bytes=vmem * 2**20),
        input_output_aliases=aliases or {},
        cost_estimate=pl.CostEstimate(flops=flops, bytes_accessed=traffic, transcendentals=0),
    )


def whole(shape):
    return pl.BlockSpec(shape, lambda *_: (0,) * len(shape))


def struct(shape, dtype):
    return jax.ShapeDtypeStruct(shape, dtype)


def spread(array, axes, size):
    return lax.all_to_all(jnp.broadcast_to(array[None], (size,) + array.shape), axes, 0, 0)


def collect(parts, axes):
    return jnp.sum(lax.all_to_all(parts, axes, 0, 0).astype(WIDE), 0)


def swap(parts, axes):
    return lax.all_to_all(parts, axes, 0, 0)


def ring(array, step, axis="y"):
    return lax.ppermute(array, axis, [(i, (i + step) % RING) for i in range(RING)])


def ring_stack(array, axis):
    return jnp.stack([array] + [ring(array, step, axis) for step in (1, -1, 2)])


def ring_collect(parts, axis):
    came = [ring(parts[slot], step, axis) for slot, step in ((1, -1), (2, 1), (3, 2))]
    return sum(term.astype(WIDE) for term in [parts[0]] + came)


def ring_gather(rows):
    half = rows.shape[0] // 2
    first, second = rows[:half], rows[half:]
    before_first, after_second = ring(first, 1), ring(second, -1)
    before_second, after_first = ring(second, 1), ring(first, -1)
    across_first, across_second = ring(before_first, 1), ring(after_second, -1)
    return jnp.concatenate(
        [
            first, second, before_first, before_second,
            after_first, after_second, across_first, across_second,
        ],
        0,
    )


def ring_sum(rows):
    own = rows.shape[0] // RING
    half = own // 2
    start, before, after, across = (rows[i * own : (i + 1) * own] for i in range(RING))
    from_before, from_after = ring(across[:half], 1), ring(across[half:], -1)
    second_after, first_before = ring(after[half:], 1), ring(before[:half], -1)
    first_after = ring((after[:half].astype(WIDE) + from_before.astype(WIDE)).astype(LOW), 1)
    second_before = ring((before[half:].astype(WIDE) + from_after.astype(WIDE)).astype(LOW), -1)
    first = start[:half].astype(WIDE) + first_after.astype(WIDE) + first_before.astype(WIDE)
    second = start[half:].astype(WIDE) + second_after.astype(WIDE) + second_before.astype(WIDE)
    return jnp.concatenate([first, second], 0)


def tie(*arrays):
    return lax.optimization_barrier(arrays)


def gather_weight(shard):
    full = lax.all_gather(shard, ("z", "c", "x"), axis=0)
    return full.reshape((8, 4) + shard.shape)


def settle(gradient):
    return lax.psum_scatter(gradient, ROWS, scatter_dimension=0)


def qkv_body(rows_ref, weight_ref, bias_ref, out_ref):
    weight = weight_ref[...].reshape(rows_ref.shape[1], -1)
    out_ref[...] = (dot(rows_ref[...], weight) + bias_ref[...]).astype(LOW)


def qkv_project(rows, weight, bias):
    count, width = rows.shape
    zc, xs, piece, _ = weight.shape
    cols = bias.shape[-1]
    return call(
        qkv_body,
        struct((xs, count, cols), LOW),
        (xs,),
        [
            whole((count, width)),
            pl.BlockSpec((zc, None, piece, cols), lambda i: (0, i, 0, 0)),
            pl.BlockSpec((None, 1, cols), lambda i: (i, 0, 0)),
        ],
        pl.BlockSpec((None, count, cols), lambda i: (i, 0, 0)),
        2 * count * width * xs * cols,
        10 * 2**20,
    )(rows, weight, bias)


def out_body(place_ref, heads_ref, weight_ref, out_ref, joined):
    @pl.when(pl.program_id(0) == 0)
    def _():
        joined[...] = jnp.concatenate([heads_ref[i] for i in range(RING)], 1)

    weight = jnp.concatenate([weight_ref[i] for i in range(RING)], 1)
    store_rows(out_ref, place_ref, dot_t(joined[...], weight).astype(LOW))


def store_rows(out_ref, place_ref, value):
    rows = value.shape[0] // RING
    for slot in range(RING):
        at = pl.multiple_of(place_ref[slot] * rows, rows)
        out_ref[pl.ds(at, rows)] = value[slot * rows : (slot + 1) * rows]


def out_project(places, heads, weight, at):
    xs, count, cols = heads.shape
    zc, _, piece, _ = weight.shape
    return call(
        out_body,
        struct((count, zc * piece), LOW),
        (zc,),
        [
            whole(heads.shape),
            pl.BlockSpec((None, xs, piece, cols), lambda i, *_: (i, 0, 0, at)),
        ],
        pl.BlockSpec((count, piece), lambda i, *_: (0, i)),
        2 * count * zc * piece * xs * cols,
        5 * 2**20,
        scratch=[pltpu.VMEM((count, xs * cols), LOW)],
        prefetch=1,
    )(places, heads, weight)


def heads_grad_body(rows_ref, weight_ref, out_ref):
    weight = weight_ref[...].reshape(rows_ref.shape[1], -1)
    out_ref[...] = dot(rows_ref[...], weight).astype(LOW)


def heads_grad(rows, weight, cols, at):
    count, width = rows.shape
    zc, xs, piece, _ = weight.shape
    return call(
        heads_grad_body,
        struct((xs, count, cols), LOW),
        (xs,),
        [
            whole((count, width)),
            pl.BlockSpec((zc, None, piece, cols), lambda i: (0, i, 0, at)),
        ],
        pl.BlockSpec((None, count, cols), lambda i: (i, 0, 0)),
        2 * count * width * xs * cols,
        5 * 2**20,
    )(rows, weight)


def weight_grad_body(rows_ref, grad_ref, *refs):
    out_ref = refs[-1]
    out_ref[...] = dot_0(rows_ref[...], grad_ref[...]).astype(LOW).reshape(out_ref.shape)


def weight_grads(rows, columns, total_cols, at, onto=None):
    count, width = rows.shape
    xs, _, cols = columns.shape
    piece = width // 8
    more = () if onto is None else (onto,)
    return call(
        weight_grad_body,
        struct((8, xs, piece, total_cols), LOW),
        (xs,),
        [whole((count, width)), pl.BlockSpec((None, count, cols), lambda i: (i, 0, 0))]
        + [pl.BlockSpec(memory_space=pl.ANY)] * len(more),
        pl.BlockSpec((8, None, piece, cols), lambda i: (0, i, 0, at)),
        2 * count * width * xs * cols,
        15 * 2**20,
        aliases={2: 0} if more else None,
    )(rows, columns, *more)


def add_up(total, term):
    @pl.when(pl.program_id(0) == 0)
    def _():
        total[...] = term

    @pl.when(pl.program_id(0) > 0)
    def _():
        total[...] += term


def ffn_first_body(
    place_ref, norm_ref, cot_ref, up_ref, down_ref, bias_ref,
    hidden_ref, grad_up_ref, norm_grad_ref, bias_grad_ref, total,
):
    width, cols = norm_ref.shape[1], up_ref.shape[-1]
    up_w = up_ref[...].reshape(width, cols)
    up = dot(norm_ref[...], up_w) + bias_ref[...]
    normal = 0.5 * (1.0 + lax.erf(up * 0.7071067811865476))
    hidden_ref[...] = (up * normal).astype(LOW)
    slope = normal + up * (jnp.exp(-0.5 * up * up) * 0.3989422804014327)
    grad_up = (dot(cot_ref[...], down_ref[...].reshape(width, cols)) * slope).astype(LOW)
    grad_up_ref[...] = grad_up
    bias_grad_ref[...] = jnp.sum(grad_up.astype(WIDE), 0, keepdims=True)
    add_up(total, dot_t(grad_up, up_w))

    @pl.when(pl.program_id(0) == pl.num_programs(0) - 1)
    def _():
        store_rows(norm_grad_ref, place_ref, total[...].astype(LOW))


def ffn_first(places, norm_rows, cot_rows, weight, bias):
    count, width = norm_rows.shape
    zc, xs, piece, cols = weight.shape
    size = cols // 2
    rows = whole((count, width))
    vector = pl.BlockSpec((None, 1, size), lambda i, *_: (i, 0, 0))
    wide = pl.BlockSpec((count, size), lambda i, *_: (0, i))
    return call(
        ffn_first_body,
        (
            struct((count, xs * size), LOW),
            struct((count, xs * size), LOW),
            struct((count, width), LOW),
            struct((xs, 1, size), WIDE),
        ),
        (xs,),
        [
            rows,
            rows,
            pl.BlockSpec((zc, None, piece, size), lambda i, *_: (0, i, 0, 0)),
            pl.BlockSpec((zc, None, piece, size), lambda i, *_: (0, i, 0, 1)),
            vector,
        ],
        (wide, wide, rows, vector),
        6 * count * width * xs * size,
        25 * 2**20,
        scratch=[pltpu.VMEM((count, width), WIDE)],
        prefetch=1,
        vmem=56,
    )(places, norm_rows, cot_rows, weight, weight, bias)


def ffn_second_body(
    norm_ref, cot_ref, hidden_ref, grad_up_ref, down_ref, branch_ref, weight_grad_ref, total
):
    width, cols = norm_ref.shape[1], down_ref.shape[-1]
    zc, piece, _ = weight_grad_ref.shape
    hidden = hidden_ref[...]
    weight_grad_ref[:, :, :cols] = (
        dot_0(norm_ref[...], grad_up_ref[...]).astype(LOW).reshape(zc, piece, cols)
    )
    weight_grad_ref[:, :, cols:] = dot_0(cot_ref[...], hidden).astype(LOW).reshape(zc, piece, cols)
    add_up(total, dot_t(hidden, down_ref[...].reshape(width, cols)))

    @pl.when(pl.program_id(0) == pl.num_programs(0) - 1)
    def _():
        branch_ref[...] = total[...].astype(LOW)


def ffn_second(norm_rows, cot_rows, hidden, grad_up, weight):
    count, width = norm_rows.shape
    zc, xs, piece, cols = weight.shape
    size = cols // 2
    rows = whole((count, width))
    wide = pl.BlockSpec((count, size), lambda i: (0, i))
    return call(
        ffn_second_body,
        (struct((count, width), LOW), struct(weight.shape, LOW)),
        (xs,),
        [rows, rows, wide, wide, pl.BlockSpec((zc, None, piece, size), lambda i: (0, i, 0, 1))],
        (rows, pl.BlockSpec((zc, None, piece, cols), lambda i: (0, i, 0, 0))),
        6 * count * width * xs * size,
        40 * 2**20,
        scratch=[pltpu.VMEM((count, width), WIDE)],
        vmem=56,
    )(norm_rows, cot_rows, hidden, grad_up, weight)


def only_head(array, head):
    lane = lax.broadcasted_iota(jnp.int32, array.shape, 1)
    return jnp.where(lane // HEAD_DIM == head, array, jnp.zeros_like(array))


def allowed_keys(start, extent, live_count):
    q_place = start + lax.broadcasted_iota(jnp.int32, (SPAN, extent), 0)
    k_place = lax.broadcasted_iota(jnp.int32, (SPAN, extent), 1)
    return k_place <= jnp.minimum(q_place, live_count - 1)


def slot_of(place, own):
    apart = (place - own + RING) % RING
    return jnp.where(apart == 0, 0, jnp.where(apart == RING - 1, 1, apart + 1))


def load_ordered(blocks_ref, own, into):
    rows = blocks_ref.shape[2]
    for x in range(RING):
        for y in range(RING):
            at = (x * RING + y) * rows
            into[at : at + rows] = blocks_ref[x, slot_of(y, own)]


def store_ordered(blocks_ref, x, own, cols, value):
    rows = blocks_ref.shape[2]
    for y in range(RING):
        blocks_ref[x, slot_of(y, own), :, cols] = value[y * rows : (y + 1) * rows]


def attend_body(live_ref, qkv_ref, heads_ref, exact_ref, log_ref, qkv):
    live_count = live_ref[pl.program_id(0)]
    own = live_ref[pl.num_programs(0)]
    length = exact_ref.shape[0]
    width = exact_ref.shape[1]
    load_ordered(qkv_ref, own, qkv)
    key = qkv[:, width : 2 * width]
    value = qkv[:, 2 * width :]
    for span in range(length // SPAN):
        start, extent = span * SPAN, (span + 1) * SPAN
        here = slice(start, extent)

        @pl.when(start < live_count)
        def _():
            query = qkv[here, :width]
            allowed = allowed_keys(start, extent, live_count)
            mixed, logs = [], []
            for head in range(width // HEAD_DIM):
                scores = dot_t(only_head(query, head), key[:extent]) * HEAD_DIM**-0.5
                scores = jnp.where(allowed, scores, -1e9)
                top = jnp.max(scores, 1, keepdims=True)
                terms = jnp.exp(scores - top)
                denom = jnp.sum(terms, 1, keepdims=True)
                mixed.append(dot(terms.astype(LOW), value[:extent]) / denom)
                logs.append(top + jnp.log(denom))
            lane = lax.broadcasted_iota(jnp.int32, (SPAN, width), 1)
            out = jnp.where(lane < HEAD_DIM, mixed[0], mixed[1])
            exact_ref[here] = out
            log_ref[here] = jnp.where(lane < HEAD_DIM, logs[0], logs[1])
            store_ordered(heads_ref, span, own, slice(None), out.astype(LOW))

        @pl.when(start >= live_count)
        def _():
            exact_ref[here] = jnp.zeros((SPAN, width), WIDE)
            log_ref[here] = jnp.zeros((SPAN, width), WIDE)
            heads_ref[span] = jnp.zeros(heads_ref.shape[1:], LOW)


def row_block(rows, cols):
    return pl.BlockSpec((4, 4, None, rows, cols), lambda s, *_: (0, 0, s, 0, 0))


def attend(live_counts, qkv, width):
    xs, ys, seqs, rows, _ = qkv.shape
    length = xs * ys * rows
    flat = pl.BlockSpec((None, length, width), lambda s, *_: (s, 0, 0))
    return call(
        attend_body,
        (
            struct((xs, ys, seqs, rows, width), LOW),
            struct((seqs, length, width), WIDE),
            struct((seqs, length, width), WIDE),
        ),
        (seqs,),
        [row_block(rows, 3 * width)],
        (row_block(rows, width), flat, flat),
        4 * 10**9,
        4 * 2**20,
        scratch=[pltpu.VMEM((length, 3 * width), LOW)],
        prefetch=1,
    )(live_counts, qkv)


def attend_back_body(
    live_ref, qkv_ref, grad_ref, exact_ref, log_ref, out_ref, sum_ref,
    key_total, value_total, qkv, grads,
):
    live_count = live_ref[pl.program_id(0)]
    own = live_ref[pl.num_programs(0)]
    length, width = exact_ref.shape
    factor = HEAD_DIM**-0.5
    load_ordered(qkv_ref, own, qkv)
    load_ordered(grad_ref, own, grads)
    key = qkv[:, width : 2 * width]
    value = qkv[:, 2 * width :]
    key_total[...] = jnp.zeros_like(key_total)
    value_total[...] = jnp.zeros_like(value_total)
    sum_ref[...] = jnp.zeros_like(sum_ref)
    for span in range(length // SPAN):
        start, extent = span * SPAN, (span + 1) * SPAN
        here = slice(start, extent)

        @pl.when(start < live_count)
        def _():
            query = qkv[here, :width]
            grad = grads[here]
            inner = grad.astype(WIDE) * exact_ref[here]
            logs = log_ref[here]
            allowed = allowed_keys(start, extent, live_count)
            query_total = jnp.zeros((SPAN, width), WIDE)
            for head in range(width // HEAD_DIM):
                query_h = only_head(query, head)
                grad_h = only_head(grad, head)
                log_h = logs[:, head * HEAD_DIM : head * HEAD_DIM + 1]
                row_inner = jnp.sum(only_head(inner, head), 1, keepdims=True)
                scores = dot_t(query_h, key[:extent]) * factor
                probs = jnp.exp(jnp.where(allowed, scores, -1e9) - log_h)
                d_probs = dot_t(grad_h, value[:extent])
                value_total[:extent] += dot_0(probs.astype(LOW), grad_h)
                d_scores = (probs * (d_probs - row_inner)).astype(LOW)
                query_total += dot(d_scores, only_head(key[:extent], head))
                key_total[:extent] += dot_0(d_scores, query_h)
            out = (query_total * factor).astype(LOW)
            store_ordered(out_ref, span, own, slice(0, width), out)
            sum_ref[:, :width] += jnp.sum(out.astype(WIDE), 0, keepdims=True)

        @pl.when(start >= live_count)
        def _():
            out_ref[span, :, :, :width] = jnp.zeros(out_ref.shape[1:3] + (width,), LOW)

    key_grad = (key_total[...] * factor).astype(LOW)
    value_grad = value_total[...].astype(LOW)
    for span in range(RING):
        here = slice(span * SPAN, (span + 1) * SPAN)
        store_ordered(out_ref, span, own, slice(width, 2 * width), key_grad[here])
        store_ordered(out_ref, span, own, slice(2 * width, None), value_grad[here])
    sum_ref[:, 2 * width :] = jnp.sum(value_grad.astype(WIDE), 0, keepdims=True)


def attend_back(live_counts, qkv, grads, exact, logs):
    xs, ys, seqs, rows, _ = qkv.shape
    _, length, width = exact.shape
    flat = pl.BlockSpec((None, length, width), lambda s, *_: (s, 0, 0))
    return call(
        attend_back_body,
        (struct(qkv.shape, LOW), struct((seqs, 1, 3 * width), WIDE)),
        (seqs,),
        [row_block(rows, 3 * width), row_block(rows, width), flat, flat],
        (
            row_block(rows, 3 * width),
            pl.BlockSpec((None, 1, 3 * width), lambda s, *_: (s, 0, 0)),
        ),
        8 * 10**9,
        8 * 2**20,
        scratch=[
            pltpu.VMEM((length, width), WIDE),
            pltpu.VMEM((length, width), WIDE),
            pltpu.VMEM((length, 3 * width), LOW),
            pltpu.VMEM((length, width), LOW),
        ],
        prefetch=1,
    )(live_counts, qkv, grads, exact, logs)


def norm_parts(values, gain_vec, shift_vec):
    average = jnp.mean(values, -1, keepdims=True)
    centered = values - average
    inverse = lax.rsqrt(jnp.mean(centered * centered, -1, keepdims=True) + 1e-05)
    unit_rows = centered * inverse
    return (unit_rows * gain_vec + shift_vec, unit_rows, inverse)


def norm_back(gradient, unit_rows, inverse, gain_vec):
    scaled = gradient * gain_vec
    return inverse * (
        scaled
        - jnp.mean(scaled, -1, keepdims=True)
        - unit_rows * jnp.mean(scaled * unit_rows, -1, keepdims=True)
    )


def split_back(flat, vectors):
    pieces, start = [], 0
    for v in vectors:
        pieces.append(flat[start : start + v.size])
        start += v.size
    return pieces


def last_totals(vectors, columns, ready, later):
    shared = jnp.concatenate([v.reshape(-1, 128) for v in vectors], 0)
    rows, more = shared.shape[0], columns.shape[0]
    parts = spread(jnp.concatenate([shared, columns, ready], 0), COLS, 16)
    parts, later = tie(parts, later)
    part = jnp.sum(parts[:, :rows], 0)
    part = jnp.concatenate([part, parts[:, rows : rows + more].reshape(-1, 128)], 0)
    part = jnp.sum(spread(part, ROWS, 8), 0)
    placed = part[rows:].reshape(16, more, 128)
    totals = split_back(part[:rows].reshape(-1), vectors)
    totals += [placed[:, i].reshape(-1) for i in range(more)]
    return totals, parts[:, rows + more :], later


def shards(
    tokens, cotangent, seq_lengths, exit_layers, layer_index,
    ln1_gain, ln1_shift, q_weight, q_bias, k_weight, v_weight, v_bias, out_weight, out_bias,
    ln2_gain, ln2_shift, up_weight, up_bias, down_weight, down_bias,
):
    seqs, own_rows, width = tokens.shape
    own = seqs * own_rows
    full_len = exit_layers.shape[1]
    x_at, y_at = lax.axis_index("x"), lax.axis_index("y")
    head_at = x_at * RING + y_at
    head_cols = q_weight.shape[1]
    ff_cols = up_weight.shape[1]

    positions = jnp.arange(full_len)
    live_all = (positions[None, :] < seq_lengths[:, None]) & (exit_layers > layer_index[0])
    live_counts = jnp.concatenate(
        [jnp.sum(live_all.astype(jnp.int32), 1), y_at.astype(jnp.int32).reshape(1)]
    )
    slots = jnp.arange(RING, dtype=jnp.int32)
    apart = jnp.array([0, RING - 1, 1, 2], jnp.int32)
    places = (y_at.astype(jnp.int32) + apart) % RING
    x_places = (x_at.astype(jnp.int32) + apart) % RING
    live_mine = lax.dynamic_slice_in_dim(live_all, head_at * own_rows, own_rows, 1)
    keep = live_mine.reshape(-1, 1).astype(WIDE)

    w_attn = gather_weight(
        jnp.concatenate([q_weight, k_weight, v_weight, out_weight], 1).astype(LOW)
    )
    w_ff = jnp.concatenate([up_weight, down_weight], 1).astype(LOW)

    inputs = tokens.astype(WIDE).reshape(own, width)
    normed1, unit1, inverse1 = norm_parts(inputs, ln1_gain, ln1_shift)
    norm1 = ring_gather(normed1.astype(LOW))
    grad_y = cotangent.astype(WIDE).reshape(own, width)
    g_ffn = (keep * grad_y).astype(LOW)
    norm1, g_ffn, w_ff = tie(norm1, g_ffn, ring_stack(w_ff, "x"))
    w_ff = lax.all_gather(w_ff, ROWS, axis=0)
    norm1, cot_rows = tie(norm1, ring_gather(g_ffn))

    def mine(vector, cols):
        return lax.dynamic_index_in_dim(vector.reshape(RING, RING, cols), y_at, 1, False)

    bias = jnp.concatenate(
        [mine(q_bias, head_cols), jnp.zeros((RING, head_cols), WIDE), mine(v_bias, head_cols)], 1
    ).reshape(RING, 1, 3 * head_cols)
    qkv = qkv_project(norm1, w_attn, bias)
    rows5 = (RING, RING, seqs, own_rows)
    qkv = swap(qkv, "x").reshape(rows5 + (3 * head_cols,))
    heads, exact, logs = attend(live_counts, qkv, head_cols)
    heads = swap(heads.reshape(RING, RING * own, head_cols), "x")
    branch1 = ring_sum(out_project(slots, heads, w_attn, 3)) + out_bias
    middle = inputs + keep * branch1
    normed2, unit2, inverse2 = norm_parts(middle, ln2_gain, ln2_shift)
    norm2 = ring_gather(normed2.astype(LOW))

    ff_bias = mine(up_bias, ff_cols)[x_places].reshape(RING, 1, ff_cols)
    hidden, grad_up, g_norm2, up_bias_part = ffn_first(places, norm2, cot_rows, w_ff, ff_bias)
    g_norm2 = swap(g_norm2.reshape(RING, own, width), "y")
    g_norm2, branch2, ff_grad = tie(
        g_norm2, *ffn_second(norm2, cot_rows, hidden, grad_up, w_ff)
    )
    g_norm2 = jnp.sum(g_norm2.astype(WIDE), 0)
    ff_grad = settle(ff_grad)
    grad_mid = grad_y + norm_back(g_norm2, unit2, inverse2, ln2_gain)
    g_attn = (keep * grad_mid).astype(LOW)
    attn_rows = ring_gather(g_attn)
    g_heads = heads_grad(attn_rows, w_attn, head_cols, 3)
    g_heads, branch2 = tie(swap(g_heads, "x").reshape(rows5 + (head_cols,)), branch2)
    branch2 = ring_collect(branch2.reshape(RING, own, width), "y") + down_bias
    result = (middle + keep * branch2).astype(LOW).reshape(tokens.shape)
    d_qkv, d_sums = attend_back(live_counts, qkv, g_heads, exact, logs)
    d_qkv, attn_rows = tie(d_qkv, attn_rows)
    attn_grad = weight_grads(attn_rows, heads, 4 * head_cols, 3)
    d_qkv = swap(d_qkv.reshape(RING, RING * own, 3 * head_cols), "x")

    up_bias_full = jnp.zeros((RING, RING, ff_cols), WIDE)
    for slot in range(RING):
        up_bias_full = lax.dynamic_update_slice(
            up_bias_full, up_bias_part[slot][None], (x_places[slot], y_at, 0)
        )
    early = (
        jnp.sum(g_attn.astype(WIDE), 0),
        jnp.sum(g_norm2 * unit2, 0),
        jnp.sum(g_norm2, 0),
        up_bias_full,
        jnp.sum(g_ffn.astype(WIDE), 0),
    )
    early_flat = jnp.concatenate([v.reshape(-1) for v in early]).reshape(16, -1, 128)
    d_qkv, attn_grad, result, early_flat = tie(d_qkv, attn_grad, result, early_flat)
    part = collect(early_flat, COLS)
    attn_grad = weight_grads(norm1, d_qkv, 4 * head_cols, 0, attn_grad)
    d_qkv, attn_grad, part = tie(d_qkv, attn_grad, part)
    attn_grad = settle(attn_grad)
    part = jnp.sum(spread(part, ROWS, 8), 0)
    g_norm1 = out_project(places, d_qkv, w_attn, 0)
    g_norm1, ff_grad, part = tie(g_norm1, ff_grad, part)
    ff_grad = ring_collect(ff_grad, "x")
    g_norm1 = jnp.sum(swap(g_norm1.reshape(RING, own, width), "y").astype(WIDE), 0)
    grad_tokens = (grad_mid + norm_back(g_norm1, unit1, inverse1, ln1_gain)).reshape(tokens.shape)
    d_sums = jnp.sum(d_sums, 0).reshape(3, head_cols)
    ln1_totals, early_totals, attn_grad = last_totals(
        (jnp.sum(g_norm1 * unit1, 0), jnp.sum(g_norm1, 0)), d_sums[::2], part, attn_grad
    )
    ln1_gain_sum, ln1_shift_sum, q_bias_sum, v_bias_sum = ln1_totals
    here = [lax.dynamic_index_in_dim(attn_grad, x_places[i], 0, False) for i in range(RING)]
    attn_grad = ring_collect(here, "x")
    out_bias_sum, ln2_gain_sum, ln2_shift_sum, up_bias_sum, down_bias_sum = split_back(
        early_totals.reshape(-1), early
    )
    return (
        result,
        grad_tokens,
        ln1_gain_sum,
        ln1_shift_sum,
        attn_grad[:, :head_cols],
        q_bias_sum,
        attn_grad[:, head_cols : 2 * head_cols],
        attn_grad[:, 2 * head_cols : 3 * head_cols],
        v_bias_sum,
        attn_grad[:, 3 * head_cols :],
        out_bias_sum,
        ln2_gain_sum,
        ln2_shift_sum,
        ff_grad[:, :ff_cols],
        up_bias_sum,
        ff_grad[:, ff_cols:],
        down_bias_sum,
    )


def solution(mesh):
    wide = Mesh(mesh.devices.reshape(4, 2, 4, 4), ("z", "c", "x", "y"))
    act = P(ROWS, COLS, None)
    weight = P(ROWS, COLS)
    vector = P()
    in_specs = (
        act, act, P(ROWS), P(ROWS, None), vector, vector, vector,
        weight, vector, weight, weight, vector, weight, vector, vector, vector,
        weight, vector, weight, vector,
    )
    out_specs = (
        act, act, vector, vector, weight, vector, weight, weight, vector, weight,
        vector, vector, vector, weight, vector, weight, vector,
    )
    return jax.shard_map(
        shards, mesh=wide, in_specs=in_specs, out_specs=out_specs, check_vma=False
    )
```

```python
from functools import partial

import jax
import jax.numpy as jnp
from jax import lax
from jax.experimental import pallas as pl
from jax.experimental.pallas import tpu as pltpu
from jax.sharding import Mesh
from jax.sharding import PartitionSpec as P

HEAD_DIM = 64
SPAN = 256
LOW = jnp.bfloat16
WIDE = jnp.float32
RING = 4
ROWS = ("z", "c")
COLS = ("x", "y")


def dot(left, right):
    return jnp.dot(left, right, preferred_element_type=WIDE)


def dot_t(left, right):
    return lax.dot_general(left, right, (((1,), (1,)), ((), ())), preferred_element_type=WIDE)


def dot_0(left, right):
    return lax.dot_general(left, right, (((0,), (0,)), ((), ())), preferred_element_type=WIDE)


def call(body, out_shape, grid, in_specs, out_specs, flops, traffic, scratch=(), prefetch=0, vmem=40, aliases=None):
    return pl.pallas_call(
        body,
        out_shape=out_shape,
        grid_spec=pltpu.PrefetchScalarGridSpec(
            num_scalar_prefetch=prefetch,
            grid=grid,
            in_specs=in_specs,
            out_specs=out_specs,
            scratch_shapes=list(scratch),
        ),
        compiler_params=pltpu.CompilerParams(vmem_limit_bytes=vmem * 2**20),
        input_output_aliases=aliases or {},
        cost_estimate=pl.CostEstimate(flops=flops, bytes_accessed=traffic, transcendentals=0),
    )


def whole(shape):
    return pl.BlockSpec(shape, lambda *_: (0,) * len(shape))


def struct(shape, dtype):
    return jax.ShapeDtypeStruct(shape, dtype)


def spread(array, axes, size):
    return lax.all_to_all(jnp.broadcast_to(array[None], (size,) + array.shape), axes, 0, 0)


def collect(parts, axes):
    return jnp.sum(lax.all_to_all(parts, axes, 0, 0).astype(WIDE), 0)


def swap(parts, axes):
    return lax.all_to_all(parts, axes, 0, 0)


def ring(array, step, axis="y"):
    return lax.ppermute(array, axis, [(i, (i + step) % RING) for i in range(RING)])


def ring_stack(array, axis):
    return jnp.stack([array] + [ring(array, step, axis) for step in (1, -1, 2)])


def ring_collect(parts, axis):
    came = [ring(parts[slot], step, axis) for slot, step in ((1, -1), (2, 1), (3, 2))]
    return sum(term.astype(WIDE) for term in [parts[0]] + came)


def ring_gather(rows):
    half = rows.shape[0] // 2
    first, second = rows[:half], rows[half:]
    before_first, after_second = ring(first, 1), ring(second, -1)
    before_second, after_first = ring(second, 1), ring(first, -1)
    across_first, across_second = ring(before_first, 1), ring(after_second, -1)
    return jnp.concatenate(
        [
            first, second, before_first, before_second,
            after_first, after_second, across_first, across_second,
        ],
        0,
    )


def ring_sum(rows):
    own = rows.shape[0] // RING
    half = own // 2
    start, before, after, across = (rows[i * own : (i + 1) * own] for i in range(RING))
    from_before, from_after = ring(across[:half], 1), ring(across[half:], -1)
    second_after, first_before = ring(after[half:], 1), ring(before[:half], -1)
    first_after = ring((after[:half].astype(WIDE) + from_before.astype(WIDE)).astype(LOW), 1)
    second_before = ring((before[half:].astype(WIDE) + from_after.astype(WIDE)).astype(LOW), -1)
    first = start[:half].astype(WIDE) + first_after.astype(WIDE) + first_before.astype(WIDE)
    second = start[half:].astype(WIDE) + second_after.astype(WIDE) + second_before.astype(WIDE)
    return jnp.concatenate([first, second], 0)


def tie(*arrays):
    return lax.optimization_barrier(arrays)


def gather_weight(shard):
    full = lax.all_gather(shard, ("z", "c", "x"), axis=0)
    return full.reshape((8, 4) + shard.shape)


def settle(gradient):
    return lax.psum_scatter(gradient, ROWS, scatter_dimension=0)


def qkv_body(rows_ref, weight_ref, bias_ref, out_ref):
    weight = weight_ref[...].reshape(rows_ref.shape[1], -1)
    out_ref[...] = (dot(rows_ref[...], weight) + bias_ref[...]).astype(LOW)


def qkv_project(rows, weight, bias):
    count, width = rows.shape
    zc, xs, piece, _ = weight.shape
    cols = bias.shape[-1]
    return call(
        qkv_body,
        struct((xs, count, cols), LOW),
        (xs,),
        [
            whole((count, width)),
            pl.BlockSpec((zc, None, piece, cols), lambda i: (0, i, 0, 0)),
            pl.BlockSpec((None, 1, cols), lambda i: (i, 0, 0)),
        ],
        pl.BlockSpec((None, count, cols), lambda i: (i, 0, 0)),
        2 * count * width * xs * cols,
        10 * 2**20,
        vmem=60,
    )(rows, weight, bias)


def out_body(place_ref, heads_ref, weight_ref, out_ref):
    count, _, piece, _ = weight_ref.shape
    for block in range(count):
        value = dot_t(heads_ref[0], weight_ref[block, 0])
        for x in range(1, RING):
            value += dot_t(heads_ref[x], weight_ref[block, x])
        here = slice(block * piece, (block + 1) * piece)
        store_rows(out_ref.at[:, here], place_ref, value.astype(LOW))


def store_rows(out_ref, place_ref, value):
    rows = value.shape[0] // RING
    for slot in range(RING):
        at = pl.multiple_of(place_ref[slot] * rows, rows)
        out_ref[pl.ds(at, rows)] = value[slot * rows : (slot + 1) * rows]


def out_project(places, heads, weight, at, blocks):
    xs, count, cols = heads.shape
    zc, _, piece, _ = weight.shape
    return call(
        out_body,
        struct((count, zc * piece), LOW),
        (zc // blocks,),
        [
            whole(heads.shape),
            pl.BlockSpec((blocks, xs, piece, cols), lambda i, *_: (i, 0, 0, at)),
        ],
        pl.BlockSpec((count, blocks * piece), lambda i, *_: (0, i)),
        2 * count * zc * piece * xs * cols,
        5 * 2**20,
        prefetch=1,
        vmem=60,
    )(places, heads, weight)


def heads_grad_body(rows_ref, weight_ref, out_ref):
    weight = weight_ref[...].reshape(rows_ref.shape[1], -1)
    out_ref[...] = dot(rows_ref[...], weight).astype(LOW)


def heads_grad(rows, weight, cols, at):
    count, width = rows.shape
    zc, xs, piece, _ = weight.shape
    return call(
        heads_grad_body,
        struct((xs, count, cols), LOW),
        (xs,),
        [
            whole((count, width)),
            pl.BlockSpec((zc, None, piece, cols), lambda i: (0, i, 0, at)),
        ],
        pl.BlockSpec((None, count, cols), lambda i: (i, 0, 0)),
        2 * count * width * xs * cols,
        5 * 2**20,
        vmem=60,
    )(rows, weight)


def weight_grad_body(rows_ref, grad_ref, *refs):
    out_ref = refs[-1]
    out_ref[...] = dot_0(rows_ref[...], grad_ref[...]).astype(LOW).reshape(out_ref.shape)


def weight_grads(rows, columns, total_cols, at, onto=None):
    count, width = rows.shape
    xs, _, cols = columns.shape
    piece = width // 8
    more = () if onto is None else (onto,)
    return call(
        weight_grad_body,
        struct((8, xs, piece, total_cols), LOW),
        (xs,),
        [whole((count, width)), pl.BlockSpec((None, count, cols), lambda i: (i, 0, 0))]
        + [pl.BlockSpec(memory_space=pl.ANY)] * len(more),
        pl.BlockSpec((8, None, piece, cols), lambda i: (0, i, 0, at)),
        2 * count * width * xs * cols,
        15 * 2**20,
        vmem=60,
        aliases={2: 0} if more else None,
    )(rows, columns, *more)


def add_up(total, term):
    @pl.when(pl.program_id(0) == 0)
    def _():
        total[...] = term

    @pl.when(pl.program_id(0) > 0)
    def _():
        total[...] += term


def ffn_first_body(
    place_ref, norm_ref, cot_ref, up_ref, down_ref, bias_ref,
    hidden_ref, grad_up_ref, norm_grad_ref, bias_grad_ref, total,
):
    width, cols = norm_ref.shape[1], up_ref.shape[-1]
    up_w = up_ref[...].reshape(width, cols)
    up = dot(norm_ref[...], up_w) + bias_ref[...]
    normal = 0.5 * (1.0 + lax.erf(up * 0.7071067811865476))
    hidden_ref[...] = (up * normal).astype(LOW)
    slope = normal + up * (jnp.exp(-0.5 * up * up) * 0.3989422804014327)
    grad_up = (dot(cot_ref[...], down_ref[...].reshape(width, cols)) * slope).astype(LOW)
    grad_up_ref[...] = grad_up
    bias_grad_ref[...] = jnp.sum(grad_up.astype(WIDE), 0, keepdims=True)
    add_up(total, dot_t(grad_up, up_w))

    @pl.when(pl.program_id(0) == pl.num_programs(0) - 1)
    def _():
        store_rows(norm_grad_ref, place_ref, total[...].astype(LOW))


def ffn_first(places, norm_rows, cot_rows, weight, bias):
    count, width = norm_rows.shape
    zc, xs, piece, cols = weight.shape
    size = cols // 2
    rows = whole((count, width))
    vector = pl.BlockSpec((None, 1, size), lambda i, *_: (i, 0, 0))
    wide = pl.BlockSpec((count, size), lambda i, *_: (0, i))
    return call(
        ffn_first_body,
        (
            struct((count, xs * size), LOW),
            struct((count, xs * size), LOW),
            struct((count, width), LOW),
            struct((xs, 1, size), WIDE),
        ),
        (xs,),
        [
            rows,
            rows,
            pl.BlockSpec((zc, None, piece, size), lambda i, *_: (0, i, 0, 0)),
            pl.BlockSpec((zc, None, piece, size), lambda i, *_: (0, i, 0, 1)),
            vector,
        ],
        (wide, wide, rows, vector),
        6 * count * width * xs * size,
        25 * 2**20,
        scratch=[pltpu.VMEM((count, width), WIDE)],
        prefetch=1,
        vmem=56,
    )(places, norm_rows, cot_rows, weight, weight, bias)


def ffn_second_body(
    norm_ref, cot_ref, hidden_ref, grad_up_ref, down_ref, branch_ref, weight_grad_ref, total
):
    width, cols = norm_ref.shape[1], down_ref.shape[-1]
    zc, piece, _ = weight_grad_ref.shape
    hidden = hidden_ref[...]
    weight_grad_ref[:, :, :cols] = (
        dot_0(norm_ref[...], grad_up_ref[...]).astype(LOW).reshape(zc, piece, cols)
    )
    weight_grad_ref[:, :, cols:] = dot_0(cot_ref[...], hidden).astype(LOW).reshape(zc, piece, cols)
    add_up(total, dot_t(hidden, down_ref[...].reshape(width, cols)))

    @pl.when(pl.program_id(0) == pl.num_programs(0) - 1)
    def _():
        branch_ref[...] = total[...].astype(LOW)


def ffn_second(norm_rows, cot_rows, hidden, grad_up, weight):
    count, width = norm_rows.shape
    zc, xs, piece, cols = weight.shape
    size = cols // 2
    rows = whole((count, width))
    wide = pl.BlockSpec((count, size), lambda i: (0, i))
    return call(
        ffn_second_body,
        (struct((count, width), LOW), struct(weight.shape, LOW)),
        (xs,),
        [rows, rows, wide, wide, pl.BlockSpec((zc, None, piece, size), lambda i: (0, i, 0, 1))],
        (rows, pl.BlockSpec((zc, None, piece, cols), lambda i: (0, i, 0, 0))),
        6 * count * width * xs * size,
        40 * 2**20,
        scratch=[pltpu.VMEM((count, width), WIDE)],
        vmem=56,
    )(norm_rows, cot_rows, hidden, grad_up, weight)


def only_head(array, head):
    lane = lax.broadcasted_iota(jnp.int32, array.shape, 1)
    return jnp.where(lane // HEAD_DIM == head, array, jnp.zeros_like(array))


def allowed_keys(start, extent, live_count):
    q_place = start + lax.broadcasted_iota(jnp.int32, (SPAN, extent), 0)
    k_place = lax.broadcasted_iota(jnp.int32, (SPAN, extent), 1)
    return k_place <= jnp.minimum(q_place, live_count - 1)


def slot_of(place, own):
    apart = (place - own + RING) % RING
    return jnp.where(apart == 0, 0, jnp.where(apart == RING - 1, 1, apart + 1))


def load_ordered(blocks_ref, own, into):
    rows = blocks_ref.shape[2]
    for x in range(RING):
        for y in range(RING):
            at = (x * RING + y) * rows
            into[at : at + rows] = blocks_ref[x, slot_of(y, own)]


def store_ordered(blocks_ref, x, own, cols, value):
    rows = blocks_ref.shape[2]
    for y in range(RING):
        blocks_ref[x, slot_of(y, own), :, cols] = value[y * rows : (y + 1) * rows]


def attend_body(live_ref, qkv_ref, heads_ref, exact_ref, log_ref, qkv):
    live_count = live_ref[pl.program_id(0)]
    own = live_ref[pl.num_programs(0)]
    length = exact_ref.shape[0]
    width = exact_ref.shape[1]
    load_ordered(qkv_ref, own, qkv)
    key = qkv[:, width : 2 * width]
    value = qkv[:, 2 * width :]
    for span in range(length // SPAN):
        start, extent = span * SPAN, (span + 1) * SPAN
        here = slice(start, extent)

        @pl.when(start < live_count)
        def _():
            query = qkv[here, :width]
            allowed = allowed_keys(start, extent, live_count)
            mixed, logs = [], []
            for head in range(width // HEAD_DIM):
                scores = dot_t(only_head(query, head), key[:extent]) * HEAD_DIM**-0.5
                scores = jnp.where(allowed, scores, -1e9)
                top = jnp.max(scores, 1, keepdims=True)
                terms = jnp.exp(scores - top)
                denom = jnp.sum(terms, 1, keepdims=True)
                mixed.append(dot(terms.astype(LOW), value[:extent]) / denom)
                logs.append(top + jnp.log(denom))
            lane = lax.broadcasted_iota(jnp.int32, (SPAN, width), 1)
            out = jnp.where(lane < HEAD_DIM, mixed[0], mixed[1])
            exact_ref[here] = out
            log_ref[here] = jnp.where(lane < HEAD_DIM, logs[0], logs[1])
            store_ordered(heads_ref, span, own, slice(None), out.astype(LOW))

        @pl.when(start >= live_count)
        def _():
            exact_ref[here] = jnp.zeros((SPAN, width), WIDE)
            log_ref[here] = jnp.zeros((SPAN, width), WIDE)
            heads_ref[span] = jnp.zeros(heads_ref.shape[1:], LOW)


def row_block(rows, cols):
    return pl.BlockSpec((4, 4, None, rows, cols), lambda s, *_: (0, 0, s, 0, 0))


def attend(live_counts, qkv, width):
    xs, ys, seqs, rows, _ = qkv.shape
    length = xs * ys * rows
    flat = pl.BlockSpec((None, length, width), lambda s, *_: (s, 0, 0))
    return call(
        attend_body,
        (
            struct((xs, ys, seqs, rows, width), LOW),
            struct((seqs, length, width), WIDE),
            struct((seqs, length, width), WIDE),
        ),
        (seqs,),
        [row_block(rows, 3 * width)],
        (row_block(rows, width), flat, flat),
        4 * 10**9,
        4 * 2**20,
        scratch=[pltpu.VMEM((length, 3 * width), LOW)],
        prefetch=1,
    )(live_counts, qkv)


def attend_back_body(
    live_ref, qkv_ref, grad_ref, exact_ref, log_ref, out_ref, sum_ref,
    key_total, value_total, qkv, grads,
):
    live_count = live_ref[pl.program_id(0)]
    own = live_ref[pl.num_programs(0)]
    length, width = exact_ref.shape
    factor = HEAD_DIM**-0.5
    load_ordered(qkv_ref, own, qkv)
    load_ordered(grad_ref, own, grads)
    key = qkv[:, width : 2 * width]
    value = qkv[:, 2 * width :]
    key_total[...] = jnp.zeros_like(key_total)
    value_total[...] = jnp.zeros_like(value_total)
    sum_ref[...] = jnp.zeros_like(sum_ref)
    for span in range(length // SPAN):
        start, extent = span * SPAN, (span + 1) * SPAN
        here = slice(start, extent)

        @pl.when(start < live_count)
        def _():
            query = qkv[here, :width]
            grad = grads[here]
            inner = grad.astype(WIDE) * exact_ref[here]
            logs = log_ref[here]
            allowed = allowed_keys(start, extent, live_count)
            query_total = jnp.zeros((SPAN, width), WIDE)
            for head in range(width // HEAD_DIM):
                query_h = only_head(query, head)
                grad_h = only_head(grad, head)
                log_h = logs[:, head * HEAD_DIM : head * HEAD_DIM + 1]
                row_inner = jnp.sum(only_head(inner, head), 1, keepdims=True)
                scores = dot_t(query_h, key[:extent]) * factor
                probs = jnp.exp(jnp.where(allowed, scores, -1e9) - log_h)
                d_probs = dot_t(grad_h, value[:extent])
                value_total[:extent] += dot_0(probs.astype(LOW), grad_h)
                d_scores = (probs * (d_probs - row_inner)).astype(LOW)
                query_total += dot(d_scores, only_head(key[:extent], head))
                key_total[:extent] += dot_0(d_scores, query_h)
            out = (query_total * factor).astype(LOW)
            store_ordered(out_ref, span, own, slice(0, width), out)
            sum_ref[:, :width] += jnp.sum(out.astype(WIDE), 0, keepdims=True)

        @pl.when(start >= live_count)
        def _():
            out_ref[span, :, :, :width] = jnp.zeros(out_ref.shape[1:3] + (width,), LOW)

    key_grad = (key_total[...] * factor).astype(LOW)
    value_grad = value_total[...].astype(LOW)
    for span in range(RING):
        here = slice(span * SPAN, (span + 1) * SPAN)
        store_ordered(out_ref, span, own, slice(width, 2 * width), key_grad[here])
        store_ordered(out_ref, span, own, slice(2 * width, None), value_grad[here])
    sum_ref[:, 2 * width :] = jnp.sum(value_grad.astype(WIDE), 0, keepdims=True)


def attend_back(live_counts, qkv, grads, exact, logs):
    xs, ys, seqs, rows, _ = qkv.shape
    _, length, width = exact.shape
    flat = pl.BlockSpec((None, length, width), lambda s, *_: (s, 0, 0))
    return call(
        attend_back_body,
        (struct(qkv.shape, LOW), struct((seqs, 1, 3 * width), WIDE)),
        (seqs,),
        [row_block(rows, 3 * width), row_block(rows, width), flat, flat],
        (
            row_block(rows, 3 * width),
            pl.BlockSpec((None, 1, 3 * width), lambda s, *_: (s, 0, 0)),
        ),
        8 * 10**9,
        8 * 2**20,
        scratch=[
            pltpu.VMEM((length, width), WIDE),
            pltpu.VMEM((length, width), WIDE),
            pltpu.VMEM((length, 3 * width), LOW),
            pltpu.VMEM((length, width), LOW),
        ],
        prefetch=1,
    )(live_counts, qkv, grads, exact, logs)


def norm_rows(values, gain_vec, shift_vec):
    centered = values - jnp.mean(values, -1, keepdims=True)
    inverse = lax.rsqrt(jnp.mean(centered * centered, -1, keepdims=True) + 1e-05)
    return (centered * inverse * gain_vec + shift_vec).astype(LOW)


def norm_back_body(with_low, parts_ref, rows_ref, grad_ref, gain_ref, *refs):
    gradient = parts_ref[0].astype(WIDE)
    for part in range(1, parts_ref.shape[0]):
        gradient += parts_ref[part].astype(WIDE)
    values = rows_ref[...].astype(WIDE)
    centered = values - jnp.mean(values, 1, keepdims=True)
    inverse = lax.rsqrt(jnp.mean(centered * centered, 1, keepdims=True) + 1e-05)
    unit = centered * inverse
    scaled = gradient * gain_ref[...]
    out = grad_ref[...].astype(WIDE) + inverse * (
        scaled
        - jnp.mean(scaled, 1, keepdims=True)
        - unit * jnp.mean(scaled * unit, 1, keepdims=True)
    )
    sums = [jnp.sum(gradient * unit, 0, keepdims=True), jnp.sum(gradient, 0, keepdims=True)]
    if with_low:
        keep_ref, out_ref, low_ref, sum_ref = refs
        low = (keep_ref[...] * out).astype(LOW)
        low_ref[...] = low
        sums.append(jnp.sum(low.astype(WIDE), 0, keepdims=True))
    else:
        out_ref, sum_ref = refs
    out_ref[...] = out
    sums.append(jnp.zeros((sum_ref.shape[0] - len(sums), sum_ref.shape[1]), WIDE))
    add_up(sum_ref, jnp.concatenate(sums, 0))


def norm_back(parts, rows, grad, gain, keep=None):
    count, own, width = parts.shape
    step = own // 4
    flat = pl.BlockSpec((step, width), lambda i: (i, 0))
    sums = pl.BlockSpec((8, width), lambda i: (0, 0))
    in_specs = [
        pl.BlockSpec((count, step, width), lambda i: (0, i, 0)), flat, flat,
        pl.BlockSpec((1, width), lambda i: (0, 0)),
    ]
    args = [parts, rows, grad, gain.reshape(1, width)]
    outs, specs = [struct((own, width), WIDE)], [flat]
    if keep is not None:
        in_specs.append(pl.BlockSpec((step, 1), lambda i: (i, 0)))
        args.append(keep)
        outs.append(struct((own, width), LOW))
        specs.append(flat)
    return call(
        partial(norm_back_body, keep is not None),
        tuple(outs + [struct((8, width), WIDE)]),
        (own // step,),
        in_specs,
        tuple(specs + [sums]),
        40 * own * width,
        6 * 2**20,
    )(*args)


def split_back(flat, vectors):
    pieces, start = [], 0
    for v in vectors:
        pieces.append(flat[start : start + v.size])
        start += v.size
    return pieces


def last_totals(vectors, columns, ready):
    shared = jnp.concatenate([v.reshape(-1, 128) for v in vectors], 0)
    rows, more = shared.shape[0], columns.shape[0]
    parts = spread(jnp.concatenate([shared, columns, ready], 0), COLS, 16)
    part = jnp.sum(parts[:, :rows], 0)
    part = jnp.concatenate([part, parts[:, rows : rows + more].reshape(-1, 128)], 0)
    part = jnp.sum(spread(part, ROWS, 8), 0)
    placed = part[rows:].reshape(16, more, 128)
    totals = split_back(part[:rows].reshape(-1), vectors)
    totals += [placed[:, i].reshape(-1) for i in range(more)]
    return totals, parts[:, rows + more :]


def shards(
    tokens, cotangent, seq_lengths, exit_layers, layer_index,
    ln1_gain, ln1_shift, q_weight, q_bias, k_weight, v_weight, v_bias, out_weight, out_bias,
    ln2_gain, ln2_shift, up_weight, up_bias, down_weight, down_bias,
):
    seqs, own_rows, width = tokens.shape
    own = seqs * own_rows
    full_len = exit_layers.shape[1]
    x_at, y_at = lax.axis_index("x"), lax.axis_index("y")
    head_at = x_at * RING + y_at
    head_cols = q_weight.shape[1]
    ff_cols = up_weight.shape[1]

    positions = jnp.arange(full_len)
    live_all = (positions[None, :] < seq_lengths[:, None]) & (exit_layers > layer_index[0])
    live_counts = jnp.concatenate(
        [jnp.sum(live_all.astype(jnp.int32), 1), y_at.astype(jnp.int32).reshape(1)]
    )
    slots = jnp.arange(RING, dtype=jnp.int32)
    apart = jnp.array([0, RING - 1, 1, 2], jnp.int32)
    places = (y_at.astype(jnp.int32) + apart) % RING
    x_places = (x_at.astype(jnp.int32) + apart) % RING
    live_mine = lax.dynamic_slice_in_dim(live_all, head_at * own_rows, own_rows, 1)
    keep = live_mine.reshape(-1, 1).astype(WIDE)

    w_attn = gather_weight(
        jnp.concatenate([q_weight, k_weight, v_weight, out_weight], 1).astype(LOW)
    )
    w_ff = jnp.concatenate([up_weight, down_weight], 1).astype(LOW)

    inputs = tokens.astype(WIDE).reshape(own, width)
    norm1 = ring_gather(norm_rows(inputs, ln1_gain, ln1_shift))
    flat_cot = cotangent.reshape(own, width)
    g_ffn = (keep * flat_cot.astype(WIDE)).astype(LOW)
    norm1, w_ff = tie(norm1, ring_stack(w_ff, "x"))
    w_ff = lax.all_gather(w_ff, ROWS, axis=0)

    def mine(vector, cols):
        return lax.dynamic_index_in_dim(vector.reshape(RING, RING, cols), y_at, 1, False)

    bias = jnp.concatenate(
        [mine(q_bias, head_cols), jnp.zeros((RING, head_cols), WIDE), mine(v_bias, head_cols)], 1
    ).reshape(RING, 1, 3 * head_cols)
    qkv = qkv_project(norm1, w_attn, bias)
    rows5 = (RING, RING, seqs, own_rows)
    qkv, g_ffn = tie(qkv, g_ffn)
    cot_rows = ring_gather(g_ffn)
    qkv = swap(qkv, "x").reshape(rows5 + (3 * head_cols,))
    heads, exact, logs = attend(live_counts, qkv, head_cols)
    heads, cot_rows = tie(heads, cot_rows)
    heads = swap(heads.reshape(RING, RING * own, head_cols), "x")
    branch1 = ring_sum(out_project(slots, heads, w_attn, 3, 4)) + out_bias
    middle = inputs + keep * branch1
    norm2 = ring_gather(norm_rows(middle, ln2_gain, ln2_shift))

    ff_bias = mine(up_bias, ff_cols)[x_places].reshape(RING, 1, ff_cols)
    hidden, grad_up, g_norm2, up_bias_part = ffn_first(places, norm2, cot_rows, w_ff, ff_bias)
    g_norm2 = swap(g_norm2.reshape(RING, own, width), "y")
    g_norm2, branch2, ff_grad = tie(
        g_norm2, *ffn_second(norm2, cot_rows, hidden, grad_up, w_ff)
    )
    ff_grad = settle(ff_grad)
    grad_mid, g_attn, sums2 = norm_back(g_norm2, middle, flat_cot, ln2_gain, keep)
    attn_rows = ring_gather(g_attn)
    g_heads = heads_grad(attn_rows, w_attn, head_cols, 3)
    g_heads, branch2 = tie(swap(g_heads, "x").reshape(rows5 + (head_cols,)), branch2)
    branch2 = ring_collect(branch2.reshape(RING, own, width), "y") + down_bias
    result = (middle + keep * branch2).astype(LOW).reshape(tokens.shape)
    d_qkv, d_sums = attend_back(live_counts, qkv, g_heads, exact, logs)
    d_qkv, attn_rows = tie(d_qkv, attn_rows)
    attn_grad = weight_grads(attn_rows, heads, 4 * head_cols, 3)
    d_qkv = swap(d_qkv.reshape(RING, RING * own, 3 * head_cols), "x")

    up_bias_full = jnp.zeros((RING, RING, ff_cols), WIDE)
    for slot in range(RING):
        up_bias_full = lax.dynamic_update_slice(
            up_bias_full, up_bias_part[slot][None], (x_places[slot], y_at, 0)
        )
    early = (
        sums2[2],
        sums2[0],
        sums2[1],
        up_bias_full,
        jnp.sum(g_ffn.astype(WIDE), 0),
    )
    early_flat = jnp.concatenate([v.reshape(-1) for v in early]).reshape(16, -1, 128)
    d_qkv, attn_grad, result, early_flat = tie(d_qkv, attn_grad, result, early_flat)
    part = collect(early_flat, COLS)
    attn_grad = weight_grads(norm1, d_qkv, 4 * head_cols, 0, attn_grad)
    d_qkv, attn_grad, part, ff_grad = tie(d_qkv, attn_grad, part, ff_grad)
    attn_grad = settle(attn_grad)
    part = jnp.sum(spread(part, ROWS, 8), 0)
    g_norm1 = out_project(places, d_qkv, w_attn, 0, 2)
    g_norm1, part = tie(g_norm1, part)
    ff_grad = ring_collect(ff_grad, "x")
    g_norm1 = swap(g_norm1.reshape(RING, own, width), "y")
    g_norm1, attn_grad = tie(g_norm1, attn_grad)
    here = [lax.dynamic_index_in_dim(attn_grad, x_places[i], 0, False) for i in range(RING)]
    attn_grad = ring_collect(here, "x")
    grad_tokens, sums1 = norm_back(g_norm1, tokens.reshape(own, width), grad_mid, ln1_gain)
    grad_tokens = grad_tokens.reshape(tokens.shape)
    d_sums = jnp.sum(d_sums, 0).reshape(3, head_cols)
    ln1_totals, early_totals = last_totals((sums1[0], sums1[1]), d_sums[::2], part)
    ln1_gain_sum, ln1_shift_sum, q_bias_sum, v_bias_sum = ln1_totals
    out_bias_sum, ln2_gain_sum, ln2_shift_sum, up_bias_sum, down_bias_sum = split_back(
        early_totals.reshape(-1), early
    )
    return (
        result,
        grad_tokens,
        ln1_gain_sum,
        ln1_shift_sum,
        attn_grad[:, :head_cols],
        q_bias_sum,
        attn_grad[:, head_cols : 2 * head_cols],
        attn_grad[:, 2 * head_cols : 3 * head_cols],
        v_bias_sum,
        attn_grad[:, 3 * head_cols :],
        out_bias_sum,
        ln2_gain_sum,
        ln2_shift_sum,
        ff_grad[:, :ff_cols],
        up_bias_sum,
        ff_grad[:, ff_cols:],
        down_bias_sum,
    )


def solution(mesh):
    wide = Mesh(mesh.devices.reshape(4, 2, 4, 4), ("z", "c", "x", "y"))
    act = P(ROWS, COLS, None)
    weight = P(ROWS, COLS)
    vector = P()
    in_specs = (
        act, act, P(ROWS), P(ROWS, None), vector, vector, vector,
        weight, vector, weight, weight, vector, weight, vector, vector, vector,
        weight, vector, weight, vector,
    )
    out_specs = (
        act, act, vector, vector, weight, vector, weight, weight, vector, weight,
        vector, vector, vector, weight, vector, weight, vector,
    )
    return jax.shard_map(
        shards, mesh=wide, in_specs=in_specs, out_specs=out_specs, check_vma=False
    )
```

```python
from functools import partial

import jax
import jax.numpy as jnp
from jax import lax
from jax.experimental import pallas as pl
from jax.experimental.pallas import tpu as pltpu
from jax.sharding import Mesh
from jax.sharding import PartitionSpec as P

HEAD_DIM = 64
SPAN = 256
LOW = jnp.bfloat16
WIDE = jnp.float32
RING = 4
ROWS = ("z", "c")
COLS = ("x", "y")


def dot(left, right):
    return jnp.dot(left, right, preferred_element_type=WIDE)


def dot_t(left, right):
    return lax.dot_general(left, right, (((1,), (1,)), ((), ())), preferred_element_type=WIDE)


def dot_0(left, right):
    return lax.dot_general(left, right, (((0,), (0,)), ((), ())), preferred_element_type=WIDE)


def call(body, out_shape, grid, in_specs, out_specs, flops, traffic, scratch=(), prefetch=0, vmem=40, aliases=None):
    return pl.pallas_call(
        body,
        out_shape=out_shape,
        grid_spec=pltpu.PrefetchScalarGridSpec(
            num_scalar_prefetch=prefetch,
            grid=grid,
            in_specs=in_specs,
            out_specs=out_specs,
            scratch_shapes=list(scratch),
        ),
        compiler_params=pltpu.CompilerParams(vmem_limit_bytes=vmem * 2**20),
        input_output_aliases=aliases or {},
        cost_estimate=pl.CostEstimate(flops=flops, bytes_accessed=traffic, transcendentals=0),
    )


def whole(shape):
    return pl.BlockSpec(shape, lambda *_: (0,) * len(shape))


def struct(shape, dtype):
    return jax.ShapeDtypeStruct(shape, dtype)


def spread(array, axes, size):
    return lax.all_to_all(jnp.broadcast_to(array[None], (size,) + array.shape), axes, 0, 0)


def collect(parts, axes):
    return jnp.sum(lax.all_to_all(parts, axes, 0, 0).astype(WIDE), 0)


def swap(parts, axes):
    return lax.all_to_all(parts, axes, 0, 0)


def ring(array, step, axis="y"):
    if step == 0:
        return array
    return lax.ppermute(array, axis, [(i, (i + step) % RING) for i in range(RING)])


def ring_collect(parts, axis):
    came = [ring(parts[slot], step, axis) for slot, step in ((1, -1), (2, 1), (3, 2))]
    return sum(term.astype(WIDE) for term in [parts[0]] + came)


def ring_gather(rows, beside=None):
    half = rows.shape[0] // 2
    first, second = rows[:half], rows[half:]
    before_first, after_second = ring(first, 1), ring(second, -1)
    before_second, after_first = ring(second, 1), ring(first, -1)
    if beside is not None:
        before_first, after_second, beside = tie(before_first, after_second, beside)
    across_first, across_second = ring(before_first, 1), ring(after_second, -1)
    gathered = jnp.concatenate(
        [
            first, second, before_first, before_second,
            after_first, after_second, across_first, across_second,
        ],
        0,
    )
    return gathered if beside is None else (gathered, beside)


def ring_sum_parts(rows):
    own = rows.shape[0] // RING
    half = own // 2
    start, before, after, across = (rows[i * own : (i + 1) * own] for i in range(RING))
    from_before, from_after = ring(across[:half], 1), ring(across[half:], -1)
    second_after, first_before = ring(after[half:], 1), ring(before[:half], -1)
    first_after = ring((after[:half].astype(WIDE) + from_before.astype(WIDE)).astype(LOW), 1)
    second_before = ring((before[half:].astype(WIDE) + from_after.astype(WIDE)).astype(LOW), -1)
    return (start, first_after, second_after, first_before, second_before)


def ring_sum(rows):
    start, first_after, second_after, first_before, second_before = ring_sum_parts(rows)
    half = first_after.shape[0]
    first = start[:half].astype(WIDE) + first_after.astype(WIDE) + first_before.astype(WIDE)
    second = start[half:].astype(WIDE) + second_after.astype(WIDE) + second_before.astype(WIDE)
    return jnp.concatenate([first, second], 0)


def tie(*arrays):
    return lax.optimization_barrier(arrays)


def gather_weight(shard):
    full = lax.all_gather(shard, ("z", "c", "x"), axis=0)
    return full.reshape((8, 4) + shard.shape)


def settle(gradient):
    return lax.psum_scatter(gradient, ROWS, scatter_dimension=0)


def qkv_body(rows_ref, weight_ref, bias_ref, out_ref):
    weight = weight_ref[...].reshape(rows_ref.shape[1], -1)
    out_ref[...] = (dot(rows_ref[...], weight) + bias_ref[...]).astype(LOW)


def qkv_project(rows, weight, bias):
    count, width = rows.shape
    zc, xs, piece, _ = weight.shape
    cols = bias.shape[-1]
    return call(
        qkv_body,
        struct((xs, count, cols), LOW),
        (xs,),
        [
            whole((count, width)),
            pl.BlockSpec((zc, None, piece, cols), lambda i: (0, i, 0, 0)),
            pl.BlockSpec((None, 1, cols), lambda i: (i, 0, 0)),
        ],
        pl.BlockSpec((None, count, cols), lambda i: (i, 0, 0)),
        2 * count * width * xs * cols,
        10 * 2**20,
        vmem=60,
    )(rows, weight, bias)


def out_body(place_ref, heads_ref, weight_ref, out_ref):
    count, _, piece, _ = weight_ref.shape
    for block in range(count):
        value = dot_t(heads_ref[0], weight_ref[block, 0])
        for x in range(1, RING):
            value += dot_t(heads_ref[x], weight_ref[block, x])
        here = slice(block * piece, (block + 1) * piece)
        store_rows(out_ref.at[:, here], place_ref, value.astype(LOW))


def store_rows(out_ref, place_ref, value):
    rows = value.shape[0] // RING
    for slot in range(RING):
        at = pl.multiple_of(place_ref[slot] * rows, rows)
        out_ref[pl.ds(at, rows)] = value[slot * rows : (slot + 1) * rows]


def out_project(places, heads, weight, at, blocks):
    xs, count, cols = heads.shape
    zc, _, piece, _ = weight.shape
    return call(
        out_body,
        struct((count, zc * piece), LOW),
        (zc // blocks,),
        [
            whole(heads.shape),
            pl.BlockSpec((blocks, xs, piece, cols), lambda i, *_: (i, 0, 0, at)),
        ],
        pl.BlockSpec((count, blocks * piece), lambda i, *_: (0, i)),
        2 * count * zc * piece * xs * cols,
        5 * 2**20,
        prefetch=1,
        vmem=60,
    )(places, heads, weight)


def heads_grad_body(rows_ref, weight_ref, out_ref):
    weight = weight_ref[...].reshape(rows_ref.shape[1], -1)
    out_ref[...] = dot(rows_ref[...], weight).astype(LOW)


def heads_grad(rows, weight, cols, at):
    count, width = rows.shape
    zc, xs, piece, _ = weight.shape
    return call(
        heads_grad_body,
        struct((xs, count, cols), LOW),
        (xs,),
        [
            whole((count, width)),
            pl.BlockSpec((zc, None, piece, cols), lambda i: (0, i, 0, at)),
        ],
        pl.BlockSpec((None, count, cols), lambda i: (i, 0, 0)),
        2 * count * width * xs * cols,
        5 * 2**20,
        vmem=60,
    )(rows, weight)


def weight_grad_body(rows_ref, grad_ref, *refs):
    out_ref = refs[-1]
    out_ref[...] = dot_0(rows_ref[...], grad_ref[...]).astype(LOW).reshape(out_ref.shape)


def weight_grads(rows, columns, total_cols, at, onto=None):
    count, width = rows.shape
    xs, _, cols = columns.shape
    piece = width // 8
    more = () if onto is None else (onto,)
    return call(
        weight_grad_body,
        struct((8, xs, piece, total_cols), LOW),
        (xs,),
        [whole((count, width)), pl.BlockSpec((None, count, cols), lambda i: (i, 0, 0))]
        + [pl.BlockSpec(memory_space=pl.ANY)] * len(more),
        pl.BlockSpec((8, None, piece, cols), lambda i: (0, i, 0, at)),
        2 * count * width * xs * cols,
        15 * 2**20,
        vmem=60,
        aliases={2: 0} if more else None,
    )(rows, columns, *more)


def add_up(total, term):
    @pl.when(pl.program_id(0) == 0)
    def _():
        total[...] = term

    @pl.when(pl.program_id(0) > 0)
    def _():
        total[...] += term


def ffn_first_body(
    place_ref, norm_ref, cot_ref, up_ref, down_ref, bias_ref,
    hidden_ref, grad_up_ref, norm_grad_ref, bias_grad_ref, total,
):
    width, cols = norm_ref.shape[1], up_ref.shape[-1]
    up_w = up_ref[...].reshape(width, cols)
    up = dot(norm_ref[...], up_w) + bias_ref[...]
    normal = 0.5 * (1.0 + lax.erf(up * 0.7071067811865476))
    hidden_ref[...] = (up * normal).astype(LOW)
    slope = normal + up * (jnp.exp(-0.5 * up * up) * 0.3989422804014327)
    grad_up = (dot(cot_ref[...], down_ref[...].reshape(width, cols)) * slope).astype(LOW)
    grad_up_ref[...] = grad_up
    bias_grad_ref[...] = jnp.sum(grad_up.astype(WIDE), 0, keepdims=True)
    add_up(total, dot_t(grad_up, up_w))

    @pl.when(pl.program_id(0) == pl.num_programs(0) - 1)
    def _():
        store_rows(norm_grad_ref, place_ref, total[...].astype(LOW))


def ffn_first(places, norm_rows, cot_rows, weight, bias):
    count, width = norm_rows.shape
    zc, xs, piece, cols = weight.shape
    size = cols // 2
    rows = whole((count, width))
    vector = pl.BlockSpec((None, 1, size), lambda i, *_: (i, 0, 0))
    wide = pl.BlockSpec((count, size), lambda i, *_: (0, i))
    return call(
        ffn_first_body,
        (
            struct((count, xs * size), LOW),
            struct((count, xs * size), LOW),
            struct((count, width), LOW),
            struct((xs, 1, size), WIDE),
        ),
        (xs,),
        [
            rows,
            rows,
            pl.BlockSpec((zc, None, piece, size), lambda i, *_: (0, i, 0, 0)),
            pl.BlockSpec((zc, None, piece, size), lambda i, *_: (0, i, 0, 1)),
            vector,
        ],
        (wide, wide, rows, vector),
        6 * count * width * xs * size,
        25 * 2**20,
        scratch=[pltpu.VMEM((count, width), WIDE)],
        prefetch=1,
        vmem=56,
    )(places, norm_rows, cot_rows, weight, weight, bias)


def ffn_second_body(
    place_ref, norm_ref, cot_ref, hidden_ref, grad_up_ref, down_ref, branch_ref, weight_grad_ref, total
):
    width, cols = norm_ref.shape[1], down_ref.shape[-1]
    zc, piece, _ = weight_grad_ref.shape
    hidden = hidden_ref[...]
    weight_grad_ref[:, :, :cols] = (
        dot_0(norm_ref[...], grad_up_ref[...]).astype(LOW).reshape(zc, piece, cols)
    )
    weight_grad_ref[:, :, cols:] = dot_0(cot_ref[...], hidden).astype(LOW).reshape(zc, piece, cols)
    add_up(total, dot_t(hidden, down_ref[...].reshape(width, cols)))

    @pl.when(pl.program_id(0) == pl.num_programs(0) - 1)
    def _():
        branch_ref[...] = total[...].astype(LOW)


def ffn_second(places, norm_rows, cot_rows, hidden, grad_up, weight):
    count, width = norm_rows.shape
    zc, xs, piece, cols = weight.shape
    size = cols // 2
    rows = whole((count, width))
    wide = pl.BlockSpec((count, size), lambda i, *_: (0, i))
    return call(
        ffn_second_body,
        (struct((count, width), LOW), struct(weight.shape, LOW)),
        (xs,),
        [rows, rows, wide, wide, pl.BlockSpec((zc, None, piece, size), lambda i, *_: (0, i, 0, 1))],
        (rows, pl.BlockSpec((zc, None, piece, cols), lambda i, places: (0, places[i], 0, 0))),
        6 * count * width * xs * size,
        40 * 2**20,
        scratch=[pltpu.VMEM((count, width), WIDE)],
        prefetch=1,
        vmem=56,
    )(places, norm_rows, cot_rows, hidden, grad_up, weight)


def only_head(array, head):
    lane = lax.broadcasted_iota(jnp.int32, array.shape, 1)
    return jnp.where(lane // HEAD_DIM == head, array, jnp.zeros_like(array))


def allowed_keys(start, extent, live_count):
    q_place = start + lax.broadcasted_iota(jnp.int32, (SPAN, extent), 0)
    k_place = lax.broadcasted_iota(jnp.int32, (SPAN, extent), 1)
    return k_place <= jnp.minimum(q_place, live_count - 1)


def slot_of(place, own):
    apart = (place - own + RING) % RING
    return jnp.where(apart == 0, 0, jnp.where(apart == RING - 1, 1, apart + 1))


def load_ordered(blocks_ref, own, into):
    rows = blocks_ref.shape[2]
    for x in range(RING):
        for y in range(RING):
            at = (x * RING + y) * rows
            into[at : at + rows] = blocks_ref[x, slot_of(y, own)]


def store_ordered(blocks_ref, x, own, cols, value):
    rows = blocks_ref.shape[2]
    for y in range(RING):
        blocks_ref[x, slot_of(y, own), :, cols] = value[y * rows : (y + 1) * rows]


def attend_body(live_ref, qkv_ref, heads_ref, exact_ref, log_ref, qkv):
    live_count = live_ref[pl.program_id(0)]
    own = live_ref[pl.num_programs(0)]
    length = exact_ref.shape[0]
    width = exact_ref.shape[1]
    load_ordered(qkv_ref, own, qkv)
    key = qkv[:, width : 2 * width]
    value = qkv[:, 2 * width :]
    for span in range(length // SPAN):
        start, extent = span * SPAN, (span + 1) * SPAN
        here = slice(start, extent)

        @pl.when(start < live_count)
        def _():
            query = qkv[here, :width]
            allowed = allowed_keys(start, extent, live_count)
            mixed, logs = [], []
            for head in range(width // HEAD_DIM):
                scores = dot_t(only_head(query, head), key[:extent]) * HEAD_DIM**-0.5
                scores = jnp.where(allowed, scores, -1e9)
                top = jnp.max(scores, 1, keepdims=True)
                terms = jnp.exp(scores - top)
                denom = jnp.sum(terms, 1, keepdims=True)
                mixed.append(dot(terms.astype(LOW), value[:extent]) / denom)
                logs.append(top + jnp.log(denom))
            lane = lax.broadcasted_iota(jnp.int32, (SPAN, width), 1)
            out = jnp.where(lane < HEAD_DIM, mixed[0], mixed[1])
            exact_ref[here] = out
            log_ref[here] = jnp.where(lane < HEAD_DIM, logs[0], logs[1])
            store_ordered(heads_ref, span, own, slice(None), out.astype(LOW))

        @pl.when(start >= live_count)
        def _():
            exact_ref[here] = jnp.zeros((SPAN, width), WIDE)
            log_ref[here] = jnp.zeros((SPAN, width), WIDE)
            heads_ref[span] = jnp.zeros(heads_ref.shape[1:], LOW)


def row_block(rows, cols):
    return pl.BlockSpec((4, 4, None, rows, cols), lambda s, *_: (0, 0, s, 0, 0))


def attend(live_counts, qkv, width):
    xs, ys, seqs, rows, _ = qkv.shape
    length = xs * ys * rows
    flat = pl.BlockSpec((None, length, width), lambda s, *_: (s, 0, 0))
    return call(
        attend_body,
        (
            struct((xs, ys, seqs, rows, width), LOW),
            struct((seqs, length, width), WIDE),
            struct((seqs, length, width), WIDE),
        ),
        (seqs,),
        [row_block(rows, 3 * width)],
        (row_block(rows, width), flat, flat),
        4 * 10**9,
        4 * 2**20,
        scratch=[pltpu.VMEM((length, 3 * width), LOW)],
        prefetch=1,
    )(live_counts, qkv)


def attend_back_body(
    live_ref, qkv_ref, grad_ref, exact_ref, log_ref, out_ref, sum_ref,
    key_total, value_total, qkv, grads,
):
    live_count = live_ref[pl.program_id(0)]
    own = live_ref[pl.num_programs(0)]
    length, width = exact_ref.shape
    factor = HEAD_DIM**-0.5
    load_ordered(qkv_ref, own, qkv)
    load_ordered(grad_ref, own, grads)
    key = qkv[:, width : 2 * width]
    value = qkv[:, 2 * width :]
    key_total[...] = jnp.zeros_like(key_total)
    value_total[...] = jnp.zeros_like(value_total)
    sum_ref[...] = jnp.zeros_like(sum_ref)
    for span in range(length // SPAN):
        start, extent = span * SPAN, (span + 1) * SPAN
        here = slice(start, extent)

        @pl.when(start < live_count)
        def _():
            query = qkv[here, :width]
            grad = grads[here]
            inner = grad.astype(WIDE) * exact_ref[here]
            logs = log_ref[here]
            allowed = allowed_keys(start, extent, live_count)
            query_total = jnp.zeros((SPAN, width), WIDE)
            for head in range(width // HEAD_DIM):
                query_h = only_head(query, head)
                grad_h = only_head(grad, head)
                log_h = logs[:, head * HEAD_DIM : head * HEAD_DIM + 1]
                row_inner = jnp.sum(only_head(inner, head), 1, keepdims=True)
                scores = dot_t(query_h, key[:extent]) * factor
                probs = jnp.exp(jnp.where(allowed, scores, -1e9) - log_h)
                d_probs = dot_t(grad_h, value[:extent])
                value_total[:extent] += dot_0(probs.astype(LOW), grad_h)
                d_scores = (probs * (d_probs - row_inner)).astype(LOW)
                query_total += dot(d_scores, only_head(key[:extent], head))
                key_total[:extent] += dot_0(d_scores, query_h)
            out = (query_total * factor).astype(LOW)
            store_ordered(out_ref, span, own, slice(0, width), out)
            sum_ref[:, :width] += jnp.sum(out.astype(WIDE), 0, keepdims=True)

        @pl.when(start >= live_count)
        def _():
            out_ref[span, :, :, :width] = jnp.zeros(out_ref.shape[1:3] + (width,), LOW)

    key_grad = (key_total[...] * factor).astype(LOW)
    value_grad = value_total[...].astype(LOW)
    for span in range(RING):
        here = slice(span * SPAN, (span + 1) * SPAN)
        store_ordered(out_ref, span, own, slice(width, 2 * width), key_grad[here])
        store_ordered(out_ref, span, own, slice(2 * width, None), value_grad[here])
    sum_ref[:, 2 * width :] = jnp.sum(value_grad.astype(WIDE), 0, keepdims=True)


def attend_back(live_counts, qkv, grads, exact, logs):
    xs, ys, seqs, rows, _ = qkv.shape
    _, length, width = exact.shape
    flat = pl.BlockSpec((None, length, width), lambda s, *_: (s, 0, 0))
    return call(
        attend_back_body,
        (struct(qkv.shape, LOW), struct((seqs, 1, 3 * width), WIDE)),
        (seqs,),
        [row_block(rows, 3 * width), row_block(rows, width), flat, flat],
        (
            row_block(rows, 3 * width),
            pl.BlockSpec((None, 1, 3 * width), lambda s, *_: (s, 0, 0)),
        ),
        8 * 10**9,
        8 * 2**20,
        scratch=[
            pltpu.VMEM((length, width), WIDE),
            pltpu.VMEM((length, width), WIDE),
            pltpu.VMEM((length, 3 * width), LOW),
            pltpu.VMEM((length, width), LOW),
        ],
        prefetch=1,
    )(live_counts, qkv, grads, exact, logs)


def norm_rows(values, gain_vec, shift_vec):
    centered = values - jnp.mean(values, -1, keepdims=True)
    inverse = lax.rsqrt(jnp.mean(centered * centered, -1, keepdims=True) + 1e-05)
    return (centered * inverse * gain_vec + shift_vec).astype(LOW)


def norm_back_body(count, with_low, *refs):
    parts, (rows_ref, grad_ref, gain_ref) = refs[:count], refs[count : count + 3]
    refs = refs[count + 3 :]
    if count == 1:
        terms = [parts[0][i] for i in range(parts[0].shape[0])]
    else:
        start, first_after, second_after, first_before, second_before = (p[...] for p in parts)
        early = pl.program_id(0) < pl.num_programs(0) // 2
        terms = [
            start,
            jnp.where(early, first_after, second_after),
            jnp.where(early, first_before, second_before),
        ]
    gradient = sum(term.astype(WIDE) for term in terms)
    values = rows_ref[...].astype(WIDE)
    centered = values - jnp.mean(values, 1, keepdims=True)
    inverse = lax.rsqrt(jnp.mean(centered * centered, 1, keepdims=True) + 1e-05)
    unit = centered * inverse
    scaled = gradient * gain_ref[...]
    out = grad_ref[...].astype(WIDE) + inverse * (
        scaled
        - jnp.mean(scaled, 1, keepdims=True)
        - unit * jnp.mean(scaled * unit, 1, keepdims=True)
    )
    sums = [jnp.sum(gradient * unit, 0, keepdims=True), jnp.sum(gradient, 0, keepdims=True)]
    if with_low:
        keep_ref, out_ref, low_ref, sum_ref = refs
        low = (keep_ref[...] * out).astype(LOW)
        low_ref[...] = low
        sums.append(jnp.sum(low.astype(WIDE), 0, keepdims=True))
    else:
        out_ref, sum_ref = refs
    out_ref[...] = out
    sums.append(jnp.zeros((sum_ref.shape[0] - len(sums), sum_ref.shape[1]), WIDE))
    add_up(sum_ref, jnp.concatenate(sums, 0))


def norm_back(parts, rows, grad, gain, keep=None):
    own, width = rows.shape
    step = own // 4
    flat = pl.BlockSpec((step, width), lambda i: (i, 0))
    sums = pl.BlockSpec((8, width), lambda i: (0, 0))
    if isinstance(parts, tuple):
        early = pl.BlockSpec((step, width), lambda i: (jnp.minimum(i, 1), 0))
        late = pl.BlockSpec((step, width), lambda i: (jnp.maximum(i - 2, 0), 0))
        in_specs, args = [flat, early, late, early, late], list(parts)
    else:
        in_specs = [pl.BlockSpec((parts.shape[0], step, width), lambda i: (0, i, 0))]
        args = [parts]
    count = len(args)
    in_specs += [flat, flat, pl.BlockSpec((1, width), lambda i: (0, 0))]
    args += [rows, grad, gain.reshape(1, width)]
    outs, specs = [struct((own, width), WIDE)], [flat]
    if keep is not None:
        in_specs.append(pl.BlockSpec((step, 1), lambda i: (i, 0)))
        args.append(keep)
        outs.append(struct((own, width), LOW))
        specs.append(flat)
    return call(
        partial(norm_back_body, count, keep is not None),
        tuple(outs + [struct((8, width), WIDE)]),
        (own // step,),
        in_specs,
        tuple(specs + [sums]),
        40 * own * width,
        6 * 2**20,
    )(*args)


def collect_vectors(vectors):
    flat = jnp.concatenate([v.reshape(-1) for v in vectors])
    return collect(flat.reshape(16, -1, 128), COLS)


def spread_vectors(part, sizes):
    flat = spread(jnp.sum(spread(part, ROWS, 8), 0), COLS, 16).reshape(-1)
    pieces, start = [], 0
    for size in sizes:
        pieces.append(flat[start : start + size])
        start += size
    return pieces


def shards(
    tokens, cotangent, seq_lengths, exit_layers, layer_index,
    ln1_gain, ln1_shift, q_weight, q_bias, k_weight, v_weight, v_bias, out_weight, out_bias,
    ln2_gain, ln2_shift, up_weight, up_bias, down_weight, down_bias,
):
    seqs, own_rows, width = tokens.shape
    own = seqs * own_rows
    full_len = exit_layers.shape[1]
    x_at, y_at = lax.axis_index("x"), lax.axis_index("y")
    head_at = x_at * RING + y_at
    head_cols = q_weight.shape[1]
    ff_cols = up_weight.shape[1]

    positions = jnp.arange(full_len)
    live_all = (positions[None, :] < seq_lengths[:, None]) & (exit_layers > layer_index[0])
    live_counts = jnp.concatenate(
        [jnp.sum(live_all.astype(jnp.int32), 1), y_at.astype(jnp.int32).reshape(1)]
    )
    slots = jnp.arange(RING, dtype=jnp.int32)
    apart = jnp.array([0, RING - 1, 1, 2], jnp.int32)
    places = (y_at.astype(jnp.int32) + apart) % RING
    x_places = (x_at.astype(jnp.int32) + apart) % RING
    live_mine = lax.dynamic_slice_in_dim(live_all, head_at * own_rows, own_rows, 1)
    keep = live_mine.reshape(-1, 1).astype(WIDE)

    w_attn = gather_weight(
        jnp.concatenate([q_weight, k_weight, v_weight, out_weight], 1).astype(LOW)
    )
    w_ff = jnp.concatenate([up_weight, down_weight], 1).astype(LOW)

    inputs = tokens.astype(WIDE).reshape(own, width)
    norm1 = ring_gather(norm_rows(inputs, ln1_gain, ln1_shift))
    flat_cot = cotangent.reshape(own, width)
    g_ffn = (keep * flat_cot.astype(WIDE)).astype(LOW)
    norm1, g_ffn, w_ff = tie(norm1, g_ffn, w_ff)
    cot_rows, w_ff = ring_gather(g_ffn, [ring(w_ff, step, "x") for step in (0, 1, -1, 2)])
    w_ff = lax.all_gather(jnp.stack(w_ff), ROWS, axis=0)
    norm1, cot_rows = tie(norm1, cot_rows)

    def mine(vector, cols):
        return lax.dynamic_index_in_dim(vector.reshape(RING, RING, cols), y_at, 1, False)

    bias = jnp.concatenate(
        [mine(q_bias, head_cols), jnp.zeros((RING, head_cols), WIDE), mine(v_bias, head_cols)], 1
    ).reshape(RING, 1, 3 * head_cols)
    qkv = qkv_project(norm1, w_attn, bias)
    rows5 = (RING, RING, seqs, own_rows)
    qkv = swap(qkv, "x").reshape(rows5 + (3 * head_cols,))
    heads, exact, logs = attend(live_counts, qkv, head_cols)
    heads = swap(heads.reshape(RING, RING * own, head_cols), "x")
    branch1 = ring_sum(out_project(slots, heads, w_attn, 3, 4)) + out_bias
    middle = inputs + keep * branch1
    norm2 = ring_gather(norm_rows(middle, ln2_gain, ln2_shift))

    ff_bias = mine(up_bias, ff_cols)[x_places].reshape(RING, 1, ff_cols)
    hidden, grad_up, g_norm2, up_bias_part = ffn_first(places, norm2, cot_rows, w_ff, ff_bias)
    g_norm2 = swap(g_norm2.reshape(RING, own, width), "y")
    g_norm2, branch2, ff_grad = tie(
        g_norm2, *ffn_second(x_places, norm2, cot_rows, hidden, grad_up, w_ff)
    )
    ff_grad = settle(ff_grad)
    grad_mid, g_attn, sums2 = norm_back(g_norm2, middle, flat_cot, ln2_gain, keep)
    attn_rows = ring_gather(g_attn)
    g_heads = heads_grad(attn_rows, w_attn, head_cols, 3)
    g_heads, branch2 = tie(swap(g_heads, "x").reshape(rows5 + (head_cols,)), branch2)
    branch2 = ring_collect(branch2.reshape(RING, own, width), "y") + down_bias
    result = (middle + keep * branch2).astype(LOW).reshape(tokens.shape)
    d_qkv, d_sums = attend_back(live_counts, qkv, g_heads, exact, logs)
    d_qkv, attn_rows = tie(d_qkv, attn_rows)
    attn_grad = weight_grads(attn_rows, heads, 4 * head_cols, 3)
    d_qkv = swap(d_qkv.reshape(RING, RING * own, 3 * head_cols), "x")

    up_bias_full = jnp.zeros((RING, RING, ff_cols), WIDE)
    for slot in range(RING):
        up_bias_full = lax.dynamic_update_slice(
            up_bias_full, up_bias_part[slot][None], (x_places[slot], y_at, 0)
        )
    early = (
        sums2[2],
        sums2[0],
        sums2[1],
        up_bias_full,
        jnp.sum(g_ffn.astype(WIDE), 0),
    )
    d_qkv, attn_grad, result = tie(d_qkv, attn_grad, result)
    attn_grad = weight_grads(norm1, d_qkv, 4 * head_cols, 0, attn_grad)
    d_qkv, attn_grad, ff_grad = tie(d_qkv, attn_grad, ff_grad)
    attn_grad = settle(attn_grad)
    g_norm1 = ring_sum_parts(out_project(slots, d_qkv, w_attn, 0, 2))
    g_norm1, ff_grad = tie(g_norm1, swap(ff_grad, "x"))
    ff_grad = jnp.sum(ff_grad.astype(WIDE), 0)
    grad_tokens, sums1 = norm_back(g_norm1, tokens.reshape(own, width), grad_mid, ln1_gain)
    grad_tokens = grad_tokens.reshape(tokens.shape)
    d_sums = jnp.sum(d_sums, 0).reshape(3, head_cols)

    def placed(row):
        blank = jnp.zeros((RING * RING, head_cols), WIDE)
        return lax.dynamic_update_slice_in_dim(blank, row[None], head_at, 0)

    part = collect_vectors(early + (sums1[0], sums1[1], placed(d_sums[0]), placed(d_sums[2])))
    part, attn_grad = tie(part, attn_grad)
    here = [lax.dynamic_index_in_dim(attn_grad, x_places[i], 0, False) for i in range(RING)]
    attn_grad = ring_collect(here, "x")
    sizes = (width, width, width, RING * RING * ff_cols) + (width,) * 5
    totals = spread_vectors(part, sizes)
    out_bias_sum, ln2_gain_sum, ln2_shift_sum, up_bias_sum, down_bias_sum = totals[:5]
    ln1_gain_sum, ln1_shift_sum, q_bias_sum, v_bias_sum = totals[5:]
    return (
        result,
        grad_tokens,
        ln1_gain_sum,
        ln1_shift_sum,
        attn_grad[:, :head_cols],
        q_bias_sum,
        attn_grad[:, head_cols : 2 * head_cols],
        attn_grad[:, 2 * head_cols : 3 * head_cols],
        v_bias_sum,
        attn_grad[:, 3 * head_cols :],
        out_bias_sum,
        ln2_gain_sum,
        ln2_shift_sum,
        ff_grad[:, :ff_cols],
        up_bias_sum,
        ff_grad[:, ff_cols:],
        down_bias_sum,
    )


def solution(mesh):
    wide = Mesh(mesh.devices.reshape(4, 2, 4, 4), ("z", "c", "x", "y"))
    act = P(ROWS, COLS, None)
    weight = P(ROWS, COLS)
    vector = P()
    in_specs = (
        act, act, P(ROWS), P(ROWS, None), vector, vector, vector,
        weight, vector, weight, weight, vector, weight, vector, vector, vector,
        weight, vector, weight, vector,
    )
    out_specs = (
        act, act, vector, vector, weight, vector, weight, weight, vector, weight,
        vector, vector, vector, weight, vector, weight, vector,
    )
    return jax.shard_map(
        shards, mesh=wide, in_specs=in_specs, out_specs=out_specs, check_vma=False
    )
```

```python
from functools import partial

import jax
import jax.numpy as jnp
from jax import lax
from jax.experimental import pallas as pl
from jax.experimental.pallas import tpu as pltpu
from jax.sharding import Mesh
from jax.sharding import PartitionSpec as P

HEAD_DIM = 64
SPAN = 256
LOW = jnp.bfloat16
WIDE = jnp.float32
RING = 4
ROWS = ("z", "c")
COLS = ("x", "y")


def dot(left, right):
    return jnp.dot(left, right, preferred_element_type=WIDE)


def dot_t(left, right):
    return lax.dot_general(left, right, (((1,), (1,)), ((), ())), preferred_element_type=WIDE)


def dot_0(left, right):
    return lax.dot_general(left, right, (((0,), (0,)), ((), ())), preferred_element_type=WIDE)


def call(body, out_shape, grid, in_specs, out_specs, flops, traffic, scratch=(), prefetch=0, vmem=40, aliases=None):
    return pl.pallas_call(
        body,
        out_shape=out_shape,
        grid_spec=pltpu.PrefetchScalarGridSpec(
            num_scalar_prefetch=prefetch,
            grid=grid,
            in_specs=in_specs,
            out_specs=out_specs,
            scratch_shapes=list(scratch),
        ),
        compiler_params=pltpu.CompilerParams(vmem_limit_bytes=vmem * 2**20),
        input_output_aliases=aliases or {},
        cost_estimate=pl.CostEstimate(flops=flops, bytes_accessed=traffic, transcendentals=0),
    )


def whole(shape):
    return pl.BlockSpec(shape, lambda *_: (0,) * len(shape))


def struct(shape, dtype):
    return jax.ShapeDtypeStruct(shape, dtype)


def spread(array, axes, size):
    return lax.all_to_all(jnp.broadcast_to(array[None], (size,) + array.shape), axes, 0, 0)


def collect(parts, axes):
    return jnp.sum(lax.all_to_all(parts, axes, 0, 0).astype(WIDE), 0)


def swap(parts, axes):
    return lax.all_to_all(parts, axes, 0, 0)


def ring(array, step, axis="y"):
    if step == 0:
        return array
    return lax.ppermute(array, axis, [(i, (i + step) % RING) for i in range(RING)])


def ring_collect(parts, axis):
    came = [ring(parts[slot], step, axis) for slot, step in ((1, -1), (2, 1), (3, 2))]
    return sum(term.astype(WIDE) for term in [parts[0]] + came)


def ring_gather(rows):
    half = rows.shape[0] // 2
    first, second = rows[:half], rows[half:]
    before_first, after_second = ring(first, 1), ring(second, -1)
    before_second, after_first = ring(second, 1), ring(first, -1)
    across_first, across_second = ring(before_first, 1), ring(after_second, -1)
    return jnp.concatenate(
        [
            first, second, before_first, before_second,
            after_first, after_second, across_first, across_second,
        ],
        0,
    )


def ring_sum_parts(rows, later=None):
    own = rows.shape[0] // RING
    half = own // 2
    start, before, after, across = (rows[i * own : (i + 1) * own] for i in range(RING))
    from_before, from_after = ring(across[:half], 1), ring(across[half:], -1)
    second_after, first_before = ring(after[half:], 1), ring(before[:half], -1)
    if later is not None:
        from_before, from_after, second_after, first_before, later = tie(
            from_before, from_after, second_after, first_before, later
        )
    first_after = ring((after[:half].astype(WIDE) + from_before.astype(WIDE)).astype(LOW), 1)
    second_before = ring((before[half:].astype(WIDE) + from_after.astype(WIDE)).astype(LOW), -1)
    came = (start, first_after, second_after, first_before, second_before)
    return came if later is None else (came, later)


def ring_sum(rows):
    start, first_after, second_after, first_before, second_before = ring_sum_parts(rows)
    half = first_after.shape[0]
    first = start[:half].astype(WIDE) + first_after.astype(WIDE) + first_before.astype(WIDE)
    second = start[half:].astype(WIDE) + second_after.astype(WIDE) + second_before.astype(WIDE)
    return jnp.concatenate([first, second], 0)


def tie(*arrays):
    return lax.optimization_barrier(arrays)


def gather_weight(shard):
    full = lax.all_gather(shard, ("z", "c", "x"), axis=0)
    return full.reshape((8, 4) + shard.shape)


def settle(gradient):
    return lax.psum_scatter(gradient, ROWS, scatter_dimension=0)


def qkv_body(rows_ref, weight_ref, bias_ref, out_ref):
    weight = weight_ref[...].reshape(rows_ref.shape[1], -1)
    out_ref[...] = (dot(rows_ref[...], weight) + bias_ref[...]).astype(LOW)


def qkv_project(rows, weight, bias):
    count, width = rows.shape
    zc, xs, piece, _ = weight.shape
    cols = bias.shape[-1]
    return call(
        qkv_body,
        struct((xs, count, cols), LOW),
        (xs,),
        [
            whole((count, width)),
            pl.BlockSpec((zc, None, piece, cols), lambda i: (0, i, 0, 0)),
            pl.BlockSpec((None, 1, cols), lambda i: (i, 0, 0)),
        ],
        pl.BlockSpec((None, count, cols), lambda i: (i, 0, 0)),
        2 * count * width * xs * cols,
        10 * 2**20,
        vmem=60,
    )(rows, weight, bias)


def out_body(heads_ref, weight_ref, out_ref):
    count, _, piece, _ = weight_ref.shape
    for block in range(count):
        value = dot_t(heads_ref[0], weight_ref[block, 0])
        for x in range(1, RING):
            value += dot_t(heads_ref[x], weight_ref[block, x])
        out_ref[:, block * piece : (block + 1) * piece] = value.astype(LOW)


def store_rows(out_ref, place_ref, value):
    rows = value.shape[0] // RING
    for slot in range(RING):
        at = pl.multiple_of(place_ref[slot] * rows, rows)
        out_ref[pl.ds(at, rows)] = value[slot * rows : (slot + 1) * rows]


def out_project(heads, weight, at, blocks):
    xs, count, cols = heads.shape
    zc, _, piece, _ = weight.shape
    return call(
        out_body,
        struct((count, zc * piece), LOW),
        (zc // blocks,),
        [
            whole(heads.shape),
            pl.BlockSpec((blocks, xs, piece, cols), lambda i: (i, 0, 0, at)),
        ],
        pl.BlockSpec((count, blocks * piece), lambda i: (0, i)),
        2 * count * zc * piece * xs * cols,
        5 * 2**20,
        vmem=60,
    )(heads, weight)


def heads_grad_body(rows_ref, weight_ref, out_ref):
    weight = weight_ref[...].reshape(rows_ref.shape[1], -1)
    out_ref[...] = dot(rows_ref[...], weight).astype(LOW)


def heads_grad(rows, weight, cols, at):
    count, width = rows.shape
    zc, xs, piece, _ = weight.shape
    return call(
        heads_grad_body,
        struct((xs, count, cols), LOW),
        (xs,),
        [
            whole((count, width)),
            pl.BlockSpec((zc, None, piece, cols), lambda i: (0, i, 0, at)),
        ],
        pl.BlockSpec((None, count, cols), lambda i: (i, 0, 0)),
        2 * count * width * xs * cols,
        5 * 2**20,
        vmem=60,
    )(rows, weight)


def weight_grad_body(rows_ref, grad_ref, *refs):
    out_ref = refs[-1]
    out_ref[...] = dot_0(rows_ref[...], grad_ref[...]).astype(LOW).reshape(out_ref.shape)


def weight_grads(rows, columns, total_cols, at, onto=None):
    count, width = rows.shape
    xs, _, cols = columns.shape
    piece = width // 8
    more = () if onto is None else (onto,)
    return call(
        weight_grad_body,
        struct((8, xs, piece, total_cols), LOW),
        (xs,),
        [whole((count, width)), pl.BlockSpec((None, count, cols), lambda i: (i, 0, 0))]
        + [pl.BlockSpec(memory_space=pl.ANY)] * len(more),
        pl.BlockSpec((8, None, piece, cols), lambda i: (0, i, 0, at)),
        2 * count * width * xs * cols,
        15 * 2**20,
        vmem=60,
        aliases={2: 0} if more else None,
    )(rows, columns, *more)


def add_up(total, term):
    @pl.when(pl.program_id(0) == 0)
    def _():
        total[...] = term

    @pl.when(pl.program_id(0) > 0)
    def _():
        total[...] += term


def ffn_first_body(
    place_ref, norm_ref, cot_ref, up_ref, down_ref, bias_ref,
    hidden_ref, grad_up_ref, norm_grad_ref, bias_grad_ref, total,
):
    width, cols = norm_ref.shape[1], up_ref.shape[-1]
    up_w = up_ref[...].reshape(width, cols)
    up = dot(norm_ref[...], up_w) + bias_ref[...]
    normal = 0.5 * (1.0 + lax.erf(up * 0.7071067811865476))
    hidden_ref[...] = (up * normal).astype(LOW)
    slope = normal + up * (jnp.exp(-0.5 * up * up) * 0.3989422804014327)
    grad_up = (dot(cot_ref[...], down_ref[...].reshape(width, cols)) * slope).astype(LOW)
    grad_up_ref[...] = grad_up
    bias_grad_ref[...] = jnp.sum(grad_up.astype(WIDE), 0, keepdims=True)
    add_up(total, dot_t(grad_up, up_w))

    @pl.when(pl.program_id(0) == pl.num_programs(0) - 1)
    def _():
        store_rows(norm_grad_ref, place_ref, total[...].astype(LOW))


def ffn_first(places, norm_rows, cot_rows, weight, bias):
    count, width = norm_rows.shape
    zc, xs, piece, cols = weight.shape
    size = cols // 2
    rows = whole((count, width))
    vector = pl.BlockSpec((None, 1, size), lambda i, places: (places[RING + i], 0, 0))
    wide = pl.BlockSpec((count, size), lambda i, *_: (0, i))
    return call(
        ffn_first_body,
        (
            struct((count, xs * size), LOW),
            struct((count, xs * size), LOW),
            struct((count, width), LOW),
            struct((xs, 1, size), WIDE),
        ),
        (xs,),
        [
            rows,
            rows,
            pl.BlockSpec((zc, None, piece, size), lambda i, *_: (0, i, 0, 0)),
            pl.BlockSpec((zc, None, piece, size), lambda i, *_: (0, i, 0, 1)),
            vector,
        ],
        (wide, wide, rows, vector),
        6 * count * width * xs * size,
        25 * 2**20,
        scratch=[pltpu.VMEM((count, width), WIDE)],
        prefetch=1,
        vmem=56,
    )(places, norm_rows, cot_rows, weight, weight, bias)


def ffn_second_body(
    norm_ref, cot_ref, hidden_ref, grad_up_ref, down_ref, branch_ref, weight_grad_ref, total
):
    width, cols = norm_ref.shape[1], down_ref.shape[-1]
    zc, piece, _ = weight_grad_ref.shape
    hidden = hidden_ref[...]
    weight_grad_ref[:, :, :cols] = (
        dot_0(norm_ref[...], grad_up_ref[...]).astype(LOW).reshape(zc, piece, cols)
    )
    weight_grad_ref[:, :, cols:] = dot_0(cot_ref[...], hidden).astype(LOW).reshape(zc, piece, cols)
    add_up(total, dot_t(hidden, down_ref[...].reshape(width, cols)))

    @pl.when(pl.program_id(0) == pl.num_programs(0) - 1)
    def _():
        branch_ref[...] = total[...].astype(LOW)


def ffn_second(norm_rows, cot_rows, hidden, grad_up, weight):
    count, width = norm_rows.shape
    zc, xs, piece, cols = weight.shape
    size = cols // 2
    rows = whole((count, width))
    wide = pl.BlockSpec((count, size), lambda i: (0, i))
    return call(
        ffn_second_body,
        (struct((count, width), LOW), struct(weight.shape, LOW)),
        (xs,),
        [rows, rows, wide, wide, pl.BlockSpec((zc, None, piece, size), lambda i: (0, i, 0, 1))],
        (rows, pl.BlockSpec((zc, None, piece, cols), lambda i: (0, i, 0, 0))),
        6 * count * width * xs * size,
        40 * 2**20,
        scratch=[pltpu.VMEM((count, width), WIDE)],
        vmem=56,
    )(norm_rows, cot_rows, hidden, grad_up, weight)


def only_head(array, head):
    lane = lax.broadcasted_iota(jnp.int32, array.shape, 1)
    return jnp.where(lane // HEAD_DIM == head, array, jnp.zeros_like(array))


def allowed_keys(start, extent, live_count):
    q_place = start + lax.broadcasted_iota(jnp.int32, (SPAN, extent), 0)
    k_place = lax.broadcasted_iota(jnp.int32, (SPAN, extent), 1)
    return k_place <= jnp.minimum(q_place, live_count - 1)


def slot_of(place, own):
    apart = (place - own + RING) % RING
    return jnp.where(apart == 0, 0, jnp.where(apart == RING - 1, 1, apart + 1))


def load_ordered(blocks_ref, own, into):
    rows = blocks_ref.shape[2]
    for x in range(RING):
        for y in range(RING):
            at = (x * RING + y) * rows
            into[at : at + rows] = blocks_ref[x, slot_of(y, own)]


def store_ordered(blocks_ref, x, own, cols, value):
    rows = blocks_ref.shape[2]
    for y in range(RING):
        blocks_ref[x, slot_of(y, own), :, cols] = value[y * rows : (y + 1) * rows]


def attend_body(live_ref, qkv_ref, heads_ref, exact_ref, log_ref, qkv):
    live_count = live_ref[pl.program_id(0)]
    own = live_ref[pl.num_programs(0)]
    length = exact_ref.shape[0]
    width = exact_ref.shape[1]
    load_ordered(qkv_ref, own, qkv)
    key = qkv[:, width : 2 * width]
    value = qkv[:, 2 * width :]
    for span in range(length // SPAN):
        start, extent = span * SPAN, (span + 1) * SPAN
        here = slice(start, extent)

        @pl.when(start < live_count)
        def _():
            query = qkv[here, :width]
            allowed = allowed_keys(start, extent, live_count)
            mixed, logs = [], []
            for head in range(width // HEAD_DIM):
                scores = dot_t(only_head(query, head), key[:extent]) * HEAD_DIM**-0.5
                scores = jnp.where(allowed, scores, -1e9)
                top = jnp.max(scores, 1, keepdims=True)
                terms = jnp.exp(scores - top)
                denom = jnp.sum(terms, 1, keepdims=True)
                mixed.append(dot(terms.astype(LOW), value[:extent]) / denom)
                logs.append(top + jnp.log(denom))
            lane = lax.broadcasted_iota(jnp.int32, (SPAN, width), 1)
            out = jnp.where(lane < HEAD_DIM, mixed[0], mixed[1])
            exact_ref[here] = out
            log_ref[here] = jnp.where(lane < HEAD_DIM, logs[0], logs[1])
            store_ordered(heads_ref, span, own, slice(None), out.astype(LOW))

        @pl.when(start >= live_count)
        def _():
            exact_ref[here] = jnp.zeros((SPAN, width), WIDE)
            log_ref[here] = jnp.zeros((SPAN, width), WIDE)
            heads_ref[span] = jnp.zeros(heads_ref.shape[1:], LOW)


def row_block(rows, cols):
    return pl.BlockSpec((4, 4, None, rows, cols), lambda s, *_: (0, 0, s, 0, 0))


def attend(live_counts, qkv, width):
    xs, ys, seqs, rows, _ = qkv.shape
    length = xs * ys * rows
    flat = pl.BlockSpec((None, length, width), lambda s, *_: (s, 0, 0))
    return call(
        attend_body,
        (
            struct((xs, ys, seqs, rows, width), LOW),
            struct((seqs, length, width), WIDE),
            struct((seqs, length, width), WIDE),
        ),
        (seqs,),
        [row_block(rows, 3 * width)],
        (row_block(rows, width), flat, flat),
        4 * 10**9,
        4 * 2**20,
        scratch=[pltpu.VMEM((length, 3 * width), LOW)],
        prefetch=1,
    )(live_counts, qkv)


def attend_back_body(
    live_ref, qkv_ref, grad_ref, exact_ref, log_ref, out_ref, sum_ref,
    key_total, value_total, qkv, grads,
):
    live_count = live_ref[pl.program_id(0)]
    own = live_ref[pl.num_programs(0)]
    length, width = exact_ref.shape
    factor = HEAD_DIM**-0.5
    load_ordered(qkv_ref, own, qkv)
    load_ordered(grad_ref, own, grads)
    key = qkv[:, width : 2 * width]
    value = qkv[:, 2 * width :]
    key_total[...] = jnp.zeros_like(key_total)
    value_total[...] = jnp.zeros_like(value_total)
    sum_ref[...] = jnp.zeros_like(sum_ref)
    for span in range(length // SPAN):
        start, extent = span * SPAN, (span + 1) * SPAN
        here = slice(start, extent)

        @pl.when(start < live_count)
        def _():
            query = qkv[here, :width]
            grad = grads[here]
            inner = grad.astype(WIDE) * exact_ref[here]
            logs = log_ref[here]
            allowed = allowed_keys(start, extent, live_count)
            query_total = jnp.zeros((SPAN, width), WIDE)
            for head in range(width // HEAD_DIM):
                query_h = only_head(query, head)
                grad_h = only_head(grad, head)
                log_h = logs[:, head * HEAD_DIM : head * HEAD_DIM + 1]
                row_inner = jnp.sum(only_head(inner, head), 1, keepdims=True)
                scores = dot_t(query_h, key[:extent]) * factor
                probs = jnp.exp(jnp.where(allowed, scores, -1e9) - log_h)
                d_probs = dot_t(grad_h, value[:extent])
                value_total[:extent] += dot_0(probs.astype(LOW), grad_h)
                d_scores = (probs * (d_probs - row_inner)).astype(LOW)
                query_total += dot(d_scores, only_head(key[:extent], head))
                key_total[:extent] += dot_0(d_scores, query_h)
            out = (query_total * factor).astype(LOW)
            store_ordered(out_ref, span, own, slice(0, width), out)
            sum_ref[:, :width] += jnp.sum(out.astype(WIDE), 0, keepdims=True)

        @pl.when(start >= live_count)
        def _():
            out_ref[span, :, :, :width] = jnp.zeros(out_ref.shape[1:3] + (width,), LOW)

    key_grad = (key_total[...] * factor).astype(LOW)
    value_grad = value_total[...].astype(LOW)
    for span in range(RING):
        here = slice(span * SPAN, (span + 1) * SPAN)
        store_ordered(out_ref, span, own, slice(width, 2 * width), key_grad[here])
        store_ordered(out_ref, span, own, slice(2 * width, None), value_grad[here])
    sum_ref[:, 2 * width :] = jnp.sum(value_grad.astype(WIDE), 0, keepdims=True)


def attend_back(live_counts, qkv, grads, exact, logs):
    xs, ys, seqs, rows, _ = qkv.shape
    _, length, width = exact.shape
    flat = pl.BlockSpec((None, length, width), lambda s, *_: (s, 0, 0))
    return call(
        attend_back_body,
        (struct(qkv.shape, LOW), struct((seqs, 1, 3 * width), WIDE)),
        (seqs,),
        [row_block(rows, 3 * width), row_block(rows, width), flat, flat],
        (
            row_block(rows, 3 * width),
            pl.BlockSpec((None, 1, 3 * width), lambda s, *_: (s, 0, 0)),
        ),
        8 * 10**9,
        8 * 2**20,
        scratch=[
            pltpu.VMEM((length, width), WIDE),
            pltpu.VMEM((length, width), WIDE),
            pltpu.VMEM((length, 3 * width), LOW),
            pltpu.VMEM((length, width), LOW),
        ],
        prefetch=1,
    )(live_counts, qkv, grads, exact, logs)


def norm_rows(values, gain_vec, shift_vec):
    centered = values - jnp.mean(values, -1, keepdims=True)
    inverse = lax.rsqrt(jnp.mean(centered * centered, -1, keepdims=True) + 1e-05)
    return (centered * inverse * gain_vec + shift_vec).astype(LOW)


def norm_back_body(count, with_low, *refs):
    parts, (rows_ref, grad_ref, gain_ref) = refs[:count], refs[count : count + 3]
    refs = refs[count + 3 :]
    if count == 1:
        terms = [parts[0][i] for i in range(parts[0].shape[0])]
    else:
        start, first_after, second_after, first_before, second_before = (p[...] for p in parts)
        early = pl.program_id(0) < pl.num_programs(0) // 2
        terms = [
            start,
            jnp.where(early, first_after, second_after),
            jnp.where(early, first_before, second_before),
        ]
    gradient = sum(term.astype(WIDE) for term in terms)
    values = rows_ref[...].astype(WIDE)
    centered = values - jnp.mean(values, 1, keepdims=True)
    inverse = lax.rsqrt(jnp.mean(centered * centered, 1, keepdims=True) + 1e-05)
    unit = centered * inverse
    scaled = gradient * gain_ref[...]
    out = grad_ref[...].astype(WIDE) + inverse * (
        scaled
        - jnp.mean(scaled, 1, keepdims=True)
        - unit * jnp.mean(scaled * unit, 1, keepdims=True)
    )
    sums = [jnp.sum(gradient * unit, 0, keepdims=True), jnp.sum(gradient, 0, keepdims=True)]
    if with_low:
        keep_ref, out_ref, low_ref, sum_ref = refs
        low = (keep_ref[...] * out).astype(LOW)
        low_ref[...] = low
        sums.append(jnp.sum(low.astype(WIDE), 0, keepdims=True))
    else:
        out_ref, sum_ref = refs
    out_ref[...] = out
    sums.append(jnp.zeros((sum_ref.shape[0] - len(sums), sum_ref.shape[1]), WIDE))
    add_up(sum_ref, jnp.concatenate(sums, 0))


def norm_back(parts, rows, grad, gain, keep=None):
    own, width = rows.shape
    step = own // 4
    flat = pl.BlockSpec((step, width), lambda i: (i, 0))
    sums = pl.BlockSpec((8, width), lambda i: (0, 0))
    if isinstance(parts, tuple):
        early = pl.BlockSpec((step, width), lambda i: (jnp.minimum(i, 1), 0))
        late = pl.BlockSpec((step, width), lambda i: (jnp.maximum(i - 2, 0), 0))
        in_specs, args = [flat, early, late, early, late], list(parts)
    else:
        in_specs = [pl.BlockSpec((parts.shape[0], step, width), lambda i: (0, i, 0))]
        args = [parts]
    count = len(args)
    in_specs += [flat, flat, pl.BlockSpec((1, width), lambda i: (0, 0))]
    args += [rows, grad, gain.reshape(1, width)]
    outs, specs = [struct((own, width), WIDE)], [flat]
    if keep is not None:
        in_specs.append(pl.BlockSpec((step, 1), lambda i: (i, 0)))
        args.append(keep)
        outs.append(struct((own, width), LOW))
        specs.append(flat)
    return call(
        partial(norm_back_body, count, keep is not None),
        tuple(outs + [struct((8, width), WIDE)]),
        (own // step,),
        in_specs,
        tuple(specs + [sums]),
        40 * own * width,
        6 * 2**20,
    )(*args)


def collect_vectors(vectors):
    flat = jnp.concatenate([v.reshape(-1) for v in vectors])
    return collect(flat.reshape(16, -1, 128), COLS)


def spread_vectors(part, sizes):
    flat = spread(jnp.sum(spread(part, ROWS, 8), 0), COLS, 16).reshape(-1)
    pieces, start = [], 0
    for size in sizes:
        pieces.append(flat[start : start + size])
        start += size
    return pieces


def shards(
    tokens, cotangent, seq_lengths, exit_layers, layer_index,
    ln1_gain, ln1_shift, q_weight, q_bias, k_weight, v_weight, v_bias, out_weight, out_bias,
    ln2_gain, ln2_shift, up_weight, up_bias, down_weight, down_bias,
):
    seqs, own_rows, width = tokens.shape
    own = seqs * own_rows
    full_len = exit_layers.shape[1]
    x_at, y_at = lax.axis_index("x"), lax.axis_index("y")
    head_at = x_at * RING + y_at
    head_cols = q_weight.shape[1]
    ff_cols = up_weight.shape[1]

    positions = jnp.arange(full_len)
    live_all = (positions[None, :] < seq_lengths[:, None]) & (exit_layers > layer_index[0])
    live_counts = jnp.concatenate(
        [jnp.sum(live_all.astype(jnp.int32), 1), y_at.astype(jnp.int32).reshape(1)]
    )
    y_places, x_places = (
        [((at + apart) % RING).astype(jnp.int32) for apart in (0, RING - 1, 1, 2)]
        for at in (y_at, x_at)
    )
    places = jnp.stack(y_places + x_places)
    live_mine = lax.dynamic_slice_in_dim(live_all, head_at * own_rows, own_rows, 1)
    keep = live_mine.reshape(-1, 1).astype(WIDE)

    w_attn = gather_weight(
        jnp.concatenate([q_weight, k_weight, v_weight, out_weight], 1).astype(LOW)
    )
    w_ff = jnp.concatenate([up_weight, down_weight], 1).astype(LOW)

    inputs = tokens.astype(WIDE).reshape(own, width)
    norm1 = ring_gather(norm_rows(inputs, ln1_gain, ln1_shift))
    flat_cot = cotangent.reshape(own, width)
    g_ffn = (keep * flat_cot.astype(WIDE)).astype(LOW)
    norm1, w_ff = tie(norm1, [ring(w_ff, step, "x") for step in (0, 1, -1, 2)])
    w_ff = lax.all_gather(jnp.stack(w_ff), ROWS, axis=0)
    norm1, cot_rows = tie(norm1, ring_gather(g_ffn))

    def mine(vector, cols):
        return lax.dynamic_index_in_dim(vector.reshape(RING, RING, cols), y_at, 1, False)

    bias = jnp.concatenate(
        [mine(q_bias, head_cols), jnp.zeros((RING, head_cols), WIDE), mine(v_bias, head_cols)], 1
    ).reshape(RING, 1, 3 * head_cols)
    qkv = qkv_project(norm1, w_attn, bias)
    rows5 = (RING, RING, seqs, own_rows)
    qkv = swap(qkv, "x").reshape(rows5 + (3 * head_cols,))
    heads, exact, logs = attend(live_counts, qkv, head_cols)
    heads = swap(heads.reshape(RING, RING * own, head_cols), "x")
    branch1 = ring_sum(out_project(heads, w_attn, 3, 4)) + out_bias
    middle = inputs + keep * branch1
    norm2 = ring_gather(norm_rows(middle, ln2_gain, ln2_shift))

    ff_bias = mine(up_bias, ff_cols).reshape(RING, 1, ff_cols)
    hidden, grad_up, g_norm2, up_bias_part = ffn_first(places, norm2, cot_rows, w_ff, ff_bias)
    g_norm2 = swap(g_norm2.reshape(RING, own, width), "y")
    g_norm2, branch2, ff_grad = tie(
        g_norm2, *ffn_second(norm2, cot_rows, hidden, grad_up, w_ff)
    )
    ff_grad = settle(ff_grad)
    grad_mid, g_attn, sums2 = norm_back(g_norm2, middle, flat_cot, ln2_gain, keep)
    attn_rows = ring_gather(g_attn)
    g_heads = heads_grad(attn_rows, w_attn, head_cols, 3)
    g_heads, branch2 = tie(swap(g_heads, "x").reshape(rows5 + (head_cols,)), branch2)
    branch2 = ring_collect(branch2.reshape(RING, own, width), "y") + down_bias
    result = (middle + keep * branch2).astype(LOW).reshape(tokens.shape)
    d_qkv, d_sums = attend_back(live_counts, qkv, g_heads, exact, logs)
    d_qkv, attn_rows = tie(d_qkv, attn_rows)
    attn_grad = weight_grads(attn_rows, heads, 4 * head_cols, 3)
    d_qkv = swap(d_qkv.reshape(RING, RING * own, 3 * head_cols), "x")

    up_bias_full = lax.dynamic_update_slice_in_dim(
        jnp.zeros((RING, RING, ff_cols), WIDE), up_bias_part.reshape(RING, 1, ff_cols), y_at, 1
    )
    early = (
        sums2[2],
        sums2[0],
        sums2[1],
        up_bias_full,
        jnp.sum(g_ffn.astype(WIDE), 0),
    )
    d_qkv, attn_grad, result = tie(d_qkv, attn_grad, result)
    attn_grad = weight_grads(norm1, d_qkv, 4 * head_cols, 0, attn_grad)
    d_qkv, attn_grad = tie(d_qkv, attn_grad)
    attn_grad = settle(attn_grad)
    g_norm1, ff_grad = ring_sum_parts(out_project(d_qkv, w_attn, 0, 2), ff_grad)
    ff_grad = ring_collect(ff_grad, "x")
    grad_tokens, sums1 = norm_back(g_norm1, tokens.reshape(own, width), grad_mid, ln1_gain)
    grad_tokens = grad_tokens.reshape(tokens.shape)
    d_sums = jnp.sum(d_sums, 0).reshape(3, head_cols)

    def placed(row):
        blank = jnp.zeros((RING * RING, head_cols), WIDE)
        return lax.dynamic_update_slice_in_dim(blank, row[None], head_at, 0)

    part = collect_vectors(early + (sums1[0], sums1[1], placed(d_sums[0]), placed(d_sums[2])))
    part, attn_grad, ff_grad = tie(part, attn_grad, ff_grad)
    here = [lax.dynamic_index_in_dim(attn_grad, x_places[i], 0, False) for i in range(RING)]
    attn_grad = ring_collect(here, "x")
    sizes = (width, width, width, RING * RING * ff_cols) + (width,) * 5
    totals = spread_vectors(part, sizes)
    out_bias_sum, ln2_gain_sum, ln2_shift_sum, up_bias_sum, down_bias_sum = totals[:5]
    ln1_gain_sum, ln1_shift_sum, q_bias_sum, v_bias_sum = totals[5:]
    return (
        result,
        grad_tokens,
        ln1_gain_sum,
        ln1_shift_sum,
        attn_grad[:, :head_cols],
        q_bias_sum,
        attn_grad[:, head_cols : 2 * head_cols],
        attn_grad[:, 2 * head_cols : 3 * head_cols],
        v_bias_sum,
        attn_grad[:, 3 * head_cols :],
        out_bias_sum,
        ln2_gain_sum,
        ln2_shift_sum,
        ff_grad[:, :ff_cols],
        up_bias_sum,
        ff_grad[:, ff_cols:],
        down_bias_sum,
    )


def solution(mesh):
    wide = Mesh(mesh.devices.reshape(4, 2, 4, 4), ("z", "c", "x", "y"))
    act = P(ROWS, COLS, None)
    weight = P(ROWS, COLS)
    vector = P()
    in_specs = (
        act, act, P(ROWS), P(ROWS, None), vector, vector, vector,
        weight, vector, weight, weight, vector, weight, vector, vector, vector,
        weight, vector, weight, vector,
    )
    out_specs = (
        act, act, vector, vector, weight, vector, weight, weight, vector, weight,
        vector, vector, vector, weight, vector, weight, vector,
    )
    return jax.shard_map(
        shards, mesh=wide, in_specs=in_specs, out_specs=out_specs, check_vma=False
    )
```

```python
from functools import partial

import jax
import jax.numpy as jnp
from jax import lax
from jax.experimental import pallas as pl
from jax.experimental.pallas import tpu as pltpu
from jax.sharding import Mesh
from jax.sharding import PartitionSpec as P

HEAD_DIM = 64
SPAN = 256
LOW = jnp.bfloat16
WIDE = jnp.float32
RING = 4
ROWS = ("z", "c")
COLS = ("x", "y")


def dot(left, right):
    return jnp.dot(left, right, preferred_element_type=WIDE)


def dot_t(left, right):
    return lax.dot_general(left, right, (((1,), (1,)), ((), ())), preferred_element_type=WIDE)


def dot_0(left, right):
    return lax.dot_general(left, right, (((0,), (0,)), ((), ())), preferred_element_type=WIDE)


def call(body, out_shape, grid, in_specs, out_specs, flops, traffic, scratch=(), prefetch=0, vmem=40, aliases=None):
    return pl.pallas_call(
        body,
        out_shape=out_shape,
        grid_spec=pltpu.PrefetchScalarGridSpec(
            num_scalar_prefetch=prefetch,
            grid=grid,
            in_specs=in_specs,
            out_specs=out_specs,
            scratch_shapes=list(scratch),
        ),
        compiler_params=pltpu.CompilerParams(vmem_limit_bytes=vmem * 2**20),
        input_output_aliases=aliases or {},
        cost_estimate=pl.CostEstimate(flops=flops, bytes_accessed=traffic, transcendentals=0),
    )


def whole(shape):
    return pl.BlockSpec(shape, lambda *_: (0,) * len(shape))


def struct(shape, dtype):
    return jax.ShapeDtypeStruct(shape, dtype)


def spread(array, axes, size):
    return lax.all_to_all(jnp.broadcast_to(array[None], (size,) + array.shape), axes, 0, 0)


def collect(parts, axes):
    return jnp.sum(lax.all_to_all(parts, axes, 0, 0).astype(WIDE), 0)


def swap(parts, axes):
    return lax.all_to_all(parts, axes, 0, 0)


def ring(array, step, axis="y"):
    if step == 0:
        return array
    return lax.ppermute(array, axis, [(i, (i + step) % RING) for i in range(RING)])


def ring_terms(parts, axis):
    return [parts[0]] + [ring(parts[slot], step, axis) for slot, step in ((1, -1), (2, 1), (3, 2))]


def ring_collect(parts, axis):
    return sum(term.astype(WIDE) for term in ring_terms(parts, axis))


def ring_near(rows):
    half = rows.shape[0] // 2
    first, second = rows[:half], rows[half:]
    return [first, second, ring(first, 1), ring(second, 1), ring(first, -1), ring(second, -1)]


def ring_far(near):
    return jnp.concatenate(list(near) + [ring(near[2], 1), ring(near[5], -1)], 0)


def ring_gather(rows):
    return ring_far(ring_near(rows))


def ring_sum_parts(rows, later=None):
    own = rows.shape[0] // RING
    half = own // 2
    start, before, after, across = (rows[i * own : (i + 1) * own] for i in range(RING))
    from_before, from_after = ring(across[:half], 1), ring(across[half:], -1)
    second_after, first_before = ring(after[half:], 1), ring(before[:half], -1)
    if later is not None:
        from_before, from_after, second_after, first_before, later = tie(
            from_before, from_after, second_after, first_before, later
        )
    first_after = ring((after[:half].astype(WIDE) + from_before.astype(WIDE)).astype(LOW), 1)
    second_before = ring((before[half:].astype(WIDE) + from_after.astype(WIDE)).astype(LOW), -1)
    came = (start, first_after, second_after, first_before, second_before)
    return came if later is None else (came, later)


def ring_sum(rows):
    start, first_after, second_after, first_before, second_before = ring_sum_parts(rows)
    half = first_after.shape[0]
    first = start[:half].astype(WIDE) + first_after.astype(WIDE) + first_before.astype(WIDE)
    second = start[half:].astype(WIDE) + second_after.astype(WIDE) + second_before.astype(WIDE)
    return jnp.concatenate([first, second], 0)


def tie(*arrays):
    return lax.optimization_barrier(arrays)


def gather_weight(shard):
    full = lax.all_gather(shard, ("z", "c", "x"), axis=0)
    return full.reshape((8, 4) + shard.shape)


def settle(gradient):
    return lax.psum_scatter(gradient, ROWS, scatter_dimension=0)


def qkv_body(rows_ref, weight_ref, bias_ref, out_ref):
    weight = weight_ref[...].reshape(rows_ref.shape[1], -1)
    out_ref[...] = (dot(rows_ref[...], weight) + bias_ref[...]).astype(LOW)


def qkv_project(rows, weight, bias):
    count, width = rows.shape
    zc, xs, piece, _ = weight.shape
    cols = bias.shape[-1]
    return call(
        qkv_body,
        struct((xs, count, cols), LOW),
        (xs,),
        [
            whole((count, width)),
            pl.BlockSpec((zc, None, piece, cols), lambda i: (0, i, 0, 0)),
            pl.BlockSpec((None, 1, cols), lambda i: (i, 0, 0)),
        ],
        pl.BlockSpec((None, count, cols), lambda i: (i, 0, 0)),
        2 * count * width * xs * cols,
        10 * 2**20,
        vmem=60,
    )(rows, weight, bias)


def out_body(heads_ref, weight_ref, out_ref):
    count, _, piece, _ = weight_ref.shape
    for block in range(count):
        value = dot_t(heads_ref[0], weight_ref[block, 0])
        for x in range(1, RING):
            value += dot_t(heads_ref[x], weight_ref[block, x])
        out_ref[:, block * piece : (block + 1) * piece] = value.astype(LOW)


def store_rows(out_ref, place_ref, value):
    rows = value.shape[0] // RING
    for slot in range(RING):
        at = pl.multiple_of(place_ref[slot] * rows, rows)
        out_ref[pl.ds(at, rows)] = value[slot * rows : (slot + 1) * rows]


def out_project(heads, weight, at, blocks):
    xs, count, cols = heads.shape
    zc, _, piece, _ = weight.shape
    return call(
        out_body,
        struct((count, zc * piece), LOW),
        (zc // blocks,),
        [
            whole(heads.shape),
            pl.BlockSpec((blocks, xs, piece, cols), lambda i: (i, 0, 0, at)),
        ],
        pl.BlockSpec((count, blocks * piece), lambda i: (0, i)),
        2 * count * zc * piece * xs * cols,
        5 * 2**20,
        vmem=60,
    )(heads, weight)


def heads_grad_body(rows_ref, weight_ref, out_ref):
    weight = weight_ref[...].reshape(rows_ref.shape[1], -1)
    out_ref[...] = dot(rows_ref[...], weight).astype(LOW)


def heads_grad(rows, weight, cols, at):
    count, width = rows.shape
    zc, xs, piece, _ = weight.shape
    return call(
        heads_grad_body,
        struct((xs, count, cols), LOW),
        (xs,),
        [
            whole((count, width)),
            pl.BlockSpec((zc, None, piece, cols), lambda i: (0, i, 0, at)),
        ],
        pl.BlockSpec((None, count, cols), lambda i: (i, 0, 0)),
        2 * count * width * xs * cols,
        5 * 2**20,
        vmem=60,
    )(rows, weight)


def weight_grad_body(rows_ref, grad_ref, *refs):
    out_ref = refs[-1]
    out_ref[...] = dot_0(rows_ref[...], grad_ref[...]).astype(LOW).reshape(out_ref.shape)


def weight_grads(rows, columns, total_cols, at, onto=None):
    count, width = rows.shape
    xs, _, cols = columns.shape
    piece = width // 8
    more = () if onto is None else (onto,)
    return call(
        weight_grad_body,
        struct((8, xs, piece, total_cols), LOW),
        (xs,),
        [whole((count, width)), pl.BlockSpec((None, count, cols), lambda i: (i, 0, 0))]
        + [pl.BlockSpec(memory_space=pl.ANY)] * len(more),
        pl.BlockSpec((8, None, piece, cols), lambda i: (0, i, 0, at)),
        2 * count * width * xs * cols,
        15 * 2**20,
        vmem=60,
        aliases={2: 0} if more else None,
    )(rows, columns, *more)


def add_up(total, term):
    @pl.when(pl.program_id(0) == 0)
    def _():
        total[...] = term

    @pl.when(pl.program_id(0) > 0)
    def _():
        total[...] += term


def hidden_grad_body(cot_ref, down_ref, out_ref):
    out_ref[...] = dot(cot_ref[...], down_ref[...].reshape(cot_ref.shape[1], -1))


def hidden_grad(cot_rows, weight):
    count, width = cot_rows.shape
    zc, xs, piece, cols = weight.shape
    size = cols // 2
    return call(
        hidden_grad_body,
        struct((count, xs * size), WIDE),
        (xs,),
        [
            whole((count, width)),
            pl.BlockSpec((zc, None, piece, size), lambda i: (0, i, 0, 1)),
        ],
        pl.BlockSpec((count, size), lambda i: (0, i)),
        2 * count * width * xs * size,
        15 * 2**20,
        vmem=56,
    )(cot_rows, weight)


def ffn_first_body(
    place_ref, norm_ref, grad_ref, up_ref, bias_ref,
    hidden_ref, grad_up_ref, norm_grad_ref, bias_grad_ref, total,
):
    width, cols = norm_ref.shape[1], up_ref.shape[-1]
    up_w = up_ref[...].reshape(width, cols)
    up = dot(norm_ref[...], up_w) + bias_ref[...]
    normal = 0.5 * (1.0 + lax.erf(up * 0.7071067811865476))
    hidden_ref[...] = (up * normal).astype(LOW)
    slope = normal + up * (jnp.exp(-0.5 * up * up) * 0.3989422804014327)
    grad_up = (grad_ref[...] * slope).astype(LOW)
    grad_up_ref[...] = grad_up
    bias_grad_ref[...] = jnp.sum(grad_up.astype(WIDE), 0, keepdims=True)
    add_up(total, dot_t(grad_up, up_w))

    @pl.when(pl.program_id(0) == pl.num_programs(0) - 1)
    def _():
        store_rows(norm_grad_ref, place_ref, total[...].astype(LOW))


def ffn_first(places, norm_rows, grad_rows, weight, bias):
    count, width = norm_rows.shape
    zc, xs, piece, cols = weight.shape
    size = cols // 2
    rows = whole((count, width))
    vector = pl.BlockSpec((None, 1, size), lambda i, places: (places[RING + i], 0, 0))
    wide = pl.BlockSpec((count, size), lambda i, *_: (0, i))
    return call(
        ffn_first_body,
        (
            struct((count, xs * size), LOW),
            struct((count, xs * size), LOW),
            struct((count, width), LOW),
            struct((xs, 1, size), WIDE),
        ),
        (xs,),
        [
            rows,
            wide,
            pl.BlockSpec((zc, None, piece, size), lambda i, *_: (0, i, 0, 0)),
            vector,
        ],
        (wide, wide, rows, vector),
        4 * count * width * xs * size,
        25 * 2**20,
        scratch=[pltpu.VMEM((count, width), WIDE)],
        prefetch=1,
        vmem=56,
    )(places, norm_rows, grad_rows, weight, bias)


def ffn_second_body(
    norm_ref, cot_ref, hidden_ref, grad_up_ref, down_ref, branch_ref, weight_grad_ref, total
):
    width, cols = norm_ref.shape[1], down_ref.shape[-1]
    zc, piece, _ = weight_grad_ref.shape
    hidden = hidden_ref[...]
    weight_grad_ref[:, :, :cols] = (
        dot_0(norm_ref[...], grad_up_ref[...]).astype(LOW).reshape(zc, piece, cols)
    )
    weight_grad_ref[:, :, cols:] = dot_0(cot_ref[...], hidden).astype(LOW).reshape(zc, piece, cols)
    add_up(total, dot_t(hidden, down_ref[...].reshape(width, cols)))

    @pl.when(pl.program_id(0) == pl.num_programs(0) - 1)
    def _():
        branch_ref[...] = total[...].astype(LOW)


def ffn_second(norm_rows, cot_rows, hidden, grad_up, weight):
    count, width = norm_rows.shape
    zc, xs, piece, cols = weight.shape
    size = cols // 2
    rows = whole((count, width))
    wide = pl.BlockSpec((count, size), lambda i: (0, i))
    return call(
        ffn_second_body,
        (struct((count, width), LOW), struct(weight.shape, LOW)),
        (xs,),
        [rows, rows, wide, wide, pl.BlockSpec((zc, None, piece, size), lambda i: (0, i, 0, 1))],
        (rows, pl.BlockSpec((zc, None, piece, cols), lambda i: (0, i, 0, 0))),
        6 * count * width * xs * size,
        40 * 2**20,
        scratch=[pltpu.VMEM((count, width), WIDE)],
        vmem=56,
    )(norm_rows, cot_rows, hidden, grad_up, weight)


def only_head(array, head):
    lane = lax.broadcasted_iota(jnp.int32, array.shape, 1)
    return jnp.where(lane // HEAD_DIM == head, array, jnp.zeros_like(array))


def allowed_keys(start, extent, live_count):
    q_place = start + lax.broadcasted_iota(jnp.int32, (SPAN, extent), 0)
    k_place = lax.broadcasted_iota(jnp.int32, (SPAN, extent), 1)
    return k_place <= jnp.minimum(q_place, live_count - 1)


def slot_of(place, own):
    apart = (place - own + RING) % RING
    return jnp.where(apart == 0, 0, jnp.where(apart == RING - 1, 1, apart + 1))


def load_ordered(blocks_ref, own, into):
    rows = blocks_ref.shape[2]
    for x in range(RING):
        for y in range(RING):
            at = (x * RING + y) * rows
            into[at : at + rows] = blocks_ref[x, slot_of(y, own)]


def store_ordered(blocks_ref, x, own, cols, value):
    rows = blocks_ref.shape[2]
    for y in range(RING):
        blocks_ref[x, slot_of(y, own), :, cols] = value[y * rows : (y + 1) * rows]


def attend_body(live_ref, qkv_ref, heads_ref, exact_ref, log_ref, qkv):
    live_count = live_ref[pl.program_id(0)]
    own = live_ref[pl.num_programs(0)]
    length = exact_ref.shape[0]
    width = exact_ref.shape[1]
    load_ordered(qkv_ref, own, qkv)
    key = qkv[:, width : 2 * width]
    value = qkv[:, 2 * width :]
    for span in range(length // SPAN):
        start, extent = span * SPAN, (span + 1) * SPAN
        here = slice(start, extent)

        @pl.when(start < live_count)
        def _():
            query = qkv[here, :width]
            allowed = allowed_keys(start, extent, live_count)
            mixed, logs = [], []
            for head in range(width // HEAD_DIM):
                scores = dot_t(only_head(query, head), key[:extent]) * HEAD_DIM**-0.5
                scores = jnp.where(allowed, scores, -1e9)
                top = jnp.max(scores, 1, keepdims=True)
                terms = jnp.exp(scores - top)
                denom = jnp.sum(terms, 1, keepdims=True)
                mixed.append(dot(terms.astype(LOW), value[:extent]) / denom)
                logs.append(top + jnp.log(denom))
            lane = lax.broadcasted_iota(jnp.int32, (SPAN, width), 1)
            out = jnp.where(lane < HEAD_DIM, mixed[0], mixed[1])
            exact_ref[here] = out
            log_ref[here] = jnp.where(lane < HEAD_DIM, logs[0], logs[1])
            store_ordered(heads_ref, span, own, slice(None), out.astype(LOW))

        @pl.when(start >= live_count)
        def _():
            exact_ref[here] = jnp.zeros((SPAN, width), WIDE)
            log_ref[here] = jnp.zeros((SPAN, width), WIDE)
            heads_ref[span] = jnp.zeros(heads_ref.shape[1:], LOW)


def row_block(rows, cols):
    return pl.BlockSpec((4, 4, None, rows, cols), lambda s, *_: (0, 0, s, 0, 0))


def attend(live_counts, qkv, width):
    xs, ys, seqs, rows, _ = qkv.shape
    length = xs * ys * rows
    flat = pl.BlockSpec((None, length, width), lambda s, *_: (s, 0, 0))
    return call(
        attend_body,
        (
            struct((xs, ys, seqs, rows, width), LOW),
            struct((seqs, length, width), WIDE),
            struct((seqs, length, width), WIDE),
        ),
        (seqs,),
        [row_block(rows, 3 * width)],
        (row_block(rows, width), flat, flat),
        4 * 10**9,
        4 * 2**20,
        scratch=[pltpu.VMEM((length, 3 * width), LOW)],
        prefetch=1,
    )(live_counts, qkv)


def attend_back_body(
    live_ref, qkv_ref, grad_ref, exact_ref, log_ref, out_ref, sum_ref,
    key_total, value_total, qkv, grads,
):
    live_count = live_ref[pl.program_id(0)]
    own = live_ref[pl.num_programs(0)]
    length, width = exact_ref.shape
    factor = HEAD_DIM**-0.5
    load_ordered(qkv_ref, own, qkv)
    load_ordered(grad_ref, own, grads)
    key = qkv[:, width : 2 * width]
    value = qkv[:, 2 * width :]
    key_total[...] = jnp.zeros_like(key_total)
    value_total[...] = jnp.zeros_like(value_total)
    sum_ref[...] = jnp.zeros_like(sum_ref)
    for span in range(length // SPAN):
        start, extent = span * SPAN, (span + 1) * SPAN
        here = slice(start, extent)

        @pl.when(start < live_count)
        def _():
            query = qkv[here, :width]
            grad = grads[here]
            inner = grad.astype(WIDE) * exact_ref[here]
            logs = log_ref[here]
            allowed = allowed_keys(start, extent, live_count)
            query_total = jnp.zeros((SPAN, width), WIDE)
            for head in range(width // HEAD_DIM):
                query_h = only_head(query, head)
                grad_h = only_head(grad, head)
                log_h = logs[:, head * HEAD_DIM : head * HEAD_DIM + 1]
                row_inner = jnp.sum(only_head(inner, head), 1, keepdims=True)
                scores = dot_t(query_h, key[:extent]) * factor
                probs = jnp.exp(jnp.where(allowed, scores, -1e9) - log_h)
                d_probs = dot_t(grad_h, value[:extent])
                value_total[:extent] += dot_0(probs.astype(LOW), grad_h)
                d_scores = (probs * (d_probs - row_inner)).astype(LOW)
                query_total += dot(d_scores, only_head(key[:extent], head))
                key_total[:extent] += dot_0(d_scores, query_h)
            out = (query_total * factor).astype(LOW)
            store_ordered(out_ref, span, own, slice(0, width), out)
            sum_ref[:, :width] += jnp.sum(out.astype(WIDE), 0, keepdims=True)

        @pl.when(start >= live_count)
        def _():
            out_ref[span, :, :, :width] = jnp.zeros(out_ref.shape[1:3] + (width,), LOW)

    key_grad = (key_total[...] * factor).astype(LOW)
    value_grad = value_total[...].astype(LOW)
    for span in range(RING):
        here = slice(span * SPAN, (span + 1) * SPAN)
        store_ordered(out_ref, span, own, slice(width, 2 * width), key_grad[here])
        store_ordered(out_ref, span, own, slice(2 * width, None), value_grad[here])
    sum_ref[:, 2 * width :] = jnp.sum(value_grad.astype(WIDE), 0, keepdims=True)


def attend_back(live_counts, qkv, grads, exact, logs):
    xs, ys, seqs, rows, _ = qkv.shape
    _, length, width = exact.shape
    flat = pl.BlockSpec((None, length, width), lambda s, *_: (s, 0, 0))
    return call(
        attend_back_body,
        (struct(qkv.shape, LOW), struct((seqs, 1, 3 * width), WIDE)),
        (seqs,),
        [row_block(rows, 3 * width), row_block(rows, width), flat, flat],
        (
            row_block(rows, 3 * width),
            pl.BlockSpec((None, 1, 3 * width), lambda s, *_: (s, 0, 0)),
        ),
        8 * 10**9,
        8 * 2**20,
        scratch=[
            pltpu.VMEM((length, width), WIDE),
            pltpu.VMEM((length, width), WIDE),
            pltpu.VMEM((length, 3 * width), LOW),
            pltpu.VMEM((length, width), LOW),
        ],
        prefetch=1,
    )(live_counts, qkv, grads, exact, logs)


def norm_rows(values, gain_vec, shift_vec):
    centered = values - jnp.mean(values, -1, keepdims=True)
    inverse = lax.rsqrt(jnp.mean(centered * centered, -1, keepdims=True) + 1e-05)
    return (centered * inverse * gain_vec + shift_vec).astype(LOW)


def norm_back_body(count, with_low, *refs):
    parts, (rows_ref, grad_ref, gain_ref) = refs[:count], refs[count : count + 3]
    refs = refs[count + 3 :]
    if count == 1:
        terms = [parts[0][i] for i in range(parts[0].shape[0])]
    else:
        start, first_after, second_after, first_before, second_before = (p[...] for p in parts)
        early = pl.program_id(0) < pl.num_programs(0) // 2
        terms = [
            start,
            jnp.where(early, first_after, second_after),
            jnp.where(early, first_before, second_before),
        ]
    gradient = sum(term.astype(WIDE) for term in terms)
    values = rows_ref[...].astype(WIDE)
    centered = values - jnp.mean(values, 1, keepdims=True)
    inverse = lax.rsqrt(jnp.mean(centered * centered, 1, keepdims=True) + 1e-05)
    unit = centered * inverse
    scaled = gradient * gain_ref[...]
    out = grad_ref[...].astype(WIDE) + inverse * (
        scaled
        - jnp.mean(scaled, 1, keepdims=True)
        - unit * jnp.mean(scaled * unit, 1, keepdims=True)
    )
    sums = [jnp.sum(gradient * unit, 0, keepdims=True), jnp.sum(gradient, 0, keepdims=True)]
    if with_low:
        keep_ref, out_ref, low_ref, sum_ref = refs
        low = (keep_ref[...] * out).astype(LOW)
        low_ref[...] = low
        sums.append(jnp.sum(low.astype(WIDE), 0, keepdims=True))
    else:
        out_ref, sum_ref = refs
    out_ref[...] = out
    sums.append(jnp.zeros((sum_ref.shape[0] - len(sums), sum_ref.shape[1]), WIDE))
    add_up(sum_ref, jnp.concatenate(sums, 0))


def norm_back(parts, rows, grad, gain, keep=None):
    own, width = rows.shape
    step = own // 4
    flat = pl.BlockSpec((step, width), lambda i: (i, 0))
    sums = pl.BlockSpec((8, width), lambda i: (0, 0))
    if isinstance(parts, tuple):
        early = pl.BlockSpec((step, width), lambda i: (jnp.minimum(i, 1), 0))
        late = pl.BlockSpec((step, width), lambda i: (jnp.maximum(i - 2, 0), 0))
        in_specs, args = [flat, early, late, early, late], list(parts)
    else:
        in_specs = [pl.BlockSpec((parts.shape[0], step, width), lambda i: (0, i, 0))]
        args = [parts]
    count = len(args)
    in_specs += [flat, flat, pl.BlockSpec((1, width), lambda i: (0, 0))]
    args += [rows, grad, gain.reshape(1, width)]
    outs, specs = [struct((own, width), WIDE)], [flat]
    if keep is not None:
        in_specs.append(pl.BlockSpec((step, 1), lambda i: (i, 0)))
        args.append(keep)
        outs.append(struct((own, width), LOW))
        specs.append(flat)
    return call(
        partial(norm_back_body, count, keep is not None),
        tuple(outs + [struct((8, width), WIDE)]),
        (own // step,),
        in_specs,
        tuple(specs + [sums]),
        40 * own * width,
        6 * 2**20,
    )(*args)


def collect_vectors(vectors):
    flat = jnp.concatenate([v.reshape(-1) for v in vectors])
    return collect(flat.reshape(16, -1, 128), COLS)


def spread_vectors(part, sizes):
    flat = spread(part, COLS, 16).reshape(-1)
    pieces, start = [], 0
    for size in sizes:
        pieces.append(flat[start : start + size])
        start += size
    return pieces


def shards(
    tokens, cotangent, seq_lengths, exit_layers, layer_index,
    ln1_gain, ln1_shift, q_weight, q_bias, k_weight, v_weight, v_bias, out_weight, out_bias,
    ln2_gain, ln2_shift, up_weight, up_bias, down_weight, down_bias,
):
    seqs, own_rows, width = tokens.shape
    own = seqs * own_rows
    full_len = exit_layers.shape[1]
    x_at, y_at = lax.axis_index("x"), lax.axis_index("y")
    head_at = x_at * RING + y_at
    head_cols = q_weight.shape[1]
    ff_cols = up_weight.shape[1]

    positions = jnp.arange(full_len)
    live_all = (positions[None, :] < seq_lengths[:, None]) & (exit_layers > layer_index[0])
    live_counts = jnp.concatenate(
        [jnp.sum(live_all.astype(jnp.int32), 1), y_at.astype(jnp.int32).reshape(1)]
    )
    y_places, x_places = (
        [((at + apart) % RING).astype(jnp.int32) for apart in (0, RING - 1, 1, 2)]
        for at in (y_at, x_at)
    )
    places = jnp.stack(y_places + x_places)
    live_mine = lax.dynamic_slice_in_dim(live_all, head_at * own_rows, own_rows, 1)
    keep = live_mine.reshape(-1, 1).astype(WIDE)

    w_attn = gather_weight(
        jnp.concatenate([q_weight, k_weight, v_weight, out_weight], 1).astype(LOW)
    )
    w_ff = jnp.concatenate([up_weight, down_weight], 1).astype(LOW)

    inputs = tokens.astype(WIDE).reshape(own, width)
    norm1 = ring_gather(norm_rows(inputs, ln1_gain, ln1_shift))
    flat_cot = cotangent.reshape(own, width)
    g_ffn = (keep * flat_cot.astype(WIDE)).astype(LOW)
    norm1, w_ff = tie(norm1, [ring(w_ff, step, "x") for step in (0, 1, -1, 2)])
    w_ff = lax.all_gather(jnp.stack(w_ff), ROWS, axis=0)

    def mine(vector, cols):
        return lax.dynamic_index_in_dim(vector.reshape(RING, RING, cols), y_at, 1, False)

    bias = jnp.concatenate(
        [mine(q_bias, head_cols), jnp.zeros((RING, head_cols), WIDE), mine(v_bias, head_cols)], 1
    ).reshape(RING, 1, 3 * head_cols)
    qkv = qkv_project(norm1, w_attn, bias)
    rows5 = (RING, RING, seqs, own_rows)
    qkv, g_ffn = tie(qkv, g_ffn)
    qkv, near = tie(swap(qkv, "x").reshape(rows5 + (3 * head_cols,)), ring_near(g_ffn))
    heads, exact, logs = attend(live_counts, qkv, head_cols)
    heads, cot_rows = tie(
        swap(heads.reshape(RING, RING * own, head_cols), "x"), ring_far(near)
    )
    branch1 = ring_sum(out_project(heads, w_attn, 3, 4)) + out_bias
    middle = inputs + keep * branch1
    normed2, cot_rows = tie(norm_rows(middle, ln2_gain, ln2_shift), cot_rows)
    near = ring_near(normed2)
    near[2], near[5], g_hidden = tie(near[2], near[5], hidden_grad(cot_rows, w_ff))
    norm2 = ring_far(near)

    ff_bias = mine(up_bias, ff_cols).reshape(RING, 1, ff_cols)
    hidden, grad_up, g_norm2, up_bias_part = ffn_first(places, norm2, g_hidden, w_ff, ff_bias)
    g_norm2 = swap(g_norm2.reshape(RING, own, width), "y")
    g_norm2, branch2, ff_grad = tie(
        g_norm2, *ffn_second(norm2, cot_rows, hidden, grad_up, w_ff)
    )
    ff_grad = settle(ff_grad)
    grad_mid, g_attn, sums2 = norm_back(g_norm2, middle, flat_cot, ln2_gain, keep)
    attn_rows = ring_gather(g_attn)
    g_heads = heads_grad(attn_rows, w_attn, head_cols, 3)
    g_heads, branch2 = tie(swap(g_heads, "x").reshape(rows5 + (head_cols,)), branch2)
    branch2 = ring_terms(branch2.reshape(RING, own, width), "y")
    d_qkv, d_sums = attend_back(live_counts, qkv, g_heads, exact, logs)
    d_qkv, attn_rows = tie(d_qkv, attn_rows)
    attn_grad = weight_grads(attn_rows, heads, 4 * head_cols, 3)
    d_qkv = swap(d_qkv.reshape(RING, RING * own, 3 * head_cols), "x")

    up_bias_full = lax.dynamic_update_slice_in_dim(
        jnp.zeros((RING, RING, ff_cols), WIDE), up_bias_part.reshape(RING, 1, ff_cols), y_at, 1
    )
    early = (
        sums2[2],
        sums2[0],
        sums2[1],
        up_bias_full,
        jnp.sum(g_ffn.astype(WIDE), 0),
    )
    d_qkv, attn_grad, branch2 = tie(d_qkv, attn_grad, branch2)
    attn_grad = weight_grads(norm1, d_qkv, 4 * head_cols, 0, attn_grad)
    d_qkv, attn_grad = tie(d_qkv, attn_grad)
    attn_grad = settle(attn_grad)
    g_norm1, ff_grad = ring_sum_parts(out_project(d_qkv, w_attn, 0, 2), ff_grad)
    ff_grad = ring_collect(ff_grad, "x")
    grad_tokens, sums1 = norm_back(g_norm1, tokens.reshape(own, width), grad_mid, ln1_gain)
    grad_tokens = grad_tokens.reshape(tokens.shape)
    sums1, branch2 = tie(sums1, branch2)
    branch2 = sum(term.astype(WIDE) for term in branch2) + down_bias
    result = (middle + keep * branch2).astype(LOW).reshape(tokens.shape)
    d_sums = jnp.sum(d_sums, 0).reshape(3, head_cols)

    def placed(row):
        blank = jnp.zeros((RING * RING, head_cols), WIDE)
        return lax.dynamic_update_slice_in_dim(blank, row[None], head_at, 0)

    part = collect_vectors(early + (sums1[0], sums1[1], placed(d_sums[0]), placed(d_sums[2])))
    part, ff_grad = tie(part, ff_grad)
    part, attn_grad = tie(jnp.sum(spread(part, ROWS, 8), 0), attn_grad)
    here = [lax.dynamic_index_in_dim(attn_grad, x_places[i], 0, False) for i in range(RING)]
    attn_grad = ring_collect(here, "x")
    sizes = (width, width, width, RING * RING * ff_cols) + (width,) * 5
    totals = spread_vectors(part, sizes)
    out_bias_sum, ln2_gain_sum, ln2_shift_sum, up_bias_sum, down_bias_sum = totals[:5]
    ln1_gain_sum, ln1_shift_sum, q_bias_sum, v_bias_sum = totals[5:]
    return (
        result,
        grad_tokens,
        ln1_gain_sum,
        ln1_shift_sum,
        attn_grad[:, :head_cols],
        q_bias_sum,
        attn_grad[:, head_cols : 2 * head_cols],
        attn_grad[:, 2 * head_cols : 3 * head_cols],
        v_bias_sum,
        attn_grad[:, 3 * head_cols :],
        out_bias_sum,
        ln2_gain_sum,
        ln2_shift_sum,
        ff_grad[:, :ff_cols],
        up_bias_sum,
        ff_grad[:, ff_cols:],
        down_bias_sum,
    )


def solution(mesh):
    wide = Mesh(mesh.devices.reshape(4, 2, 4, 4), ("z", "c", "x", "y"))
    act = P(ROWS, COLS, None)
    weight = P(ROWS, COLS)
    vector = P()
    in_specs = (
        act, act, P(ROWS), P(ROWS, None), vector, vector, vector,
        weight, vector, weight, weight, vector, weight, vector, vector, vector,
        weight, vector, weight, vector,
    )
    out_specs = (
        act, act, vector, vector, weight, vector, weight, weight, vector, weight,
        vector, vector, vector, weight, vector, weight, vector,
    )
    return jax.shard_map(
        shards, mesh=wide, in_specs=in_specs, out_specs=out_specs, check_vma=False
    )
```

```python
from functools import partial

import jax
import jax.numpy as jnp
from jax import lax
from jax.experimental import pallas as pl
from jax.experimental.pallas import tpu as pltpu
from jax.sharding import Mesh
from jax.sharding import PartitionSpec as P

HEAD_DIM = 64
SPAN = 256
LOW = jnp.bfloat16
WIDE = jnp.float32
RING = 4
ROWS = ("z", "c")
COLS = ("x", "y")


def dot(left, right):
    return jnp.dot(left, right, preferred_element_type=WIDE)


def dot_t(left, right):
    return lax.dot_general(left, right, (((1,), (1,)), ((), ())), preferred_element_type=WIDE)


def dot_0(left, right):
    return lax.dot_general(left, right, (((0,), (0,)), ((), ())), preferred_element_type=WIDE)


def call(body, out_shape, grid, in_specs, out_specs, flops, traffic, scratch=(), prefetch=0, vmem=40, aliases=None):
    return pl.pallas_call(
        body,
        out_shape=out_shape,
        grid_spec=pltpu.PrefetchScalarGridSpec(
            num_scalar_prefetch=prefetch,
            grid=grid,
            in_specs=in_specs,
            out_specs=out_specs,
            scratch_shapes=list(scratch),
        ),
        compiler_params=pltpu.CompilerParams(vmem_limit_bytes=vmem * 2**20),
        input_output_aliases=aliases or {},
        cost_estimate=pl.CostEstimate(flops=flops, bytes_accessed=traffic, transcendentals=0),
    )


def whole(shape):
    return pl.BlockSpec(shape, lambda *_: (0,) * len(shape))


def struct(shape, dtype):
    return jax.ShapeDtypeStruct(shape, dtype)


def spread(array, axes, size):
    return lax.all_to_all(jnp.broadcast_to(array[None], (size,) + array.shape), axes, 0, 0)


def collect(parts, axes):
    return jnp.sum(lax.all_to_all(parts, axes, 0, 0).astype(WIDE), 0)


def swap(parts, axes):
    return lax.all_to_all(parts, axes, 0, 0)


def ring(array, step, axis="y"):
    if step == 0:
        return array
    return lax.ppermute(array, axis, [(i, (i + step) % RING) for i in range(RING)])


def ring_terms(parts, axis):
    return [parts[0]] + [ring(parts[slot], step, axis) for slot, step in ((1, -1), (2, 1), (3, 2))]


def ring_collect(parts, axis):
    return sum(term.astype(WIDE) for term in ring_terms(parts, axis))


def ring_gather_two(left, right, beside):
    left_before, right_after = ring(left, 1), ring(right, -1)
    right_before, left_after = ring(right, 1), ring(left, -1)
    left_before, right_after, right_before, left_after, beside = tie(
        left_before, right_after, right_before, left_after, beside
    )
    left_across, right_across = ring(left_before, 1), ring(right_after, -1)
    return (
        jnp.concatenate([left, left_before, left_after, left_across], 0),
        jnp.concatenate([right, right_before, right_after, right_across], 0),
        beside,
    )


def ring_gather(rows):
    half = rows.shape[0] // 2
    first, second = rows[:half], rows[half:]
    before_first, after_second = ring(first, 1), ring(second, -1)
    before_second, after_first = ring(second, 1), ring(first, -1)
    across_first, across_second = ring(before_first, 1), ring(after_second, -1)
    return jnp.concatenate(
        [
            first, second, before_first, before_second,
            after_first, after_second, across_first, across_second,
        ],
        0,
    )


def ring_sum_parts(rows, later=None):
    own = rows.shape[0] // RING
    half = own // 2
    start, before, after, across = (rows[i * own : (i + 1) * own] for i in range(RING))
    from_before, from_after = ring(across[:half], 1), ring(across[half:], -1)
    second_after, first_before = ring(after[half:], 1), ring(before[:half], -1)
    if later is not None:
        from_before, from_after, second_after, first_before, later = tie(
            from_before, from_after, second_after, first_before, later
        )
    first_after = ring((after[:half].astype(WIDE) + from_before.astype(WIDE)).astype(LOW), 1)
    second_before = ring((before[half:].astype(WIDE) + from_after.astype(WIDE)).astype(LOW), -1)
    came = (start, first_after, second_after, first_before, second_before)
    return came if later is None else (came, later)


def ring_sum(rows):
    start, first_after, second_after, first_before, second_before = ring_sum_parts(rows)
    half = first_after.shape[0]
    first = start[:half].astype(WIDE) + first_after.astype(WIDE) + first_before.astype(WIDE)
    second = start[half:].astype(WIDE) + second_after.astype(WIDE) + second_before.astype(WIDE)
    return jnp.concatenate([first, second], 0)


def tie(*arrays):
    return lax.optimization_barrier(arrays)


def gather_weight(shard):
    full = lax.all_gather(shard, ("z", "c", "x"), axis=0)
    return full.reshape((8, 4) + shard.shape)


def settle(gradient):
    return lax.psum_scatter(gradient, ROWS, scatter_dimension=0)


def qkv_body(rows_ref, weight_ref, bias_ref, out_ref):
    weight = weight_ref[...].reshape(rows_ref.shape[1], -1)
    out_ref[...] = (dot(rows_ref[...], weight) + bias_ref[...]).astype(LOW)


def qkv_project(rows, weight, bias):
    count, width = rows.shape
    zc, xs, piece, _ = weight.shape
    cols = bias.shape[-1]
    return call(
        qkv_body,
        struct((xs, count, cols), LOW),
        (xs,),
        [
            whole((count, width)),
            pl.BlockSpec((zc, None, piece, cols), lambda i: (0, i, 0, 0)),
            pl.BlockSpec((None, 1, cols), lambda i: (i, 0, 0)),
        ],
        pl.BlockSpec((None, count, cols), lambda i: (i, 0, 0)),
        2 * count * width * xs * cols,
        10 * 2**20,
        vmem=60,
    )(rows, weight, bias)


def out_body(heads_ref, weight_ref, out_ref):
    count, _, piece, _ = weight_ref.shape
    for block in range(count):
        value = dot_t(heads_ref[0], weight_ref[block, 0])
        for x in range(1, RING):
            value += dot_t(heads_ref[x], weight_ref[block, x])
        out_ref[:, block * piece : (block + 1) * piece] = value.astype(LOW)


def store_rows(out_ref, place_ref, value):
    rows = value.shape[0] // RING
    for slot in range(RING):
        at = pl.multiple_of(place_ref[slot] * rows, rows)
        out_ref[pl.ds(at, rows)] = value[slot * rows : (slot + 1) * rows]


def out_project(heads, weight, at, blocks):
    xs, count, cols = heads.shape
    zc, _, piece, _ = weight.shape
    return call(
        out_body,
        struct((count, zc * piece), LOW),
        (zc // blocks,),
        [
            whole(heads.shape),
            pl.BlockSpec((blocks, xs, piece, cols), lambda i: (i, 0, 0, at)),
        ],
        pl.BlockSpec((count, blocks * piece), lambda i: (0, i)),
        2 * count * zc * piece * xs * cols,
        5 * 2**20,
        vmem=60,
    )(heads, weight)


def heads_grad_body(rows_ref, weight_ref, out_ref):
    cols = out_ref.shape[2]
    for x in range(0, RING, 2):
        pair = [weight_ref[:, x + i].reshape(rows_ref.shape[1], cols) for i in range(2)]
        value = dot(rows_ref[...], jnp.concatenate(pair, 1)).astype(LOW)
        out_ref[x] = value[:, :cols]
        out_ref[x + 1] = value[:, cols:]


def heads_grad(rows, weight, cols, at):
    count, width = rows.shape
    zc, xs, piece, _ = weight.shape
    return call(
        heads_grad_body,
        struct((xs, count, cols), LOW),
        (1,),
        [
            whole((count, width)),
            pl.BlockSpec((zc, xs, piece, cols), lambda i: (0, 0, 0, at)),
        ],
        whole((xs, count, cols)),
        2 * count * width * xs * cols,
        5 * 2**20,
        vmem=60,
    )(rows, weight)


def weight_grad_body(rows_ref, grad_ref, *refs):
    out_ref = refs[-1]
    out_ref[...] = dot_0(rows_ref[...], grad_ref[...]).astype(LOW).reshape(out_ref.shape)


def weight_grads(rows, columns, total_cols, at, onto=None):
    count, width = rows.shape
    xs, _, cols = columns.shape
    piece = width // 8
    more = () if onto is None else (onto,)
    return call(
        weight_grad_body,
        struct((8, xs, piece, total_cols), LOW),
        (xs,),
        [whole((count, width)), pl.BlockSpec((None, count, cols), lambda i: (i, 0, 0))]
        + [pl.BlockSpec(memory_space=pl.ANY)] * len(more),
        pl.BlockSpec((8, None, piece, cols), lambda i: (0, i, 0, at)),
        2 * count * width * xs * cols,
        15 * 2**20,
        vmem=60,
        aliases={2: 0} if more else None,
    )(rows, columns, *more)


def add_up(total, term):
    @pl.when(pl.program_id(0) == 0)
    def _():
        total[...] = term

    @pl.when(pl.program_id(0) > 0)
    def _():
        total[...] += term


def ffn_first_body(
    place_ref, norm_ref, cot_ref, up_ref, down_ref, bias_ref,
    hidden_ref, grad_up_ref, norm_grad_ref, bias_grad_ref, total,
):
    width, cols = norm_ref.shape[1], up_ref.shape[-1]
    up_w = up_ref[...].reshape(width, cols)
    up = dot(norm_ref[...], up_w) + bias_ref[...]
    normal = 0.5 * (1.0 + lax.erf(up * 0.7071067811865476))
    hidden_ref[...] = (up * normal).astype(LOW)
    slope = normal + up * (jnp.exp(-0.5 * up * up) * 0.3989422804014327)
    grad_up = (dot(cot_ref[...], down_ref[...].reshape(width, cols)) * slope).astype(LOW)
    grad_up_ref[...] = grad_up
    bias_grad_ref[...] = jnp.sum(grad_up.astype(WIDE), 0, keepdims=True)
    add_up(total, dot_t(grad_up, up_w))

    @pl.when(pl.program_id(0) == pl.num_programs(0) - 1)
    def _():
        store_rows(norm_grad_ref, place_ref, total[...].astype(LOW))


def ffn_first(places, norm_rows, cot_rows, weight, bias):
    count, width = norm_rows.shape
    zc, xs, piece, cols = weight.shape
    size = cols // 2
    rows = whole((count, width))
    vector = pl.BlockSpec((None, 1, size), lambda i, places: (places[RING + i], 0, 0))
    wide = pl.BlockSpec((count, size), lambda i, *_: (0, i))
    return call(
        ffn_first_body,
        (
            struct((count, xs * size), LOW),
            struct((count, xs * size), LOW),
            struct((count, width), LOW),
            struct((xs, 1, size), WIDE),
        ),
        (xs,),
        [
            rows,
            rows,
            pl.BlockSpec((zc, None, piece, size), lambda i, *_: (0, i, 0, 0)),
            pl.BlockSpec((zc, None, piece, size), lambda i, *_: (0, i, 0, 1)),
            vector,
        ],
        (wide, wide, rows, vector),
        6 * count * width * xs * size,
        25 * 2**20,
        scratch=[pltpu.VMEM((count, width), WIDE)],
        prefetch=1,
        vmem=56,
    )(places, norm_rows, cot_rows, weight, weight, bias)


def ffn_second_body(
    norm_ref, cot_ref, hidden_ref, grad_up_ref, down_ref, branch_ref, weight_grad_ref, total
):
    width, cols = norm_ref.shape[1], down_ref.shape[-1]
    zc, piece, _ = weight_grad_ref.shape
    hidden = hidden_ref[...]
    weight_grad_ref[:, :, :cols] = (
        dot_0(norm_ref[...], grad_up_ref[...]).astype(LOW).reshape(zc, piece, cols)
    )
    weight_grad_ref[:, :, cols:] = dot_0(cot_ref[...], hidden).astype(LOW).reshape(zc, piece, cols)
    add_up(total, dot_t(hidden, down_ref[...].reshape(width, cols)))

    @pl.when(pl.program_id(0) == pl.num_programs(0) - 1)
    def _():
        branch_ref[...] = total[...].astype(LOW)


def ffn_second(norm_rows, cot_rows, hidden, grad_up, weight):
    count, width = norm_rows.shape
    zc, xs, piece, cols = weight.shape
    size = cols // 2
    rows = whole((count, width))
    wide = pl.BlockSpec((count, size), lambda i: (0, i))
    return call(
        ffn_second_body,
        (struct((count, width), LOW), struct(weight.shape, LOW)),
        (xs,),
        [rows, rows, wide, wide, pl.BlockSpec((zc, None, piece, size), lambda i: (0, i, 0, 1))],
        (rows, pl.BlockSpec((zc, None, piece, cols), lambda i: (0, i, 0, 0))),
        6 * count * width * xs * size,
        40 * 2**20,
        scratch=[pltpu.VMEM((count, width), WIDE)],
        vmem=56,
    )(norm_rows, cot_rows, hidden, grad_up, weight)


def only_head(array, head):
    lane = lax.broadcasted_iota(jnp.int32, array.shape, 1)
    return jnp.where(lane // HEAD_DIM == head, array, jnp.zeros_like(array))


def allowed_keys(start, extent, live_count):
    q_place = start + lax.broadcasted_iota(jnp.int32, (SPAN, extent), 0)
    k_place = lax.broadcasted_iota(jnp.int32, (SPAN, extent), 1)
    return k_place <= jnp.minimum(q_place, live_count - 1)


def slot_of(place, own):
    apart = (place - own + RING) % RING
    return jnp.where(apart == 0, 0, jnp.where(apart == RING - 1, 1, apart + 1))


def load_ordered(blocks_ref, own, into):
    rows = blocks_ref.shape[2]
    for x in range(RING):
        for y in range(RING):
            at = (x * RING + y) * rows
            into[at : at + rows] = blocks_ref[x, slot_of(y, own)]


def store_ordered(blocks_ref, x, own, cols, value):
    rows = blocks_ref.shape[2]
    for y in range(RING):
        blocks_ref[x, slot_of(y, own), :, cols] = value[y * rows : (y + 1) * rows]


def attend_body(live_ref, qkv_ref, heads_ref, exact_ref, log_ref, qkv):
    live_count = live_ref[pl.program_id(0)]
    own = live_ref[pl.num_programs(0)]
    length = exact_ref.shape[0]
    width = exact_ref.shape[1]
    load_ordered(qkv_ref, own, qkv)
    key = qkv[:, width : 2 * width]
    value = qkv[:, 2 * width :]
    for span in range(length // SPAN):
        start, extent = span * SPAN, (span + 1) * SPAN
        here = slice(start, extent)

        @pl.when(start < live_count)
        def _():
            query = qkv[here, :width]
            allowed = allowed_keys(start, extent, live_count)
            mixed, logs = [], []
            for head in range(width // HEAD_DIM):
                scores = dot_t(only_head(query, head), key[:extent]) * HEAD_DIM**-0.5
                scores = jnp.where(allowed, scores, -1e9)
                top = jnp.max(scores, 1, keepdims=True)
                terms = jnp.exp(scores - top)
                denom = jnp.sum(terms, 1, keepdims=True)
                mixed.append(dot(terms.astype(LOW), value[:extent]) / denom)
                logs.append(top + jnp.log(denom))
            lane = lax.broadcasted_iota(jnp.int32, (SPAN, width), 1)
            out = jnp.where(lane < HEAD_DIM, mixed[0], mixed[1])
            exact_ref[here] = out
            log_ref[here] = jnp.where(lane < HEAD_DIM, logs[0], logs[1])
            store_ordered(heads_ref, span, own, slice(None), out.astype(LOW))

        @pl.when(start >= live_count)
        def _():
            exact_ref[here] = jnp.zeros((SPAN, width), WIDE)
            log_ref[here] = jnp.zeros((SPAN, width), WIDE)
            heads_ref[span] = jnp.zeros(heads_ref.shape[1:], LOW)


def row_block(rows, cols):
    return pl.BlockSpec((4, 4, None, rows, cols), lambda s, *_: (0, 0, s, 0, 0))


def attend(live_counts, qkv, width):
    xs, ys, seqs, rows, _ = qkv.shape
    length = xs * ys * rows
    flat = pl.BlockSpec((None, length, width), lambda s, *_: (s, 0, 0))
    return call(
        attend_body,
        (
            struct((xs, ys, seqs, rows, width), LOW),
            struct((seqs, length, width), WIDE),
            struct((seqs, length, width), WIDE),
        ),
        (seqs,),
        [row_block(rows, 3 * width)],
        (row_block(rows, width), flat, flat),
        4 * 10**9,
        4 * 2**20,
        scratch=[pltpu.VMEM((length, 3 * width), LOW)],
        prefetch=1,
    )(live_counts, qkv)


def attend_back_body(
    live_ref, qkv_ref, grad_ref, exact_ref, log_ref, out_ref, sum_ref,
    key_total, value_total, qkv, grads,
):
    live_count = live_ref[pl.program_id(0)]
    own = live_ref[pl.num_programs(0)]
    length, width = exact_ref.shape
    factor = HEAD_DIM**-0.5
    load_ordered(qkv_ref, own, qkv)
    load_ordered(grad_ref, own, grads)
    key = qkv[:, width : 2 * width]
    value = qkv[:, 2 * width :]
    key_total[...] = jnp.zeros_like(key_total)
    value_total[...] = jnp.zeros_like(value_total)
    sum_ref[...] = jnp.zeros_like(sum_ref)
    for span in range(length // SPAN):
        start, extent = span * SPAN, (span + 1) * SPAN
        here = slice(start, extent)

        @pl.when(start < live_count)
        def _():
            query = qkv[here, :width]
            grad = grads[here]
            inner = grad.astype(WIDE) * exact_ref[here]
            logs = log_ref[here]
            allowed = allowed_keys(start, extent, live_count)
            query_total = jnp.zeros((SPAN, width), WIDE)
            for head in range(width // HEAD_DIM):
                query_h = only_head(query, head)
                grad_h = only_head(grad, head)
                log_h = logs[:, head * HEAD_DIM : head * HEAD_DIM + 1]
                row_inner = jnp.sum(only_head(inner, head), 1, keepdims=True)
                scores = dot_t(query_h, key[:extent]) * factor
                probs = jnp.exp(jnp.where(allowed, scores, -1e9) - log_h)
                d_probs = dot_t(grad_h, value[:extent])
                value_total[:extent] += dot_0(probs.astype(LOW), grad_h)
                d_scores = (probs * (d_probs - row_inner)).astype(LOW)
                query_total += dot(d_scores, only_head(key[:extent], head))
                key_total[:extent] += dot_0(d_scores, query_h)
            out = (query_total * factor).astype(LOW)
            store_ordered(out_ref, span, own, slice(0, width), out)
            sum_ref[:, :width] += jnp.sum(out.astype(WIDE), 0, keepdims=True)

        @pl.when(start >= live_count)
        def _():
            out_ref[span, :, :, :width] = jnp.zeros(out_ref.shape[1:3] + (width,), LOW)

    key_grad = (key_total[...] * factor).astype(LOW)
    value_grad = value_total[...].astype(LOW)
    for span in range(RING):
        here = slice(span * SPAN, (span + 1) * SPAN)
        store_ordered(out_ref, span, own, slice(width, 2 * width), key_grad[here])
        store_ordered(out_ref, span, own, slice(2 * width, None), value_grad[here])
    sum_ref[:, 2 * width :] = jnp.sum(value_grad.astype(WIDE), 0, keepdims=True)


def attend_back(live_counts, qkv, grads, exact, logs):
    xs, ys, seqs, rows, _ = qkv.shape
    _, length, width = exact.shape
    flat = pl.BlockSpec((None, length, width), lambda s, *_: (s, 0, 0))
    return call(
        attend_back_body,
        (struct(qkv.shape, LOW), struct((seqs, 1, 3 * width), WIDE)),
        (seqs,),
        [row_block(rows, 3 * width), row_block(rows, width), flat, flat],
        (
            row_block(rows, 3 * width),
            pl.BlockSpec((None, 1, 3 * width), lambda s, *_: (s, 0, 0)),
        ),
        8 * 10**9,
        8 * 2**20,
        scratch=[
            pltpu.VMEM((length, width), WIDE),
            pltpu.VMEM((length, width), WIDE),
            pltpu.VMEM((length, 3 * width), LOW),
            pltpu.VMEM((length, width), LOW),
        ],
        prefetch=1,
    )(live_counts, qkv, grads, exact, logs)


def norm_rows(values, gain_vec, shift_vec):
    centered = values - jnp.mean(values, -1, keepdims=True)
    inverse = lax.rsqrt(jnp.mean(centered * centered, -1, keepdims=True) + 1e-05)
    return (centered * inverse * gain_vec + shift_vec).astype(LOW)


def norm_back_body(count, with_low, *refs):
    parts, (rows_ref, grad_ref, gain_ref) = refs[:count], refs[count : count + 3]
    refs = refs[count + 3 :]
    if count == 1:
        terms = [parts[0][i] for i in range(parts[0].shape[0])]
    else:
        start, first_after, second_after, first_before, second_before = (p[...] for p in parts)
        early = pl.program_id(0) < pl.num_programs(0) // 2
        terms = [
            start,
            jnp.where(early, first_after, second_after),
            jnp.where(early, first_before, second_before),
        ]
    gradient = sum(term.astype(WIDE) for term in terms)
    values = rows_ref[...].astype(WIDE)
    centered = values - jnp.mean(values, 1, keepdims=True)
    inverse = lax.rsqrt(jnp.mean(centered * centered, 1, keepdims=True) + 1e-05)
    unit = centered * inverse
    scaled = gradient * gain_ref[...]
    out = grad_ref[...].astype(WIDE) + inverse * (
        scaled
        - jnp.mean(scaled, 1, keepdims=True)
        - unit * jnp.mean(scaled * unit, 1, keepdims=True)
    )
    sums = [jnp.sum(gradient * unit, 0, keepdims=True), jnp.sum(gradient, 0, keepdims=True)]
    if with_low:
        keep_ref, out_ref, low_ref, sum_ref = refs
        low = (keep_ref[...] * out).astype(LOW)
        low_ref[...] = low
        sums.append(jnp.sum(low.astype(WIDE), 0, keepdims=True))
    else:
        out_ref, sum_ref = refs
    out_ref[...] = out
    sums.append(jnp.zeros((sum_ref.shape[0] - len(sums), sum_ref.shape[1]), WIDE))
    add_up(sum_ref, jnp.concatenate(sums, 0))


def norm_back(parts, rows, grad, gain, keep=None):
    own, width = rows.shape
    step = own // 4
    flat = pl.BlockSpec((step, width), lambda i: (i, 0))
    sums = pl.BlockSpec((8, width), lambda i: (0, 0))
    if isinstance(parts, tuple):
        early = pl.BlockSpec((step, width), lambda i: (jnp.minimum(i, 1), 0))
        late = pl.BlockSpec((step, width), lambda i: (jnp.maximum(i - 2, 0), 0))
        in_specs, args = [flat, early, late, early, late], list(parts)
    else:
        in_specs = [pl.BlockSpec((parts.shape[0], step, width), lambda i: (0, i, 0))]
        args = [parts]
    count = len(args)
    in_specs += [flat, flat, pl.BlockSpec((1, width), lambda i: (0, 0))]
    args += [rows, grad, gain.reshape(1, width)]
    outs, specs = [struct((own, width), WIDE)], [flat]
    if keep is not None:
        in_specs.append(pl.BlockSpec((step, 1), lambda i: (i, 0)))
        args.append(keep)
        outs.append(struct((own, width), LOW))
        specs.append(flat)
    return call(
        partial(norm_back_body, count, keep is not None),
        tuple(outs + [struct((8, width), WIDE)]),
        (own // step,),
        in_specs,
        tuple(specs + [sums]),
        40 * own * width,
        6 * 2**20,
    )(*args)


def collect_vectors(vectors):
    flat = jnp.concatenate([v.reshape(-1) for v in vectors])
    return collect(flat.reshape(16, -1, 128), COLS)


def spread_vectors(part, sizes):
    flat = spread(jnp.sum(spread(part, ROWS, 8), 0), COLS, 16).reshape(-1)
    pieces, start = [], 0
    for size in sizes:
        pieces.append(flat[start : start + size])
        start += size
    return pieces


def shards(
    tokens, cotangent, seq_lengths, exit_layers, layer_index,
    ln1_gain, ln1_shift, q_weight, q_bias, k_weight, v_weight, v_bias, out_weight, out_bias,
    ln2_gain, ln2_shift, up_weight, up_bias, down_weight, down_bias,
):
    seqs, own_rows, width = tokens.shape
    own = seqs * own_rows
    full_len = exit_layers.shape[1]
    x_at, y_at = lax.axis_index("x"), lax.axis_index("y")
    head_at = x_at * RING + y_at
    head_cols = q_weight.shape[1]
    ff_cols = up_weight.shape[1]

    positions = jnp.arange(full_len)
    live_all = (positions[None, :] < seq_lengths[:, None]) & (exit_layers > layer_index[0])
    live_counts = jnp.concatenate(
        [jnp.sum(live_all.astype(jnp.int32), 1), y_at.astype(jnp.int32).reshape(1)]
    )
    y_places, x_places = (
        [((at + apart) % RING).astype(jnp.int32) for apart in (0, RING - 1, 1, 2)]
        for at in (y_at, x_at)
    )
    places = jnp.stack(y_places + x_places)
    live_mine = lax.dynamic_slice_in_dim(live_all, head_at * own_rows, own_rows, 1)
    keep = live_mine.reshape(-1, 1).astype(WIDE)

    w_attn = gather_weight(
        jnp.concatenate([q_weight, k_weight, v_weight, out_weight], 1).astype(LOW)
    )
    w_ff = jnp.concatenate([up_weight, down_weight], 1).astype(LOW)

    inputs = tokens.astype(WIDE).reshape(own, width)
    flat_cot = cotangent.reshape(own, width)
    g_ffn = (keep * flat_cot.astype(WIDE)).astype(LOW)
    norm1, cot_rows, w_ff = ring_gather_two(
        norm_rows(inputs, ln1_gain, ln1_shift),
        g_ffn,
        [ring(w_ff, step, "x") for step in (0, 1, -1, 2)],
    )
    norm1, cot_rows = tie(norm1, cot_rows)
    w_ff = lax.all_gather(jnp.stack(w_ff), ROWS, axis=0)

    def mine(vector, cols):
        return lax.dynamic_index_in_dim(vector.reshape(RING, RING, cols), y_at, 1, False)

    bias = jnp.concatenate(
        [mine(q_bias, head_cols), jnp.zeros((RING, head_cols), WIDE), mine(v_bias, head_cols)], 1
    ).reshape(RING, 1, 3 * head_cols)
    qkv = qkv_project(norm1, w_attn, bias)
    rows5 = (RING, RING, seqs, own_rows)
    qkv = swap(qkv, "x").reshape(rows5 + (3 * head_cols,))
    heads, exact, logs = attend(live_counts, qkv, head_cols)
    heads = swap(heads.reshape(RING, RING * own, head_cols), "x")
    branch1 = ring_sum(out_project(heads, w_attn, 3, 4)) + out_bias
    middle = inputs + keep * branch1
    norm2 = ring_gather(norm_rows(middle, ln2_gain, ln2_shift))

    ff_bias = mine(up_bias, ff_cols).reshape(RING, 1, ff_cols)
    hidden, grad_up, g_norm2, up_bias_part = ffn_first(places, norm2, cot_rows, w_ff, ff_bias)
    g_norm2 = swap(g_norm2.reshape(RING, own, width), "y")
    g_norm2, branch2, ff_grad = tie(
        g_norm2, *ffn_second(norm2, cot_rows, hidden, grad_up, w_ff)
    )
    ff_grad = settle(ff_grad)
    grad_mid, g_attn, sums2 = norm_back(g_norm2, middle, flat_cot, ln2_gain, keep)
    attn_rows = ring_gather(g_attn)
    g_heads = heads_grad(attn_rows, w_attn, head_cols, 3)
    g_heads, branch2 = tie(swap(g_heads, "x").reshape(rows5 + (head_cols,)), branch2)
    branch2 = ring_terms(branch2.reshape(RING, own, width), "y")
    d_qkv, d_sums = attend_back(live_counts, qkv, g_heads, exact, logs)
    d_qkv, attn_rows = tie(d_qkv, attn_rows)
    attn_grad = weight_grads(attn_rows, heads, 4 * head_cols, 3)
    d_qkv = swap(d_qkv.reshape(RING, RING * own, 3 * head_cols), "x")

    up_bias_full = lax.dynamic_update_slice_in_dim(
        jnp.zeros((RING, RING, ff_cols), WIDE), up_bias_part.reshape(RING, 1, ff_cols), y_at, 1
    )
    early = (
        sums2[2],
        sums2[0],
        sums2[1],
        up_bias_full,
        jnp.sum(g_ffn.astype(WIDE), 0),
    )
    d_qkv, attn_grad, branch2 = tie(d_qkv, attn_grad, branch2)
    attn_grad = weight_grads(norm1, d_qkv, 4 * head_cols, 0, attn_grad)
    d_qkv, attn_grad = tie(d_qkv, attn_grad)
    attn_grad = settle(attn_grad)
    g_norm1, ff_grad = ring_sum_parts(out_project(d_qkv, w_attn, 0, 2), ff_grad)
    ff_grad = ring_collect(ff_grad, "x")
    grad_tokens, sums1 = norm_back(g_norm1, tokens.reshape(own, width), grad_mid, ln1_gain)
    grad_tokens = grad_tokens.reshape(tokens.shape)
    sums1, branch2 = tie(sums1, branch2)
    branch2 = sum(term.astype(WIDE) for term in branch2) + down_bias
    result = (middle + keep * branch2).astype(LOW).reshape(tokens.shape)
    d_sums = jnp.sum(d_sums, 0).reshape(3, head_cols)

    def placed(row):
        blank = jnp.zeros((RING * RING, head_cols), WIDE)
        return lax.dynamic_update_slice_in_dim(blank, row[None], head_at, 0)

    part = collect_vectors(early + (sums1[0], sums1[1], placed(d_sums[0]), placed(d_sums[2])))
    part, attn_grad, ff_grad = tie(part, attn_grad, ff_grad)
    here = [lax.dynamic_index_in_dim(attn_grad, x_places[i], 0, False) for i in range(RING)]
    attn_grad = ring_collect(here, "x")
    sizes = (width, width, width, RING * RING * ff_cols) + (width,) * 5
    totals = spread_vectors(part, sizes)
    out_bias_sum, ln2_gain_sum, ln2_shift_sum, up_bias_sum, down_bias_sum = totals[:5]
    ln1_gain_sum, ln1_shift_sum, q_bias_sum, v_bias_sum = totals[5:]
    return (
        result,
        grad_tokens,
        ln1_gain_sum,
        ln1_shift_sum,
        attn_grad[:, :head_cols],
        q_bias_sum,
        attn_grad[:, head_cols : 2 * head_cols],
        attn_grad[:, 2 * head_cols : 3 * head_cols],
        v_bias_sum,
        attn_grad[:, 3 * head_cols :],
        out_bias_sum,
        ln2_gain_sum,
        ln2_shift_sum,
        ff_grad[:, :ff_cols],
        up_bias_sum,
        ff_grad[:, ff_cols:],
        down_bias_sum,
    )


def solution(mesh):
    wide = Mesh(mesh.devices.reshape(4, 2, 4, 4), ("z", "c", "x", "y"))
    act = P(ROWS, COLS, None)
    weight = P(ROWS, COLS)
    vector = P()
    in_specs = (
        act, act, P(ROWS), P(ROWS, None), vector, vector, vector,
        weight, vector, weight, weight, vector, weight, vector, vector, vector,
        weight, vector, weight, vector,
    )
    out_specs = (
        act, act, vector, vector, weight, vector, weight, weight, vector, weight,
        vector, vector, vector, weight, vector, weight, vector,
    )
    return jax.shard_map(
        shards, mesh=wide, in_specs=in_specs, out_specs=out_specs, check_vma=False
    )
```

```python
from functools import partial

import jax
import jax.numpy as jnp
from jax import lax
from jax.experimental import pallas as pl
from jax.experimental.pallas import tpu as pltpu
from jax.sharding import Mesh
from jax.sharding import PartitionSpec as P

HEAD_DIM = 64
SPAN = 256
LOW = jnp.bfloat16
WIDE = jnp.float32
RING = 4
ROWS = ("z", "c")
COLS = ("x", "y")


def dot(left, right):
    return jnp.dot(left, right, preferred_element_type=WIDE)


def dot_t(left, right):
    return lax.dot_general(left, right, (((1,), (1,)), ((), ())), preferred_element_type=WIDE)


def dot_0(left, right):
    return lax.dot_general(left, right, (((0,), (0,)), ((), ())), preferred_element_type=WIDE)


def call(body, out_shape, grid, in_specs, out_specs, flops, traffic, scratch=(), prefetch=0, vmem=40, aliases=None):
    return pl.pallas_call(
        body,
        out_shape=out_shape,
        grid_spec=pltpu.PrefetchScalarGridSpec(
            num_scalar_prefetch=prefetch,
            grid=grid,
            in_specs=in_specs,
            out_specs=out_specs,
            scratch_shapes=list(scratch),
        ),
        compiler_params=pltpu.CompilerParams(vmem_limit_bytes=vmem * 2**20),
        input_output_aliases=aliases or {},
        cost_estimate=pl.CostEstimate(flops=flops, bytes_accessed=traffic, transcendentals=0),
    )


def whole(shape):
    return pl.BlockSpec(shape, lambda *_: (0,) * len(shape))


def struct(shape, dtype):
    return jax.ShapeDtypeStruct(shape, dtype)


def spread(array, axes, size):
    return lax.all_to_all(jnp.broadcast_to(array[None], (size,) + array.shape), axes, 0, 0)


def collect(parts, axes):
    return jnp.sum(lax.all_to_all(parts, axes, 0, 0).astype(WIDE), 0)


def swap(parts, axes):
    return lax.all_to_all(parts, axes, 0, 0)


def ring(array, step, axis="y"):
    if step == 0:
        return array
    return lax.ppermute(array, axis, [(i, (i + step) % RING) for i in range(RING)])


def ring_terms(parts, axis):
    return [parts[0]] + [ring(parts[slot], step, axis) for slot, step in ((1, -1), (2, 1), (3, 2))]


def ring_collect(parts, axis):
    return sum(term.astype(WIDE) for term in ring_terms(parts, axis))


def ring_gather(rows):
    half = rows.shape[0] // 2
    first, second = rows[:half], rows[half:]
    before_first, after_second = ring(first, 1), ring(second, -1)
    before_second, after_first = ring(second, 1), ring(first, -1)
    across_first, across_second = ring(before_first, 1), ring(after_second, -1)
    return jnp.concatenate(
        [
            first, second, before_first, before_second,
            after_first, after_second, across_first, across_second,
        ],
        0,
    )


def ring_sum_parts(rows, later=None):
    own = rows.shape[0] // RING
    half = own // 2
    start, before, after, across = (rows[i * own : (i + 1) * own] for i in range(RING))
    from_before, from_after = ring(across[:half], 1), ring(across[half:], -1)
    second_after, first_before = ring(after[half:], 1), ring(before[:half], -1)
    if later is not None:
        from_before, from_after, second_after, first_before, later = tie(
            from_before, from_after, second_after, first_before, later
        )
    first_after = ring((after[:half].astype(WIDE) + from_before.astype(WIDE)).astype(LOW), 1)
    second_before = ring((before[half:].astype(WIDE) + from_after.astype(WIDE)).astype(LOW), -1)
    came = (start, first_after, second_after, first_before, second_before)
    return came if later is None else (came, later)


def tie(*arrays):
    return lax.optimization_barrier(arrays)


def gather_weight(shard):
    full = lax.all_gather(shard, ("z", "c", "x"), axis=0)
    return full.reshape((8, 4) + shard.shape)


def settle(gradient):
    return lax.psum_scatter(gradient, ROWS, scatter_dimension=0)


def qkv_body(rows_ref, weight_ref, bias_ref, out_ref):
    weight = weight_ref[...].reshape(rows_ref.shape[1], -1)
    out_ref[...] = (dot(rows_ref[...], weight) + bias_ref[...]).astype(LOW)


def qkv_project(rows, weight, bias):
    count, width = rows.shape
    zc, xs, piece, _ = weight.shape
    cols = bias.shape[-1]
    return call(
        qkv_body,
        struct((xs, count, cols), LOW),
        (xs,),
        [
            whole((count, width)),
            pl.BlockSpec((zc, None, piece, cols), lambda i: (0, i, 0, 0)),
            pl.BlockSpec((None, 1, cols), lambda i: (i, 0, 0)),
        ],
        pl.BlockSpec((None, count, cols), lambda i: (i, 0, 0)),
        2 * count * width * xs * cols,
        10 * 2**20,
        vmem=60,
    )(rows, weight, bias)


def out_body(heads_ref, weight_ref, out_ref):
    count, _, piece, _ = weight_ref.shape
    for block in range(count):
        value = dot_t(heads_ref[0], weight_ref[block, 0])
        for x in range(1, RING):
            value += dot_t(heads_ref[x], weight_ref[block, x])
        out_ref[:, block * piece : (block + 1) * piece] = value.astype(LOW)


def store_rows(out_ref, place_ref, value):
    rows = value.shape[0] // RING
    for slot in range(RING):
        at = pl.multiple_of(place_ref[slot] * rows, rows)
        out_ref[pl.ds(at, rows)] = value[slot * rows : (slot + 1) * rows]


def out_project(heads, weight, at, blocks):
    xs, count, cols = heads.shape
    zc, _, piece, _ = weight.shape
    return call(
        out_body,
        struct((count, zc * piece), LOW),
        (zc // blocks,),
        [
            whole(heads.shape),
            pl.BlockSpec((blocks, xs, piece, cols), lambda i: (i, 0, 0, at)),
        ],
        pl.BlockSpec((count, blocks * piece), lambda i: (0, i)),
        2 * count * zc * piece * xs * cols,
        5 * 2**20,
        vmem=60,
    )(heads, weight)


def heads_grad_body(rows_ref, weight_ref, out_ref):
    cols = out_ref.shape[2]
    for x in range(0, RING, 2):
        pair = [weight_ref[:, x + i].reshape(rows_ref.shape[1], cols) for i in range(2)]
        value = dot(rows_ref[...], jnp.concatenate(pair, 1)).astype(LOW)
        out_ref[x] = value[:, :cols]
        out_ref[x + 1] = value[:, cols:]


def heads_grad(rows, weight, cols, at):
    count, width = rows.shape
    zc, xs, piece, _ = weight.shape
    return call(
        heads_grad_body,
        struct((xs, count, cols), LOW),
        (1,),
        [
            whole((count, width)),
            pl.BlockSpec((zc, xs, piece, cols), lambda i: (0, 0, 0, at)),
        ],
        whole((xs, count, cols)),
        2 * count * width * xs * cols,
        5 * 2**20,
        vmem=60,
    )(rows, weight)


def weight_grad_body(rows_ref, grad_ref, *refs):
    out_ref = refs[-1]
    out_ref[...] = dot_0(rows_ref[...], grad_ref[...]).astype(LOW).reshape(out_ref.shape)


def weight_grads(rows, columns, total_cols, at, onto=None):
    count, width = rows.shape
    xs, _, cols = columns.shape
    piece = width // 8
    more = () if onto is None else (onto,)
    return call(
        weight_grad_body,
        struct((8, xs, piece, total_cols), LOW),
        (xs,),
        [whole((count, width)), pl.BlockSpec((None, count, cols), lambda i: (i, 0, 0))]
        + [pl.BlockSpec(memory_space=pl.ANY)] * len(more),
        pl.BlockSpec((8, None, piece, cols), lambda i: (0, i, 0, at)),
        2 * count * width * xs * cols,
        15 * 2**20,
        vmem=60,
        aliases={2: 0} if more else None,
    )(rows, columns, *more)


def add_up(total, term):
    @pl.when(pl.program_id(0) == 0)
    def _():
        total[...] = term

    @pl.when(pl.program_id(0) > 0)
    def _():
        total[...] += term


def ffn_first_body(
    place_ref, norm_ref, cot_ref, up_ref, down_ref, bias_ref,
    hidden_ref, grad_up_ref, norm_grad_ref, bias_grad_ref, total,
):
    width, cols = norm_ref.shape[1], up_ref.shape[-1]
    up_w = up_ref[...].reshape(width, cols)
    up = dot(norm_ref[...], up_w) + bias_ref[...]
    normal = 0.5 * (1.0 + lax.erf(up * 0.7071067811865476))
    hidden_ref[...] = (up * normal).astype(LOW)
    slope = normal + up * (jnp.exp(-0.5 * up * up) * 0.3989422804014327)
    grad_up = (dot(cot_ref[...], down_ref[...].reshape(width, cols)) * slope).astype(LOW)
    grad_up_ref[...] = grad_up
    bias_grad_ref[...] = jnp.sum(grad_up.astype(WIDE), 0, keepdims=True)
    add_up(total, dot_t(grad_up, up_w))

    @pl.when(pl.program_id(0) == pl.num_programs(0) - 1)
    def _():
        store_rows(norm_grad_ref, place_ref, total[...].astype(LOW))


def ffn_first(places, norm_rows, cot_rows, weight, bias):
    count, width = norm_rows.shape
    zc, xs, piece, cols = weight.shape
    size = cols // 2
    rows = whole((count, width))
    vector = pl.BlockSpec((None, 1, size), lambda i, places: (places[RING + i], 0, 0))
    wide = pl.BlockSpec((count, size), lambda i, *_: (0, i))
    return call(
        ffn_first_body,
        (
            struct((count, xs * size), LOW),
            struct((count, xs * size), LOW),
            struct((count, width), LOW),
            struct((xs, 1, size), WIDE),
        ),
        (xs,),
        [
            rows,
            rows,
            pl.BlockSpec((zc, None, piece, size), lambda i, *_: (0, i, 0, 0)),
            pl.BlockSpec((zc, None, piece, size), lambda i, *_: (0, i, 0, 1)),
            vector,
        ],
        (wide, wide, rows, vector),
        6 * count * width * xs * size,
        25 * 2**20,
        scratch=[pltpu.VMEM((count, width), WIDE)],
        prefetch=1,
        vmem=56,
    )(places, norm_rows, cot_rows, weight, weight, bias)


def ffn_second_body(
    norm_ref, cot_ref, hidden_ref, grad_up_ref, down_ref, branch_ref, weight_grad_ref, total
):
    width, cols = norm_ref.shape[1], down_ref.shape[-1]
    zc, piece, _ = weight_grad_ref.shape
    hidden = hidden_ref[...]
    weight_grad_ref[:, :, :cols] = (
        dot_0(norm_ref[...], grad_up_ref[...]).astype(LOW).reshape(zc, piece, cols)
    )
    weight_grad_ref[:, :, cols:] = dot_0(cot_ref[...], hidden).astype(LOW).reshape(zc, piece, cols)
    add_up(total, dot_t(hidden, down_ref[...].reshape(width, cols)))

    @pl.when(pl.program_id(0) == pl.num_programs(0) - 1)
    def _():
        branch_ref[...] = total[...].astype(LOW)


def ffn_second(norm_rows, cot_rows, hidden, grad_up, weight):
    count, width = norm_rows.shape
    zc, xs, piece, cols = weight.shape
    size = cols // 2
    rows = whole((count, width))
    wide = pl.BlockSpec((count, size), lambda i: (0, i))
    return call(
        ffn_second_body,
        (struct((count, width), LOW), struct(weight.shape, LOW)),
        (xs,),
        [rows, rows, wide, wide, pl.BlockSpec((zc, None, piece, size), lambda i: (0, i, 0, 1))],
        (rows, pl.BlockSpec((zc, None, piece, cols), lambda i: (0, i, 0, 0))),
        6 * count * width * xs * size,
        40 * 2**20,
        scratch=[pltpu.VMEM((count, width), WIDE)],
        vmem=56,
    )(norm_rows, cot_rows, hidden, grad_up, weight)


def only_head(array, head):
    lane = lax.broadcasted_iota(jnp.int32, array.shape, 1)
    return jnp.where(lane // HEAD_DIM == head, array, jnp.zeros_like(array))


def allowed_keys(start, extent, live_count):
    q_place = start + lax.broadcasted_iota(jnp.int32, (SPAN, extent), 0)
    k_place = lax.broadcasted_iota(jnp.int32, (SPAN, extent), 1)
    return k_place <= jnp.minimum(q_place, live_count - 1)


def slot_of(place, own):
    apart = (place - own + RING) % RING
    return jnp.where(apart == 0, 0, jnp.where(apart == RING - 1, 1, apart + 1))


def load_ordered(blocks_ref, own, into):
    rows = blocks_ref.shape[2]
    for x in range(RING):
        for y in range(RING):
            at = (x * RING + y) * rows
            into[at : at + rows] = blocks_ref[x, slot_of(y, own)]


def store_ordered(blocks_ref, x, own, cols, value):
    rows = blocks_ref.shape[2]
    for y in range(RING):
        blocks_ref[x, slot_of(y, own), :, cols] = value[y * rows : (y + 1) * rows]


def attend_body(live_ref, qkv_ref, heads_ref, exact_ref, log_ref, qkv):
    live_count = live_ref[pl.program_id(0)]
    own = live_ref[pl.num_programs(0)]
    length = exact_ref.shape[0]
    width = exact_ref.shape[1]
    load_ordered(qkv_ref, own, qkv)
    key = qkv[:, width : 2 * width]
    value = qkv[:, 2 * width :]
    for span in range(length // SPAN):
        start, extent = span * SPAN, (span + 1) * SPAN
        here = slice(start, extent)

        @pl.when(start < live_count)
        def _():
            query = qkv[here, :width]
            allowed = allowed_keys(start, extent, live_count)
            mixed, logs = [], []
            for head in range(width // HEAD_DIM):
                scores = dot_t(only_head(query, head), key[:extent]) * HEAD_DIM**-0.5
                scores = jnp.where(allowed, scores, -1e9)
                top = jnp.max(scores, 1, keepdims=True)
                terms = jnp.exp(scores - top)
                denom = jnp.sum(terms, 1, keepdims=True)
                mixed.append(dot(terms.astype(LOW), value[:extent]) / denom)
                logs.append(top + jnp.log(denom))
            lane = lax.broadcasted_iota(jnp.int32, (SPAN, width), 1)
            out = jnp.where(lane < HEAD_DIM, mixed[0], mixed[1])
            exact_ref[here] = out
            log_ref[here] = jnp.where(lane < HEAD_DIM, logs[0], logs[1])
            store_ordered(heads_ref, span, own, slice(None), out.astype(LOW))

        @pl.when(start >= live_count)
        def _():
            exact_ref[here] = jnp.zeros((SPAN, width), WIDE)
            log_ref[here] = jnp.zeros((SPAN, width), WIDE)
            heads_ref[span] = jnp.zeros(heads_ref.shape[1:], LOW)


def row_block(rows, cols):
    return pl.BlockSpec((4, 4, None, rows, cols), lambda s, *_: (0, 0, s, 0, 0))


def attend(live_counts, qkv, width):
    xs, ys, seqs, rows, _ = qkv.shape
    length = xs * ys * rows
    flat = pl.BlockSpec((None, length, width), lambda s, *_: (s, 0, 0))
    return call(
        attend_body,
        (
            struct((xs, ys, seqs, rows, width), LOW),
            struct((seqs, length, width), WIDE),
            struct((seqs, length, width), WIDE),
        ),
        (seqs,),
        [row_block(rows, 3 * width)],
        (row_block(rows, width), flat, flat),
        4 * 10**9,
        4 * 2**20,
        scratch=[pltpu.VMEM((length, 3 * width), LOW)],
        prefetch=1,
    )(live_counts, qkv)


def attend_back_body(
    live_ref, qkv_ref, grad_ref, exact_ref, log_ref, out_ref, sum_ref,
    key_total, value_total, qkv, grads,
):
    live_count = live_ref[pl.program_id(0)]
    own = live_ref[pl.num_programs(0)]
    length, width = exact_ref.shape
    factor = HEAD_DIM**-0.5
    load_ordered(qkv_ref, own, qkv)
    load_ordered(grad_ref, own, grads)
    key = qkv[:, width : 2 * width]
    value = qkv[:, 2 * width :]
    key_total[...] = jnp.zeros_like(key_total)
    value_total[...] = jnp.zeros_like(value_total)
    sum_ref[...] = jnp.zeros_like(sum_ref)
    for span in range(length // SPAN):
        start, extent = span * SPAN, (span + 1) * SPAN
        here = slice(start, extent)

        @pl.when(start < live_count)
        def _():
            query = qkv[here, :width]
            grad = grads[here]
            inner = grad.astype(WIDE) * exact_ref[here]
            logs = log_ref[here]
            allowed = allowed_keys(start, extent, live_count)
            query_total = jnp.zeros((SPAN, width), WIDE)
            for head in range(width // HEAD_DIM):
                query_h = only_head(query, head)
                grad_h = only_head(grad, head)
                log_h = logs[:, head * HEAD_DIM : head * HEAD_DIM + 1]
                row_inner = jnp.sum(only_head(inner, head), 1, keepdims=True)
                scores = dot_t(query_h, key[:extent]) * factor
                probs = jnp.exp(jnp.where(allowed, scores, -1e9) - log_h)
                d_probs = dot_t(grad_h, value[:extent])
                value_total[:extent] += dot_0(probs.astype(LOW), grad_h)
                d_scores = (probs * (d_probs - row_inner)).astype(LOW)
                query_total += dot(d_scores, only_head(key[:extent], head))
                key_total[:extent] += dot_0(d_scores, query_h)
            out = (query_total * factor).astype(LOW)
            store_ordered(out_ref, span, own, slice(0, width), out)
            sum_ref[:, :width] += jnp.sum(out.astype(WIDE), 0, keepdims=True)

        @pl.when(start >= live_count)
        def _():
            out_ref[span, :, :, :width] = jnp.zeros(out_ref.shape[1:3] + (width,), LOW)

    key_grad = (key_total[...] * factor).astype(LOW)
    value_grad = value_total[...].astype(LOW)
    for span in range(RING):
        here = slice(span * SPAN, (span + 1) * SPAN)
        store_ordered(out_ref, span, own, slice(width, 2 * width), key_grad[here])
        store_ordered(out_ref, span, own, slice(2 * width, None), value_grad[here])
    sum_ref[:, 2 * width :] = jnp.sum(value_grad.astype(WIDE), 0, keepdims=True)


def attend_back(live_counts, qkv, grads, exact, logs):
    xs, ys, seqs, rows, _ = qkv.shape
    _, length, width = exact.shape
    flat = pl.BlockSpec((None, length, width), lambda s, *_: (s, 0, 0))
    return call(
        attend_back_body,
        (struct(qkv.shape, LOW), struct((seqs, 1, 3 * width), WIDE)),
        (seqs,),
        [row_block(rows, 3 * width), row_block(rows, width), flat, flat],
        (
            row_block(rows, 3 * width),
            pl.BlockSpec((None, 1, 3 * width), lambda s, *_: (s, 0, 0)),
        ),
        8 * 10**9,
        8 * 2**20,
        scratch=[
            pltpu.VMEM((length, width), WIDE),
            pltpu.VMEM((length, width), WIDE),
            pltpu.VMEM((length, 3 * width), LOW),
            pltpu.VMEM((length, width), LOW),
        ],
        prefetch=1,
    )(live_counts, qkv, grads, exact, logs)


def norm_rows(values, gain_vec, shift_vec):
    centered = values - jnp.mean(values, -1, keepdims=True)
    inverse = lax.rsqrt(jnp.mean(centered * centered, -1, keepdims=True) + 1e-05)
    return (centered * inverse * gain_vec + shift_vec).astype(LOW)


def pick_half(first_ref, second_ref):
    early = pl.program_id(0) < pl.num_programs(0) // 2
    return jnp.where(early, first_ref[...], second_ref[...])


def half_blocks(step, width):
    early = pl.BlockSpec((step, width), lambda i: (jnp.minimum(i, 1), 0))
    late = pl.BlockSpec((step, width), lambda i: (jnp.maximum(i - 2, 0), 0))
    return [early, late]


def add_norm_body(
    start_ref, first_after, second_after, first_before, second_before,
    rows_ref, keep_ref, bias_ref, gain_ref, shift_ref, out_ref, norm_ref,
):
    branch = start_ref[...].astype(WIDE) + pick_half(first_after, second_after).astype(WIDE)
    branch += pick_half(first_before, second_before).astype(WIDE)
    values = rows_ref[...].astype(WIDE) + keep_ref[...] * (branch + bias_ref[...])
    out_ref[...] = values
    centered = values - jnp.mean(values, 1, keepdims=True)
    inverse = lax.rsqrt(jnp.mean(centered * centered, 1, keepdims=True) + 1e-05)
    norm_ref[...] = (centered * inverse * gain_ref[...] + shift_ref[...]).astype(LOW)


def add_norm(parts, rows, keep, bias, gain, shift):
    own, width = rows.shape
    step = own // 4
    flat = pl.BlockSpec((step, width), lambda i: (i, 0))
    vector = pl.BlockSpec((1, width), lambda i: (0, 0))
    halves = half_blocks(step, width) * 2
    return call(
        add_norm_body,
        (struct((own, width), WIDE), struct((own, width), LOW)),
        (own // step,),
        [flat] + halves + [flat, pl.BlockSpec((step, 1), lambda i: (i, 0)), vector, vector, vector],
        (flat, flat),
        20 * own * width,
        4 * 2**20,
    )(*parts, rows, keep, *(v.reshape(1, width) for v in (bias, gain, shift)))


def norm_back_body(count, with_low, *refs):
    parts, (rows_ref, grad_ref, gain_ref) = refs[:count], refs[count : count + 3]
    refs = refs[count + 3 :]
    if count == 1:
        terms = [parts[0][i] for i in range(parts[0].shape[0])]
    else:
        terms = [parts[0][...], pick_half(*parts[1:3]), pick_half(*parts[3:5])]
    gradient = sum(term.astype(WIDE) for term in terms)
    values = rows_ref[...].astype(WIDE)
    centered = values - jnp.mean(values, 1, keepdims=True)
    inverse = lax.rsqrt(jnp.mean(centered * centered, 1, keepdims=True) + 1e-05)
    unit = centered * inverse
    scaled = gradient * gain_ref[...]
    out = grad_ref[...].astype(WIDE) + inverse * (
        scaled
        - jnp.mean(scaled, 1, keepdims=True)
        - unit * jnp.mean(scaled * unit, 1, keepdims=True)
    )
    sums = [jnp.sum(gradient * unit, 0, keepdims=True), jnp.sum(gradient, 0, keepdims=True)]
    if with_low:
        keep_ref, out_ref, low_ref, sum_ref = refs
        low = (keep_ref[...] * out).astype(LOW)
        low_ref[...] = low
        sums.append(jnp.sum(low.astype(WIDE), 0, keepdims=True))
    else:
        out_ref, sum_ref = refs
    out_ref[...] = out
    sums.append(jnp.zeros((sum_ref.shape[0] - len(sums), sum_ref.shape[1]), WIDE))
    add_up(sum_ref, jnp.concatenate(sums, 0))


def norm_back(parts, rows, grad, gain, keep=None):
    own, width = rows.shape
    step = own // 4
    flat = pl.BlockSpec((step, width), lambda i: (i, 0))
    sums = pl.BlockSpec((8, width), lambda i: (0, 0))
    if isinstance(parts, tuple):
        in_specs, args = [flat] + half_blocks(step, width) * 2, list(parts)
    else:
        in_specs = [pl.BlockSpec((parts.shape[0], step, width), lambda i: (0, i, 0))]
        args = [parts]
    count = len(args)
    in_specs += [flat, flat, pl.BlockSpec((1, width), lambda i: (0, 0))]
    args += [rows, grad, gain.reshape(1, width)]
    outs, specs = [struct((own, width), WIDE)], [flat]
    if keep is not None:
        in_specs.append(pl.BlockSpec((step, 1), lambda i: (i, 0)))
        args.append(keep)
        outs.append(struct((own, width), LOW))
        specs.append(flat)
    return call(
        partial(norm_back_body, count, keep is not None),
        tuple(outs + [struct((8, width), WIDE)]),
        (own // step,),
        in_specs,
        tuple(specs + [sums]),
        40 * own * width,
        6 * 2**20,
    )(*args)


def collect_vectors(vectors):
    flat = jnp.concatenate([v.reshape(-1) for v in vectors])
    return collect(flat.reshape(16, -1, 128), COLS)


def spread_vectors(part, sizes):
    flat = spread(jnp.sum(spread(part, ROWS, 8), 0), COLS, 16).reshape(-1)
    pieces, start = [], 0
    for size in sizes:
        pieces.append(flat[start : start + size])
        start += size
    return pieces


def shards(
    tokens, cotangent, seq_lengths, exit_layers, layer_index,
    ln1_gain, ln1_shift, q_weight, q_bias, k_weight, v_weight, v_bias, out_weight, out_bias,
    ln2_gain, ln2_shift, up_weight, up_bias, down_weight, down_bias,
):
    seqs, own_rows, width = tokens.shape
    own = seqs * own_rows
    full_len = exit_layers.shape[1]
    x_at, y_at = lax.axis_index("x"), lax.axis_index("y")
    head_at = x_at * RING + y_at
    head_cols = q_weight.shape[1]
    ff_cols = up_weight.shape[1]

    positions = jnp.arange(full_len)
    live_all = (positions[None, :] < seq_lengths[:, None]) & (exit_layers > layer_index[0])
    live_counts = jnp.concatenate(
        [jnp.sum(live_all.astype(jnp.int32), 1), y_at.astype(jnp.int32).reshape(1)]
    )
    y_places, x_places = (
        [((at + apart) % RING).astype(jnp.int32) for apart in (0, RING - 1, 1, 2)]
        for at in (y_at, x_at)
    )
    places = jnp.stack(y_places + x_places)
    live_mine = lax.dynamic_slice_in_dim(live_all, head_at * own_rows, own_rows, 1)
    keep = live_mine.reshape(-1, 1).astype(WIDE)

    w_attn = gather_weight(
        jnp.concatenate([q_weight, k_weight, v_weight, out_weight], 1).astype(LOW)
    )
    w_ff = jnp.concatenate([up_weight, down_weight], 1).astype(LOW)

    inputs = tokens.astype(WIDE).reshape(own, width)
    flat_cot = cotangent.reshape(own, width)
    g_ffn = (keep * flat_cot.astype(WIDE)).astype(LOW)
    norm1 = ring_gather(norm_rows(inputs, ln1_gain, ln1_shift))
    norm1, w_ff = tie(norm1, [ring(w_ff, step, "x") for step in (0, 1, -1, 2)])
    w_ff = lax.all_gather(jnp.stack(w_ff), ROWS, axis=0)
    norm1, cot_rows = tie(norm1, ring_gather(g_ffn))

    def mine(vector, cols):
        return lax.dynamic_index_in_dim(vector.reshape(RING, RING, cols), y_at, 1, False)

    bias = jnp.concatenate(
        [mine(q_bias, head_cols), jnp.zeros((RING, head_cols), WIDE), mine(v_bias, head_cols)], 1
    ).reshape(RING, 1, 3 * head_cols)
    qkv = qkv_project(norm1, w_attn, bias)
    rows5 = (RING, RING, seqs, own_rows)
    qkv = swap(qkv, "x").reshape(rows5 + (3 * head_cols,))
    heads, exact, logs = attend(live_counts, qkv, head_cols)
    heads = swap(heads.reshape(RING, RING * own, head_cols), "x")
    middle, normed2 = add_norm(
        ring_sum_parts(out_project(heads, w_attn, 3, 4)),
        tokens.reshape(own, width), keep, out_bias, ln2_gain, ln2_shift,
    )
    norm2 = ring_gather(normed2)

    ff_bias = mine(up_bias, ff_cols).reshape(RING, 1, ff_cols)
    hidden, grad_up, g_norm2, up_bias_part = ffn_first(places, norm2, cot_rows, w_ff, ff_bias)
    g_norm2 = swap(g_norm2.reshape(RING, own, width), "y")
    g_norm2, branch2, ff_grad = tie(
        g_norm2, *ffn_second(norm2, cot_rows, hidden, grad_up, w_ff)
    )
    ff_grad = settle(ff_grad)
    grad_mid, g_attn, sums2 = norm_back(g_norm2, middle, flat_cot, ln2_gain, keep)
    attn_rows = ring_gather(g_attn)
    g_heads = heads_grad(attn_rows, w_attn, head_cols, 3)
    g_heads, branch2 = tie(swap(g_heads, "x").reshape(rows5 + (head_cols,)), branch2)
    branch2 = ring_terms(branch2.reshape(RING, own, width), "y")
    d_qkv, d_sums = attend_back(live_counts, qkv, g_heads, exact, logs)
    d_qkv, attn_rows = tie(d_qkv, attn_rows)
    attn_grad = weight_grads(attn_rows, heads, 4 * head_cols, 3)
    d_qkv = swap(d_qkv.reshape(RING, RING * own, 3 * head_cols), "x")

    up_bias_full = lax.dynamic_update_slice_in_dim(
        jnp.zeros((RING, RING, ff_cols), WIDE), up_bias_part.reshape(RING, 1, ff_cols), y_at, 1
    )
    early = (
        sums2[2],
        sums2[0],
        sums2[1],
        up_bias_full,
        jnp.sum(g_ffn.astype(WIDE), 0),
    )
    d_qkv, attn_grad, branch2 = tie(d_qkv, attn_grad, branch2)
    g_norm1, d_qkv = tie(out_project(d_qkv, w_attn, 0, 2), d_qkv)
    attn_grad = weight_grads(norm1, d_qkv, 4 * head_cols, 0, attn_grad)
    g_norm1, (ff_grad, attn_grad) = ring_sum_parts(g_norm1, (ff_grad, attn_grad))
    attn_grad = settle(attn_grad)
    ff_grad = ring_collect(ff_grad, "x")
    grad_tokens, sums1 = norm_back(g_norm1, tokens.reshape(own, width), grad_mid, ln1_gain)
    grad_tokens = grad_tokens.reshape(tokens.shape)
    sums1, branch2 = tie(sums1, branch2)
    branch2 = sum(term.astype(WIDE) for term in branch2) + down_bias
    result = (middle + keep * branch2).astype(LOW).reshape(tokens.shape)
    d_sums = jnp.sum(d_sums, 0).reshape(3, head_cols)

    def placed(row):
        blank = jnp.zeros((RING * RING, head_cols), WIDE)
        return lax.dynamic_update_slice_in_dim(blank, row[None], head_at, 0)

    part = collect_vectors(early + (sums1[0], sums1[1], placed(d_sums[0]), placed(d_sums[2])))
    part, ff_grad = tie(part, ff_grad)
    sizes = (width, width, width, RING * RING * ff_cols) + (width,) * 5
    totals, attn_grad = tie(spread_vectors(part, sizes), attn_grad)
    here = [lax.dynamic_index_in_dim(attn_grad, x_places[i], 0, False) for i in range(RING)]
    attn_grad = ring_collect(here, "x")
    out_bias_sum, ln2_gain_sum, ln2_shift_sum, up_bias_sum, down_bias_sum = totals[:5]
    ln1_gain_sum, ln1_shift_sum, q_bias_sum, v_bias_sum = totals[5:]
    return (
        result,
        grad_tokens,
        ln1_gain_sum,
        ln1_shift_sum,
        attn_grad[:, :head_cols],
        q_bias_sum,
        attn_grad[:, head_cols : 2 * head_cols],
        attn_grad[:, 2 * head_cols : 3 * head_cols],
        v_bias_sum,
        attn_grad[:, 3 * head_cols :],
        out_bias_sum,
        ln2_gain_sum,
        ln2_shift_sum,
        ff_grad[:, :ff_cols],
        up_bias_sum,
        ff_grad[:, ff_cols:],
        down_bias_sum,
    )


def solution(mesh):
    wide = Mesh(mesh.devices.reshape(4, 2, 4, 4), ("z", "c", "x", "y"))
    act = P(ROWS, COLS, None)
    weight = P(ROWS, COLS)
    vector = P()
    in_specs = (
        act, act, P(ROWS), P(ROWS, None), vector, vector, vector,
        weight, vector, weight, weight, vector, weight, vector, vector, vector,
        weight, vector, weight, vector,
    )
    out_specs = (
        act, act, vector, vector, weight, vector, weight, weight, vector, weight,
        vector, vector, vector, weight, vector, weight, vector,
    )
    return jax.shard_map(
        shards, mesh=wide, in_specs=in_specs, out_specs=out_specs, check_vma=False
    )
```

```python
from functools import partial

import jax
import jax.numpy as jnp
from jax import lax
from jax.experimental import pallas as pl
from jax.experimental.pallas import tpu as pltpu
from jax.sharding import Mesh
from jax.sharding import PartitionSpec as P

HEAD_DIM = 64
SPAN = 256
LOW = jnp.bfloat16
WIDE = jnp.float32
RING = 4
ROWS = ("z", "c")
COLS = ("x", "y")


def dot(left, right):
    return jnp.dot(left, right, preferred_element_type=WIDE)


def dot_t(left, right):
    return lax.dot_general(left, right, (((1,), (1,)), ((), ())), preferred_element_type=WIDE)


def dot_0(left, right):
    return lax.dot_general(left, right, (((0,), (0,)), ((), ())), preferred_element_type=WIDE)


def call(body, out_shape, grid, in_specs, out_specs, flops, traffic, scratch=(), prefetch=0, vmem=40):
    return pl.pallas_call(
        body,
        out_shape=out_shape,
        grid_spec=pltpu.PrefetchScalarGridSpec(
            num_scalar_prefetch=prefetch,
            grid=grid,
            in_specs=in_specs,
            out_specs=out_specs,
            scratch_shapes=list(scratch),
        ),
        compiler_params=pltpu.CompilerParams(vmem_limit_bytes=vmem * 2**20),
        cost_estimate=pl.CostEstimate(flops=flops, bytes_accessed=traffic, transcendentals=0),
    )


def whole(shape):
    return pl.BlockSpec(shape, lambda *_: (0,) * len(shape))


def struct(shape, dtype):
    return jax.ShapeDtypeStruct(shape, dtype)


def spread(array, axes, size):
    return lax.all_to_all(jnp.broadcast_to(array[None], (size,) + array.shape), axes, 0, 0)


def collect(parts, axes):
    return jnp.sum(lax.all_to_all(parts, axes, 0, 0).astype(WIDE), 0)


def swap(parts, axes):
    return lax.all_to_all(parts, axes, 0, 0)


def ring(array, step, axis="y"):
    if step == 0:
        return array
    return lax.ppermute(array, axis, [(i, (i + step) % RING) for i in range(RING)])


def ring_terms(parts, axis):
    return [parts[0]] + [ring(parts[slot], step, axis) for slot, step in ((1, -1), (2, 1), (3, 2))]


def ring_collect(parts, axis):
    return sum(term.astype(WIDE) for term in ring_terms(parts, axis))


def ring_gather(rows):
    half = rows.shape[0] // 2
    first, second = rows[:half], rows[half:]
    before_first, after_second = ring(first, 1), ring(second, -1)
    before_second, after_first = ring(second, 1), ring(first, -1)
    across_first, across_second = ring(before_first, 1), ring(after_second, -1)
    return jnp.concatenate(
        [
            first, second, before_first, before_second,
            after_first, after_second, across_first, across_second,
        ],
        0,
    )


def ring_sum_parts(rows, later=None):
    own = rows.shape[0] // RING
    half = own // 2
    start, before, after, across = (rows[i * own : (i + 1) * own] for i in range(RING))
    from_before, from_after = ring(across[:half], 1), ring(across[half:], -1)
    second_after, first_before = ring(after[half:], 1), ring(before[:half], -1)
    if later is not None:
        from_before, from_after, second_after, first_before, later = tie(
            from_before, from_after, second_after, first_before, later
        )
    first_after = ring((after[:half].astype(WIDE) + from_before.astype(WIDE)).astype(LOW), 1)
    second_before = ring((before[half:].astype(WIDE) + from_after.astype(WIDE)).astype(LOW), -1)
    came = (start, first_after, second_after, first_before, second_before)
    return came if later is None else (came, later)


def tie(*arrays):
    return lax.optimization_barrier(arrays)


def gather_weight(shard):
    full = lax.all_gather(shard, ("z", "c", "x"), axis=0)
    return full.reshape((8, 4) + shard.shape)


def settle(gradient):
    return lax.psum_scatter(gradient, ROWS, scatter_dimension=0)


def qkv_body(rows_ref, weight_ref, bias_ref, out_ref):
    weight = weight_ref[...].reshape(rows_ref.shape[1], -1)
    out_ref[...] = (dot(rows_ref[...], weight) + bias_ref[...]).astype(LOW)


def qkv_project(rows, weight, bias):
    count, width = rows.shape
    zc, xs, piece, _ = weight.shape
    cols = bias.shape[-1]
    return call(
        qkv_body,
        struct((xs, count, cols), LOW),
        (xs,),
        [
            whole((count, width)),
            pl.BlockSpec((zc, None, piece, cols), lambda i: (0, i, 0, 0)),
            pl.BlockSpec((None, 1, cols), lambda i: (i, 0, 0)),
        ],
        pl.BlockSpec((None, count, cols), lambda i: (i, 0, 0)),
        2 * count * width * xs * cols,
        10 * 2**20,
        vmem=60,
    )(rows, weight, bias)


def out_body(heads_ref, weight_ref, out_ref):
    count, _, piece, _ = weight_ref.shape
    for block in range(count):
        value = dot_t(heads_ref[0], weight_ref[block, 0])
        for x in range(1, RING):
            value += dot_t(heads_ref[x], weight_ref[block, x])
        out_ref[:, block * piece : (block + 1) * piece] = value.astype(LOW)


def store_rows(out_ref, place_ref, value):
    rows = value.shape[0] // RING
    for slot in range(RING):
        at = pl.multiple_of(place_ref[slot] * rows, rows)
        out_ref[pl.ds(at, rows)] = value[slot * rows : (slot + 1) * rows]


def out_project(heads, weight, at, blocks):
    xs, count, cols = heads.shape
    zc, _, piece, _ = weight.shape
    return call(
        out_body,
        struct((count, zc * piece), LOW),
        (zc // blocks,),
        [
            whole(heads.shape),
            pl.BlockSpec((blocks, xs, piece, cols), lambda i: (i, 0, 0, at)),
        ],
        pl.BlockSpec((count, blocks * piece), lambda i: (0, i)),
        2 * count * zc * piece * xs * cols,
        5 * 2**20,
        vmem=60,
    )(heads, weight)


def heads_grad_body(rows_ref, weight_ref, out_ref):
    cols = out_ref.shape[2]
    for x in range(0, RING, 2):
        pair = [weight_ref[:, x + i].reshape(rows_ref.shape[1], cols) for i in range(2)]
        value = dot(rows_ref[...], jnp.concatenate(pair, 1)).astype(LOW)
        out_ref[x] = value[:, :cols]
        out_ref[x + 1] = value[:, cols:]


def heads_grad(rows, weight, cols, at):
    count, width = rows.shape
    zc, xs, piece, _ = weight.shape
    return call(
        heads_grad_body,
        struct((xs, count, cols), LOW),
        (1,),
        [
            whole((count, width)),
            pl.BlockSpec((zc, xs, piece, cols), lambda i: (0, 0, 0, at)),
        ],
        whole((xs, count, cols)),
        2 * count * width * xs * cols,
        5 * 2**20,
        vmem=60,
    )(rows, weight)


def weight_grad_body(rows_ref, grad_ref, out_ref):
    out_ref[...] = dot_0(rows_ref[...], grad_ref[...]).astype(LOW).reshape(out_ref.shape)


def weight_grads(rows, columns):
    count, width = rows.shape
    xs, _, cols = columns.shape
    piece = width // 8
    return call(
        weight_grad_body,
        struct((8, xs, piece, cols), LOW),
        (xs,),
        [whole((count, width)), pl.BlockSpec((None, count, cols), lambda i: (i, 0, 0))],
        pl.BlockSpec((8, None, piece, cols), lambda i: (0, i, 0, 0)),
        2 * count * width * xs * cols,
        15 * 2**20,
        vmem=60,
    )(rows, columns)


def split_grad_body(place_ref, rows_ref, grad_ref, keep_ref, send_ref):
    value = dot_0(rows_ref[...], grad_ref[...]).astype(LOW)
    value = value.reshape(4, 2, -1, value.shape[-1])
    first = place_ref[0] == 0
    keep_ref[...] = jnp.where(first, value[:, 0], value[:, 1])
    send_ref[...] = jnp.where(first, value[:, 1], value[:, 0])


def split_grads(core_at, rows, columns):
    count, width = rows.shape
    xs, _, cols = columns.shape
    piece = width // 8
    half = struct((4, xs, piece, cols), LOW)
    block = pl.BlockSpec((4, None, piece, cols), lambda i, *_: (0, i, 0, 0))
    return call(
        split_grad_body,
        (half, half),
        (xs,),
        [whole((count, width)), pl.BlockSpec((None, count, cols), lambda i, *_: (i, 0, 0))],
        (block, block),
        2 * count * width * xs * cols,
        5 * 2**20,
        prefetch=1,
        vmem=60,
    )(core_at, rows, columns)


def core_sum(kept, sent):
    other = lax.ppermute(sent, "c", [(0, 1), (1, 0)])
    both = (kept.astype(WIDE) + other.astype(WIDE)).astype(LOW)
    return both.reshape((16,) + both.shape[2:])


def add_up(total, term):
    @pl.when(pl.program_id(0) == 0)
    def _():
        total[...] = term

    @pl.when(pl.program_id(0) > 0)
    def _():
        total[...] += term


def ffn_first_body(
    place_ref, norm_ref, cot_ref, up_ref, down_ref, bias_ref,
    hidden_ref, grad_up_ref, norm_grad_ref, bias_grad_ref, total,
):
    width, cols = norm_ref.shape[1], up_ref.shape[-1]
    up_w = up_ref[...].reshape(width, cols)
    up = dot(norm_ref[...], up_w) + bias_ref[...]
    normal = 0.5 * (1.0 + lax.erf(up * 0.7071067811865476))
    hidden_ref[...] = (up * normal).astype(LOW)
    slope = normal + up * (jnp.exp(-0.5 * up * up) * 0.3989422804014327)
    grad_up = (dot(cot_ref[...], down_ref[...].reshape(width, cols)) * slope).astype(LOW)
    grad_up_ref[...] = grad_up
    bias_grad_ref[...] = jnp.sum(grad_up.astype(WIDE), 0, keepdims=True)
    add_up(total, dot_t(grad_up, up_w))

    @pl.when(pl.program_id(0) == pl.num_programs(0) - 1)
    def _():
        store_rows(norm_grad_ref, place_ref, total[...].astype(LOW))


def ffn_first(places, norm_rows, cot_rows, weight, bias):
    count, width = norm_rows.shape
    zc, xs, piece, cols = weight.shape
    size = cols // 2
    rows = whole((count, width))
    vector = pl.BlockSpec((None, 1, size), lambda i, places: (places[RING + i], 0, 0))
    wide = pl.BlockSpec((count, size), lambda i, *_: (0, i))
    return call(
        ffn_first_body,
        (
            struct((count, xs * size), LOW),
            struct((count, xs * size), LOW),
            struct((count, width), LOW),
            struct((xs, 1, size), WIDE),
        ),
        (xs,),
        [
            rows,
            rows,
            pl.BlockSpec((zc, None, piece, size), lambda i, *_: (0, i, 0, 0)),
            pl.BlockSpec((zc, None, piece, size), lambda i, *_: (0, i, 0, 1)),
            vector,
        ],
        (wide, wide, rows, vector),
        6 * count * width * xs * size,
        25 * 2**20,
        scratch=[pltpu.VMEM((count, width), WIDE)],
        prefetch=1,
        vmem=56,
    )(places, norm_rows, cot_rows, weight, weight, bias)


def ffn_second_body(
    norm_ref, cot_ref, hidden_ref, grad_up_ref, down_ref, branch_ref, weight_grad_ref, total
):
    width, cols = norm_ref.shape[1], down_ref.shape[-1]
    zc, piece, _ = weight_grad_ref.shape
    hidden = hidden_ref[...]
    weight_grad_ref[:, :, :cols] = (
        dot_0(norm_ref[...], grad_up_ref[...]).astype(LOW).reshape(zc, piece, cols)
    )
    weight_grad_ref[:, :, cols:] = dot_0(cot_ref[...], hidden).astype(LOW).reshape(zc, piece, cols)
    add_up(total, dot_t(hidden, down_ref[...].reshape(width, cols)))

    @pl.when(pl.program_id(0) == pl.num_programs(0) - 1)
    def _():
        branch_ref[...] = total[...].astype(LOW)


def ffn_second(norm_rows, cot_rows, hidden, grad_up, weight):
    count, width = norm_rows.shape
    zc, xs, piece, cols = weight.shape
    size = cols // 2
    rows = whole((count, width))
    wide = pl.BlockSpec((count, size), lambda i: (0, i))
    return call(
        ffn_second_body,
        (struct((count, width), LOW), struct(weight.shape, LOW)),
        (xs,),
        [rows, rows, wide, wide, pl.BlockSpec((zc, None, piece, size), lambda i: (0, i, 0, 1))],
        (rows, pl.BlockSpec((zc, None, piece, cols), lambda i: (0, i, 0, 0))),
        6 * count * width * xs * size,
        40 * 2**20,
        scratch=[pltpu.VMEM((count, width), WIDE)],
        vmem=56,
    )(norm_rows, cot_rows, hidden, grad_up, weight)


def only_head(array, head):
    lane = lax.broadcasted_iota(jnp.int32, array.shape, 1)
    return jnp.where(lane // HEAD_DIM == head, array, jnp.zeros_like(array))


def allowed_keys(start, extent, live_count):
    q_place = start + lax.broadcasted_iota(jnp.int32, (SPAN, extent), 0)
    k_place = lax.broadcasted_iota(jnp.int32, (SPAN, extent), 1)
    return k_place <= jnp.minimum(q_place, live_count - 1)


def slot_of(place, own):
    apart = (place - own + RING) % RING
    return jnp.where(apart == 0, 0, jnp.where(apart == RING - 1, 1, apart + 1))


def load_ordered(blocks_ref, own, into):
    rows = blocks_ref.shape[2]
    for x in range(RING):
        for y in range(RING):
            at = (x * RING + y) * rows
            into[at : at + rows] = blocks_ref[x, slot_of(y, own)]


def store_ordered(blocks_ref, x, own, cols, value):
    rows = blocks_ref.shape[2]
    for y in range(RING):
        blocks_ref[x, slot_of(y, own), :, cols] = value[y * rows : (y + 1) * rows]


def attend_body(live_ref, qkv_ref, heads_ref, exact_ref, log_ref, qkv):
    live_count = live_ref[pl.program_id(0)]
    own = live_ref[pl.num_programs(0)]
    length = exact_ref.shape[0]
    width = exact_ref.shape[1]
    load_ordered(qkv_ref, own, qkv)
    key = qkv[:, width : 2 * width]
    value = qkv[:, 2 * width :]
    for span in range(length // SPAN):
        start, extent = span * SPAN, (span + 1) * SPAN
        here = slice(start, extent)

        @pl.when(start < live_count)
        def _():
            query = qkv[here, :width]
            allowed = allowed_keys(start, extent, live_count)
            mixed, logs = [], []
            for head in range(width // HEAD_DIM):
                scores = dot_t(only_head(query, head), key[:extent]) * HEAD_DIM**-0.5
                scores = jnp.where(allowed, scores, -1e9)
                top = jnp.max(scores, 1, keepdims=True)
                terms = jnp.exp(scores - top)
                denom = jnp.sum(terms, 1, keepdims=True)
                mixed.append(dot(terms.astype(LOW), value[:extent]) / denom)
                logs.append(top + jnp.log(denom))
            lane = lax.broadcasted_iota(jnp.int32, (SPAN, width), 1)
            out = jnp.where(lane < HEAD_DIM, mixed[0], mixed[1])
            exact_ref[here] = out
            log_ref[here] = jnp.where(lane < HEAD_DIM, logs[0], logs[1])
            store_ordered(heads_ref, span, own, slice(None), out.astype(LOW))

        @pl.when(start >= live_count)
        def _():
            exact_ref[here] = jnp.zeros((SPAN, width), WIDE)
            log_ref[here] = jnp.zeros((SPAN, width), WIDE)
            heads_ref[span] = jnp.zeros(heads_ref.shape[1:], LOW)


def row_block(rows, cols):
    return pl.BlockSpec((4, 4, None, rows, cols), lambda s, *_: (0, 0, s, 0, 0))


def attend(live_counts, qkv, width):
    xs, ys, seqs, rows, _ = qkv.shape
    length = xs * ys * rows
    flat = pl.BlockSpec((None, length, width), lambda s, *_: (s, 0, 0))
    return call(
        attend_body,
        (
            struct((xs, ys, seqs, rows, width), LOW),
            struct((seqs, length, width), WIDE),
            struct((seqs, length, width), WIDE),
        ),
        (seqs,),
        [row_block(rows, 3 * width)],
        (row_block(rows, width), flat, flat),
        4 * 10**9,
        4 * 2**20,
        scratch=[pltpu.VMEM((length, 3 * width), LOW)],
        prefetch=1,
    )(live_counts, qkv)


def attend_back_body(
    live_ref, qkv_ref, grad_ref, exact_ref, log_ref, out_ref, sum_ref,
    key_total, value_total, qkv, grads,
):
    live_count = live_ref[pl.program_id(0)]
    own = live_ref[pl.num_programs(0)]
    length, width = exact_ref.shape
    factor = HEAD_DIM**-0.5
    load_ordered(qkv_ref, own, qkv)
    load_ordered(grad_ref, own, grads)
    key = qkv[:, width : 2 * width]
    value = qkv[:, 2 * width :]
    key_total[...] = jnp.zeros_like(key_total)
    value_total[...] = jnp.zeros_like(value_total)
    sum_ref[...] = jnp.zeros_like(sum_ref)
    for span in range(length // SPAN):
        start, extent = span * SPAN, (span + 1) * SPAN
        here = slice(start, extent)

        @pl.when(start < live_count)
        def _():
            query = qkv[here, :width]
            grad = grads[here]
            inner = grad.astype(WIDE) * exact_ref[here]
            logs = log_ref[here]
            allowed = allowed_keys(start, extent, live_count)
            query_total = jnp.zeros((SPAN, width), WIDE)
            for head in range(width // HEAD_DIM):
                query_h = only_head(query, head)
                grad_h = only_head(grad, head)
                log_h = logs[:, head * HEAD_DIM : head * HEAD_DIM + 1]
                row_inner = jnp.sum(only_head(inner, head), 1, keepdims=True)
                scores = dot_t(query_h, key[:extent]) * factor
                probs = jnp.exp(jnp.where(allowed, scores, -1e9) - log_h)
                d_probs = dot_t(grad_h, value[:extent])
                value_total[:extent] += dot_0(probs.astype(LOW), grad_h)
                d_scores = (probs * (d_probs - row_inner)).astype(LOW)
                query_total += dot(d_scores, only_head(key[:extent], head))
                key_total[:extent] += dot_0(d_scores, query_h)
            out = (query_total * factor).astype(LOW)
            store_ordered(out_ref, span, own, slice(0, width), out)
            sum_ref[:, :width] += jnp.sum(out.astype(WIDE), 0, keepdims=True)

        @pl.when(start >= live_count)
        def _():
            out_ref[span, :, :, :width] = jnp.zeros(out_ref.shape[1:3] + (width,), LOW)

    key_grad = (key_total[...] * factor).astype(LOW)
    value_grad = value_total[...].astype(LOW)
    for span in range(RING):
        here = slice(span * SPAN, (span + 1) * SPAN)
        store_ordered(out_ref, span, own, slice(width, 2 * width), key_grad[here])
        store_ordered(out_ref, span, own, slice(2 * width, None), value_grad[here])
    sum_ref[:, 2 * width :] = jnp.sum(value_grad.astype(WIDE), 0, keepdims=True)


def attend_back(live_counts, qkv, grads, exact, logs):
    xs, ys, seqs, rows, _ = qkv.shape
    _, length, width = exact.shape
    flat = pl.BlockSpec((None, length, width), lambda s, *_: (s, 0, 0))
    return call(
        attend_back_body,
        (struct(qkv.shape, LOW), struct((seqs, 1, 3 * width), WIDE)),
        (seqs,),
        [row_block(rows, 3 * width), row_block(rows, width), flat, flat],
        (
            row_block(rows, 3 * width),
            pl.BlockSpec((None, 1, 3 * width), lambda s, *_: (s, 0, 0)),
        ),
        8 * 10**9,
        8 * 2**20,
        scratch=[
            pltpu.VMEM((length, width), WIDE),
            pltpu.VMEM((length, width), WIDE),
            pltpu.VMEM((length, 3 * width), LOW),
            pltpu.VMEM((length, width), LOW),
        ],
        prefetch=1,
    )(live_counts, qkv, grads, exact, logs)


def norm_rows(values, gain_vec, shift_vec):
    centered = values - jnp.mean(values, -1, keepdims=True)
    inverse = lax.rsqrt(jnp.mean(centered * centered, -1, keepdims=True) + 1e-05)
    return (centered * inverse * gain_vec + shift_vec).astype(LOW)


def pick_half(first_ref, second_ref):
    early = pl.program_id(0) < pl.num_programs(0) // 2
    return jnp.where(early, first_ref[...], second_ref[...])


def half_blocks(step, width):
    early = pl.BlockSpec((step, width), lambda i: (jnp.minimum(i, 1), 0))
    late = pl.BlockSpec((step, width), lambda i: (jnp.maximum(i - 2, 0), 0))
    return [early, late]


def add_norm_body(
    start_ref, first_after, second_after, first_before, second_before,
    rows_ref, keep_ref, bias_ref, gain_ref, shift_ref, out_ref, norm_ref,
):
    branch = start_ref[...].astype(WIDE) + pick_half(first_after, second_after).astype(WIDE)
    branch += pick_half(first_before, second_before).astype(WIDE)
    values = rows_ref[...].astype(WIDE) + keep_ref[...] * (branch + bias_ref[...])
    out_ref[...] = values
    centered = values - jnp.mean(values, 1, keepdims=True)
    inverse = lax.rsqrt(jnp.mean(centered * centered, 1, keepdims=True) + 1e-05)
    norm_ref[...] = (centered * inverse * gain_ref[...] + shift_ref[...]).astype(LOW)


def add_norm(parts, rows, keep, bias, gain, shift):
    own, width = rows.shape
    step = own // 4
    flat = pl.BlockSpec((step, width), lambda i: (i, 0))
    vector = pl.BlockSpec((1, width), lambda i: (0, 0))
    halves = half_blocks(step, width) * 2
    return call(
        add_norm_body,
        (struct((own, width), WIDE), struct((own, width), LOW)),
        (own // step,),
        [flat] + halves + [flat, pl.BlockSpec((step, 1), lambda i: (i, 0)), vector, vector, vector],
        (flat, flat),
        20 * own * width,
        4 * 2**20,
    )(*parts, rows, keep, *(v.reshape(1, width) for v in (bias, gain, shift)))


def norm_back_body(count, with_low, *refs):
    parts, (rows_ref, grad_ref, gain_ref) = refs[:count], refs[count : count + 3]
    refs = refs[count + 3 :]
    if count == 1:
        terms = [parts[0][i] for i in range(parts[0].shape[0])]
    else:
        terms = [parts[0][...], pick_half(*parts[1:3]), pick_half(*parts[3:5])]
    gradient = sum(term.astype(WIDE) for term in terms)
    values = rows_ref[...].astype(WIDE)
    centered = values - jnp.mean(values, 1, keepdims=True)
    inverse = lax.rsqrt(jnp.mean(centered * centered, 1, keepdims=True) + 1e-05)
    unit = centered * inverse
    scaled = gradient * gain_ref[...]
    out = grad_ref[...].astype(WIDE) + inverse * (
        scaled
        - jnp.mean(scaled, 1, keepdims=True)
        - unit * jnp.mean(scaled * unit, 1, keepdims=True)
    )
    sums = [jnp.sum(gradient * unit, 0, keepdims=True), jnp.sum(gradient, 0, keepdims=True)]
    if with_low:
        keep_ref, out_ref, low_ref, sum_ref = refs
        low = (keep_ref[...] * out).astype(LOW)
        low_ref[...] = low
        sums.append(jnp.sum(low.astype(WIDE), 0, keepdims=True))
    else:
        out_ref, sum_ref = refs
    out_ref[...] = out
    sums.append(jnp.zeros((sum_ref.shape[0] - len(sums), sum_ref.shape[1]), WIDE))
    add_up(sum_ref, jnp.concatenate(sums, 0))


def norm_back(parts, rows, grad, gain, keep=None):
    own, width = rows.shape
    step = own // 4
    flat = pl.BlockSpec((step, width), lambda i: (i, 0))
    sums = pl.BlockSpec((8, width), lambda i: (0, 0))
    if isinstance(parts, tuple):
        in_specs, args = [flat] + half_blocks(step, width) * 2, list(parts)
    else:
        in_specs = [pl.BlockSpec((parts.shape[0], step, width), lambda i: (0, i, 0))]
        args = [parts]
    count = len(args)
    in_specs += [flat, flat, pl.BlockSpec((1, width), lambda i: (0, 0))]
    args += [rows, grad, gain.reshape(1, width)]
    outs, specs = [struct((own, width), WIDE)], [flat]
    if keep is not None:
        in_specs.append(pl.BlockSpec((step, 1), lambda i: (i, 0)))
        args.append(keep)
        outs.append(struct((own, width), LOW))
        specs.append(flat)
    return call(
        partial(norm_back_body, count, keep is not None),
        tuple(outs + [struct((8, width), WIDE)]),
        (own // step,),
        in_specs,
        tuple(specs + [sums]),
        40 * own * width,
        6 * 2**20,
    )(*args)


def collect_vectors(vectors):
    flat = jnp.concatenate([v.reshape(-1) for v in vectors])
    return collect(flat.reshape(16, -1, 128), COLS)


def spread_vectors(part, sizes):
    flat = spread(jnp.sum(spread(part, ROWS, 8), 0), COLS, 16).reshape(-1)
    pieces, start = [], 0
    for size in sizes:
        pieces.append(flat[start : start + size])
        start += size
    return pieces


def shards(
    tokens, cotangent, seq_lengths, exit_layers, layer_index,
    ln1_gain, ln1_shift, q_weight, q_bias, k_weight, v_weight, v_bias, out_weight, out_bias,
    ln2_gain, ln2_shift, up_weight, up_bias, down_weight, down_bias,
):
    seqs, own_rows, width = tokens.shape
    own = seqs * own_rows
    full_len = exit_layers.shape[1]
    x_at, y_at = lax.axis_index("x"), lax.axis_index("y")
    head_at = x_at * RING + y_at
    head_cols = q_weight.shape[1]
    ff_cols = up_weight.shape[1]

    positions = jnp.arange(full_len)
    live_all = (positions[None, :] < seq_lengths[:, None]) & (exit_layers > layer_index[0])
    live_counts = jnp.concatenate(
        [jnp.sum(live_all.astype(jnp.int32), 1), y_at.astype(jnp.int32).reshape(1)]
    )
    y_places, x_places = (
        [((at + apart) % RING).astype(jnp.int32) for apart in (0, RING - 1, 1, 2)]
        for at in (y_at, x_at)
    )
    places = jnp.stack(y_places + x_places)
    live_mine = lax.dynamic_slice_in_dim(live_all, head_at * own_rows, own_rows, 1)
    keep = live_mine.reshape(-1, 1).astype(WIDE)

    w_attn = gather_weight(
        jnp.concatenate([q_weight, k_weight, v_weight, out_weight], 1).astype(LOW)
    )
    w_ff = jnp.concatenate([up_weight, down_weight], 1).astype(LOW)

    inputs = tokens.astype(WIDE).reshape(own, width)
    flat_cot = cotangent.reshape(own, width)
    g_ffn = (keep * flat_cot.astype(WIDE)).astype(LOW)
    norm1 = ring_gather(norm_rows(inputs, ln1_gain, ln1_shift))
    norm1, w_ff = tie(norm1, [ring(w_ff, step, "x") for step in (0, 1, -1, 2)])
    w_ff = lax.all_gather(jnp.stack(w_ff), ROWS, axis=0)
    norm1, cot_rows = tie(norm1, ring_gather(g_ffn))

    def mine(vector, cols):
        return lax.dynamic_index_in_dim(vector.reshape(RING, RING, cols), y_at, 1, False)

    bias = jnp.concatenate(
        [mine(q_bias, head_cols), jnp.zeros((RING, head_cols), WIDE), mine(v_bias, head_cols)], 1
    ).reshape(RING, 1, 3 * head_cols)
    qkv = qkv_project(norm1, w_attn, bias)
    rows5 = (RING, RING, seqs, own_rows)
    qkv = swap(qkv, "x").reshape(rows5 + (3 * head_cols,))
    heads, exact, logs = attend(live_counts, qkv, head_cols)
    heads = swap(heads.reshape(RING, RING * own, head_cols), "x")
    middle, normed2 = add_norm(
        ring_sum_parts(out_project(heads, w_attn, 3, 4)),
        tokens.reshape(own, width), keep, out_bias, ln2_gain, ln2_shift,
    )
    norm2 = ring_gather(normed2)

    ff_bias = mine(up_bias, ff_cols).reshape(RING, 1, ff_cols)
    hidden, grad_up, g_norm2, up_bias_part = ffn_first(places, norm2, cot_rows, w_ff, ff_bias)
    g_norm2 = swap(g_norm2.reshape(RING, own, width), "y")
    g_norm2, branch2, ff_grad = tie(
        g_norm2, *ffn_second(norm2, cot_rows, hidden, grad_up, w_ff)
    )
    ff_grad = settle(ff_grad)
    grad_mid, g_attn, sums2 = norm_back(g_norm2, middle, flat_cot, ln2_gain, keep)
    attn_rows = ring_gather(g_attn)
    g_heads, attn_rows = tie(heads_grad(attn_rows, w_attn, head_cols, 3), attn_rows)
    core_at = lax.axis_index("c").astype(jnp.int32).reshape(1)
    g_heads, branch2, out_kept, out_sent = tie(
        swap(g_heads, "x").reshape(rows5 + (head_cols,)),
        branch2,
        *split_grads(core_at, attn_rows, heads),
    )
    branch2 = ring_terms(branch2.reshape(RING, own, width), "y")
    d_qkv, d_sums = attend_back(live_counts, qkv, g_heads, exact, logs)
    out_grad = core_sum(out_kept, out_sent)
    d_qkv = swap(d_qkv.reshape(RING, RING * own, 3 * head_cols), "x")

    up_bias_full = lax.dynamic_update_slice_in_dim(
        jnp.zeros((RING, RING, ff_cols), WIDE), up_bias_part.reshape(RING, 1, ff_cols), y_at, 1
    )
    early = (
        sums2[2],
        sums2[0],
        sums2[1],
        up_bias_full,
        jnp.sum(g_ffn.astype(WIDE), 0),
    )
    d_qkv, out_grad, branch2 = tie(d_qkv, out_grad, branch2)
    out_grad = collect(out_grad, ("z", "x"))
    g_norm1, d_qkv = tie(out_project(d_qkv, w_attn, 0, 2), d_qkv)
    attn_grad = weight_grads(norm1, d_qkv)
    g_norm1, (ff_grad, attn_grad, out_grad) = ring_sum_parts(
        g_norm1, (ff_grad, attn_grad, out_grad)
    )
    attn_grad = settle(attn_grad)
    ff_grad = ring_collect(ff_grad, "x")
    grad_tokens, sums1 = norm_back(g_norm1, tokens.reshape(own, width), grad_mid, ln1_gain)
    grad_tokens = grad_tokens.reshape(tokens.shape)
    sums1, branch2 = tie(sums1, branch2)
    branch2 = sum(term.astype(WIDE) for term in branch2) + down_bias
    result = (middle + keep * branch2).astype(LOW).reshape(tokens.shape)
    d_sums = jnp.sum(d_sums, 0).reshape(3, head_cols)

    def placed(row):
        blank = jnp.zeros((RING * RING, head_cols), WIDE)
        return lax.dynamic_update_slice_in_dim(blank, row[None], head_at, 0)

    part = collect_vectors(early + (sums1[0], sums1[1], placed(d_sums[0]), placed(d_sums[2])))
    part, ff_grad = tie(part, ff_grad)
    sizes = (width, width, width, RING * RING * ff_cols) + (width,) * 5
    totals, attn_grad = tie(spread_vectors(part, sizes), attn_grad)
    here = [lax.dynamic_index_in_dim(attn_grad, x_places[i], 0, False) for i in range(RING)]
    attn_grad = ring_collect(here, "x")
    out_bias_sum, ln2_gain_sum, ln2_shift_sum, up_bias_sum, down_bias_sum = totals[:5]
    ln1_gain_sum, ln1_shift_sum, q_bias_sum, v_bias_sum = totals[5:]
    return (
        result,
        grad_tokens,
        ln1_gain_sum,
        ln1_shift_sum,
        attn_grad[:, :head_cols],
        q_bias_sum,
        attn_grad[:, head_cols : 2 * head_cols],
        attn_grad[:, 2 * head_cols :],
        v_bias_sum,
        out_grad,
        out_bias_sum,
        ln2_gain_sum,
        ln2_shift_sum,
        ff_grad[:, :ff_cols],
        up_bias_sum,
        ff_grad[:, ff_cols:],
        down_bias_sum,
    )


def solution(mesh):
    wide = Mesh(mesh.devices.reshape(4, 2, 4, 4), ("z", "c", "x", "y"))
    act = P(ROWS, COLS, None)
    weight = P(ROWS, COLS)
    vector = P()
    in_specs = (
        act, act, P(ROWS), P(ROWS, None), vector, vector, vector,
        weight, vector, weight, weight, vector, weight, vector, vector, vector,
        weight, vector, weight, vector,
    )
    out_specs = (
        act, act, vector, vector, weight, vector, weight, weight, vector, weight,
        vector, vector, vector, weight, vector, weight, vector,
    )
    return jax.shard_map(
        shards, mesh=wide, in_specs=in_specs, out_specs=out_specs, check_vma=False
    )
```

```python
from functools import partial

import jax
import jax.numpy as jnp
from jax import lax
from jax.experimental import pallas as pl
from jax.experimental.pallas import tpu as pltpu
from jax.sharding import Mesh
from jax.sharding import PartitionSpec as P

HEAD_DIM = 64
SPAN = 256
LOW = jnp.bfloat16
WIDE = jnp.float32
RING = 4
ROWS = ("z", "c")
COLS = ("x", "y")


def dot(left, right):
    return jnp.dot(left, right, preferred_element_type=WIDE)


def dot_t(left, right):
    return lax.dot_general(left, right, (((1,), (1,)), ((), ())), preferred_element_type=WIDE)


def dot_0(left, right):
    return lax.dot_general(left, right, (((0,), (0,)), ((), ())), preferred_element_type=WIDE)


def call(body, out_shape, grid, in_specs, out_specs, flops, traffic, scratch=(), prefetch=0, vmem=40, aliases=None):
    return pl.pallas_call(
        body,
        out_shape=out_shape,
        grid_spec=pltpu.PrefetchScalarGridSpec(
            num_scalar_prefetch=prefetch,
            grid=grid,
            in_specs=in_specs,
            out_specs=out_specs,
            scratch_shapes=list(scratch),
        ),
        compiler_params=pltpu.CompilerParams(vmem_limit_bytes=vmem * 2**20),
        input_output_aliases=aliases or {},
        cost_estimate=pl.CostEstimate(flops=flops, bytes_accessed=traffic, transcendentals=0),
    )


def whole(shape):
    return pl.BlockSpec(shape, lambda *_: (0,) * len(shape))


def struct(shape, dtype):
    return jax.ShapeDtypeStruct(shape, dtype)


def spread(array, axes, size):
    return lax.all_to_all(jnp.broadcast_to(array[None], (size,) + array.shape), axes, 0, 0)


def collect(parts, axes):
    return jnp.sum(lax.all_to_all(parts, axes, 0, 0).astype(WIDE), 0)


def swap(parts, axes):
    return lax.all_to_all(parts, axes, 0, 0)


def ring(array, step, axis="y"):
    if step == 0:
        return array
    return lax.ppermute(array, axis, [(i, (i + step) % RING) for i in range(RING)])


def ring_terms(parts, axis):
    return [parts[0]] + [ring(parts[slot], step, axis) for slot, step in ((1, -1), (2, 1), (3, 2))]


def ring_collect(parts, axis):
    return sum(term.astype(WIDE) for term in ring_terms(parts, axis))


def ring_gather(rows):
    half = rows.shape[0] // 2
    first, second = rows[:half], rows[half:]
    before_first, after_second = ring(first, 1), ring(second, -1)
    before_second, after_first = ring(second, 1), ring(first, -1)
    across_first, across_second = ring(before_first, 1), ring(after_second, -1)
    return jnp.concatenate(
        [
            first, second, before_first, before_second,
            after_first, after_second, across_first, across_second,
        ],
        0,
    )


def ring_sum_parts(rows, later=None):
    own = rows.shape[0] // RING
    half = own // 2
    start, before, after, across = (rows[i * own : (i + 1) * own] for i in range(RING))
    from_before, from_after = ring(across[:half], 1), ring(across[half:], -1)
    second_after, first_before = ring(after[half:], 1), ring(before[:half], -1)
    if later is not None:
        from_before, from_after, second_after, first_before, later = tie(
            from_before, from_after, second_after, first_before, later
        )
    first_after = ring((after[:half].astype(WIDE) + from_before.astype(WIDE)).astype(LOW), 1)
    second_before = ring((before[half:].astype(WIDE) + from_after.astype(WIDE)).astype(LOW), -1)
    came = (start, first_after, second_after, first_before, second_before)
    return came if later is None else (came, later)


def tie(*arrays):
    return lax.optimization_barrier(arrays)


def gather_weight(shard):
    full = lax.all_gather(shard, ("z", "c", "x"), axis=0)
    return full.reshape((8, 4) + shard.shape)


def settle(gradient):
    return lax.psum_scatter(gradient, ROWS, scatter_dimension=0)


def qkv_body(rows_ref, weight_ref, bias_ref, out_ref):
    weight = weight_ref[...].reshape(rows_ref.shape[1], -1)
    out_ref[...] = (dot(rows_ref[...], weight) + bias_ref[...]).astype(LOW)


def qkv_project(rows, weight, bias):
    count, width = rows.shape
    zc, xs, piece, _ = weight.shape
    cols = bias.shape[-1]
    return call(
        qkv_body,
        struct((xs, count, cols), LOW),
        (xs,),
        [
            whole((count, width)),
            pl.BlockSpec((zc, None, piece, cols), lambda i: (0, i, 0, 0)),
            pl.BlockSpec((None, 1, cols), lambda i: (i, 0, 0)),
        ],
        pl.BlockSpec((None, count, cols), lambda i: (i, 0, 0)),
        2 * count * width * xs * cols,
        10 * 2**20,
        vmem=60,
    )(rows, weight, bias)


def out_body(heads_ref, weight_ref, out_ref):
    count, _, piece, _ = weight_ref.shape
    for block in range(count):
        value = dot_t(heads_ref[0], weight_ref[block, 0])
        for x in range(1, RING):
            value += dot_t(heads_ref[x], weight_ref[block, x])
        out_ref[:, block * piece : (block + 1) * piece] = value.astype(LOW)


def store_rows(out_ref, place_ref, value):
    rows = value.shape[0] // RING
    for slot in range(RING):
        at = pl.multiple_of(place_ref[slot] * rows, rows)
        out_ref[pl.ds(at, rows)] = value[slot * rows : (slot + 1) * rows]


def out_project(heads, weight, at, blocks):
    xs, count, cols = heads.shape
    zc, _, piece, _ = weight.shape
    return call(
        out_body,
        struct((count, zc * piece), LOW),
        (zc // blocks,),
        [
            whole(heads.shape),
            pl.BlockSpec((blocks, xs, piece, cols), lambda i: (i, 0, 0, at)),
        ],
        pl.BlockSpec((count, blocks * piece), lambda i: (0, i)),
        2 * count * zc * piece * xs * cols,
        5 * 2**20,
        vmem=60,
    )(heads, weight)


def heads_grad_body(rows_ref, weight_ref, out_ref):
    cols = out_ref.shape[2]
    for x in range(0, RING, 2):
        pair = [weight_ref[:, x + i].reshape(rows_ref.shape[1], cols) for i in range(2)]
        value = dot(rows_ref[...], jnp.concatenate(pair, 1)).astype(LOW)
        out_ref[x] = value[:, :cols]
        out_ref[x + 1] = value[:, cols:]


def heads_grad(rows, weight, cols, at):
    count, width = rows.shape
    zc, xs, piece, _ = weight.shape
    return call(
        heads_grad_body,
        struct((xs, count, cols), LOW),
        (1,),
        [
            whole((count, width)),
            pl.BlockSpec((zc, xs, piece, cols), lambda i: (0, 0, 0, at)),
        ],
        whole((xs, count, cols)),
        2 * count * width * xs * cols,
        5 * 2**20,
        vmem=60,
    )(rows, weight)


def weight_grad_body(rows_ref, grad_ref, *refs):
    out_ref = refs[-1]
    out_ref[...] = dot_0(rows_ref[...], grad_ref[...]).astype(LOW).reshape(out_ref.shape)


def weight_grads(rows, columns, total_cols, at, onto=None):
    count, width = rows.shape
    xs, _, cols = columns.shape
    piece = width // 8
    more = () if onto is None else (onto,)
    return call(
        weight_grad_body,
        struct((8, xs, piece, total_cols), LOW),
        (xs,),
        [whole((count, width)), pl.BlockSpec((None, count, cols), lambda i: (i, 0, 0))]
        + [pl.BlockSpec(memory_space=pl.ANY)] * len(more),
        pl.BlockSpec((8, None, piece, cols), lambda i: (0, i, 0, at)),
        2 * count * width * xs * cols,
        15 * 2**20,
        vmem=60,
        aliases={2: 0} if more else None,
    )(rows, columns, *more)


def add_up(total, term):
    @pl.when(pl.program_id(0) == 0)
    def _():
        total[...] = term

    @pl.when(pl.program_id(0) > 0)
    def _():
        total[...] += term


def ffn_first_body(
    place_ref, norm_ref, cot_ref, up_ref, down_ref, bias_ref,
    hidden_ref, grad_up_ref, norm_grad_ref, bias_grad_ref, total,
):
    width, cols = norm_ref.shape[1], up_ref.shape[-1]
    up_w = up_ref[...].reshape(width, cols)
    up = dot(norm_ref[...], up_w) + bias_ref[...]
    normal = 0.5 * (1.0 + lax.erf(up * 0.7071067811865476))
    hidden_ref[...] = (up * normal).astype(LOW)
    slope = normal + up * (jnp.exp(-0.5 * up * up) * 0.3989422804014327)
    grad_up = (dot(cot_ref[...], down_ref[...].reshape(width, cols)) * slope).astype(LOW)
    grad_up_ref[...] = grad_up
    bias_grad_ref[...] = jnp.sum(grad_up.astype(WIDE), 0, keepdims=True)
    add_up(total, dot_t(grad_up, up_w))

    @pl.when(pl.program_id(0) == pl.num_programs(0) - 1)
    def _():
        store_rows(norm_grad_ref, place_ref, total[...].astype(LOW))


def ffn_first(places, norm_rows, cot_rows, weight, bias):
    count, width = norm_rows.shape
    zc, xs, piece, cols = weight.shape
    size = cols // 2
    rows = whole((count, width))
    vector = pl.BlockSpec((None, 1, size), lambda i, places: (places[RING + i], 0, 0))
    wide = pl.BlockSpec((count, size), lambda i, *_: (0, i))
    return call(
        ffn_first_body,
        (
            struct((count, xs * size), LOW),
            struct((count, xs * size), LOW),
            struct((count, width), LOW),
            struct((xs, 1, size), WIDE),
        ),
        (xs,),
        [
            rows,
            rows,
            pl.BlockSpec((zc, None, piece, size), lambda i, *_: (0, i, 0, 0)),
            pl.BlockSpec((zc, None, piece, size), lambda i, *_: (0, i, 0, 1)),
            vector,
        ],
        (wide, wide, rows, vector),
        6 * count * width * xs * size,
        25 * 2**20,
        scratch=[pltpu.VMEM((count, width), WIDE)],
        prefetch=1,
        vmem=56,
    )(places, norm_rows, cot_rows, weight, weight, bias)


def ffn_second_body(
    norm_ref, cot_ref, hidden_ref, grad_up_ref, down_ref, branch_ref, weight_grad_ref, total
):
    width, cols = norm_ref.shape[1], down_ref.shape[-1]
    zc, piece, _ = weight_grad_ref.shape
    hidden = hidden_ref[...]
    weight_grad_ref[:, :, :cols] = (
        dot_0(norm_ref[...], grad_up_ref[...]).astype(LOW).reshape(zc, piece, cols)
    )
    weight_grad_ref[:, :, cols:] = dot_0(cot_ref[...], hidden).astype(LOW).reshape(zc, piece, cols)
    add_up(total, dot_t(hidden, down_ref[...].reshape(width, cols)))

    @pl.when(pl.program_id(0) == pl.num_programs(0) - 1)
    def _():
        branch_ref[...] = total[...].astype(LOW)


def ffn_second(norm_rows, cot_rows, hidden, grad_up, weight):
    count, width = norm_rows.shape
    zc, xs, piece, cols = weight.shape
    size = cols // 2
    rows = whole((count, width))
    wide = pl.BlockSpec((count, size), lambda i: (0, i))
    return call(
        ffn_second_body,
        (struct((count, width), LOW), struct(weight.shape, LOW)),
        (xs,),
        [rows, rows, wide, wide, pl.BlockSpec((zc, None, piece, size), lambda i: (0, i, 0, 1))],
        (rows, pl.BlockSpec((zc, None, piece, cols), lambda i: (0, i, 0, 0))),
        6 * count * width * xs * size,
        40 * 2**20,
        scratch=[pltpu.VMEM((count, width), WIDE)],
        vmem=56,
    )(norm_rows, cot_rows, hidden, grad_up, weight)


def only_head(array, head):
    lane = lax.broadcasted_iota(jnp.int32, array.shape, 1)
    return jnp.where(lane // HEAD_DIM == head, array, jnp.zeros_like(array))


def allowed_keys(start, extent, live_count):
    q_place = start + lax.broadcasted_iota(jnp.int32, (SPAN, extent), 0)
    k_place = lax.broadcasted_iota(jnp.int32, (SPAN, extent), 1)
    return k_place <= jnp.minimum(q_place, live_count - 1)


def slot_of(place, own):
    apart = (place - own + RING) % RING
    return jnp.where(apart == 0, 0, jnp.where(apart == RING - 1, 1, apart + 1))


def load_ordered(blocks_ref, own, into):
    rows = blocks_ref.shape[2]
    for x in range(RING):
        for y in range(RING):
            at = (x * RING + y) * rows
            into[at : at + rows] = blocks_ref[x, slot_of(y, own)]


def store_ordered(blocks_ref, x, own, cols, value):
    rows = blocks_ref.shape[2]
    for y in range(RING):
        blocks_ref[x, slot_of(y, own), :, cols] = value[y * rows : (y + 1) * rows]


def attend_body(live_ref, qkv_ref, heads_ref, exact_ref, log_ref, qkv):
    live_count = live_ref[pl.program_id(0)]
    own = live_ref[pl.num_programs(0)]
    length = exact_ref.shape[0]
    width = exact_ref.shape[1]
    load_ordered(qkv_ref, own, qkv)
    key = qkv[:, width : 2 * width]
    value = qkv[:, 2 * width :]
    for span in range(length // SPAN):
        start, extent = span * SPAN, (span + 1) * SPAN
        here = slice(start, extent)

        @pl.when(start < live_count)
        def _():
            query = qkv[here, :width]
            allowed = allowed_keys(start, extent, live_count)
            mixed, logs = [], []
            for head in range(width // HEAD_DIM):
                scores = dot_t(only_head(query, head), key[:extent]) * HEAD_DIM**-0.5
                scores = jnp.where(allowed, scores, -1e9)
                top = jnp.max(scores, 1, keepdims=True)
                terms = jnp.exp(scores - top)
                denom = jnp.sum(terms, 1, keepdims=True)
                mixed.append(dot(terms.astype(LOW), value[:extent]) / denom)
                logs.append(top + jnp.log(denom))
            lane = lax.broadcasted_iota(jnp.int32, (SPAN, width), 1)
            out = jnp.where(lane < HEAD_DIM, mixed[0], mixed[1])
            exact_ref[here] = out
            log_ref[here] = jnp.where(lane < HEAD_DIM, logs[0], logs[1])
            store_ordered(heads_ref, span, own, slice(None), out.astype(LOW))

        @pl.when(start >= live_count)
        def _():
            exact_ref[here] = jnp.zeros((SPAN, width), WIDE)
            log_ref[here] = jnp.zeros((SPAN, width), WIDE)
            heads_ref[span] = jnp.zeros(heads_ref.shape[1:], LOW)


def row_block(rows, cols):
    return pl.BlockSpec((4, 4, None, rows, cols), lambda s, *_: (0, 0, s, 0, 0))


def attend(live_counts, qkv, width):
    xs, ys, seqs, rows, _ = qkv.shape
    length = xs * ys * rows
    flat = pl.BlockSpec((None, length, width), lambda s, *_: (s, 0, 0))
    return call(
        attend_body,
        (
            struct((xs, ys, seqs, rows, width), LOW),
            struct((seqs, length, width), WIDE),
            struct((seqs, length, width), WIDE),
        ),
        (seqs,),
        [row_block(rows, 3 * width)],
        (row_block(rows, width), flat, flat),
        4 * 10**9,
        4 * 2**20,
        scratch=[pltpu.VMEM((length, 3 * width), LOW)],
        prefetch=1,
    )(live_counts, qkv)


def attend_back_body(
    live_ref, qkv_ref, grad_ref, exact_ref, log_ref, out_ref, sum_ref,
    key_total, value_total, qkv, grads,
):
    live_count = live_ref[pl.program_id(0)]
    own = live_ref[pl.num_programs(0)]
    length, width = exact_ref.shape
    factor = HEAD_DIM**-0.5
    load_ordered(qkv_ref, own, qkv)
    load_ordered(grad_ref, own, grads)
    key = qkv[:, width : 2 * width]
    value = qkv[:, 2 * width :]
    key_total[...] = jnp.zeros_like(key_total)
    value_total[...] = jnp.zeros_like(value_total)
    sum_ref[...] = jnp.zeros_like(sum_ref)
    for span in range(length // SPAN):
        start, extent = span * SPAN, (span + 1) * SPAN
        here = slice(start, extent)

        @pl.when(start < live_count)
        def _():
            query = qkv[here, :width]
            grad = grads[here]
            inner = grad.astype(WIDE) * exact_ref[here]
            logs = log_ref[here]
            allowed = allowed_keys(start, extent, live_count)
            query_total = jnp.zeros((SPAN, width), WIDE)
            for head in range(width // HEAD_DIM):
                query_h = only_head(query, head)
                grad_h = only_head(grad, head)
                log_h = logs[:, head * HEAD_DIM : head * HEAD_DIM + 1]
                row_inner = jnp.sum(only_head(inner, head), 1, keepdims=True)
                scores = dot_t(query_h, key[:extent]) * factor
                probs = jnp.exp(jnp.where(allowed, scores, -1e9) - log_h)
                d_probs = dot_t(grad_h, value[:extent])
                value_total[:extent] += dot_0(probs.astype(LOW), grad_h)
                d_scores = (probs * (d_probs - row_inner)).astype(LOW)
                query_total += dot(d_scores, only_head(key[:extent], head))
                key_total[:extent] += dot_0(d_scores, query_h)
            out = (query_total * factor).astype(LOW)
            store_ordered(out_ref, span, own, slice(0, width), out)
            sum_ref[:, :width] += jnp.sum(out.astype(WIDE), 0, keepdims=True)

        @pl.when(start >= live_count)
        def _():
            out_ref[span, :, :, :width] = jnp.zeros(out_ref.shape[1:3] + (width,), LOW)

    key_grad = (key_total[...] * factor).astype(LOW)
    value_grad = value_total[...].astype(LOW)
    for span in range(RING):
        here = slice(span * SPAN, (span + 1) * SPAN)
        store_ordered(out_ref, span, own, slice(width, 2 * width), key_grad[here])
        store_ordered(out_ref, span, own, slice(2 * width, None), value_grad[here])
    sum_ref[:, 2 * width :] = jnp.sum(value_grad.astype(WIDE), 0, keepdims=True)


def attend_back(live_counts, qkv, grads, exact, logs):
    xs, ys, seqs, rows, _ = qkv.shape
    _, length, width = exact.shape
    flat = pl.BlockSpec((None, length, width), lambda s, *_: (s, 0, 0))
    return call(
        attend_back_body,
        (struct(qkv.shape, LOW), struct((seqs, 1, 3 * width), WIDE)),
        (seqs,),
        [row_block(rows, 3 * width), row_block(rows, width), flat, flat],
        (
            row_block(rows, 3 * width),
            pl.BlockSpec((None, 1, 3 * width), lambda s, *_: (s, 0, 0)),
        ),
        8 * 10**9,
        8 * 2**20,
        scratch=[
            pltpu.VMEM((length, width), WIDE),
            pltpu.VMEM((length, width), WIDE),
            pltpu.VMEM((length, 3 * width), LOW),
            pltpu.VMEM((length, width), LOW),
        ],
        prefetch=1,
    )(live_counts, qkv, grads, exact, logs)


def norm_rows(values, gain_vec, shift_vec):
    centered = values - jnp.mean(values, -1, keepdims=True)
    inverse = lax.rsqrt(jnp.mean(centered * centered, -1, keepdims=True) + 1e-05)
    return (centered * inverse * gain_vec + shift_vec).astype(LOW)


def pick_half(first_ref, second_ref):
    early = pl.program_id(0) < pl.num_programs(0) // 2
    return jnp.where(early, first_ref[...], second_ref[...])


def half_blocks(step, width):
    early = pl.BlockSpec((step, width), lambda i: (jnp.minimum(i, 1), 0))
    late = pl.BlockSpec((step, width), lambda i: (jnp.maximum(i - 2, 0), 0))
    return [early, late]


def add_norm_body(
    start_ref, first_after, second_after, first_before, second_before,
    rows_ref, keep_ref, bias_ref, gain_ref, shift_ref, out_ref, norm_ref,
):
    branch = start_ref[...].astype(WIDE) + pick_half(first_after, second_after).astype(WIDE)
    branch += pick_half(first_before, second_before).astype(WIDE)
    values = rows_ref[...].astype(WIDE) + keep_ref[...] * (branch + bias_ref[...])
    out_ref[...] = values
    centered = values - jnp.mean(values, 1, keepdims=True)
    inverse = lax.rsqrt(jnp.mean(centered * centered, 1, keepdims=True) + 1e-05)
    norm_ref[...] = (centered * inverse * gain_ref[...] + shift_ref[...]).astype(LOW)


def add_norm(parts, rows, keep, bias, gain, shift):
    own, width = rows.shape
    step = own // 4
    flat = pl.BlockSpec((step, width), lambda i: (i, 0))
    vector = pl.BlockSpec((1, width), lambda i: (0, 0))
    halves = half_blocks(step, width) * 2
    return call(
        add_norm_body,
        (struct((own, width), WIDE), struct((own, width), LOW)),
        (own // step,),
        [flat] + halves + [flat, pl.BlockSpec((step, 1), lambda i: (i, 0)), vector, vector, vector],
        (flat, flat),
        20 * own * width,
        4 * 2**20,
    )(*parts, rows, keep, *(v.reshape(1, width) for v in (bias, gain, shift)))


def norm_back_body(count, with_low, *refs):
    parts, (rows_ref, grad_ref, gain_ref) = refs[:count], refs[count : count + 3]
    refs = refs[count + 3 :]
    if count == 1:
        terms = [parts[0][i] for i in range(parts[0].shape[0])]
    else:
        terms = [parts[0][...], pick_half(*parts[1:3]), pick_half(*parts[3:5])]
    gradient = sum(term.astype(WIDE) for term in terms)
    values = rows_ref[...].astype(WIDE)
    centered = values - jnp.mean(values, 1, keepdims=True)
    inverse = lax.rsqrt(jnp.mean(centered * centered, 1, keepdims=True) + 1e-05)
    unit = centered * inverse
    scaled = gradient * gain_ref[...]
    out = grad_ref[...].astype(WIDE) + inverse * (
        scaled
        - jnp.mean(scaled, 1, keepdims=True)
        - unit * jnp.mean(scaled * unit, 1, keepdims=True)
    )
    sums = [jnp.sum(gradient * unit, 0, keepdims=True), jnp.sum(gradient, 0, keepdims=True)]
    if with_low:
        keep_ref, out_ref, low_ref, sum_ref = refs
        low = (keep_ref[...] * out).astype(LOW)
        low_ref[...] = low
        sums.append(jnp.sum(low.astype(WIDE), 0, keepdims=True))
    else:
        out_ref, sum_ref = refs
    out_ref[...] = out
    sums.append(jnp.zeros((sum_ref.shape[0] - len(sums), sum_ref.shape[1]), WIDE))
    add_up(sum_ref, jnp.concatenate(sums, 0))


def norm_back(parts, rows, grad, gain, keep=None):
    own, width = rows.shape
    step = own // 4
    flat = pl.BlockSpec((step, width), lambda i: (i, 0))
    sums = pl.BlockSpec((8, width), lambda i: (0, 0))
    if isinstance(parts, tuple):
        in_specs, args = [flat] + half_blocks(step, width) * 2, list(parts)
    else:
        in_specs = [pl.BlockSpec((parts.shape[0], step, width), lambda i: (0, i, 0))]
        args = [parts]
    count = len(args)
    in_specs += [flat, flat, pl.BlockSpec((1, width), lambda i: (0, 0))]
    args += [rows, grad, gain.reshape(1, width)]
    outs, specs = [struct((own, width), WIDE)], [flat]
    if keep is not None:
        in_specs.append(pl.BlockSpec((step, 1), lambda i: (i, 0)))
        args.append(keep)
        outs.append(struct((own, width), LOW))
        specs.append(flat)
    return call(
        partial(norm_back_body, count, keep is not None),
        tuple(outs + [struct((8, width), WIDE)]),
        (own // step,),
        in_specs,
        tuple(specs + [sums]),
        40 * own * width,
        6 * 2**20,
    )(*args)


def collect_vectors(vectors):
    flat = jnp.concatenate([v.reshape(-1) for v in vectors])
    return collect(flat.reshape(16, -1, 128), COLS)


def spread_vectors(part, sizes):
    flat = spread(part, COLS, 16).reshape(-1)
    pieces, start = [], 0
    for size in sizes:
        pieces.append(flat[start : start + size])
        start += size
    return pieces


def shards(
    tokens, cotangent, seq_lengths, exit_layers, layer_index,
    ln1_gain, ln1_shift, q_weight, q_bias, k_weight, v_weight, v_bias, out_weight, out_bias,
    ln2_gain, ln2_shift, up_weight, up_bias, down_weight, down_bias,
):
    seqs, own_rows, width = tokens.shape
    own = seqs * own_rows
    full_len = exit_layers.shape[1]
    x_at, y_at = lax.axis_index("x"), lax.axis_index("y")
    head_at = x_at * RING + y_at
    head_cols = q_weight.shape[1]
    ff_cols = up_weight.shape[1]

    positions = jnp.arange(full_len)
    live_all = (positions[None, :] < seq_lengths[:, None]) & (exit_layers > layer_index[0])
    live_counts = jnp.concatenate(
        [jnp.sum(live_all.astype(jnp.int32), 1), y_at.astype(jnp.int32).reshape(1)]
    )
    y_places, x_places = (
        [((at + apart) % RING).astype(jnp.int32) for apart in (0, RING - 1, 1, 2)]
        for at in (y_at, x_at)
    )
    places = jnp.stack(y_places + x_places)
    live_mine = lax.dynamic_slice_in_dim(live_all, head_at * own_rows, own_rows, 1)
    keep = live_mine.reshape(-1, 1).astype(WIDE)

    w_attn = gather_weight(
        jnp.concatenate([q_weight, k_weight, v_weight, out_weight], 1).astype(LOW)
    )
    w_ff = jnp.concatenate([up_weight, down_weight], 1).astype(LOW)

    inputs = tokens.astype(WIDE).reshape(own, width)
    flat_cot = cotangent.reshape(own, width)
    g_ffn = (keep * flat_cot.astype(WIDE)).astype(LOW)
    norm1 = ring_gather(norm_rows(inputs, ln1_gain, ln1_shift))
    norm1, w_ff = tie(norm1, [ring(w_ff, step, "x") for step in (0, 1, -1, 2)])
    w_ff = lax.all_gather(jnp.stack(w_ff), ROWS, axis=0)
    norm1, cot_rows = tie(norm1, ring_gather(g_ffn))

    def mine(vector, cols):
        return lax.dynamic_index_in_dim(vector.reshape(RING, RING, cols), y_at, 1, False)

    bias = jnp.concatenate(
        [mine(q_bias, head_cols), jnp.zeros((RING, head_cols), WIDE), mine(v_bias, head_cols)], 1
    ).reshape(RING, 1, 3 * head_cols)
    qkv = qkv_project(norm1, w_attn, bias)
    rows5 = (RING, RING, seqs, own_rows)
    qkv = swap(qkv, "x").reshape(rows5 + (3 * head_cols,))
    heads, exact, logs = attend(live_counts, qkv, head_cols)
    heads = swap(heads.reshape(RING, RING * own, head_cols), "x")
    middle, normed2 = add_norm(
        ring_sum_parts(out_project(heads, w_attn, 3, 4)),
        tokens.reshape(own, width), keep, out_bias, ln2_gain, ln2_shift,
    )
    norm2 = ring_gather(normed2)

    ff_bias = mine(up_bias, ff_cols).reshape(RING, 1, ff_cols)
    hidden, grad_up, g_norm2, up_bias_part = ffn_first(places, norm2, cot_rows, w_ff, ff_bias)
    g_norm2 = swap(g_norm2.reshape(RING, own, width), "y")
    g_norm2, branch2, ff_grad = tie(
        g_norm2, *ffn_second(norm2, cot_rows, hidden, grad_up, w_ff)
    )
    ff_grad = settle(ff_grad)
    grad_mid, g_attn, sums2 = norm_back(g_norm2, middle, flat_cot, ln2_gain, keep)
    attn_rows = ring_gather(g_attn)
    g_heads = heads_grad(attn_rows, w_attn, head_cols, 3)
    g_heads, branch2 = tie(swap(g_heads, "x").reshape(rows5 + (head_cols,)), branch2)
    branch2 = ring_terms(branch2.reshape(RING, own, width), "y")
    d_qkv, d_sums = attend_back(live_counts, qkv, g_heads, exact, logs)
    d_qkv, attn_rows = tie(d_qkv, attn_rows)
    attn_grad = weight_grads(attn_rows, heads, 4 * head_cols, 3)
    d_qkv = swap(d_qkv.reshape(RING, RING * own, 3 * head_cols), "x")

    up_bias_full = lax.dynamic_update_slice_in_dim(
        jnp.zeros((RING, RING, ff_cols), WIDE), up_bias_part.reshape(RING, 1, ff_cols), y_at, 1
    )
    early = (
        sums2[2],
        sums2[0],
        sums2[1],
        up_bias_full,
        jnp.sum(g_ffn.astype(WIDE), 0),
    )
    d_qkv, attn_grad, branch2 = tie(d_qkv, attn_grad, branch2)
    attn_grad = weight_grads(norm1, d_qkv, 4 * head_cols, 0, attn_grad)
    d_qkv, attn_grad = tie(d_qkv, attn_grad)
    attn_grad = settle(attn_grad)
    g_norm1, ff_grad = ring_sum_parts(out_project(d_qkv, w_attn, 0, 2), ff_grad)
    ff_grad = ring_collect(ff_grad, "x")
    grad_tokens, sums1 = norm_back(g_norm1, tokens.reshape(own, width), grad_mid, ln1_gain)
    grad_tokens = grad_tokens.reshape(tokens.shape)
    sums1, branch2 = tie(sums1, branch2)
    branch2 = sum(term.astype(WIDE) for term in branch2) + down_bias
    result = (middle + keep * branch2).astype(LOW).reshape(tokens.shape)
    d_sums = jnp.sum(d_sums, 0).reshape(3, head_cols)

    def placed(row):
        blank = jnp.zeros((RING * RING, head_cols), WIDE)
        return lax.dynamic_update_slice_in_dim(blank, row[None], head_at, 0)

    part = collect_vectors(early + (sums1[0], sums1[1], placed(d_sums[0]), placed(d_sums[2])))
    part, ff_grad = tie(part, ff_grad)
    sizes = (width, width, width, RING * RING * ff_cols) + (width,) * 5
    part, attn_grad = tie(jnp.sum(spread(part, ROWS, 8), 0), attn_grad)
    here = [lax.dynamic_index_in_dim(attn_grad, x_places[i], 0, False) for i in range(RING)]
    attn_grad = ring_collect(here, "x")
    totals = spread_vectors(part, sizes)
    out_bias_sum, ln2_gain_sum, ln2_shift_sum, up_bias_sum, down_bias_sum = totals[:5]
    ln1_gain_sum, ln1_shift_sum, q_bias_sum, v_bias_sum = totals[5:]
    return (
        result,
        grad_tokens,
        ln1_gain_sum,
        ln1_shift_sum,
        attn_grad[:, :head_cols],
        q_bias_sum,
        attn_grad[:, head_cols : 2 * head_cols],
        attn_grad[:, 2 * head_cols : 3 * head_cols],
        v_bias_sum,
        attn_grad[:, 3 * head_cols :],
        out_bias_sum,
        ln2_gain_sum,
        ln2_shift_sum,
        ff_grad[:, :ff_cols],
        up_bias_sum,
        ff_grad[:, ff_cols:],
        down_bias_sum,
    )


def solution(mesh):
    wide = Mesh(mesh.devices.reshape(4, 2, 4, 4), ("z", "c", "x", "y"))
    act = P(ROWS, COLS, None)
    weight = P(ROWS, COLS)
    vector = P()
    in_specs = (
        act, act, P(ROWS), P(ROWS, None), vector, vector, vector,
        weight, vector, weight, weight, vector, weight, vector, vector, vector,
        weight, vector, weight, vector,
    )
    out_specs = (
        act, act, vector, vector, weight, vector, weight, weight, vector, weight,
        vector, vector, vector, weight, vector, weight, vector,
    )
    return jax.shard_map(
        shards, mesh=wide, in_specs=in_specs, out_specs=out_specs, check_vma=False
    )
```

```python
from functools import partial

import jax
import jax.numpy as jnp
from jax import lax
from jax.experimental import pallas as pl
from jax.experimental.pallas import tpu as pltpu
from jax.sharding import Mesh
from jax.sharding import PartitionSpec as P

HEAD_DIM = 64
SPAN = 256
LOW = jnp.bfloat16
WIDE = jnp.float32
RING = 4
ROWS = ("z", "c")
COLS = ("x", "y")


def dot(left, right):
    return jnp.dot(left, right, preferred_element_type=WIDE)


def dot_t(left, right):
    return lax.dot_general(left, right, (((1,), (1,)), ((), ())), preferred_element_type=WIDE)


def dot_0(left, right):
    return lax.dot_general(left, right, (((0,), (0,)), ((), ())), preferred_element_type=WIDE)


def call(body, out_shape, grid, in_specs, out_specs, flops, traffic, scratch=(), prefetch=0, vmem=40, aliases=None):
    return pl.pallas_call(
        body,
        out_shape=out_shape,
        grid_spec=pltpu.PrefetchScalarGridSpec(
            num_scalar_prefetch=prefetch,
            grid=grid,
            in_specs=in_specs,
            out_specs=out_specs,
            scratch_shapes=list(scratch),
        ),
        compiler_params=pltpu.CompilerParams(vmem_limit_bytes=vmem * 2**20),
        input_output_aliases=aliases or {},
        cost_estimate=pl.CostEstimate(flops=flops, bytes_accessed=traffic, transcendentals=0),
    )


def whole(shape):
    return pl.BlockSpec(shape, lambda *_: (0,) * len(shape))


def struct(shape, dtype):
    return jax.ShapeDtypeStruct(shape, dtype)


def spread(array, axes, size):
    return lax.all_to_all(jnp.broadcast_to(array[None], (size,) + array.shape), axes, 0, 0)


def collect(parts, axes):
    return jnp.sum(lax.all_to_all(parts, axes, 0, 0).astype(WIDE), 0)


def swap(parts, axes):
    return lax.all_to_all(parts, axes, 0, 0)


def ring(array, step, axis="y"):
    if step == 0:
        return array
    return lax.ppermute(array, axis, [(i, (i + step) % RING) for i in range(RING)])


def ring_terms(parts, axis):
    return [parts[0]] + [ring(parts[slot], step, axis) for slot, step in ((1, -1), (2, 1), (3, 2))]


def ring_collect(parts, axis):
    return sum(term.astype(WIDE) for term in ring_terms(parts, axis))


def ring_gather(rows):
    half = rows.shape[0] // 2
    first, second = rows[:half], rows[half:]
    before_first, after_second = ring(first, 1), ring(second, -1)
    before_second, after_first = ring(second, 1), ring(first, -1)
    across_first, across_second = ring(before_first, 1), ring(after_second, -1)
    return jnp.concatenate(
        [
            first, second, before_first, before_second,
            after_first, after_second, across_first, across_second,
        ],
        0,
    )


def ring_sum_parts(rows, later=None):
    start, before_first, before_second, after_first, after_second, across_first, across_second = rows
    from_before, from_after = ring(across_first, 1), ring(across_second, -1)
    second_after, first_before = ring(after_second, 1), ring(before_first, -1)
    if later is not None:
        from_before, from_after, second_after, first_before, later = tie(
            from_before, from_after, second_after, first_before, later
        )
    first_after = ring((after_first.astype(WIDE) + from_before.astype(WIDE)).astype(LOW), 1)
    second_before = ring((before_second.astype(WIDE) + from_after.astype(WIDE)).astype(LOW), -1)
    came = (start, first_after, second_after, first_before, second_before)
    return came if later is None else (came, later)


def tie(*arrays):
    return lax.optimization_barrier(arrays)


def gather_weight(shard):
    full = lax.all_gather(shard, ("z", "c", "x"), axis=0)
    return full.reshape((8, 4) + shard.shape)


def settle(gradient):
    return lax.psum_scatter(gradient, ROWS, scatter_dimension=0)


def qkv_body(rows_ref, weight_ref, bias_ref, out_ref):
    weight = weight_ref[...].reshape(rows_ref.shape[1], -1)
    out_ref[...] = (dot(rows_ref[...], weight) + bias_ref[...]).astype(LOW)


def qkv_project(rows, weight, bias):
    count, width = rows.shape
    zc, xs, piece, _ = weight.shape
    cols = bias.shape[-1]
    return call(
        qkv_body,
        struct((xs, count, cols), LOW),
        (xs,),
        [
            whole((count, width)),
            pl.BlockSpec((zc, None, piece, cols), lambda i: (0, i, 0, 0)),
            pl.BlockSpec((None, 1, cols), lambda i: (i, 0, 0)),
        ],
        pl.BlockSpec((None, count, cols), lambda i: (i, 0, 0)),
        2 * count * width * xs * cols,
        10 * 2**20,
        vmem=60,
    )(rows, weight, bias)


def out_body(heads_ref, weight_ref, *out_refs):
    count, _, piece, _ = weight_ref.shape
    for block in range(count):
        value = dot_t(heads_ref[0], weight_ref[block, 0])
        for x in range(1, RING):
            value += dot_t(heads_ref[x], weight_ref[block, x])
        value = value.astype(LOW)
        start = 0
        for out_ref in out_refs:
            rows = out_ref.shape[0]
            out_ref[:, block * piece : (block + 1) * piece] = value[start : start + rows]
            start += rows


def store_rows(out_ref, place_ref, value):
    rows = value.shape[0] // RING
    for slot in range(RING):
        at = pl.multiple_of(place_ref[slot] * rows, rows)
        out_ref[pl.ds(at, rows)] = value[slot * rows : (slot + 1) * rows]


def out_project(heads, weight, at, blocks):
    xs, count, cols = heads.shape
    zc, _, piece, _ = weight.shape
    own = count // RING
    sizes = (own,) + (own // 2,) * 6
    return call(
        out_body,
        tuple(struct((rows, zc * piece), LOW) for rows in sizes),
        (zc // blocks,),
        [
            whole(heads.shape),
            pl.BlockSpec((blocks, xs, piece, cols), lambda i: (i, 0, 0, at)),
        ],
        tuple(pl.BlockSpec((rows, blocks * piece), lambda i: (0, i)) for rows in sizes),
        2 * count * zc * piece * xs * cols,
        5 * 2**20,
        vmem=60,
    )(heads, weight)


def heads_grad_body(rows_ref, weight_ref, out_ref):
    cols = out_ref.shape[2]
    for x in range(0, RING, 2):
        pair = [weight_ref[:, x + i].reshape(rows_ref.shape[1], cols) for i in range(2)]
        value = dot(rows_ref[...], jnp.concatenate(pair, 1)).astype(LOW)
        out_ref[x] = value[:, :cols]
        out_ref[x + 1] = value[:, cols:]


def heads_grad(rows, weight, cols, at):
    count, width = rows.shape
    zc, xs, piece, _ = weight.shape
    return call(
        heads_grad_body,
        struct((xs, count, cols), LOW),
        (1,),
        [
            whole((count, width)),
            pl.BlockSpec((zc, xs, piece, cols), lambda i: (0, 0, 0, at)),
        ],
        whole((xs, count, cols)),
        2 * count * width * xs * cols,
        5 * 2**20,
        vmem=60,
    )(rows, weight)


def weight_grad_body(rows_ref, grad_ref, *refs):
    out_ref = refs[-1]
    out_ref[...] = dot_0(rows_ref[...], grad_ref[...]).astype(LOW).reshape(out_ref.shape)


def weight_grads(rows, columns, total_cols, at, onto=None):
    count, width = rows.shape
    xs, _, cols = columns.shape
    piece = width // 8
    more = () if onto is None else (onto,)
    return call(
        weight_grad_body,
        struct((8, xs, piece, total_cols), LOW),
        (xs,),
        [whole((count, width)), pl.BlockSpec((None, count, cols), lambda i: (i, 0, 0))]
        + [pl.BlockSpec(memory_space=pl.ANY)] * len(more),
        pl.BlockSpec((8, None, piece, cols), lambda i: (0, i, 0, at)),
        2 * count * width * xs * cols,
        15 * 2**20,
        vmem=60,
        aliases={2: 0} if more else None,
    )(rows, columns, *more)


def add_up(total, term):
    @pl.when(pl.program_id(0) == 0)
    def _():
        total[...] = term

    @pl.when(pl.program_id(0) > 0)
    def _():
        total[...] += term


def ffn_first_body(
    place_ref, norm_ref, cot_ref, up_ref, down_ref, bias_ref,
    hidden_ref, grad_up_ref, norm_grad_ref, bias_grad_ref, total,
):
    width, cols = norm_ref.shape[1], up_ref.shape[-1]
    up_w = up_ref[...].reshape(width, cols)
    up = dot(norm_ref[...], up_w) + bias_ref[...]
    normal = 0.5 * (1.0 + lax.erf(up * 0.7071067811865476))
    hidden_ref[...] = (up * normal).astype(LOW)
    slope = normal + up * (jnp.exp(-0.5 * up * up) * 0.3989422804014327)
    grad_up = (dot(cot_ref[...], down_ref[...].reshape(width, cols)) * slope).astype(LOW)
    grad_up_ref[...] = grad_up
    bias_grad_ref[...] = jnp.sum(grad_up.astype(WIDE), 0, keepdims=True)
    add_up(total, dot_t(grad_up, up_w))

    @pl.when(pl.program_id(0) == pl.num_programs(0) - 1)
    def _():
        store_rows(norm_grad_ref, place_ref, total[...].astype(LOW))


def ffn_first(places, norm_rows, cot_rows, weight, bias):
    count, width = norm_rows.shape
    zc, xs, piece, cols = weight.shape
    size = cols // 2
    rows = whole((count, width))
    vector = pl.BlockSpec((None, 1, size), lambda i, places: (places[RING + i], 0, 0))
    wide = pl.BlockSpec((count, size), lambda i, *_: (0, i))
    return call(
        ffn_first_body,
        (
            struct((count, xs * size), LOW),
            struct((count, xs * size), LOW),
            struct((count, width), LOW),
            struct((xs, 1, size), WIDE),
        ),
        (xs,),
        [
            rows,
            rows,
            pl.BlockSpec((zc, None, piece, size), lambda i, *_: (0, i, 0, 0)),
            pl.BlockSpec((zc, None, piece, size), lambda i, *_: (0, i, 0, 1)),
            vector,
        ],
        (wide, wide, rows, vector),
        6 * count * width * xs * size,
        25 * 2**20,
        scratch=[pltpu.VMEM((count, width), WIDE)],
        prefetch=1,
        vmem=56,
    )(places, norm_rows, cot_rows, weight, weight, bias)


def ffn_second_body(
    norm_ref, cot_ref, hidden_ref, grad_up_ref, down_ref, branch_ref, weight_grad_ref, total
):
    width, cols = norm_ref.shape[1], down_ref.shape[-1]
    zc, piece, _ = weight_grad_ref.shape
    hidden = hidden_ref[...]
    weight_grad_ref[:, :, :cols] = (
        dot_0(norm_ref[...], grad_up_ref[...]).astype(LOW).reshape(zc, piece, cols)
    )
    weight_grad_ref[:, :, cols:] = dot_0(cot_ref[...], hidden).astype(LOW).reshape(zc, piece, cols)
    add_up(total, dot_t(hidden, down_ref[...].reshape(width, cols)))

    @pl.when(pl.program_id(0) == pl.num_programs(0) - 1)
    def _():
        branch_ref[...] = total[...].astype(LOW)


def ffn_second(norm_rows, cot_rows, hidden, grad_up, weight):
    count, width = norm_rows.shape
    zc, xs, piece, cols = weight.shape
    size = cols // 2
    rows = whole((count, width))
    wide = pl.BlockSpec((count, size), lambda i: (0, i))
    return call(
        ffn_second_body,
        (struct((count, width), LOW), struct(weight.shape, LOW)),
        (xs,),
        [rows, rows, wide, wide, pl.BlockSpec((zc, None, piece, size), lambda i: (0, i, 0, 1))],
        (rows, pl.BlockSpec((zc, None, piece, cols), lambda i: (0, i, 0, 0))),
        6 * count * width * xs * size,
        40 * 2**20,
        scratch=[pltpu.VMEM((count, width), WIDE)],
        vmem=56,
    )(norm_rows, cot_rows, hidden, grad_up, weight)


def only_head(array, head):
    lane = lax.broadcasted_iota(jnp.int32, array.shape, 1)
    return jnp.where(lane // HEAD_DIM == head, array, jnp.zeros_like(array))


def allowed_keys(start, extent, live_count):
    q_place = start + lax.broadcasted_iota(jnp.int32, (SPAN, extent), 0)
    k_place = lax.broadcasted_iota(jnp.int32, (SPAN, extent), 1)
    return k_place <= jnp.minimum(q_place, live_count - 1)


def slot_of(place, own):
    apart = (place - own + RING) % RING
    return jnp.where(apart == 0, 0, jnp.where(apart == RING - 1, 1, apart + 1))


def load_ordered(blocks_ref, own, into):
    rows = blocks_ref.shape[2]
    for x in range(RING):
        for y in range(RING):
            at = (x * RING + y) * rows
            into[at : at + rows] = blocks_ref[x, slot_of(y, own)]


def store_ordered(blocks_ref, x, own, cols, value):
    rows = blocks_ref.shape[2]
    for y in range(RING):
        blocks_ref[x, slot_of(y, own), :, cols] = value[y * rows : (y + 1) * rows]


def attend_body(live_ref, qkv_ref, heads_ref, exact_ref, log_ref, qkv):
    live_count = live_ref[pl.program_id(0)]
    own = live_ref[pl.num_programs(0)]
    length = exact_ref.shape[0]
    width = exact_ref.shape[1]
    load_ordered(qkv_ref, own, qkv)
    key = qkv[:, width : 2 * width]
    value = qkv[:, 2 * width :]
    for span in range(length // SPAN):
        start, extent = span * SPAN, (span + 1) * SPAN
        here = slice(start, extent)

        @pl.when(start < live_count)
        def _():
            query = qkv[here, :width]
            allowed = allowed_keys(start, extent, live_count)
            mixed, logs = [], []
            for head in range(width // HEAD_DIM):
                scores = dot_t(only_head(query, head), key[:extent]) * HEAD_DIM**-0.5
                scores = jnp.where(allowed, scores, -1e9)
                top = jnp.max(scores, 1, keepdims=True)
                terms = jnp.exp(scores - top)
                denom = jnp.sum(terms, 1, keepdims=True)
                mixed.append(dot(terms.astype(LOW), value[:extent]) / denom)
                logs.append(top + jnp.log(denom))
            lane = lax.broadcasted_iota(jnp.int32, (SPAN, width), 1)
            out = jnp.where(lane < HEAD_DIM, mixed[0], mixed[1])
            exact_ref[here] = out
            log_ref[here] = jnp.where(lane < HEAD_DIM, logs[0], logs[1])
            store_ordered(heads_ref, span, own, slice(None), out.astype(LOW))

        @pl.when(start >= live_count)
        def _():
            exact_ref[here] = jnp.zeros((SPAN, width), WIDE)
            log_ref[here] = jnp.zeros((SPAN, width), WIDE)
            heads_ref[span] = jnp.zeros(heads_ref.shape[1:], LOW)


def row_block(rows, cols):
    return pl.BlockSpec((4, 4, None, rows, cols), lambda s, *_: (0, 0, s, 0, 0))


def attend(live_counts, qkv, width):
    xs, ys, seqs, rows, _ = qkv.shape
    length = xs * ys * rows
    flat = pl.BlockSpec((None, length, width), lambda s, *_: (s, 0, 0))
    return call(
        attend_body,
        (
            struct((xs, ys, seqs, rows, width), LOW),
            struct((seqs, length, width), WIDE),
            struct((seqs, length, width), WIDE),
        ),
        (seqs,),
        [row_block(rows, 3 * width)],
        (row_block(rows, width), flat, flat),
        4 * 10**9,
        4 * 2**20,
        scratch=[pltpu.VMEM((length, 3 * width), LOW)],
        prefetch=1,
    )(live_counts, qkv)


def attend_back_body(
    live_ref, qkv_ref, grad_ref, exact_ref, log_ref, out_ref, sum_ref,
    key_total, value_total, qkv, grads,
):
    live_count = live_ref[pl.program_id(0)]
    own = live_ref[pl.num_programs(0)]
    length, width = exact_ref.shape
    factor = HEAD_DIM**-0.5
    load_ordered(qkv_ref, own, qkv)
    load_ordered(grad_ref, own, grads)
    key = qkv[:, width : 2 * width]
    value = qkv[:, 2 * width :]
    key_total[...] = jnp.zeros_like(key_total)
    value_total[...] = jnp.zeros_like(value_total)
    sum_ref[...] = jnp.zeros_like(sum_ref)
    for span in range(length // SPAN):
        start, extent = span * SPAN, (span + 1) * SPAN
        here = slice(start, extent)

        @pl.when(start < live_count)
        def _():
            query = qkv[here, :width]
            grad = grads[here]
            inner = grad.astype(WIDE) * exact_ref[here]
            logs = log_ref[here]
            allowed = allowed_keys(start, extent, live_count)
            query_total = jnp.zeros((SPAN, width), WIDE)
            for head in range(width // HEAD_DIM):
                query_h = only_head(query, head)
                grad_h = only_head(grad, head)
                log_h = logs[:, head * HEAD_DIM : head * HEAD_DIM + 1]
                row_inner = jnp.sum(only_head(inner, head), 1, keepdims=True)
                scores = dot_t(query_h, key[:extent]) * factor
                probs = jnp.exp(jnp.where(allowed, scores, -1e9) - log_h)
                d_probs = dot_t(grad_h, value[:extent])
                value_total[:extent] += dot_0(probs.astype(LOW), grad_h)
                d_scores = (probs * (d_probs - row_inner)).astype(LOW)
                query_total += dot(d_scores, only_head(key[:extent], head))
                key_total[:extent] += dot_0(d_scores, query_h)
            out = (query_total * factor).astype(LOW)
            store_ordered(out_ref, span, own, slice(0, width), out)
            sum_ref[:, :width] += jnp.sum(out.astype(WIDE), 0, keepdims=True)

        @pl.when(start >= live_count)
        def _():
            out_ref[span, :, :, :width] = jnp.zeros(out_ref.shape[1:3] + (width,), LOW)

    key_grad = (key_total[...] * factor).astype(LOW)
    value_grad = value_total[...].astype(LOW)
    for span in range(RING):
        here = slice(span * SPAN, (span + 1) * SPAN)
        store_ordered(out_ref, span, own, slice(width, 2 * width), key_grad[here])
        store_ordered(out_ref, span, own, slice(2 * width, None), value_grad[here])
    sum_ref[:, 2 * width :] = jnp.sum(value_grad.astype(WIDE), 0, keepdims=True)


def attend_back(live_counts, qkv, grads, exact, logs):
    xs, ys, seqs, rows, _ = qkv.shape
    _, length, width = exact.shape
    flat = pl.BlockSpec((None, length, width), lambda s, *_: (s, 0, 0))
    return call(
        attend_back_body,
        (struct(qkv.shape, LOW), struct((seqs, 1, 3 * width), WIDE)),
        (seqs,),
        [row_block(rows, 3 * width), row_block(rows, width), flat, flat],
        (
            row_block(rows, 3 * width),
            pl.BlockSpec((None, 1, 3 * width), lambda s, *_: (s, 0, 0)),
        ),
        8 * 10**9,
        8 * 2**20,
        scratch=[
            pltpu.VMEM((length, width), WIDE),
            pltpu.VMEM((length, width), WIDE),
            pltpu.VMEM((length, 3 * width), LOW),
            pltpu.VMEM((length, width), LOW),
        ],
        prefetch=1,
    )(live_counts, qkv, grads, exact, logs)


def norm_rows(values, gain_vec, shift_vec):
    centered = values - jnp.mean(values, -1, keepdims=True)
    inverse = lax.rsqrt(jnp.mean(centered * centered, -1, keepdims=True) + 1e-05)
    return (centered * inverse * gain_vec + shift_vec).astype(LOW)


def pick_half(first_ref, second_ref):
    early = pl.program_id(0) < pl.num_programs(0) // 2
    return jnp.where(early, first_ref[...], second_ref[...])


def half_blocks(step, width):
    early = pl.BlockSpec((step, width), lambda i: (jnp.minimum(i, 1), 0))
    late = pl.BlockSpec((step, width), lambda i: (jnp.maximum(i - 2, 0), 0))
    return [early, late]


def add_norm_body(
    start_ref, first_after, second_after, first_before, second_before,
    rows_ref, keep_ref, bias_ref, gain_ref, shift_ref, out_ref, norm_ref,
):
    branch = start_ref[...].astype(WIDE) + pick_half(first_after, second_after).astype(WIDE)
    branch += pick_half(first_before, second_before).astype(WIDE)
    values = rows_ref[...].astype(WIDE) + keep_ref[...] * (branch + bias_ref[...])
    out_ref[...] = values
    centered = values - jnp.mean(values, 1, keepdims=True)
    inverse = lax.rsqrt(jnp.mean(centered * centered, 1, keepdims=True) + 1e-05)
    norm_ref[...] = (centered * inverse * gain_ref[...] + shift_ref[...]).astype(LOW)


def add_norm(parts, rows, keep, bias, gain, shift):
    own, width = rows.shape
    step = own // 4
    flat = pl.BlockSpec((step, width), lambda i: (i, 0))
    vector = pl.BlockSpec((1, width), lambda i: (0, 0))
    halves = half_blocks(step, width) * 2
    return call(
        add_norm_body,
        (struct((own, width), WIDE), struct((own, width), LOW)),
        (own // step,),
        [flat] + halves + [flat, pl.BlockSpec((step, 1), lambda i: (i, 0)), vector, vector, vector],
        (flat, flat),
        20 * own * width,
        4 * 2**20,
    )(*parts, rows, keep, *(v.reshape(1, width) for v in (bias, gain, shift)))


def norm_back_body(count, with_low, *refs):
    parts, (rows_ref, grad_ref, gain_ref) = refs[:count], refs[count : count + 3]
    refs = refs[count + 3 :]
    if count == 1:
        terms = [parts[0][i] for i in range(parts[0].shape[0])]
    else:
        terms = [parts[0][...], pick_half(*parts[1:3]), pick_half(*parts[3:5])]
    gradient = sum(term.astype(WIDE) for term in terms)
    values = rows_ref[...].astype(WIDE)
    centered = values - jnp.mean(values, 1, keepdims=True)
    inverse = lax.rsqrt(jnp.mean(centered * centered, 1, keepdims=True) + 1e-05)
    unit = centered * inverse
    scaled = gradient * gain_ref[...]
    out = grad_ref[...].astype(WIDE) + inverse * (
        scaled
        - jnp.mean(scaled, 1, keepdims=True)
        - unit * jnp.mean(scaled * unit, 1, keepdims=True)
    )
    sums = [jnp.sum(gradient * unit, 0, keepdims=True), jnp.sum(gradient, 0, keepdims=True)]
    if with_low:
        keep_ref, out_ref, low_ref, sum_ref = refs
        low = (keep_ref[...] * out).astype(LOW)
        low_ref[...] = low
        sums.append(jnp.sum(low.astype(WIDE), 0, keepdims=True))
    else:
        out_ref, sum_ref = refs
    out_ref[...] = out
    sums.append(jnp.zeros((sum_ref.shape[0] - len(sums), sum_ref.shape[1]), WIDE))
    add_up(sum_ref, jnp.concatenate(sums, 0))


def norm_back(parts, rows, grad, gain, keep=None):
    own, width = rows.shape
    step = own // 4
    flat = pl.BlockSpec((step, width), lambda i: (i, 0))
    sums = pl.BlockSpec((8, width), lambda i: (0, 0))
    if isinstance(parts, tuple):
        in_specs, args = [flat] + half_blocks(step, width) * 2, list(parts)
    else:
        in_specs = [pl.BlockSpec((parts.shape[0], step, width), lambda i: (0, i, 0))]
        args = [parts]
    count = len(args)
    in_specs += [flat, flat, pl.BlockSpec((1, width), lambda i: (0, 0))]
    args += [rows, grad, gain.reshape(1, width)]
    outs, specs = [struct((own, width), WIDE)], [flat]
    if keep is not None:
        in_specs.append(pl.BlockSpec((step, 1), lambda i: (i, 0)))
        args.append(keep)
        outs.append(struct((own, width), LOW))
        specs.append(flat)
    return call(
        partial(norm_back_body, count, keep is not None),
        tuple(outs + [struct((8, width), WIDE)]),
        (own // step,),
        in_specs,
        tuple(specs + [sums]),
        40 * own * width,
        6 * 2**20,
    )(*args)


def collect_vectors(vectors):
    flat = jnp.concatenate([v.reshape(-1) for v in vectors])
    return collect(flat.reshape(16, -1, 128), COLS)


def spread_vectors(part, sizes):
    flat = spread(part, COLS, 16).reshape(-1)
    pieces, start = [], 0
    for size in sizes:
        pieces.append(flat[start : start + size])
        start += size
    return pieces


def shards(
    tokens, cotangent, seq_lengths, exit_layers, layer_index,
    ln1_gain, ln1_shift, q_weight, q_bias, k_weight, v_weight, v_bias, out_weight, out_bias,
    ln2_gain, ln2_shift, up_weight, up_bias, down_weight, down_bias,
):
    seqs, own_rows, width = tokens.shape
    own = seqs * own_rows
    full_len = exit_layers.shape[1]
    x_at, y_at = lax.axis_index("x"), lax.axis_index("y")
    head_at = x_at * RING + y_at
    head_cols = q_weight.shape[1]
    ff_cols = up_weight.shape[1]

    positions = jnp.arange(full_len)
    live_all = (positions[None, :] < seq_lengths[:, None]) & (exit_layers > layer_index[0])
    live_counts = jnp.concatenate(
        [jnp.sum(live_all.astype(jnp.int32), 1), y_at.astype(jnp.int32).reshape(1)]
    )
    y_places, x_places = (
        [((at + apart) % RING).astype(jnp.int32) for apart in (0, RING - 1, 1, 2)]
        for at in (y_at, x_at)
    )
    places = jnp.stack(y_places + x_places)
    live_mine = lax.dynamic_slice_in_dim(live_all, head_at * own_rows, own_rows, 1)
    keep = live_mine.reshape(-1, 1).astype(WIDE)

    w_attn = gather_weight(
        jnp.concatenate([q_weight, k_weight, v_weight, out_weight], 1).astype(LOW)
    )
    w_ff = jnp.concatenate([up_weight, down_weight], 1).astype(LOW)

    inputs = tokens.astype(WIDE).reshape(own, width)
    flat_cot = cotangent.reshape(own, width)
    g_ffn = (keep * flat_cot.astype(WIDE)).astype(LOW)
    norm1 = ring_gather(norm_rows(inputs, ln1_gain, ln1_shift))
    norm1, w_ff = tie(norm1, [ring(w_ff, step, "x") for step in (0, 1, -1, 2)])
    w_ff = lax.all_gather(jnp.stack(w_ff), ROWS, axis=0)
    norm1, cot_rows = tie(norm1, ring_gather(g_ffn))

    def mine(vector, cols):
        return lax.dynamic_index_in_dim(vector.reshape(RING, RING, cols), y_at, 1, False)

    bias = jnp.concatenate(
        [mine(q_bias, head_cols), jnp.zeros((RING, head_cols), WIDE), mine(v_bias, head_cols)], 1
    ).reshape(RING, 1, 3 * head_cols)
    qkv = qkv_project(norm1, w_attn, bias)
    rows5 = (RING, RING, seqs, own_rows)
    qkv = swap(qkv, "x").reshape(rows5 + (3 * head_cols,))
    heads, exact, logs = attend(live_counts, qkv, head_cols)
    heads = swap(heads.reshape(RING, RING * own, head_cols), "x")
    middle, normed2 = add_norm(
        ring_sum_parts(out_project(heads, w_attn, 3, 4)),
        tokens.reshape(own, width), keep, out_bias, ln2_gain, ln2_shift,
    )
    norm2 = ring_gather(normed2)

    ff_bias = mine(up_bias, ff_cols).reshape(RING, 1, ff_cols)
    hidden, grad_up, g_norm2, up_bias_part = ffn_first(places, norm2, cot_rows, w_ff, ff_bias)
    g_norm2 = swap(g_norm2.reshape(RING, own, width), "y")
    g_norm2, branch2, ff_grad = tie(
        g_norm2, *ffn_second(norm2, cot_rows, hidden, grad_up, w_ff)
    )
    ff_grad = settle(ff_grad)
    grad_mid, g_attn, sums2 = norm_back(g_norm2, middle, flat_cot, ln2_gain, keep)
    attn_rows = ring_gather(g_attn)
    g_heads = heads_grad(attn_rows, w_attn, head_cols, 3)
    g_heads, branch2 = tie(swap(g_heads, "x").reshape(rows5 + (head_cols,)), branch2)
    branch2 = ring_terms(branch2.reshape(RING, own, width), "y")
    d_qkv, d_sums = attend_back(live_counts, qkv, g_heads, exact, logs)
    d_qkv, attn_rows = tie(d_qkv, attn_rows)
    attn_grad = weight_grads(attn_rows, heads, 4 * head_cols, 3)
    d_qkv = swap(d_qkv.reshape(RING, RING * own, 3 * head_cols), "x")

    up_bias_full = lax.dynamic_update_slice_in_dim(
        jnp.zeros((RING, RING, ff_cols), WIDE), up_bias_part.reshape(RING, 1, ff_cols), y_at, 1
    )
    early = (
        sums2[2],
        sums2[0],
        sums2[1],
        up_bias_full,
        jnp.sum(g_ffn.astype(WIDE), 0),
    )
    d_qkv, attn_grad, branch2 = tie(d_qkv, attn_grad, branch2)
    attn_grad = weight_grads(norm1, d_qkv, 4 * head_cols, 0, attn_grad)
    d_qkv, attn_grad = tie(d_qkv, attn_grad)
    attn_grad = settle(attn_grad)
    g_norm1, ff_grad = ring_sum_parts(out_project(d_qkv, w_attn, 0, 2), ff_grad)
    ff_grad = ring_collect(ff_grad, "x")
    grad_tokens, sums1 = norm_back(g_norm1, tokens.reshape(own, width), grad_mid, ln1_gain)
    grad_tokens = grad_tokens.reshape(tokens.shape)
    sums1, branch2 = tie(sums1, branch2)
    branch2 = sum(term.astype(WIDE) for term in branch2) + down_bias
    result = (middle + keep * branch2).astype(LOW).reshape(tokens.shape)
    d_sums = jnp.sum(d_sums, 0).reshape(3, head_cols)

    def placed(row):
        blank = jnp.zeros((RING * RING, head_cols), WIDE)
        return lax.dynamic_update_slice_in_dim(blank, row[None], head_at, 0)

    part = collect_vectors(early + (sums1[0], sums1[1], placed(d_sums[0]), placed(d_sums[2])))
    part, ff_grad = tie(part, ff_grad)
    sizes = (width, width, width, RING * RING * ff_cols) + (width,) * 5
    part, attn_grad = tie(jnp.sum(spread(part, ROWS, 8), 0), attn_grad)
    here = [lax.dynamic_index_in_dim(attn_grad, x_places[i], 0, False) for i in range(RING)]
    attn_grad = ring_collect(here, "x")
    totals = spread_vectors(part, sizes)
    out_bias_sum, ln2_gain_sum, ln2_shift_sum, up_bias_sum, down_bias_sum = totals[:5]
    ln1_gain_sum, ln1_shift_sum, q_bias_sum, v_bias_sum = totals[5:]
    return (
        result,
        grad_tokens,
        ln1_gain_sum,
        ln1_shift_sum,
        attn_grad[:, :head_cols],
        q_bias_sum,
        attn_grad[:, head_cols : 2 * head_cols],
        attn_grad[:, 2 * head_cols : 3 * head_cols],
        v_bias_sum,
        attn_grad[:, 3 * head_cols :],
        out_bias_sum,
        ln2_gain_sum,
        ln2_shift_sum,
        ff_grad[:, :ff_cols],
        up_bias_sum,
        ff_grad[:, ff_cols:],
        down_bias_sum,
    )


def solution(mesh):
    wide = Mesh(mesh.devices.reshape(4, 2, 4, 4), ("z", "c", "x", "y"))
    act = P(ROWS, COLS, None)
    weight = P(ROWS, COLS)
    vector = P()
    in_specs = (
        act, act, P(ROWS), P(ROWS, None), vector, vector, vector,
        weight, vector, weight, weight, vector, weight, vector, vector, vector,
        weight, vector, weight, vector,
    )
    out_specs = (
        act, act, vector, vector, weight, vector, weight, weight, vector, weight,
        vector, vector, vector, weight, vector, weight, vector,
    )
    return jax.shard_map(
        shards, mesh=wide, in_specs=in_specs, out_specs=out_specs, check_vma=False
    )
```
